32 devices in a mesh: dp: 4 (over y, x), phase: 4 (over z), mp: 2 (over core).
Axes of the slice: x: 2, y: 2, z: 4, core: 2. Of those that a mesh axis runs over, the one named last changes fastest.
Arguments:
- prompt_rows: bfloat16 [4, 8, 24, 8192], P('dp', 'phase', None, 'mp'), may hold values from -6 to 6
- row_dest: int32 [4, 8, 24], P(None, 'phase'), may hold values from 0 to 95, as said below
- segment_ids: int32 [4, 4, 48], P('dp'), may hold values from 0 to 5, never falling along the last dimension, each value on 1 to 24 neighbouring positions
- owner: int32 [4, 8, 3, 1], P('dp', 'phase'), may hold values from 0 to 3; in each aligned block of 3 rows (0 to 2, 3 to 5, ..., all dimensions but the last counted through in order) at most 2 rows name the same one
- gain: float32 [4, 8192], P('phase'), may hold values from 0.1 to 1.9
- w_query: bfloat16 [4, 8192, 4096], P('phase', 'dp', 'mp')
- w_key: bfloat16 [4, 8192, 512], P('phase', 'dp', 'mp')
- w_value: bfloat16 [4, 8192, 512], P('phase', 'dp', 'mp'), may hold values from -0.0625 to 0.0625
- w_out: bfloat16 [4, 4096, 8192], P('phase', 'dp', 'mp'), may hold values from -0.09375 to 0.09375
Outputs:
- embeddings: bfloat16 [4, 8, 8, 8192], P('dp', 'phase', None, 'mp')
The draws below stay inside these ranges and needn't reach their ends.
Inputs may be any that keep to these rules, and one draw needn't show every extreme that they name: `row_dest`: for each half micro-batch t, the values g * 24 + j over all loaders and rows name every group g and slot j exactly once; one loader sends at most 6 rows of one half micro-batch to one group, and every loader sends exactly 6 rows to some group. `segment_ids`: in each micro-batch every prompt number from 0 to 5 appears, on consecutive slots, at most 24 slots each. Within one half micro-batch of one group at most 2 prompts have the same owner, and in some half micro-batch exactly 2 do.
All inputs are finite; a program needn't handle non-finite values.
Results may differ from the reference program's by a relative error of at most 0.015.
Values may be sent and summed in bfloat16 or wider, within the bound.
No kernel may reach another device: no remote copies, remote signals or barrier semaphores. Data moves between devices by JAX's collectives and lax.ppermute only.
A program may use at most 192 MiB of HBM per device.

```python
import math
import jax
import jax.numpy as jnp
import numpy as np
from jax import lax

D = 8192
HD = 128
QH = 32
KVH = 4
MB = 48
HALF = 24
M = 4
HALVES = 8
SEGS = 6
PH = 3
RCAP = 2
N_DP = 4
N_PHASE = 4


def shared_projection(key):
    return jax.random.normal(key, (N_PHASE, D, KVH * HD), jnp.float32)


def draw_w_key(key, part):
    shared = shared_projection(key)
    return (shared * D ** (-0.5)).astype(jnp.bfloat16)


def draw_w_query(key, part):
    key = jax.random.fold_in(key, 5)
    fresh_draw = jax.random.normal(key, (N_PHASE, D, QH * HD), jnp.float32)
    return (fresh_draw * D ** (-0.5)).astype(jnp.bfloat16)


def draw_row_dest(key, part):
    key = jax.random.fold_in(key, 11)
    widest = HALF // min(N_DP, 4)
    remain = HALF - widest
    others = max(N_DP - 1, 1)
    offsets = jnp.arange(N_DP, dtype=jnp.int32)
    quotas = jnp.where(offsets == 0, widest, remain // others + (offsets - 1 < remain % others).astype(jnp.int32))
    bounds = jnp.cumsum(quotas)
    row_ids = jnp.arange(HALF, dtype=jnp.int32)
    offset_of = jnp.sum((row_ids[:, None] >= bounds[None, :]).astype(jnp.int32), axis=1)

    def one_half(half_key):
        keys_four = jax.random.split(half_key, 4)
        loader_perm = jax.random.permutation(keys_four[0], N_DP).astype(jnp.int32)
        group_perm = jax.random.permutation(keys_four[1], N_DP).astype(jnp.int32)
        dest_groups = group_perm[(offsets[:, None] + offset_of[None, :]) % N_DP]
        row_keys = jax.random.split(keys_four[2], N_DP)
        shuffled = jax.vmap(lambda row_key, groups_row: groups_row[jax.random.permutation(row_key, HALF)])(row_keys, dest_groups)
        by_loader = jnp.zeros_like(shuffled).at[loader_perm].set(shuffled)
        flat_groups = by_loader.reshape(-1)
        hits_table = (flat_groups[:, None] == offsets[None, :]).astype(jnp.int32)
        ranks = jnp.sum((jnp.cumsum(hits_table, axis=0) - hits_table) * hits_table, axis=1)
        slot_perms = jax.vmap(lambda slot_key: jax.random.permutation(slot_key, HALF))(jax.random.split(keys_four[3], N_DP)).astype(jnp.int32)
        slot_values = slot_perms[flat_groups, ranks]
        return (flat_groups * HALF + slot_values).reshape(N_DP, HALF)
    return jnp.transpose(jax.vmap(one_half)(jax.random.split(key, HALVES)), (1, 0, 2)).astype(jnp.int32)


def block_levels(key, shape, cuts, least, top_value):
    loudness = 1.0
    for axis_at, blocks in cuts:
        steps = jax.random.uniform(jax.random.fold_in(jax.random.fold_in(key, 6), axis_at), (blocks,), jnp.float32, least / len(cuts), top_value / len(cuts))
        loudness = loudness * jnp.repeat(jnp.exp(steps), shape[axis_at] // blocks).reshape((-1,) + (1,) * (len(shape) - 1 - axis_at))
    return loudness


def profile(amount, total, bound, lean):
    weights = [(1 << 20) // math.isqrt(standing ** lean) + 1 for standing in range(2, amount + 1)]
    surplus, given = total - bound - (amount - 1), [1] * (amount - 1)
    while surplus > 0:
        movable = [i for i in range(amount - 1) if given[i] < bound]
        mass, budget = sum([weights[i] for i in movable]), surplus
        for i in movable:
            addition = min(bound - given[i], max(1, budget * weights[i] // mass), surplus)
            given[i] = given[i] + addition
            surplus = surplus - addition
    return np.array([bound] + given)


def ragged_sizes(own_key, number_of, total, reach, slope):
    if number_of == 2:
        one = jax.random.randint(own_key, (), max(1, total - reach), min(reach, total - 1) + 1)
        return jnp.stack([one, total - one])
    tallies = jnp.asarray(profile(number_of, total, reach, slope), jnp.int32)
    pairs = (number_of - 1) // 2
    source_of, sink = tallies[1:1 + 2 * pairs:2], tallies[2:2 + 2 * pairs:2]
    slack = jnp.minimum(source_of - 1, reach - sink)
    passed = jax.random.randint(jax.random.fold_in(own_key, 1), (pairs,), 0, 1 << 20) % (slack + 1)
    tallies = tallies.at[1:1 + 2 * pairs:2].set(source_of - passed).at[2:2 + 2 * pairs:2].set(sink + passed)
    return tallies[jax.random.permutation(jax.random.fold_in(own_key, 2), number_of)]


def shared_out(stream_key, own, number, rows, number_of, top, most, lean):
    ranking = jax.random.permutation(stream_key, number_of)
    crowded, usual = portions_of(number_of, rows * top, most, lean, True), portions_of(number_of, rows * top, most, lean, False)
    places = jnp.arange(number_of)

    def named(sizes, rotation):
        used = int((sizes > 0).sum())
        fixed = max(1, used // 4)
        shifted = fixed + (places - fixed + rotation * (used - fixed)) % max(1, number_of - fixed)
        return jnp.zeros((number_of,), jnp.int32).at[ranking[jnp.where(places < fixed, places, shifted)]].set(jnp.asarray(sizes, jnp.int32))

    sizes = jnp.where(number % 4 == 0, named(crowded, number // 4), named(usual, number - number // 4 - 1))
    mixed = jax.random.permutation(jax.random.fold_in(own, 3), number_of)
    giver, receiver = mixed[0:number_of // 2 * 2:2], mixed[1:number_of // 2 * 2:2]
    slack = jnp.minimum(sizes[giver] - 1, most - sizes[receiver]) // 2
    slack = jnp.where((giver == ranking[0]) | (receiver == ranking[0]) | (sizes[receiver] == 0), 0, jnp.maximum(slack, 0))
    shifted = jax.random.randint(jax.random.fold_in(own, 4), (number_of // 2,), 0, 1 << 20) % (slack + 1)
    sizes = sizes.at[giver].add(-shifted).at[receiver].add(shifted)
    labels = jnp.searchsorted(jnp.cumsum(sizes), jnp.arange(rows * top), side="right").astype(jnp.int32)
    table = labels.reshape(top, rows).T
    table = table[jax.random.permutation(jax.random.fold_in(own, 1), rows)]
    rotation = jax.random.randint(jax.random.fold_in(own, 2), (rows, 1), 0, top)
    return jnp.take_along_axis(table, (jnp.arange(top)[None, :] + rotation) % top, axis=1)


def portions_of(number_of, total, most, skew, full):
    portions = [(1 << 20) // math.isqrt(grade ** skew) + 1 for grade in range(1, number_of + 1)]
    largest = most if full else min(most, max(-(-total // number_of), total * portions[0] // sum(portions)))
    least = 1 if total - largest >= number_of - 1 else 0
    given, spare = [largest] + [least] * (number_of - 1), total - largest - least * (number_of - 1)
    while spare > 0:
        movable = [i for i in range(1, number_of) if given[i] < largest] or [i for i in range(1, number_of) if given[i] < most]
        whole, remaining = sum([portions[i] for i in movable]), spare
        for i in movable:
            extra = min(most - given[i], max(1, remaining * portions[i] // whole), spare)
            given[i] = given[i] + extra
            spare = spare - extra
    return np.array(given)


def bell_draw(own_key, extent, width, limit, cuts=(), kind=jnp.bfloat16):
    level = block_levels(own_key, extent, cuts, -0.22, 0.18) if cuts else 1.0
    values = jax.random.normal(own_key, extent, jnp.float32) * width * level
    return jnp.minimum(jnp.maximum(values, -limit), limit).astype(kind)


def setup_inputs(seed: int = 0) -> dict:
    seeds = jax.random.split(jax.random.key(seed), 10)
    prompt_rows = bell_draw(seeds[0], (N_DP, HALVES, HALF, D), 1.0, 6.0, ((0, 4), (1, 4), (3, 2)))
    row_dest = draw_row_dest(jax.random.fold_in(seeds[9], 71), 0)
    segment_ids = jax.vmap(lambda own: jnp.searchsorted(jnp.cumsum(ragged_sizes(own, SEGS, MB, MB // 2, 2)), jnp.arange(MB), side="right"))(jax.random.split(seeds[2], N_DP * M)).reshape((N_DP, M, MB)).astype(jnp.int32)
    owner_keys = jax.random.split(jax.random.fold_in(seeds[3], 1), N_DP * HALVES * PH // PH)
    owner_turns = jax.random.permutation(jax.random.fold_in(seeds[3], 3), N_DP * HALVES * PH // PH)
    owner = jax.vmap(lambda own, number: shared_out(jax.random.fold_in(seeds[3], 2), own, number, PH, N_DP, 1, RCAP, 2))(owner_keys, owner_turns).reshape((N_DP, HALVES, PH, 1))
    gain = jnp.clip(1.0 + 0.18 * jax.random.normal(seeds[4], (N_PHASE, D), jnp.float32), 0.1, 1.9)
    w_query = draw_w_query(jax.random.fold_in(seeds[9], 71), 0)
    w_key = draw_w_key(jax.random.fold_in(seeds[9], 71), 0)
    w_value = bell_draw(seeds[7], (N_PHASE, D, KVH * HD), D ** -0.5, 0.0625, ((0, 4), (1, 4), (2, 2)))
    w_out = bell_draw(seeds[8], (N_PHASE, QH * HD, D), (QH * HD) ** -0.5, 0.09375, ((0, 4), (1, 4), (2, 2)))
    return {"prompt_rows": prompt_rows, "row_dest": row_dest, "segment_ids": segment_ids, "owner": owner, "gain": gain, "w_query": w_query, "w_key": w_key, "w_value": w_value, "w_out": w_out}


NORM_EPS = 1e-05

def pack_stream(prompt_rows, row_dest):
    flat_rows = prompt_rows.transpose(1, 0, 2, 3).reshape(HALVES, N_DP * HALF, D)
    flat_dest = row_dest.transpose(1, 0, 2).reshape(HALVES, N_DP * HALF).astype(jnp.int32)
    half_ids = jnp.broadcast_to(jnp.arange(HALVES, dtype=jnp.int32)[:, None], flat_dest.shape)
    packed = jnp.zeros((HALVES, N_DP * HALF, D), jnp.bfloat16).at[half_ids, flat_dest].set(flat_rows)
    packed = packed.reshape(HALVES, N_DP, HALF, D).transpose(1, 0, 2, 3)
    return packed.reshape(N_DP * M, MB, D)

def attend_batch(qkv_rows, segments):
    query_width = QH * HD
    pair_width = KVH * HD
    query_rows = qkv_rows[:, :query_width].astype(jnp.float32).reshape(MB, QH, HD)
    key_rows = qkv_rows[:, query_width:query_width + pair_width].astype(jnp.float32).reshape(MB, KVH, HD)
    value_rows = qkv_rows[:, query_width + pair_width:].astype(jnp.float32).reshape(MB, KVH, HD)
    key_rows = jnp.repeat(key_rows, QH // KVH, axis=1)
    value_rows = jnp.repeat(value_rows, QH // KVH, axis=1)
    scores = jnp.einsum('qhd,khd->hqk', query_rows, key_rows) * HD ** (-0.5)
    places = jnp.arange(MB, dtype=jnp.int32)
    allowed = (segments[:, None] == segments[None, :]) & (places[None, :] <= places[:, None])
    scores = jnp.where(allowed[None, :, :], scores, -jnp.inf)
    row_top = lax.optimization_barrier(jnp.max(scores, axis=2, keepdims=True))
    weights = jnp.exp(scores - row_top)
    probabilities = (weights / lax.optimization_barrier(jnp.sum(weights, axis=2, keepdims=True))).astype(jnp.bfloat16)
    mixed = jnp.einsum('hqk,khd->qhd', probabilities.astype(jnp.float32), value_rows)
    return mixed.astype(jnp.bfloat16).reshape(MB, QH * HD)

def apply_layer(hidden, gain_row, w_qkv, w_back, segments):
    tok_float = hidden.astype(jnp.float32).reshape(-1, D)
    squares = lax.optimization_barrier(jnp.sum(tok_float * tok_float, axis=1))
    gated = (tok_float * gain_row[None, :]).astype(jnp.bfloat16)
    qkv_sums = jnp.dot(gated, w_qkv, preferred_element_type=jnp.float32)
    qkv_rows = (qkv_sums * lax.rsqrt(squares / D + NORM_EPS)[:, None]).astype(jnp.bfloat16)
    mixed = jax.vmap(attend_batch)(qkv_rows.reshape(-1, MB, (QH + 2 * KVH) * HD), segments)
    updated = tok_float + jnp.dot(mixed.reshape(-1, QH * HD), w_back, preferred_element_type=jnp.float32)
    return updated.astype(jnp.bfloat16).reshape(hidden.shape)

def reference(prompt_rows, row_dest, segment_ids, owner, gain, w_query, w_key, w_value, w_out):
    hidden = pack_stream(prompt_rows, row_dest)
    segments = segment_ids.reshape(N_DP * M, MB).astype(jnp.int32)
    for section in range(N_PHASE):
        w_qkv = jnp.concatenate([w_query[section], w_key[section], w_value[section]], axis=1)
        hidden = apply_layer(hidden, gain[section], w_qkv, w_out[section], segments)
    segment_hits = (segments[:, None, :] == jnp.arange(SEGS, dtype=jnp.int32)[None, :, None]).astype(jnp.float32)
    segment_sums = jnp.einsum('bsn,bnd->bsd', segment_hits, hidden.astype(jnp.float32))
    counts = lax.optimization_barrier(jnp.sum(segment_hits, axis=2))
    pooled = (segment_sums / counts[:, :, None]).astype(jnp.bfloat16).reshape(N_DP, HALVES, PH, D)
    owner_ids = owner[..., 0].astype(jnp.int32)
    hits_table = (owner_ids[..., None] == jnp.arange(N_DP, dtype=jnp.int32)).astype(jnp.int32)
    ranks = lax.optimization_barrier(jnp.sum((jnp.cumsum(hits_table, axis=2) - hits_table) * hits_table, axis=-1))
    columns = jnp.arange(N_DP, dtype=jnp.int32)[:, None, None] * RCAP + ranks
    half_ids = jnp.broadcast_to(jnp.arange(HALVES, dtype=jnp.int32)[None, :, None], owner_ids.shape)
    result = jnp.zeros((N_DP, HALVES, N_DP * RCAP, D), jnp.bfloat16)
    return result.at[owner_ids, half_ids, columns].set(pooled)
```

```python
import functools

import jax
import jax.numpy as jnp
from jax import lax
from jax.experimental import pallas as pl
from jax.experimental.pallas import tpu as pltpu
from jax.sharding import PartitionSpec as P

D = 8192
HD = 128
QH = 32
KVH = 4
SEGS = 6
PH = 3


NORM_EPS = 1e-05


def from_behind(value, axis, steps):
    count = lax.axis_size(axis)
    initial, last = (max(0, -steps), min(count, count - steps))
    return lax.ppermute(value, axis, [(source, source + steps) for source in range(initial, last)])


def broadcast(value, axis, root):
    mine = lax.axis_index(axis) == root
    return lax.psum(jnp.where(mine, value, jnp.zeros_like(value)), axis)


def bucket_ranks(labels, buckets):
    hits_table = (labels[..., None] == jnp.arange(buckets, dtype=jnp.int32)).astype(jnp.int32)
    earlier = jnp.cumsum(hits_table, axis=-2) - hits_table
    return jnp.sum(earlier * hits_table, axis=-1)


def attend_heads(query, key_sel, value_sel, segments):
    head_dim = query.shape[2]
    scores = jnp.einsum("qhd,khd->hqk", query, key_sel, preferred_element_type=jnp.float32)
    scores = scores * head_dim ** (-0.5)
    places = jnp.arange(query.shape[0], dtype=jnp.int32)
    allowed = (segments[:, None] == segments[None, :]) & (places[None, :] <= places[:, None])
    scores = jnp.where(allowed[None, :, :], scores, -jnp.inf)
    row_top = jnp.max(scores, axis=2, keepdims=True)
    weights = jnp.exp(scores - row_top)
    probabilities = (weights / jnp.sum(weights, axis=2, keepdims=True)).astype(jnp.bfloat16)
    mixed = jnp.einsum("hqk,khd->qhd", probabilities, value_sel, preferred_element_type=jnp.float32)
    return mixed.astype(jnp.bfloat16).reshape(query.shape[0], -1)


def general_shards(prompt_rows, row_dest, segment_ids, owner, gain, w_query, w_key, w_value, w_out):
    dp_count = lax.axis_size("dp")
    phase_count = lax.axis_size("phase")
    group_here = lax.axis_index("dp")
    phase_here = lax.axis_index("phase")
    part_here = lax.axis_index("mp")
    halves_here = prompt_rows.shape[1]
    half_rows = prompt_rows.shape[2]
    feature_cols = prompt_rows.shape[3]
    batch_rows = halves_here * half_rows
    capacity = half_rows // min(dp_count, 4)
    half_index = jnp.arange(halves_here, dtype=jnp.int32)[:, None]
    dest_group = row_dest // half_rows
    dest_ranks = bucket_ranks(dest_group, dp_count)
    own_groups = lax.dynamic_index_in_dim(dest_group, group_here, 0, keepdims=False)
    own_ranks = lax.dynamic_index_in_dim(dest_ranks, group_here, 0, keepdims=False)
    send_at = own_groups * capacity + own_ranks
    outgoing = (
        jnp.zeros((halves_here, dp_count * capacity, feature_cols), jnp.bfloat16)
        .at[half_index, send_at]
        .set(prompt_rows[0])
    )
    incoming = lax.all_to_all(
        outgoing.reshape(halves_here, dp_count, capacity, feature_cols),
        "dp",
        split_axis=1,
        concat_axis=1,
        tiled=True,
    )
    source_ids = jnp.arange(dp_count, dtype=jnp.int32)[:, None, None]
    where_from = jnp.transpose(source_ids * capacity + dest_ranks, (1, 0, 2)).reshape(
        halves_here, -1
    )
    target = jnp.where(dest_group == group_here, row_dest % half_rows, half_rows)
    target = jnp.transpose(target, (1, 0, 2)).reshape(halves_here, -1)
    arrived = incoming.reshape(halves_here, dp_count * capacity, feature_cols)[
        half_index, where_from
    ]
    own_halves = (
        jnp.zeros((halves_here, half_rows, feature_cols), jnp.bfloat16)
        .at[half_index, target]
        .set(arrived, mode="drop")
    )
    own_batch = own_halves.reshape(batch_rows, feature_cols)
    waiting = lax.all_gather(own_batch, "phase", axis=0, tiled=True).reshape(
        phase_count, batch_rows, feature_cols
    )
    query_rows, key_rows, value_rows, back_rows = (
        lax.all_gather(w_query[0], "dp", axis=0, tiled=True),
        lax.all_gather(w_key[0], "dp", axis=0, tiled=True),
        lax.all_gather(w_value[0], "dp", axis=0, tiled=True),
        lax.all_gather(w_out[0], "dp", axis=0, tiled=True),
    )
    query_cols = query_rows.shape[1]
    pair_cols = key_rows.shape[1]
    w_proj = jnp.concatenate([query_rows, key_rows, value_rows], axis=1)
    proj_cols = w_proj.shape[1]
    heads_here = query_cols // HD
    group_size = QH // KVH
    key_heads = (part_here * heads_here + jnp.arange(heads_here, dtype=jnp.int32)) // group_size
    gain_row = gain[0]
    segment_table = segment_ids[0]
    last_phase = phase_count - 1
    prompt_numbers = jnp.arange(SEGS, dtype=jnp.int32)

    def advance(tick_index, loop_state):
        current, pooled = loop_state
        batch_index = tick_index - phase_here
        active = (batch_index >= 0) & (batch_index < phase_count)
        batch_slot = jnp.clip(batch_index, 0, phase_count - 1)
        fresh_rows = lax.dynamic_index_in_dim(
            waiting, jnp.clip(tick_index, 0, phase_count - 1), 0, keepdims=False
        )
        tok_rows = jnp.where(phase_here == 0, fresh_rows, current)
        tok_segments = lax.dynamic_index_in_dim(segment_table, batch_slot, 0, keepdims=False)
        tok_float = tok_rows.astype(jnp.float32)
        whole_rows = lax.all_gather(tok_rows, "mp", axis=1, tiled=True)
        whole_float = whole_rows.astype(jnp.float32)
        squares = jnp.sum(whole_float * whole_float, axis=1)
        projected = lax.cond(
            active,
            lambda: jnp.dot(
                (whole_float * gain_row[None, :]).astype(jnp.bfloat16),
                w_proj,
                preferred_element_type=jnp.float32,
            ),
            lambda: jnp.zeros((batch_rows, proj_cols), jnp.float32),
        )
        qkv_rows = (projected * lax.rsqrt(squares / D + NORM_EPS)[:, None]).astype(jnp.bfloat16)
        query = qkv_rows[:, :query_cols].reshape(batch_rows, heads_here, HD)
        key_own = qkv_rows[:, query_cols : query_cols + pair_cols]
        value_own = qkv_rows[:, query_cols + pair_cols :]
        key_all, value_all = (
            lax.all_gather(key_own, "mp", axis=1, tiled=True),
            lax.all_gather(value_own, "mp", axis=1, tiled=True),
        )
        key_sel = jnp.take(key_all.reshape(batch_rows, KVH, HD), key_heads, axis=1)
        value_sel = jnp.take(value_all.reshape(batch_rows, KVH, HD), key_heads, axis=1)
        mixed_own = attend_heads(query, key_sel, value_sel, tok_segments)
        mixed = lax.all_gather(mixed_own, "mp", axis=1, tiled=True)
        updated = lax.cond(
            active,
            lambda: (
                tok_float + jnp.dot(mixed, back_rows, preferred_element_type=jnp.float32)
            ).astype(jnp.bfloat16),
            lambda: tok_rows,
        )
        segment_hits = tok_segments[None, :] == prompt_numbers[:, None]
        segment_sums = jnp.dot(
            segment_hits.astype(jnp.bfloat16), updated, preferred_element_type=jnp.float32
        )
        counts = jnp.sum(segment_hits.astype(jnp.float32), axis=1)
        segment_means = segment_sums / counts[:, None]
        store_here = active & (phase_here == last_phase)
        stored = lax.dynamic_index_in_dim(pooled, batch_slot, 0, keepdims=False)
        pooled = lax.dynamic_update_index_in_dim(
            pooled, jnp.where(store_here, segment_means, stored), batch_slot, 0
        )
        passed = from_behind(updated, "phase", 1)
        return (passed, pooled)

    start_state = (
        jnp.zeros((batch_rows, feature_cols), jnp.bfloat16),
        jnp.zeros((phase_count, SEGS, feature_cols), jnp.float32),
    )
    current, pooled = lax.fori_loop(0, phase_count + phase_count - 1, advance, start_state)
    shared = broadcast(pooled.astype(jnp.bfloat16), "phase", last_phase)
    own_prompts = lax.dynamic_index_in_dim(shared, phase_here, 0, keepdims=False).reshape(
        halves_here, PH, feature_cols
    )
    owner_ids = owner[0, :, :, 0]
    return_cap = max(2, PH // min(dp_count, 4))
    send_slots = owner_ids * return_cap + bucket_ranks(owner_ids, dp_count)
    parcel = (
        jnp.zeros((halves_here, dp_count * return_cap, feature_cols), jnp.bfloat16)
        .at[half_index, send_slots]
        .set(own_prompts)
    )
    returned = lax.all_to_all(
        parcel.reshape(halves_here, dp_count, return_cap, feature_cols),
        "dp",
        split_axis=1,
        concat_axis=1,
        tiled=True,
    )
    return returned.reshape(1, halves_here, dp_count * return_cap, feature_cols)


LAG = 2
CHIPS = 4
GROUP_Q = QH // KVH
Q_COLS = GROUP_Q * HD
KV_AT = Q_COLS + 2 * HD
MSG_COLS = KV_AT + 128
RANKS = 8
TABLE_ROW = 6
F32 = jnp.float32
BF16 = jnp.bfloat16


def vmem_spec():
    return pl.BlockSpec(memory_space=pltpu.VMEM)


def smem_spec():
    return pl.BlockSpec(memory_space=pltpu.SMEM)


def hbm_spec():
    return pl.BlockSpec(memory_space=pltpu.HBM)


def call(kernel, outs, args, specs, scratch=(), limit=12):
    return pl.pallas_call(
        kernel,
        out_shape=outs,
        in_specs=specs,
        out_specs=[vmem_spec()] * len(outs),
        scratch_shapes=list(scratch),
        compiler_params=pltpu.CompilerParams(vmem_limit_bytes=limit * 1024 * 1024),
    )(*args)


def dot(a, b):
    return jnp.dot(a, b, preferred_element_type=F32)


def lane(start, size):
    return pl.ds(pl.multiple_of(start, size), size)


def iota(rows, cols, axis):
    return lax.broadcasted_iota(jnp.int32, (rows, cols), axis)


def as_column(row):
    count = row.shape[1]
    diagonal = iota(count, count, 0) == iota(count, count, 1)
    return jnp.sum(jnp.where(diagonal, row, 0), axis=1, keepdims=True)


def marks(hits):
    return hits.astype(F32).astype(BF16)


def pack_kernel(pos_ref, rows_ref, dest_ref, table_ref, *out_refs):
    chip = pos_ref[0]
    dest = dest_ref[pl.ds(chip, 1), :]
    count = dest.shape[1]
    half = count // 2
    group_row = dest // half
    group_col = as_column(group_row)
    source, here = (iota(count, count, 0), iota(count, count, 1))
    before = (group_col == group_row) & (source // half == here // half) & (source < here)
    rank = jnp.sum(jnp.where(before, 1, 0), axis=0, keepdims=True)
    target = group_row * (2 * RANKS) + (iota(1, count, 1) // half) * RANKS + rank
    width = out_refs[0].shape[1]
    message_row = iota(4 * RANKS, width, 0)
    for k in range(CHIPS):
        turn = chip ^ k
        core, block = (turn & 1, turn >> 1)
        pick = marks(iota(4 * RANKS, count, 0) + core * (4 * RANKS) == target)
        rows = dot(pick, rows_ref[:, lane(block * width, width)])
        rows = jnp.where(message_row == TABLE_ROW, table_ref[...], rows)
        out_refs[k][...] = rows.astype(BF16)


def unpack_kernel(pos_ref, m0, m1, m2, m3, dest_ref, out_ref, table_ref):
    chip, core = (pos_ref[0], pos_ref[2])
    count = dest_ref.shape[1]
    half = count // 2
    turn = 2 * (chip & 1) + core
    total = jnp.zeros(out_ref.shape, F32)
    table = jnp.zeros(table_ref.shape, F32)
    above, across = (iota(count, count, 0), iota(count, count, 1))
    for k, ref in enumerate((m0, m1, m2, m3)):
        loader = turn ^ k
        dest_row = dest_ref[pl.ds(loader, 1), :]
        group_row = dest_row // half
        group_col = as_column(group_row)
        earlier = (group_col == group_row) & (above // half == across // half) & (across < above)
        rank = jnp.sum(jnp.where(earlier, 1, 0), axis=1, keepdims=True)
        at = (group_col - 2 * core) * (2 * RANKS) + (iota(count, 1, 0) // half) * RANKS + rank
        from_message = marks(iota(count, 4 * RANKS, 1) == at)
        slot = (group_row - 2 * core) * count + (iota(1, count, 1) // half) * half + dest_row % half
        to_slot = marks(iota(2 * count, count, 0) == slot)
        rows = ref[...]
        total += dot(dot(to_slot, from_message).astype(BF16), rows)
        mine = (loader >> 1) == core
        table += jnp.where(mine, rows[TABLE_ROW : TABLE_ROW + 1].astype(F32), 0.0)
    out_ref[...] = total.astype(BF16)
    table_ref[...] = table


def pick_rows(pos_ref, wait_ref, recv_ref):
    if recv_ref is None:
        return wait_ref[...]
    if wait_ref is None:
        return recv_ref[...]
    return jnp.where(pos_ref[1] == 0, wait_ref[...], recv_ref[...])


def project_kernel(has_wait, has_recv, pos_ref, *refs):
    refs = list(refs)
    wait_ref = refs.pop(0) if has_wait else None
    recv_ref = refs.pop(0) if has_recv else None
    gain_ref, *sources, out_ref, buf, sems = refs
    chip, core = (pos_ref[0], pos_ref[2])
    copies = {}
    for part in range(2):
        at = 0
        for i, source in enumerate(sources[3 * part : 3 * part + 3]):
            width = source.shape[2]
            step = min(width, 512)
            for start in range(0, width, step):
                place = buf.at[part, :, pl.ds(at + start, step)]
                copy = pltpu.make_async_copy(
                    source.at[0, :, pl.ds(start, step)], place, sems.at[len(copies)]
                )
                copy.start()
                copies[part, i, start] = (copy, at + start, step)
            at += width
    rows = pick_rows(pos_ref, wait_ref, recv_ref).astype(F32)
    depth = rows.shape[1]
    gated = (rows * gain_ref[:, lane(chip * depth, depth)]).astype(BF16)
    squares = jnp.sum(rows * rows, axis=1, keepdims=True)
    high = squares.astype(BF16).astype(F32)
    tail = jnp.where(iota(rows.shape[0], 128, 1) < 64, high, squares - high).astype(BF16)
    for (part, i, start), (copy, at, step) in copies.items():
        copy.wait()
        first = 2 * (core if part == 0 else 1 - core)
        result = dot(gated, buf[part, :, at : at + step]).astype(BF16)
        if i == 0:
            inside = start % Q_COLS
            out_ref[first + start // Q_COLS, :, inside : inside + step] = result
        else:
            inside = Q_COLS + (i - 1) * HD
            for j in range(2):
                out_ref[first + j, :, inside : inside + HD] = result[:, j * HD : (j + 1) * HD]
    for e in range(CHIPS):
        out_ref[e, :, KV_AT:] = tail


def means(table_ref, chunk, count, rows):
    number = iota(16, count, 0)
    segment = table_ref[:, chunk * 128 : chunk * 128 + count].astype(jnp.int32)
    hits = segment == (number % 8) + SEGS * (number // 8)
    hits = hits & (number % 8 < SEGS)
    counts = jnp.sum(jnp.where(hits, 1.0, 0.0), axis=1, keepdims=True)
    return dot(marks(hits), rows) / jnp.maximum(counts, 1.0)


def attend_kernel(features, pool_chunk, pos_ref, slot_ref, got_ref, table_ref, *refs):
    own_ref, other_ref, out_ref, buf, sems = refs
    core = pos_ref[2]
    copies = []
    step = own_ref.shape[2] // 4
    for part, source in enumerate((own_ref, other_ref)):
        for i in range(4):
            piece = pl.ds(i * step, step)
            copy = pltpu.make_async_copy(source.at[0, :, piece], buf.at[part, :, piece], sems.at[4 * part + i])
            copy.start()
            copies.append(copy)
    count = got_ref.shape[1]
    sums = got_ref[0].astype(F32)
    for e in range(1, CHIPS):
        sums += got_ref[e].astype(F32)
    tail = sums[:, KV_AT:]
    squares = tail[:, 0:1] + tail[:, 64:65]
    scaled = (sums[:, :KV_AT] * lax.rsqrt(squares / features + NORM_EPS)).astype(BF16)
    query = jnp.concatenate([scaled[:, h * HD : (h + 1) * HD] for h in range(GROUP_Q)], axis=0)
    key = scaled[:, Q_COLS : Q_COLS + HD]
    value = scaled[:, Q_COLS + HD :]
    scores = lax.dot_general(query, key, (((1,), (1,)), ((), ())), preferred_element_type=F32)
    scores = (scores * HD ** (-0.5)).reshape(GROUP_Q, count, count)
    segment = table_ref[:, lane(slot_ref[0] * 128, 128)][:, :count].astype(jnp.int32)
    allowed = (as_column(segment) == segment) & (iota(count, count, 1) <= iota(count, count, 0))
    scores = jnp.where(allowed[None], scores, -jnp.inf)
    top = jnp.max(scores, axis=2, keepdims=True)
    weights = jnp.exp(scores - top)
    probs = (weights / jnp.sum(weights, axis=2, keepdims=True)).astype(BF16)
    mixed = dot(probs.reshape(GROUP_Q * count, count), value).astype(BF16)
    mixed = jnp.concatenate([mixed[h * count : (h + 1) * count] for h in range(GROUP_Q)], axis=1)
    if pool_chunk is not None:
        mixed = means(table_ref, pool_chunk, count, mixed).astype(BF16)
    for i, copy in enumerate(copies):
        copy.wait()
        first = 2 * (core if i < 4 else 1 - core)
        inside = (i % 2) * step
        result = dot(mixed, buf[i // 4, :, (i % 4) * step : (i % 4 + 1) * step])
        out_ref[first + (i % 4) // 2, :, inside : inside + step] = result.astype(BF16)


def update_kernel(has_wait, has_recv, send, pool_chunk, pooled_sums, pos_ref, *refs):
    refs = list(refs)
    wait_ref = refs.pop(0) if has_wait else None
    recv_ref = refs.pop(0) if has_recv else None
    got_ref, table_ref, *out_refs = refs
    rows = pick_rows(pos_ref, wait_ref, recv_ref)
    if pooled_sums:
        total = means(table_ref, pool_chunk, rows.shape[0], rows)
    else:
        total = rows.astype(F32)
    for e in range(CHIPS):
        total += got_ref[e].astype(F32)
    hidden = total.astype(BF16)
    if send:
        out_refs.pop(0)[...] = hidden
    if pooled_sums:
        out_refs.pop(0)[...] = hidden
    elif pool_chunk is not None:
        out_refs.pop(0)[...] = means(table_ref, pool_chunk, rows.shape[0], hidden).astype(BF16)


def parcel_kernel(owner_at, pos_ref, p0, p1, p2, p3, table_ref, *out_refs):
    chip, phase, core = (pos_ref[0], pos_ref[1], pos_ref[2])
    rows = jnp.where(phase == 0, p0[...], p1[...])
    rows = jnp.where(phase < 2, rows, jnp.where(phase == 2, p2[...], p3[...]))
    count = rows.shape[0]
    own_row = table_ref[:, owner_at : owner_at + count].astype(jnp.int32) - 1
    own_col = as_column(own_row)
    above, across = (iota(count, count, 0), iota(count, count, 1))
    same = (above // 8 == across // 8) & ((above % 8 >= PH) == (across % 8 >= PH))
    earlier = (own_col == own_row) & same & (above < across)
    rank = jnp.sum(jnp.where(earlier, 1, 0), axis=0, keepdims=True)
    place = iota(1, count, 1)
    half = jnp.where(place % 8 >= PH, 1, 0)
    slot = half * 8 + (2 * core + place // 8) * 2 + rank
    turn = 2 * (chip & 1) + core
    for k in range(CHIPS):
        pick = marks((iota(16, count, 0) == slot) & (own_row == (turn ^ k)))
        out_refs[k][...] = dot(pick, rows).astype(BF16)


def deliver_kernel(pos_ref, m0, m1, m2, m3, out_ref):
    chip = pos_ref[0]
    width = m0.shape[1]
    out_ref[...] = jnp.zeros_like(out_ref)
    for k, ref in enumerate((m0, m1, m2, m3)):
        cols = lane(((chip ^ k) >> 1) * width, width)
        out_ref[:, cols] = out_ref[:, cols] + ref[...]


def chip_shards(prompt_rows, row_dest, segment_ids, owner, gain, w_query, w_key, w_value, w_out):
    chip, phase, core = (lax.axis_index("dp"), lax.axis_index("phase"), lax.axis_index("mp"))
    phases = lax.axis_size("phase")
    pos = jnp.stack([chip, phase, core]).astype(jnp.int32)
    halves, half_rows, cols_here = prompt_rows.shape[1:]
    batch = halves * half_rows
    features = 2 * cols_here
    block = features // CHIPS
    count = 2 * batch
    square = [(e, k) for e in range(CHIPS) for k in range(2)]

    def crosswise(value, k):
        pairs = [(2 * e + m, 2 * (2 * m + ((e ^ k) >> 1)) + ((e ^ k) & 1)) for e, m in square]
        return lax.ppermute(value, ("dp", "mp"), pairs)

    def homewards(value, k):
        pairs = [(2 * e + c, 2 * ((2 * (e & 1) + c) ^ k) + (e >> 1)) for e, c in square]
        return lax.ppermute(value, ("dp", "mp"), pairs)

    def across(value):
        return lax.all_to_all(value, "dp", split_axis=0, concat_axis=0)

    def swap(value):
        return lax.ppermute(value, "mp", [(0, 1), (1, 0)])

    with jax.named_scope("packing"):
        parity = chip % 2
        owner_at = phases * 128
        table = jnp.zeros((phases, 128), F32)
        numbers = (segment_ids[0] + SEGS * parity).astype(F32)
        table = lax.dynamic_update_slice(table, numbers, (0, batch * parity)).reshape(1, -1)
        owners = (owner.reshape(1, -1) + 1).astype(F32)
        last = lax.dynamic_update_slice(jnp.zeros((1, block - owner_at), F32), owners, (0, 8 * parity))
        table = jnp.concatenate([table, last], axis=1)
        dest = row_dest.reshape(CHIPS, batch)
        packed = call(
            pack_kernel,
            [jax.ShapeDtypeStruct((4 * RANKS, block), BF16)] * CHIPS,
            (pos, prompt_rows.reshape(batch, cols_here), dest, table),
            [smem_spec()] + [vmem_spec()] * 3,
        )
        arrived = [crosswise(value, k) for k, value in enumerate(packed)]
        start, table = call(
            unpack_kernel,
            [jax.ShapeDtypeStruct((count, block), BF16), jax.ShapeDtypeStruct((1, block), F32)],
            (pos, *arrived, dest),
            [smem_spec()] + [vmem_spec()] * 5,
        )
        waiting = [start] + [lax.ppermute(start, "phase", [(p, 0)]) for p in range(1, phases)]

    with jax.named_scope("weights"):
        def in_hbm(*values):
            return [pltpu.with_memory_space_constraint(value, pltpu.HBM) for value in values]

        w_in = in_hbm(w_query, w_key, w_value, swap(w_query), swap(w_key), swap(w_value))
        w_back = in_hbm(w_out, swap(w_out))
        in_cols = sum(w.shape[2] for w in w_in[:3])
        in_buffer = pltpu.VMEM((2, block, in_cols), BF16)
        back_buffer = pltpu.VMEM((2, *w_out.shape[1:]), BF16)

    hops, pooled = ({}, {})
    for slot in range(phases + LAG * (phases - 1)):
        has_wait, has_recv = (slot < phases, slot >= LAG)
        chunk = slot - LAG * (phases - 1)
        pool = chunk >= 0
        send = slot < phases + LAG * (phases - 2)
        early_pool = pool and not send
        pool_chunk = chunk if pool else None
        inputs = waiting[slot : slot + 1] + [hops[at] for at in (slot - LAG,) if has_recv]
        specs = [smem_spec()] + [vmem_spec()] * len(inputs)
        with jax.named_scope("project"):
            (sent,) = call(
                functools.partial(project_kernel, has_wait, has_recv),
                [jax.ShapeDtypeStruct((CHIPS, count, MSG_COLS), BF16)],
                (pos, *inputs, gain, *w_in),
                specs + [vmem_spec()] + [hbm_spec()] * 6,
                (in_buffer, pltpu.SemaphoreType.DMA((12,))),
                36,
            )
            got = across(sent)
        with jax.named_scope("attend"):
            at = jnp.clip(slot - LAG * phase, 0, phases - 1).astype(jnp.int32).reshape(1)
            rows = 16 if early_pool else count
            (sent,) = call(
                functools.partial(attend_kernel, features, pool_chunk if early_pool else None),
                [jax.ShapeDtypeStruct((CHIPS, rows, block), BF16)],
                (pos, at, got, table, *w_back),
                [smem_spec(), smem_spec(), vmem_spec(), vmem_spec()] + [hbm_spec()] * 2,
                (back_buffer, pltpu.SemaphoreType.DMA((8,))),
                36,
            )
            got = across(sent)
        with jax.named_scope("update"):
            outs = [jax.ShapeDtypeStruct((count, block), BF16)] * send
            outs = outs + [jax.ShapeDtypeStruct((16, block), BF16)] * pool
            out = list(
                call(
                    functools.partial(update_kernel, has_wait, has_recv, send, pool_chunk, early_pool),
                    outs,
                    (pos, *inputs, got, table),
                    specs + [vmem_spec()] * 2,
                )
            )
            if send:
                live = [p for p in range(phases - 1) if 0 <= slot - LAG * p < phases]
                hops[slot] = lax.ppermute(out.pop(0), "phase", [(p, p + 1) for p in live])
            if pool:
                pooled[chunk] = out.pop(0)

    with jax.named_scope("deliver"):
        shares = [lax.ppermute(pooled[m], "phase", [(phases - 1, m)]) for m in range(phases - 1)]
        parcels = call(
            functools.partial(parcel_kernel, owner_at),
            [jax.ShapeDtypeStruct((16, block), BF16)] * CHIPS,
            (pos, *shares, pooled[phases - 1], table),
            [smem_spec()] + [vmem_spec()] * 5,
        )
        final = [homewards(value, k) for k, value in enumerate(parcels)]
        (result,) = call(
            deliver_kernel,
            [jax.ShapeDtypeStruct((16, cols_here), BF16)],
            (pos, *final),
            [smem_spec()] + [vmem_spec()] * 4,
        )
    return result.reshape(1, 2, 8, cols_here)


def solution(mesh):
    in_specs = (
        P("dp", "phase", None, "mp"),
        P(None, "phase", None),
        P("dp", None, None),
        P("dp", "phase", None, None),
        P("phase", None),
        P("phase", "dp", "mp"),
        P("phase", "dp", "mp"),
        P("phase", "dp", "mp"),
        P("phase", "dp", "mp"),
    )
    out_specs = P("dp", "phase", None, "mp")
    square = mesh.shape["dp"] == CHIPS and mesh.shape["mp"] == 2 and mesh.shape["phase"] == 4
    shards = chip_shards if square else general_shards
    return jax.shard_map(shards, mesh=mesh, in_specs=in_specs, out_specs=out_specs, check_vma=False)
```

```python
import functools

import jax
import jax.numpy as jnp
from jax import lax
from jax.experimental import pallas as pl
from jax.experimental.pallas import tpu as pltpu
from jax.sharding import PartitionSpec as P

D = 8192
HD = 128
QH = 32
KVH = 4
SEGS = 6
PH = 3


NORM_EPS = 1e-05


def from_behind(value, axis, steps):
    count = lax.axis_size(axis)
    initial, last = (max(0, -steps), min(count, count - steps))
    return lax.ppermute(value, axis, [(source, source + steps) for source in range(initial, last)])


def broadcast(value, axis, root):
    mine = lax.axis_index(axis) == root
    return lax.psum(jnp.where(mine, value, jnp.zeros_like(value)), axis)


def bucket_ranks(labels, buckets):
    hits_table = (labels[..., None] == jnp.arange(buckets, dtype=jnp.int32)).astype(jnp.int32)
    earlier = jnp.cumsum(hits_table, axis=-2) - hits_table
    return jnp.sum(earlier * hits_table, axis=-1)


def attend_heads(query, key_sel, value_sel, segments):
    head_dim = query.shape[2]
    scores = jnp.einsum("qhd,khd->hqk", query, key_sel, preferred_element_type=jnp.float32)
    scores = scores * head_dim ** (-0.5)
    places = jnp.arange(query.shape[0], dtype=jnp.int32)
    allowed = (segments[:, None] == segments[None, :]) & (places[None, :] <= places[:, None])
    scores = jnp.where(allowed[None, :, :], scores, -jnp.inf)
    row_top = jnp.max(scores, axis=2, keepdims=True)
    weights = jnp.exp(scores - row_top)
    probabilities = (weights / jnp.sum(weights, axis=2, keepdims=True)).astype(jnp.bfloat16)
    mixed = jnp.einsum("hqk,khd->qhd", probabilities, value_sel, preferred_element_type=jnp.float32)
    return mixed.astype(jnp.bfloat16).reshape(query.shape[0], -1)


def general_shards(prompt_rows, row_dest, segment_ids, owner, gain, w_query, w_key, w_value, w_out):
    dp_count = lax.axis_size("dp")
    phase_count = lax.axis_size("phase")
    group_here = lax.axis_index("dp")
    phase_here = lax.axis_index("phase")
    part_here = lax.axis_index("mp")
    halves_here = prompt_rows.shape[1]
    half_rows = prompt_rows.shape[2]
    feature_cols = prompt_rows.shape[3]
    batch_rows = halves_here * half_rows
    capacity = half_rows // min(dp_count, 4)
    half_index = jnp.arange(halves_here, dtype=jnp.int32)[:, None]
    dest_group = row_dest // half_rows
    dest_ranks = bucket_ranks(dest_group, dp_count)
    own_groups = lax.dynamic_index_in_dim(dest_group, group_here, 0, keepdims=False)
    own_ranks = lax.dynamic_index_in_dim(dest_ranks, group_here, 0, keepdims=False)
    send_at = own_groups * capacity + own_ranks
    outgoing = (
        jnp.zeros((halves_here, dp_count * capacity, feature_cols), jnp.bfloat16)
        .at[half_index, send_at]
        .set(prompt_rows[0])
    )
    incoming = lax.all_to_all(
        outgoing.reshape(halves_here, dp_count, capacity, feature_cols),
        "dp",
        split_axis=1,
        concat_axis=1,
        tiled=True,
    )
    source_ids = jnp.arange(dp_count, dtype=jnp.int32)[:, None, None]
    where_from = jnp.transpose(source_ids * capacity + dest_ranks, (1, 0, 2)).reshape(
        halves_here, -1
    )
    target = jnp.where(dest_group == group_here, row_dest % half_rows, half_rows)
    target = jnp.transpose(target, (1, 0, 2)).reshape(halves_here, -1)
    arrived = incoming.reshape(halves_here, dp_count * capacity, feature_cols)[
        half_index, where_from
    ]
    own_halves = (
        jnp.zeros((halves_here, half_rows, feature_cols), jnp.bfloat16)
        .at[half_index, target]
        .set(arrived, mode="drop")
    )
    own_batch = own_halves.reshape(batch_rows, feature_cols)
    waiting = lax.all_gather(own_batch, "phase", axis=0, tiled=True).reshape(
        phase_count, batch_rows, feature_cols
    )
    query_rows, key_rows, value_rows, back_rows = (
        lax.all_gather(w_query[0], "dp", axis=0, tiled=True),
        lax.all_gather(w_key[0], "dp", axis=0, tiled=True),
        lax.all_gather(w_value[0], "dp", axis=0, tiled=True),
        lax.all_gather(w_out[0], "dp", axis=0, tiled=True),
    )
    query_cols = query_rows.shape[1]
    pair_cols = key_rows.shape[1]
    w_proj = jnp.concatenate([query_rows, key_rows, value_rows], axis=1)
    proj_cols = w_proj.shape[1]
    heads_here = query_cols // HD
    group_size = QH // KVH
    key_heads = (part_here * heads_here + jnp.arange(heads_here, dtype=jnp.int32)) // group_size
    gain_row = gain[0]
    segment_table = segment_ids[0]
    last_phase = phase_count - 1
    prompt_numbers = jnp.arange(SEGS, dtype=jnp.int32)

    def advance(tick_index, loop_state):
        current, pooled = loop_state
        batch_index = tick_index - phase_here
        active = (batch_index >= 0) & (batch_index < phase_count)
        batch_slot = jnp.clip(batch_index, 0, phase_count - 1)
        fresh_rows = lax.dynamic_index_in_dim(
            waiting, jnp.clip(tick_index, 0, phase_count - 1), 0, keepdims=False
        )
        tok_rows = jnp.where(phase_here == 0, fresh_rows, current)
        tok_segments = lax.dynamic_index_in_dim(segment_table, batch_slot, 0, keepdims=False)
        tok_float = tok_rows.astype(jnp.float32)
        whole_rows = lax.all_gather(tok_rows, "mp", axis=1, tiled=True)
        whole_float = whole_rows.astype(jnp.float32)
        squares = jnp.sum(whole_float * whole_float, axis=1)
        projected = lax.cond(
            active,
            lambda: jnp.dot(
                (whole_float * gain_row[None, :]).astype(jnp.bfloat16),
                w_proj,
                preferred_element_type=jnp.float32,
            ),
            lambda: jnp.zeros((batch_rows, proj_cols), jnp.float32),
        )
        qkv_rows = (projected * lax.rsqrt(squares / D + NORM_EPS)[:, None]).astype(jnp.bfloat16)
        query = qkv_rows[:, :query_cols].reshape(batch_rows, heads_here, HD)
        key_own = qkv_rows[:, query_cols : query_cols + pair_cols]
        value_own = qkv_rows[:, query_cols + pair_cols :]
        key_all, value_all = (
            lax.all_gather(key_own, "mp", axis=1, tiled=True),
            lax.all_gather(value_own, "mp", axis=1, tiled=True),
        )
        key_sel = jnp.take(key_all.reshape(batch_rows, KVH, HD), key_heads, axis=1)
        value_sel = jnp.take(value_all.reshape(batch_rows, KVH, HD), key_heads, axis=1)
        mixed_own = attend_heads(query, key_sel, value_sel, tok_segments)
        mixed = lax.all_gather(mixed_own, "mp", axis=1, tiled=True)
        updated = lax.cond(
            active,
            lambda: (
                tok_float + jnp.dot(mixed, back_rows, preferred_element_type=jnp.float32)
            ).astype(jnp.bfloat16),
            lambda: tok_rows,
        )
        segment_hits = tok_segments[None, :] == prompt_numbers[:, None]
        segment_sums = jnp.dot(
            segment_hits.astype(jnp.bfloat16), updated, preferred_element_type=jnp.float32
        )
        counts = jnp.sum(segment_hits.astype(jnp.float32), axis=1)
        segment_means = segment_sums / counts[:, None]
        store_here = active & (phase_here == last_phase)
        stored = lax.dynamic_index_in_dim(pooled, batch_slot, 0, keepdims=False)
        pooled = lax.dynamic_update_index_in_dim(
            pooled, jnp.where(store_here, segment_means, stored), batch_slot, 0
        )
        passed = from_behind(updated, "phase", 1)
        return (passed, pooled)

    start_state = (
        jnp.zeros((batch_rows, feature_cols), jnp.bfloat16),
        jnp.zeros((phase_count, SEGS, feature_cols), jnp.float32),
    )
    current, pooled = lax.fori_loop(0, phase_count + phase_count - 1, advance, start_state)
    shared = broadcast(pooled.astype(jnp.bfloat16), "phase", last_phase)
    own_prompts = lax.dynamic_index_in_dim(shared, phase_here, 0, keepdims=False).reshape(
        halves_here, PH, feature_cols
    )
    owner_ids = owner[0, :, :, 0]
    return_cap = max(2, PH // min(dp_count, 4))
    send_slots = owner_ids * return_cap + bucket_ranks(owner_ids, dp_count)
    parcel = (
        jnp.zeros((halves_here, dp_count * return_cap, feature_cols), jnp.bfloat16)
        .at[half_index, send_slots]
        .set(own_prompts)
    )
    returned = lax.all_to_all(
        parcel.reshape(halves_here, dp_count, return_cap, feature_cols),
        "dp",
        split_axis=1,
        concat_axis=1,
        tiled=True,
    )
    return returned.reshape(1, halves_here, dp_count * return_cap, feature_cols)


LAG = 2
CHIPS = 4
GROUP_Q = QH // KVH
Q_COLS = GROUP_Q * HD
KV_AT = Q_COLS + 2 * HD
MSG_COLS = KV_AT + 128
RANKS = 8
TABLE_ROW = 6
F32 = jnp.float32
BF16 = jnp.bfloat16


def vmem_spec():
    return pl.BlockSpec(memory_space=pltpu.VMEM)


def smem_spec():
    return pl.BlockSpec(memory_space=pltpu.SMEM)


def hbm_spec():
    return pl.BlockSpec(memory_space=pltpu.HBM)


def call(kernel, outs, args, specs, scratch=(), limit=12):
    return pl.pallas_call(
        kernel,
        out_shape=outs,
        in_specs=specs,
        out_specs=[vmem_spec()] * len(outs),
        scratch_shapes=list(scratch),
        compiler_params=pltpu.CompilerParams(vmem_limit_bytes=limit * 1024 * 1024),
    )(*args)


def dot(a, b):
    return jnp.dot(a, b, preferred_element_type=F32)


def lane(start, size):
    return pl.ds(pl.multiple_of(start, size), size)


def iota(rows, cols, axis):
    return lax.broadcasted_iota(jnp.int32, (rows, cols), axis)


def as_column(row):
    count = row.shape[1]
    diagonal = iota(count, count, 0) == iota(count, count, 1)
    return jnp.sum(jnp.where(diagonal, row, 0), axis=1, keepdims=True)


def marks(hits):
    return hits.astype(F32).astype(BF16)


def pack_kernel(pos_ref, rows_ref, dest_ref, table_ref, *out_refs):
    chip = pos_ref[0]
    dest = dest_ref[pl.ds(chip, 1), :]
    count = dest.shape[1]
    half = count // 2
    group_row = dest // half
    group_col = as_column(group_row)
    source, here = (iota(count, count, 0), iota(count, count, 1))
    before = (group_col == group_row) & (source // half == here // half) & (source < here)
    rank = jnp.sum(jnp.where(before, 1, 0), axis=0, keepdims=True)
    target = group_row * (2 * RANKS) + (iota(1, count, 1) // half) * RANKS + rank
    width = out_refs[0].shape[1]
    message_row = iota(4 * RANKS, width, 0)
    for k in range(CHIPS):
        turn = chip ^ k
        core, block = (turn & 1, turn >> 1)
        pick = marks(iota(4 * RANKS, count, 0) + core * (4 * RANKS) == target)
        rows = dot(pick, rows_ref[:, lane(block * width, width)])
        rows = jnp.where(message_row == TABLE_ROW, table_ref[...], rows)
        out_refs[k][...] = rows.astype(BF16)


def unpack_kernel(pos_ref, m0, m1, m2, m3, dest_ref, out_ref, table_ref):
    chip, core = (pos_ref[0], pos_ref[2])
    count = dest_ref.shape[1]
    half = count // 2
    turn = 2 * (chip & 1) + core
    total = jnp.zeros(out_ref.shape, F32)
    table = jnp.zeros(table_ref.shape, F32)
    above, across = (iota(count, count, 0), iota(count, count, 1))
    for k, ref in enumerate((m0, m1, m2, m3)):
        loader = turn ^ k
        dest_row = dest_ref[pl.ds(loader, 1), :]
        group_row = dest_row // half
        group_col = as_column(group_row)
        earlier = (group_col == group_row) & (above // half == across // half) & (across < above)
        rank = jnp.sum(jnp.where(earlier, 1, 0), axis=1, keepdims=True)
        at = (group_col - 2 * core) * (2 * RANKS) + (iota(count, 1, 0) // half) * RANKS + rank
        from_message = marks(iota(count, 4 * RANKS, 1) == at)
        slot = (group_row - 2 * core) * count + (iota(1, count, 1) // half) * half + dest_row % half
        to_slot = marks(iota(2 * count, count, 0) == slot)
        rows = ref[...]
        total += dot(dot(to_slot, from_message).astype(BF16), rows)
        mine = (loader >> 1) == core
        table += jnp.where(mine, rows[TABLE_ROW : TABLE_ROW + 1].astype(F32), 0.0)
    out_ref[...] = total.astype(BF16)
    table_ref[...] = table


def pick_rows(pos_ref, wait_ref, recv_ref):
    if recv_ref is None:
        return wait_ref[...]
    if wait_ref is None:
        return recv_ref[...]
    return jnp.where(pos_ref[1] == 0, wait_ref[...], recv_ref[...])


def place_result(pos_ref, head, keep_ref, send_ref, cols, result):
    chip, core = (pos_ref[0], pos_ref[2])
    gap = head ^ chip
    first = 1 + core
    at = jnp.where((gap == 0) | (gap == first), 0, 1)
    away = (gap == first) | (gap == 3)

    @pl.when(away)
    def _():
        send_ref[at, :, cols] = result

    @pl.when(jnp.logical_not(away))
    def _():
        keep_ref[at, :, cols] = result


def project_kernel(has_wait, has_recv, pos_ref, *refs):
    refs = list(refs)
    wait_ref = refs.pop(0) if has_wait else None
    recv_ref = refs.pop(0) if has_recv else None
    gain_ref, *sources, keep_ref, send_ref, buf, sems = refs
    own, other = (sources[:3], sources[3:])
    chip, core = (pos_ref[0], pos_ref[2])
    copies, at = ([], 0)
    for i, source in enumerate(other):
        width = source.shape[2]
        step = min(width, 512)
        for start in range(0, width, step):
            piece = source.at[0, :, pl.ds(start, step)]
            copy = pltpu.make_async_copy(piece, buf.at[:, pl.ds(at, step)], sems.at[len(copies)])
            copy.start()
            copies.append((copy, i, start, at, step))
            at += step
    rows = pick_rows(pos_ref, wait_ref, recv_ref).astype(F32)
    depth = rows.shape[1]
    gated = (rows * gain_ref[:, lane(chip * depth, depth)]).astype(BF16)
    squares = jnp.sum(rows * rows, axis=1, keepdims=True)
    high = squares.astype(BF16).astype(F32)
    tail = jnp.where(iota(rows.shape[0], 128, 1) < 64, high, squares - high).astype(BF16)

    def spread(part, i, start, step, result):
        result = result.astype(BF16)
        if i == 0:
            inside = start % Q_COLS
            cols = slice(inside, inside + step)
            place_result(pos_ref, 2 * part + start // Q_COLS, keep_ref, send_ref, cols, result)
        else:
            inside = Q_COLS + (i - 1) * HD
            for j in range(2):
                piece = result[:, j * HD : (j + 1) * HD]
                place_result(pos_ref, 2 * part + j, keep_ref, send_ref, slice(inside, inside + HD), piece)

    for i, source in enumerate(own):
        width = source.shape[2]
        step = min(width, 512)
        for start in range(0, width, step):
            spread(core, i, start, step, dot(gated, source[0, :, start : start + step]))
    for copy, i, start, at, step in copies:
        copy.wait()
        spread(1 - core, i, start, step, dot(gated, buf[:, at : at + step]))
    for j in range(2):
        keep_ref[j, :, KV_AT:] = tail
        send_ref[j, :, KV_AT:] = tail


def join_kernel(keep_ref, got_ref, out_ref):
    out_ref[...] = (keep_ref[1].astype(F32) + got_ref[1].astype(F32)).astype(BF16)


def means(table_ref, chunk, count, rows):
    number = iota(16, count, 0)
    segment = table_ref[:, chunk * 128 : chunk * 128 + count].astype(jnp.int32)
    hits = segment == (number % 8) + SEGS * (number // 8)
    hits = hits & (number % 8 < SEGS)
    counts = jnp.sum(jnp.where(hits, 1.0, 0.0), axis=1, keepdims=True)
    return dot(marks(hits), rows) / jnp.maximum(counts, 1.0)


def attend_kernel(features, pool_chunk, pos_ref, slot_ref, keep_in, first_in, second_in, table_ref, *refs):
    own_ref, other_ref, keep_ref, send_ref, buf, sems = refs
    core = pos_ref[2]
    copies = []
    step = own_ref.shape[2] // 4
    for i in range(4):
        piece = pl.ds(i * step, step)
        copy = pltpu.make_async_copy(other_ref.at[0, :, piece], buf.at[:, piece], sems.at[i])
        copy.start()
        copies.append(copy)
    sums = keep_in[0].astype(F32) + first_in[0].astype(F32) + second_in[...].astype(F32)
    count = sums.shape[0]
    tail = sums[:, KV_AT:]
    squares = tail[:, 0:1] + tail[:, 64:65]
    scaled = (sums[:, :KV_AT] * lax.rsqrt(squares / features + NORM_EPS)).astype(BF16)
    query = jnp.concatenate([scaled[:, h * HD : (h + 1) * HD] for h in range(GROUP_Q)], axis=0)
    key = scaled[:, Q_COLS : Q_COLS + HD]
    value = scaled[:, Q_COLS + HD :]
    scores = lax.dot_general(query, key, (((1,), (1,)), ((), ())), preferred_element_type=F32)
    scores = (scores * HD ** (-0.5)).reshape(GROUP_Q, count, count)
    segment = table_ref[:, lane(slot_ref[0] * 128, 128)][:, :count].astype(jnp.int32)
    allowed = (as_column(segment) == segment) & (iota(count, count, 1) <= iota(count, count, 0))
    scores = jnp.where(allowed[None], scores, -jnp.inf)
    top = jnp.max(scores, axis=2, keepdims=True)
    weights = jnp.exp(scores - top)
    probs = (weights / jnp.sum(weights, axis=2, keepdims=True)).astype(BF16)
    mixed = dot(probs.reshape(GROUP_Q * count, count), value).astype(BF16)
    mixed = jnp.concatenate([mixed[h * count : (h + 1) * count] for h in range(GROUP_Q)], axis=1)
    if pool_chunk is not None:
        mixed = means(table_ref, pool_chunk, count, mixed).astype(BF16)
    for i in range(8):
        part, source = (core, own_ref.at[0]) if i < 4 else (1 - core, buf)
        if i >= 4:
            copies[i - 4].wait()
        at = i % 4
        result = dot(mixed, source[:, at * step : (at + 1) * step]).astype(BF16)
        inside = (i % 2) * step
        place_result(pos_ref, 2 * part + at // 2, keep_ref, send_ref, slice(inside, inside + step), result)


def update_kernel(has_wait, has_recv, send, pool_chunk, pooled_sums, pos_ref, *refs):
    refs = list(refs)
    wait_ref = refs.pop(0) if has_wait else None
    recv_ref = refs.pop(0) if has_recv else None
    keep_in, first_in, second_in, table_ref, *out_refs = refs
    rows = pick_rows(pos_ref, wait_ref, recv_ref)
    if pooled_sums:
        total = means(table_ref, pool_chunk, rows.shape[0], rows)
    else:
        total = rows.astype(F32)
    total += keep_in[0].astype(F32) + first_in[0].astype(F32) + second_in[...].astype(F32)
    hidden = total.astype(BF16)
    if send:
        out_refs.pop(0)[...] = hidden
    if pooled_sums:
        out_refs.pop(0)[...] = hidden
    elif pool_chunk is not None:
        out_refs.pop(0)[...] = means(table_ref, pool_chunk, rows.shape[0], hidden).astype(BF16)


def parcel_kernel(owner_at, pos_ref, p0, p1, p2, p3, table_ref, *out_refs):
    chip, phase, core = (pos_ref[0], pos_ref[1], pos_ref[2])
    rows = jnp.where(phase == 0, p0[...], p1[...])
    rows = jnp.where(phase < 2, rows, jnp.where(phase == 2, p2[...], p3[...]))
    count = rows.shape[0]
    own_row = table_ref[:, owner_at : owner_at + count].astype(jnp.int32) - 1
    own_col = as_column(own_row)
    above, across = (iota(count, count, 0), iota(count, count, 1))
    same = (above // 8 == across // 8) & ((above % 8 >= PH) == (across % 8 >= PH))
    earlier = (own_col == own_row) & same & (above < across)
    rank = jnp.sum(jnp.where(earlier, 1, 0), axis=0, keepdims=True)
    place = iota(1, count, 1)
    half = jnp.where(place % 8 >= PH, 1, 0)
    slot = half * 8 + (2 * core + place // 8) * 2 + rank
    turn = 2 * (chip & 1) + core
    for k in range(CHIPS):
        pick = marks((iota(16, count, 0) == slot) & (own_row == (turn ^ k)))
        out_refs[k][...] = dot(pick, rows).astype(BF16)


def deliver_kernel(pos_ref, m0, m1, m2, m3, out_ref):
    chip = pos_ref[0]
    width = m0.shape[1]
    out_ref[...] = jnp.zeros_like(out_ref)
    for k, ref in enumerate((m0, m1, m2, m3)):
        cols = lane(((chip ^ k) >> 1) * width, width)
        out_ref[:, cols] = out_ref[:, cols] + ref[...]


def chip_shards(prompt_rows, row_dest, segment_ids, owner, gain, w_query, w_key, w_value, w_out):
    chip, phase, core = (lax.axis_index("dp"), lax.axis_index("phase"), lax.axis_index("mp"))
    phases = lax.axis_size("phase")
    pos = jnp.stack([chip, phase, core]).astype(jnp.int32)
    halves, half_rows, cols_here = prompt_rows.shape[1:]
    batch = halves * half_rows
    features = 2 * cols_here
    block = features // CHIPS
    count = 2 * batch
    square = [(e, k) for e in range(CHIPS) for k in range(2)]

    def crosswise(value, k):
        pairs = [(2 * e + m, 2 * (2 * m + ((e ^ k) >> 1)) + ((e ^ k) & 1)) for e, m in square]
        return lax.ppermute(value, ("dp", "mp"), pairs)

    def homewards(value, k):
        pairs = [(2 * e + c, 2 * ((2 * (e & 1) + c) ^ k) + (e >> 1)) for e, c in square]
        return lax.ppermute(value, ("dp", "mp"), pairs)

    def partner(value, first):
        pairs = [(2 * e + c, 2 * (e ^ (1 + c if first else 2 - c)) + c) for e, c in square]
        return lax.ppermute(value, ("dp", "mp"), pairs)

    def exchange(keep, send):
        first = partner(send, True)
        (joined,) = call(
            join_kernel,
            [jax.ShapeDtypeStruct(keep.shape[1:], BF16)],
            (keep, first),
            [vmem_spec()] * 2,
        )
        return (keep, first, partner(joined, False))

    def swap(value):
        return lax.ppermute(value, "mp", [(0, 1), (1, 0)])

    with jax.named_scope("packing"):
        parity = chip % 2
        owner_at = phases * 128
        table = jnp.zeros((phases, 128), F32)
        numbers = (segment_ids[0] + SEGS * parity).astype(F32)
        table = lax.dynamic_update_slice(table, numbers, (0, batch * parity)).reshape(1, -1)
        owners = (owner.reshape(1, -1) + 1).astype(F32)
        last = lax.dynamic_update_slice(jnp.zeros((1, block - owner_at), F32), owners, (0, 8 * parity))
        table = jnp.concatenate([table, last], axis=1)
        dest = row_dest.reshape(CHIPS, batch)
        packed = call(
            pack_kernel,
            [jax.ShapeDtypeStruct((4 * RANKS, block), BF16)] * CHIPS,
            (pos, prompt_rows.reshape(batch, cols_here), dest, table),
            [smem_spec()] + [vmem_spec()] * 3,
        )
        arrived = [crosswise(value, k) for k, value in enumerate(packed)]
        start, table = call(
            unpack_kernel,
            [jax.ShapeDtypeStruct((count, block), BF16), jax.ShapeDtypeStruct((1, block), F32)],
            (pos, *arrived, dest),
            [smem_spec()] + [vmem_spec()] * 5,
        )
        waiting = [start]

    with jax.named_scope("weights"):

        def held(space, values):
            return [pltpu.with_memory_space_constraint(value, space) for value in values]

        own_in = (w_query, w_key, w_value)
        first, *_ = lax.optimization_barrier((own_in, *arrived))
        other_in = [swap(value) for value in first]
        last, _ = lax.optimization_barrier((w_out, start))
        w_in = held(pltpu.VMEM, own_in) + held(pltpu.HBM, other_in)
        w_back = held(pltpu.VMEM, [w_out]) + held(pltpu.HBM, [swap(last)])
        in_buffer = pltpu.VMEM((block, sum(w.shape[2] for w in own_in)), BF16)
        back_buffer = pltpu.VMEM(w_out.shape[1:], BF16)

    hops, pooled = ({}, {})
    for slot in range(phases + LAG * (phases - 1)):
        has_wait, has_recv = (slot < phases, slot >= LAG)
        chunk = slot - LAG * (phases - 1)
        pool = chunk >= 0
        send = slot < phases + LAG * (phases - 2)
        early_pool = pool and not send
        pool_chunk = chunk if pool else None
        inputs = waiting[slot : slot + 1] + [hops[at] for at in (slot - LAG,) if has_recv]
        specs = [smem_spec()] + [vmem_spec()] * len(inputs)
        if slot < phases - 1:
            down = [(p, p - 1) for p in range(1, phases - slot)]
            waiting.append(lax.ppermute(waiting[slot], "phase", down))
        with jax.named_scope("project"):
            sent = call(
                functools.partial(project_kernel, has_wait, has_recv),
                [jax.ShapeDtypeStruct((2, count, MSG_COLS), BF16)] * 2,
                (pos, *inputs, gain, *w_in),
                specs + [vmem_spec()] * 4 + [hbm_spec()] * 3,
                (in_buffer, pltpu.SemaphoreType.DMA((6,))),
                24,
            )
            got = exchange(*sent)
        with jax.named_scope("attend"):
            at = jnp.clip(slot - LAG * phase, 0, phases - 1).astype(jnp.int32).reshape(1)
            rows = 16 if early_pool else count
            sent = call(
                functools.partial(attend_kernel, features, pool_chunk if early_pool else None),
                [jax.ShapeDtypeStruct((2, rows, block), BF16)] * 2,
                (pos, at, *got, table, *w_back),
                [smem_spec(), smem_spec()] + [vmem_spec()] * 5 + [hbm_spec()],
                (back_buffer, pltpu.SemaphoreType.DMA((4,))),
                24,
            )
            got = exchange(*sent)
        with jax.named_scope("update"):
            outs = [jax.ShapeDtypeStruct((count, block), BF16)] * send
            outs = outs + [jax.ShapeDtypeStruct((16, block), BF16)] * pool
            out = list(
                call(
                    functools.partial(update_kernel, has_wait, has_recv, send, pool_chunk, early_pool),
                    outs,
                    (pos, *inputs, *got, table),
                    specs + [vmem_spec()] * 4,
                )
            )
            if send:
                live = [p for p in range(phases - 1) if 0 <= slot - LAG * p < phases]
                hops[slot] = lax.ppermute(out.pop(0), "phase", [(p, p + 1) for p in live])
            if pool:
                pooled[chunk] = out.pop(0)

    with jax.named_scope("deliver"):
        shares = [lax.ppermute(pooled[m], "phase", [(phases - 1, m)]) for m in range(phases - 1)]
        parcels = call(
            functools.partial(parcel_kernel, owner_at),
            [jax.ShapeDtypeStruct((16, block), BF16)] * CHIPS,
            (pos, *shares, pooled[phases - 1], table),
            [smem_spec()] + [vmem_spec()] * 5,
        )
        final = [homewards(value, k) for k, value in enumerate(parcels)]
        (result,) = call(
            deliver_kernel,
            [jax.ShapeDtypeStruct((16, cols_here), BF16)],
            (pos, *final),
            [smem_spec()] + [vmem_spec()] * 4,
        )
    return result.reshape(1, 2, 8, cols_here)


def solution(mesh):
    in_specs = (
        P("dp", "phase", None, "mp"),
        P(None, "phase", None),
        P("dp", None, None),
        P("dp", "phase", None, None),
        P("phase", None),
        P("phase", "dp", "mp"),
        P("phase", "dp", "mp"),
        P("phase", "dp", "mp"),
        P("phase", "dp", "mp"),
    )
    out_specs = P("dp", "phase", None, "mp")
    square = mesh.shape["dp"] == CHIPS and mesh.shape["mp"] == 2 and mesh.shape["phase"] == 4
    shards = chip_shards if square else general_shards
    return jax.shard_map(shards, mesh=mesh, in_specs=in_specs, out_specs=out_specs, check_vma=False)
```

```python
import functools

import jax
import jax.numpy as jnp
from jax import lax
from jax.experimental import pallas as pl
from jax.experimental.pallas import tpu as pltpu
from jax.sharding import PartitionSpec as P

D = 8192
HD = 128
QH = 32
KVH = 4
SEGS = 6
PH = 3


NORM_EPS = 1e-05


def from_behind(value, axis, steps):
    count = lax.axis_size(axis)
    initial, last = (max(0, -steps), min(count, count - steps))
    return lax.ppermute(value, axis, [(source, source + steps) for source in range(initial, last)])


def broadcast(value, axis, root):
    mine = lax.axis_index(axis) == root
    return lax.psum(jnp.where(mine, value, jnp.zeros_like(value)), axis)


def bucket_ranks(labels, buckets):
    hits_table = (labels[..., None] == jnp.arange(buckets, dtype=jnp.int32)).astype(jnp.int32)
    earlier = jnp.cumsum(hits_table, axis=-2) - hits_table
    return jnp.sum(earlier * hits_table, axis=-1)


def attend_heads(query, key_sel, value_sel, segments):
    head_dim = query.shape[2]
    scores = jnp.einsum("qhd,khd->hqk", query, key_sel, preferred_element_type=jnp.float32)
    scores = scores * head_dim ** (-0.5)
    places = jnp.arange(query.shape[0], dtype=jnp.int32)
    allowed = (segments[:, None] == segments[None, :]) & (places[None, :] <= places[:, None])
    scores = jnp.where(allowed[None, :, :], scores, -jnp.inf)
    row_top = jnp.max(scores, axis=2, keepdims=True)
    weights = jnp.exp(scores - row_top)
    probabilities = (weights / jnp.sum(weights, axis=2, keepdims=True)).astype(jnp.bfloat16)
    mixed = jnp.einsum("hqk,khd->qhd", probabilities, value_sel, preferred_element_type=jnp.float32)
    return mixed.astype(jnp.bfloat16).reshape(query.shape[0], -1)


def general_shards(prompt_rows, row_dest, segment_ids, owner, gain, w_query, w_key, w_value, w_out):
    dp_count = lax.axis_size("dp")
    phase_count = lax.axis_size("phase")
    group_here = lax.axis_index("dp")
    phase_here = lax.axis_index("phase")
    part_here = lax.axis_index("mp")
    halves_here = prompt_rows.shape[1]
    half_rows = prompt_rows.shape[2]
    feature_cols = prompt_rows.shape[3]
    batch_rows = halves_here * half_rows
    capacity = half_rows // min(dp_count, 4)
    half_index = jnp.arange(halves_here, dtype=jnp.int32)[:, None]
    dest_group = row_dest // half_rows
    dest_ranks = bucket_ranks(dest_group, dp_count)
    own_groups = lax.dynamic_index_in_dim(dest_group, group_here, 0, keepdims=False)
    own_ranks = lax.dynamic_index_in_dim(dest_ranks, group_here, 0, keepdims=False)
    send_at = own_groups * capacity + own_ranks
    outgoing = (
        jnp.zeros((halves_here, dp_count * capacity, feature_cols), jnp.bfloat16)
        .at[half_index, send_at]
        .set(prompt_rows[0])
    )
    incoming = lax.all_to_all(
        outgoing.reshape(halves_here, dp_count, capacity, feature_cols),
        "dp",
        split_axis=1,
        concat_axis=1,
        tiled=True,
    )
    source_ids = jnp.arange(dp_count, dtype=jnp.int32)[:, None, None]
    where_from = jnp.transpose(source_ids * capacity + dest_ranks, (1, 0, 2)).reshape(
        halves_here, -1
    )
    target = jnp.where(dest_group == group_here, row_dest % half_rows, half_rows)
    target = jnp.transpose(target, (1, 0, 2)).reshape(halves_here, -1)
    arrived = incoming.reshape(halves_here, dp_count * capacity, feature_cols)[
        half_index, where_from
    ]
    own_halves = (
        jnp.zeros((halves_here, half_rows, feature_cols), jnp.bfloat16)
        .at[half_index, target]
        .set(arrived, mode="drop")
    )
    own_batch = own_halves.reshape(batch_rows, feature_cols)
    waiting = lax.all_gather(own_batch, "phase", axis=0, tiled=True).reshape(
        phase_count, batch_rows, feature_cols
    )
    query_rows, key_rows, value_rows, back_rows = (
        lax.all_gather(w_query[0], "dp", axis=0, tiled=True),
        lax.all_gather(w_key[0], "dp", axis=0, tiled=True),
        lax.all_gather(w_value[0], "dp", axis=0, tiled=True),
        lax.all_gather(w_out[0], "dp", axis=0, tiled=True),
    )
    query_cols = query_rows.shape[1]
    pair_cols = key_rows.shape[1]
    w_proj = jnp.concatenate([query_rows, key_rows, value_rows], axis=1)
    proj_cols = w_proj.shape[1]
    heads_here = query_cols // HD
    group_size = QH // KVH
    key_heads = (part_here * heads_here + jnp.arange(heads_here, dtype=jnp.int32)) // group_size
    gain_row = gain[0]
    segment_table = segment_ids[0]
    last_phase = phase_count - 1
    prompt_numbers = jnp.arange(SEGS, dtype=jnp.int32)

    def advance(tick_index, loop_state):
        current, pooled = loop_state
        batch_index = tick_index - phase_here
        active = (batch_index >= 0) & (batch_index < phase_count)
        batch_slot = jnp.clip(batch_index, 0, phase_count - 1)
        fresh_rows = lax.dynamic_index_in_dim(
            waiting, jnp.clip(tick_index, 0, phase_count - 1), 0, keepdims=False
        )
        tok_rows = jnp.where(phase_here == 0, fresh_rows, current)
        tok_segments = lax.dynamic_index_in_dim(segment_table, batch_slot, 0, keepdims=False)
        tok_float = tok_rows.astype(jnp.float32)
        whole_rows = lax.all_gather(tok_rows, "mp", axis=1, tiled=True)
        whole_float = whole_rows.astype(jnp.float32)
        squares = jnp.sum(whole_float * whole_float, axis=1)
        projected = lax.cond(
            active,
            lambda: jnp.dot(
                (whole_float * gain_row[None, :]).astype(jnp.bfloat16),
                w_proj,
                preferred_element_type=jnp.float32,
            ),
            lambda: jnp.zeros((batch_rows, proj_cols), jnp.float32),
        )
        qkv_rows = (projected * lax.rsqrt(squares / D + NORM_EPS)[:, None]).astype(jnp.bfloat16)
        query = qkv_rows[:, :query_cols].reshape(batch_rows, heads_here, HD)
        key_own = qkv_rows[:, query_cols : query_cols + pair_cols]
        value_own = qkv_rows[:, query_cols + pair_cols :]
        key_all, value_all = (
            lax.all_gather(key_own, "mp", axis=1, tiled=True),
            lax.all_gather(value_own, "mp", axis=1, tiled=True),
        )
        key_sel = jnp.take(key_all.reshape(batch_rows, KVH, HD), key_heads, axis=1)
        value_sel = jnp.take(value_all.reshape(batch_rows, KVH, HD), key_heads, axis=1)
        mixed_own = attend_heads(query, key_sel, value_sel, tok_segments)
        mixed = lax.all_gather(mixed_own, "mp", axis=1, tiled=True)
        updated = lax.cond(
            active,
            lambda: (
                tok_float + jnp.dot(mixed, back_rows, preferred_element_type=jnp.float32)
            ).astype(jnp.bfloat16),
            lambda: tok_rows,
        )
        segment_hits = tok_segments[None, :] == prompt_numbers[:, None]
        segment_sums = jnp.dot(
            segment_hits.astype(jnp.bfloat16), updated, preferred_element_type=jnp.float32
        )
        counts = jnp.sum(segment_hits.astype(jnp.float32), axis=1)
        segment_means = segment_sums / counts[:, None]
        store_here = active & (phase_here == last_phase)
        stored = lax.dynamic_index_in_dim(pooled, batch_slot, 0, keepdims=False)
        pooled = lax.dynamic_update_index_in_dim(
            pooled, jnp.where(store_here, segment_means, stored), batch_slot, 0
        )
        passed = from_behind(updated, "phase", 1)
        return (passed, pooled)

    start_state = (
        jnp.zeros((batch_rows, feature_cols), jnp.bfloat16),
        jnp.zeros((phase_count, SEGS, feature_cols), jnp.float32),
    )
    current, pooled = lax.fori_loop(0, phase_count + phase_count - 1, advance, start_state)
    shared = broadcast(pooled.astype(jnp.bfloat16), "phase", last_phase)
    own_prompts = lax.dynamic_index_in_dim(shared, phase_here, 0, keepdims=False).reshape(
        halves_here, PH, feature_cols
    )
    owner_ids = owner[0, :, :, 0]
    return_cap = max(2, PH // min(dp_count, 4))
    send_slots = owner_ids * return_cap + bucket_ranks(owner_ids, dp_count)
    parcel = (
        jnp.zeros((halves_here, dp_count * return_cap, feature_cols), jnp.bfloat16)
        .at[half_index, send_slots]
        .set(own_prompts)
    )
    returned = lax.all_to_all(
        parcel.reshape(halves_here, dp_count, return_cap, feature_cols),
        "dp",
        split_axis=1,
        concat_axis=1,
        tiled=True,
    )
    return returned.reshape(1, halves_here, dp_count * return_cap, feature_cols)


LAG = 2
CHIPS = 4
GROUP_Q = QH // KVH
Q_COLS = GROUP_Q * HD
KV_AT = Q_COLS + 2 * HD
MSG_COLS = KV_AT + 128
RANKS = 8
TABLE_ROW = 6
F32 = jnp.float32
BF16 = jnp.bfloat16


def vmem_spec():
    return pl.BlockSpec(memory_space=pltpu.VMEM)


def smem_spec():
    return pl.BlockSpec(memory_space=pltpu.SMEM)


def hbm_spec():
    return pl.BlockSpec(memory_space=pltpu.HBM)


def call(kernel, outs, args, specs, scratch=(), limit=6, token=None):
    count = len(args)

    def body(*refs):
        at = count + 1 + len(outs)
        refs[at][...] = jnp.zeros(refs[at].shape, F32)
        kernel(*refs[:count], *refs[count + 1 : at], *refs[at + 1 :])

    outs = list(outs)
    if token is not None:
        outs_all = outs + [jax.ShapeDtypeStruct((8, 128), F32)]
        args, specs = ((*args, token), [*specs, pl.BlockSpec(memory_space=pl.ANY)])
    else:
        outs_all = outs
    return pl.pallas_call(
        kernel if token is None else body,
        out_shape=outs_all,
        in_specs=specs,
        out_specs=[vmem_spec()] * len(outs_all),
        scratch_shapes=list(scratch),
        compiler_params=pltpu.CompilerParams(vmem_limit_bytes=limit * 1024 * 1024),
    )(*args)


def dot(a, b):
    return jnp.dot(a, b, preferred_element_type=F32)


def lane(start, size):
    return pl.ds(pl.multiple_of(start, size), size)


def iota(rows, cols, axis):
    return lax.broadcasted_iota(jnp.int32, (rows, cols), axis)


def as_column(row):
    count = row.shape[1]
    diagonal = iota(count, count, 0) == iota(count, count, 1)
    return jnp.sum(jnp.where(diagonal, row, 0), axis=1, keepdims=True)


def marks(hits):
    return hits.astype(F32).astype(BF16)


def pack_kernel(pos_ref, rows_ref, dest_ref, table_ref, *out_refs):
    chip = pos_ref[0]
    dest = dest_ref[pl.ds(chip, 1), :]
    count = dest.shape[1]
    half = count // 2
    group_row = dest // half
    group_col = as_column(group_row)
    source, here = (iota(count, count, 0), iota(count, count, 1))
    before = (group_col == group_row) & (source // half == here // half) & (source < here)
    rank = jnp.sum(jnp.where(before, 1, 0), axis=0, keepdims=True)
    target = group_row * (2 * RANKS) + (iota(1, count, 1) // half) * RANKS + rank
    width = out_refs[0].shape[1]
    message_row = iota(4 * RANKS, width, 0)
    for k in range(CHIPS):
        turn = chip ^ k
        core, block = (turn & 1, turn >> 1)
        pick = marks(iota(4 * RANKS, count, 0) + core * (4 * RANKS) == target)
        rows = dot(pick, rows_ref[:, lane(block * width, width)])
        rows = jnp.where(message_row == TABLE_ROW, table_ref[...], rows)
        out_refs[k][...] = rows.astype(BF16)


def unpack_kernel(pos_ref, m0, m1, m2, m3, dest_ref, out_ref, table_ref):
    chip, core = (pos_ref[0], pos_ref[2])
    count = dest_ref.shape[1]
    half = count // 2
    turn = 2 * (chip & 1) + core
    total = jnp.zeros(out_ref.shape, F32)
    table = jnp.zeros(table_ref.shape, F32)
    above, across = (iota(count, count, 0), iota(count, count, 1))
    for k, ref in enumerate((m0, m1, m2, m3)):
        loader = turn ^ k
        dest_row = dest_ref[pl.ds(loader, 1), :]
        group_row = dest_row // half
        group_col = as_column(group_row)
        earlier = (group_col == group_row) & (above // half == across // half) & (across < above)
        rank = jnp.sum(jnp.where(earlier, 1, 0), axis=1, keepdims=True)
        at = (group_col - 2 * core) * (2 * RANKS) + (iota(count, 1, 0) // half) * RANKS + rank
        from_message = marks(iota(count, 4 * RANKS, 1) == at)
        slot = (group_row - 2 * core) * count + (iota(1, count, 1) // half) * half + dest_row % half
        to_slot = marks(iota(2 * count, count, 0) == slot)
        rows = ref[...]
        total += dot(dot(to_slot, from_message).astype(BF16), rows)
        mine = (loader >> 1) == core
        table += jnp.where(mine, rows[TABLE_ROW : TABLE_ROW + 1].astype(F32), 0.0)
    out_ref[...] = total.astype(BF16)
    table_ref[...] = table


def pick_rows(pos_ref, wait_ref, recv_ref):
    if recv_ref is None:
        return wait_ref[...]
    if wait_ref is None:
        return recv_ref[...]
    return jnp.where(pos_ref[1] == 0, wait_ref[...], recv_ref[...])


def place_result(pos_ref, head, keep_ref, send_ref, cols, result):
    chip, core = (pos_ref[0], pos_ref[2])
    gap = head ^ chip
    first = 1 + core
    at = jnp.where((gap == 0) | (gap == first), 0, 1)
    away = (gap == first) | (gap == 3)

    @pl.when(away)
    def _():
        send_ref[at, :, cols] = result

    @pl.when(jnp.logical_not(away))
    def _():
        keep_ref[at, :, cols] = result


def project_kernel(has_wait, has_recv, pos_ref, *refs):
    refs = list(refs)
    wait_ref = refs.pop(0) if has_wait else None
    recv_ref = refs.pop(0) if has_recv else None
    gain_ref, *sources, keep_ref, send_ref, buf, sems = refs
    own, other = (sources[:3], sources[3:])
    chip, core = (pos_ref[0], pos_ref[2])
    copies, at = ([], 0)
    for i, source in enumerate(other):
        width = source.shape[2]
        step = min(width, 512)
        for start in range(0, width, step):
            piece = source.at[0, :, pl.ds(start, step)]
            copy = pltpu.make_async_copy(piece, buf.at[:, pl.ds(at, step)], sems.at[len(copies)])
            copy.start()
            copies.append((copy, i, start, at, step))
            at += step
    rows = pick_rows(pos_ref, wait_ref, recv_ref).astype(F32)
    depth = rows.shape[1]
    gated = (rows * gain_ref[:, lane(chip * depth, depth)]).astype(BF16)
    squares = jnp.sum(rows * rows, axis=1, keepdims=True)
    high = squares.astype(BF16).astype(F32)
    tail = jnp.where(iota(rows.shape[0], 128, 1) < 64, high, squares - high).astype(BF16)

    def spread(part, i, start, step, result):
        result = result.astype(BF16)
        if i == 0:
            inside = start % Q_COLS
            cols = slice(inside, inside + step)
            place_result(pos_ref, 2 * part + start // Q_COLS, keep_ref, send_ref, cols, result)
        else:
            inside = Q_COLS + (i - 1) * HD
            for j in range(2):
                piece = result[:, j * HD : (j + 1) * HD]
                place_result(pos_ref, 2 * part + j, keep_ref, send_ref, slice(inside, inside + HD), piece)

    for i, source in enumerate(own):
        width = source.shape[2]
        step = min(width, 512)
        for start in range(0, width, step):
            spread(core, i, start, step, dot(gated, source[0, :, start : start + step]))
    for copy, i, start, at, step in copies:
        copy.wait()
        spread(1 - core, i, start, step, dot(gated, buf[:, at : at + step]))
    for j in range(2):
        keep_ref[j, :, KV_AT:] = tail
        send_ref[j, :, KV_AT:] = tail


def join_kernel(keep_ref, got_ref, out_ref):
    out_ref[...] = (keep_ref[1].astype(F32) + got_ref[1].astype(F32)).astype(BF16)


def means(table_ref, chunk, count, rows):
    number = iota(16, count, 0)
    segment = table_ref[:, chunk * 128 : chunk * 128 + count].astype(jnp.int32)
    hits = segment == (number % 8) + SEGS * (number // 8)
    hits = hits & (number % 8 < SEGS)
    counts = jnp.sum(jnp.where(hits, 1.0, 0.0), axis=1, keepdims=True)
    return dot(marks(hits), rows) / jnp.maximum(counts, 1.0)


def attend_kernel(features, pool_chunk, pos_ref, slot_ref, keep_in, first_in, second_in, table_ref, *refs):
    own_ref, other_ref, keep_ref, send_ref, buf, sems = refs
    core = pos_ref[2]
    copies = []
    step = own_ref.shape[2] // 4
    for i in range(4):
        piece = pl.ds(i * step, step)
        copy = pltpu.make_async_copy(other_ref.at[0, :, piece], buf.at[:, piece], sems.at[i])
        copy.start()
        copies.append(copy)
    sums = keep_in[0].astype(F32) + first_in[0].astype(F32) + second_in[...].astype(F32)
    count = sums.shape[0]
    tail = sums[:, KV_AT:]
    squares = tail[:, 0:1] + tail[:, 64:65]
    scaled = (sums[:, :KV_AT] * lax.rsqrt(squares / features + NORM_EPS)).astype(BF16)
    query = jnp.concatenate([scaled[:, h * HD : (h + 1) * HD] for h in range(GROUP_Q)], axis=0)
    key = scaled[:, Q_COLS : Q_COLS + HD]
    value = scaled[:, Q_COLS + HD :]
    scores = lax.dot_general(query, key, (((1,), (1,)), ((), ())), preferred_element_type=F32)
    scores = (scores * HD ** (-0.5)).reshape(GROUP_Q, count, count)
    segment = table_ref[:, lane(slot_ref[0] * 128, 128)][:, :count].astype(jnp.int32)
    allowed = (as_column(segment) == segment) & (iota(count, count, 1) <= iota(count, count, 0))
    scores = jnp.where(allowed[None], scores, -jnp.inf)
    top = jnp.max(scores, axis=2, keepdims=True)
    weights = jnp.exp(scores - top)
    probs = (weights / jnp.sum(weights, axis=2, keepdims=True)).astype(BF16)
    mixed = dot(probs.reshape(GROUP_Q * count, count), value).astype(BF16)
    mixed = jnp.concatenate([mixed[h * count : (h + 1) * count] for h in range(GROUP_Q)], axis=1)
    if pool_chunk is not None:
        mixed = means(table_ref, pool_chunk, count, mixed).astype(BF16)
    for i in range(8):
        part, source = (core, own_ref.at[0]) if i < 4 else (1 - core, buf)
        if i >= 4:
            copies[i - 4].wait()
        at = i % 4
        result = dot(mixed, source[:, at * step : (at + 1) * step]).astype(BF16)
        inside = (i % 2) * step
        place_result(pos_ref, 2 * part + at // 2, keep_ref, send_ref, slice(inside, inside + step), result)


def update_kernel(has_wait, has_recv, send, pool_chunk, pooled_sums, pos_ref, *refs):
    refs = list(refs)
    wait_ref = refs.pop(0) if has_wait else None
    recv_ref = refs.pop(0) if has_recv else None
    keep_in, first_in, second_in, table_ref, *out_refs = refs
    rows = pick_rows(pos_ref, wait_ref, recv_ref)
    if pooled_sums:
        total = means(table_ref, pool_chunk, rows.shape[0], rows)
    else:
        total = rows.astype(F32)
    total += keep_in[0].astype(F32) + first_in[0].astype(F32) + second_in[...].astype(F32)
    hidden = total.astype(BF16)
    if send:
        out_refs.pop(0)[...] = hidden
    if pooled_sums:
        out_refs.pop(0)[...] = hidden
    elif pool_chunk is not None:
        out_refs.pop(0)[...] = means(table_ref, pool_chunk, rows.shape[0], hidden).astype(BF16)


def parcel_kernel(owner_at, pos_ref, p0, p1, p2, p3, table_ref, *out_refs):
    chip, phase, core = (pos_ref[0], pos_ref[1], pos_ref[2])
    rows = jnp.where(phase == 0, p0[...], p1[...])
    rows = jnp.where(phase < 2, rows, jnp.where(phase == 2, p2[...], p3[...]))
    count = rows.shape[0]
    own_row = table_ref[:, owner_at : owner_at + count].astype(jnp.int32) - 1
    own_col = as_column(own_row)
    above, across = (iota(count, count, 0), iota(count, count, 1))
    same = (above // 8 == across // 8) & ((above % 8 >= PH) == (across % 8 >= PH))
    earlier = (own_col == own_row) & same & (above < across)
    rank = jnp.sum(jnp.where(earlier, 1, 0), axis=0, keepdims=True)
    place = iota(1, count, 1)
    half = jnp.where(place % 8 >= PH, 1, 0)
    slot = half * 8 + (2 * core + place // 8) * 2 + rank
    turn = 2 * (chip & 1) + core
    for k in range(CHIPS):
        pick = marks((iota(16, count, 0) == slot) & (own_row == (turn ^ k)))
        out_refs[k][...] = dot(pick, rows).astype(BF16)


def deliver_kernel(pos_ref, m0, m1, m2, m3, out_ref):
    chip = pos_ref[0]
    width = m0.shape[1]
    out_ref[...] = jnp.zeros_like(out_ref)
    for k, ref in enumerate((m0, m1, m2, m3)):
        cols = lane(((chip ^ k) >> 1) * width, width)
        out_ref[:, cols] = out_ref[:, cols] + ref[...]


def chip_shards(prompt_rows, row_dest, segment_ids, owner, gain, w_query, w_key, w_value, w_out):
    chip, phase, core = (lax.axis_index("dp"), lax.axis_index("phase"), lax.axis_index("mp"))
    phases = lax.axis_size("phase")
    pos = jnp.stack([chip, phase, core]).astype(jnp.int32)
    halves, half_rows, cols_here = prompt_rows.shape[1:]
    batch = halves * half_rows
    features = 2 * cols_here
    block = features // CHIPS
    count = 2 * batch
    square = [(e, k) for e in range(CHIPS) for k in range(2)]

    def crosswise(value, k):
        pairs = [(2 * e + m, 2 * (2 * m + ((e ^ k) >> 1)) + ((e ^ k) & 1)) for e, m in square]
        return lax.ppermute(value, ("dp", "mp"), pairs)

    def homewards(value, k):
        pairs = [(2 * e + c, 2 * ((2 * (e & 1) + c) ^ k) + (e >> 1)) for e, c in square]
        return lax.ppermute(value, ("dp", "mp"), pairs)

    def partner(value, first):
        pairs = [(2 * e + c, 2 * (e ^ (1 + c if first else 2 - c)) + c) for e, c in square]
        return lax.ppermute(value, ("dp", "mp"), pairs)

    def swap(value):
        return lax.ppermute(value, "mp", [(0, 1), (1, 0)])

    with jax.named_scope("packing"):
        parity = chip % 2
        owner_at = phases * 128
        table = jnp.zeros((phases, 128), F32)
        numbers = (segment_ids[0] + SEGS * parity).astype(F32)
        table = lax.dynamic_update_slice(table, numbers, (0, batch * parity)).reshape(1, -1)
        owners = (owner.reshape(1, -1) + 1).astype(F32)
        last = lax.dynamic_update_slice(jnp.zeros((1, block - owner_at), F32), owners, (0, 8 * parity))
        table = jnp.concatenate([table, last], axis=1)
        dest = row_dest.reshape(CHIPS, batch)
        packed = call(
            pack_kernel,
            [jax.ShapeDtypeStruct((4 * RANKS, block), BF16)] * CHIPS,
            (pos, prompt_rows.reshape(batch, cols_here), dest, table),
            [smem_spec()] + [vmem_spec()] * 3,
        )
        arrived = [crosswise(value, k) for k, value in enumerate(packed)]
        start, table = call(
            unpack_kernel,
            [jax.ShapeDtypeStruct((count, block), BF16), jax.ShapeDtypeStruct((1, block), F32)],
            (pos, *arrived, dest),
            [smem_spec()] + [vmem_spec()] * 5,
        )
        waiting = [start]

    with jax.named_scope("weights"):

        def held(space, values):
            return [pltpu.with_memory_space_constraint(value, space) for value in values]

        own_in = (w_query, w_key, w_value)
        own_late, *_ = lax.optimization_barrier((own_in, *packed))
        other_in = [swap(value) for value in own_late]
        last, _ = lax.optimization_barrier((w_out, start))
        w_in = held(pltpu.VMEM, own_in) + held(pltpu.HBM, other_in)
        w_back = held(pltpu.VMEM, [w_out]) + held(pltpu.HBM, [swap(last)])
        in_buffer = pltpu.VMEM((block, sum(w.shape[2] for w in own_in)), BF16)
        back_buffer = pltpu.VMEM(w_out.shape[1:], BF16)

    hops, pooled, kept, first, second = ({}, {}, {}, {}, {})
    slots = phases + LAG * (phases - 1)
    token = jnp.zeros((8, 128), F32)

    def plan(slot):
        chunk = slot - LAG * (phases - 1)
        send = slot < phases + LAG * (phases - 2)
        pool_chunk = chunk if chunk >= 0 else None
        return (send, pool_chunk, pool_chunk is not None and not send)

    def entering(slot):
        inputs = waiting[slot : slot + 1] + [hops[at] for at in (slot - LAG,) if at >= 0]
        return (slot < phases, slot >= LAG, inputs, [smem_spec()] + [vmem_spec()] * len(inputs))

    def project(slot, token):
        has_wait, has_recv, inputs, specs = entering(slot)
        kept[slot], sent, token = call(
            functools.partial(project_kernel, has_wait, has_recv),
            [jax.ShapeDtypeStruct((2, count, MSG_COLS), BF16)] * 2,
            (pos, *inputs, gain, *w_in),
            specs + [vmem_spec()] * 4 + [hbm_spec()] * 3,
            (in_buffer, pltpu.SemaphoreType.DMA((6,))),
            16,
            token,
        )
        first[slot] = partner(sent, True)
        return token

    def join(slot, token):
        joined, token = call(
            join_kernel,
            [jax.ShapeDtypeStruct(kept[slot].shape[1:], BF16)],
            (kept[slot], first[slot]),
            [vmem_spec()] * 2,
            token=token,
        )
        second[slot] = partner(joined, False)
        return token

    def attend(slot, token):
        _, pool_chunk, early_pool = plan(slot)
        at = jnp.clip(slot - LAG * phase, 0, phases - 1).astype(jnp.int32).reshape(1)
        rows = 16 if early_pool else count
        kept[slot], sent, token = call(
            functools.partial(attend_kernel, features, pool_chunk if early_pool else None),
            [jax.ShapeDtypeStruct((2, rows, block), BF16)] * 2,
            (pos, at, kept[slot], first[slot], second[slot], table, *w_back),
            [smem_spec(), smem_spec()] + [vmem_spec()] * 5 + [hbm_spec()],
            (back_buffer, pltpu.SemaphoreType.DMA((4,))),
            16,
            token,
        )
        first[slot] = partner(sent, True)
        return token

    def update(slot, token):
        has_wait, has_recv, inputs, specs = entering(slot)
        send, pool_chunk, early_pool = plan(slot)
        outs = [jax.ShapeDtypeStruct((count, block), BF16)] * send
        outs = outs + [jax.ShapeDtypeStruct((16, block), BF16)] * (pool_chunk is not None)
        *out, token = call(
            functools.partial(update_kernel, has_wait, has_recv, send, pool_chunk, early_pool),
            outs,
            (pos, *inputs, kept[slot], first[slot], second[slot], table),
            specs + [vmem_spec()] * 4,
            token=token,
        )
        if send:
            live = [p for p in range(phases - 1) if 0 <= slot - LAG * p < phases]
            hops[slot] = lax.ppermute(out.pop(0), "phase", [(p, p + 1) for p in live])
        if pool_chunk is not None:
            pooled[pool_chunk] = out.pop(0)
        return token

    for step in range(slots + 1):
        before, now = (step > 0, step < slots)
        if step < phases - 1:
            down = [(p, p - 1) for p in range(1, phases - step)]
            waiting.append(lax.ppermute(waiting[step], "phase", down))
        if now:
            with jax.named_scope("project"):
                token = project(step, token)
        if before:
            with jax.named_scope("join_output"):
                token = join(step - 1, token)
        if now:
            with jax.named_scope("join_projection"):
                token = join(step, token)
        if before:
            with jax.named_scope("update"):
                token = update(step - 1, token)
        if now:
            with jax.named_scope("attend"):
                token = attend(step, token)

    with jax.named_scope("deliver"):
        shares = [lax.ppermute(pooled[m], "phase", [(phases - 1, m)]) for m in range(phases - 1)]
        parcels = call(
            functools.partial(parcel_kernel, owner_at),
            [jax.ShapeDtypeStruct((16, block), BF16)] * CHIPS,
            (pos, *shares, pooled[phases - 1], table),
            [smem_spec()] + [vmem_spec()] * 5,
        )
        final = [homewards(value, k) for k, value in enumerate(parcels)]
        (result,) = call(
            deliver_kernel,
            [jax.ShapeDtypeStruct((16, cols_here), BF16)],
            (pos, *final),
            [smem_spec()] + [vmem_spec()] * 4,
        )
    return result.reshape(1, 2, 8, cols_here)


def solution(mesh):
    in_specs = (
        P("dp", "phase", None, "mp"),
        P(None, "phase", None),
        P("dp", None, None),
        P("dp", "phase", None, None),
        P("phase", None),
        P("phase", "dp", "mp"),
        P("phase", "dp", "mp"),
        P("phase", "dp", "mp"),
        P("phase", "dp", "mp"),
    )
    out_specs = P("dp", "phase", None, "mp")
    square = mesh.shape["dp"] == CHIPS and mesh.shape["mp"] == 2 and mesh.shape["phase"] == 4
    shards = chip_shards if square else general_shards
    return jax.shard_map(shards, mesh=mesh, in_specs=in_specs, out_specs=out_specs, check_vma=False)
```

```python
import functools

import jax
import jax.numpy as jnp
from jax import lax
from jax.experimental import pallas as pl
from jax.experimental.pallas import tpu as pltpu
from jax.sharding import PartitionSpec as P

D = 8192
HD = 128
QH = 32
KVH = 4
SEGS = 6
PH = 3


NORM_EPS = 1e-05


def from_behind(value, axis, steps):
    count = lax.axis_size(axis)
    initial, last = (max(0, -steps), min(count, count - steps))
    return lax.ppermute(value, axis, [(source, source + steps) for source in range(initial, last)])


def broadcast(value, axis, root):
    mine = lax.axis_index(axis) == root
    return lax.psum(jnp.where(mine, value, jnp.zeros_like(value)), axis)


def bucket_ranks(labels, buckets):
    hits_table = (labels[..., None] == jnp.arange(buckets, dtype=jnp.int32)).astype(jnp.int32)
    earlier = jnp.cumsum(hits_table, axis=-2) - hits_table
    return jnp.sum(earlier * hits_table, axis=-1)


def attend_heads(query, key_sel, value_sel, segments):
    head_dim = query.shape[2]
    scores = jnp.einsum("qhd,khd->hqk", query, key_sel, preferred_element_type=jnp.float32)
    scores = scores * head_dim ** (-0.5)
    places = jnp.arange(query.shape[0], dtype=jnp.int32)
    allowed = (segments[:, None] == segments[None, :]) & (places[None, :] <= places[:, None])
    scores = jnp.where(allowed[None, :, :], scores, -jnp.inf)
    row_top = jnp.max(scores, axis=2, keepdims=True)
    weights = jnp.exp(scores - row_top)
    probabilities = (weights / jnp.sum(weights, axis=2, keepdims=True)).astype(jnp.bfloat16)
    mixed = jnp.einsum("hqk,khd->qhd", probabilities, value_sel, preferred_element_type=jnp.float32)
    return mixed.astype(jnp.bfloat16).reshape(query.shape[0], -1)


def general_shards(prompt_rows, row_dest, segment_ids, owner, gain, w_query, w_key, w_value, w_out):
    dp_count = lax.axis_size("dp")
    phase_count = lax.axis_size("phase")
    group_here = lax.axis_index("dp")
    phase_here = lax.axis_index("phase")
    part_here = lax.axis_index("mp")
    halves_here = prompt_rows.shape[1]
    half_rows = prompt_rows.shape[2]
    feature_cols = prompt_rows.shape[3]
    batch_rows = halves_here * half_rows
    capacity = half_rows // min(dp_count, 4)
    half_index = jnp.arange(halves_here, dtype=jnp.int32)[:, None]
    dest_group = row_dest // half_rows
    dest_ranks = bucket_ranks(dest_group, dp_count)
    own_groups = lax.dynamic_index_in_dim(dest_group, group_here, 0, keepdims=False)
    own_ranks = lax.dynamic_index_in_dim(dest_ranks, group_here, 0, keepdims=False)
    send_at = own_groups * capacity + own_ranks
    outgoing = (
        jnp.zeros((halves_here, dp_count * capacity, feature_cols), jnp.bfloat16)
        .at[half_index, send_at]
        .set(prompt_rows[0])
    )
    incoming = lax.all_to_all(
        outgoing.reshape(halves_here, dp_count, capacity, feature_cols),
        "dp",
        split_axis=1,
        concat_axis=1,
        tiled=True,
    )
    source_ids = jnp.arange(dp_count, dtype=jnp.int32)[:, None, None]
    where_from = jnp.transpose(source_ids * capacity + dest_ranks, (1, 0, 2)).reshape(
        halves_here, -1
    )
    target = jnp.where(dest_group == group_here, row_dest % half_rows, half_rows)
    target = jnp.transpose(target, (1, 0, 2)).reshape(halves_here, -1)
    arrived = incoming.reshape(halves_here, dp_count * capacity, feature_cols)[
        half_index, where_from
    ]
    own_halves = (
        jnp.zeros((halves_here, half_rows, feature_cols), jnp.bfloat16)
        .at[half_index, target]
        .set(arrived, mode="drop")
    )
    own_batch = own_halves.reshape(batch_rows, feature_cols)
    waiting = lax.all_gather(own_batch, "phase", axis=0, tiled=True).reshape(
        phase_count, batch_rows, feature_cols
    )
    query_rows, key_rows, value_rows, back_rows = (
        lax.all_gather(w_query[0], "dp", axis=0, tiled=True),
        lax.all_gather(w_key[0], "dp", axis=0, tiled=True),
        lax.all_gather(w_value[0], "dp", axis=0, tiled=True),
        lax.all_gather(w_out[0], "dp", axis=0, tiled=True),
    )
    query_cols = query_rows.shape[1]
    pair_cols = key_rows.shape[1]
    w_proj = jnp.concatenate([query_rows, key_rows, value_rows], axis=1)
    proj_cols = w_proj.shape[1]
    heads_here = query_cols // HD
    group_size = QH // KVH
    key_heads = (part_here * heads_here + jnp.arange(heads_here, dtype=jnp.int32)) // group_size
    gain_row = gain[0]
    segment_table = segment_ids[0]
    last_phase = phase_count - 1
    prompt_numbers = jnp.arange(SEGS, dtype=jnp.int32)

    def advance(tick_index, loop_state):
        current, pooled = loop_state
        batch_index = tick_index - phase_here
        active = (batch_index >= 0) & (batch_index < phase_count)
        batch_slot = jnp.clip(batch_index, 0, phase_count - 1)
        fresh_rows = lax.dynamic_index_in_dim(
            waiting, jnp.clip(tick_index, 0, phase_count - 1), 0, keepdims=False
        )
        tok_rows = jnp.where(phase_here == 0, fresh_rows, current)
        tok_segments = lax.dynamic_index_in_dim(segment_table, batch_slot, 0, keepdims=False)
        tok_float = tok_rows.astype(jnp.float32)
        whole_rows = lax.all_gather(tok_rows, "mp", axis=1, tiled=True)
        whole_float = whole_rows.astype(jnp.float32)
        squares = jnp.sum(whole_float * whole_float, axis=1)
        projected = lax.cond(
            active,
            lambda: jnp.dot(
                (whole_float * gain_row[None, :]).astype(jnp.bfloat16),
                w_proj,
                preferred_element_type=jnp.float32,
            ),
            lambda: jnp.zeros((batch_rows, proj_cols), jnp.float32),
        )
        qkv_rows = (projected * lax.rsqrt(squares / D + NORM_EPS)[:, None]).astype(jnp.bfloat16)
        query = qkv_rows[:, :query_cols].reshape(batch_rows, heads_here, HD)
        key_own = qkv_rows[:, query_cols : query_cols + pair_cols]
        value_own = qkv_rows[:, query_cols + pair_cols :]
        key_all, value_all = (
            lax.all_gather(key_own, "mp", axis=1, tiled=True),
            lax.all_gather(value_own, "mp", axis=1, tiled=True),
        )
        key_sel = jnp.take(key_all.reshape(batch_rows, KVH, HD), key_heads, axis=1)
        value_sel = jnp.take(value_all.reshape(batch_rows, KVH, HD), key_heads, axis=1)
        mixed_own = attend_heads(query, key_sel, value_sel, tok_segments)
        mixed = lax.all_gather(mixed_own, "mp", axis=1, tiled=True)
        updated = lax.cond(
            active,
            lambda: (
                tok_float + jnp.dot(mixed, back_rows, preferred_element_type=jnp.float32)
            ).astype(jnp.bfloat16),
            lambda: tok_rows,
        )
        segment_hits = tok_segments[None, :] == prompt_numbers[:, None]
        segment_sums = jnp.dot(
            segment_hits.astype(jnp.bfloat16), updated, preferred_element_type=jnp.float32
        )
        counts = jnp.sum(segment_hits.astype(jnp.float32), axis=1)
        segment_means = segment_sums / counts[:, None]
        store_here = active & (phase_here == last_phase)
        stored = lax.dynamic_index_in_dim(pooled, batch_slot, 0, keepdims=False)
        pooled = lax.dynamic_update_index_in_dim(
            pooled, jnp.where(store_here, segment_means, stored), batch_slot, 0
        )
        passed = from_behind(updated, "phase", 1)
        return (passed, pooled)

    start_state = (
        jnp.zeros((batch_rows, feature_cols), jnp.bfloat16),
        jnp.zeros((phase_count, SEGS, feature_cols), jnp.float32),
    )
    current, pooled = lax.fori_loop(0, phase_count + phase_count - 1, advance, start_state)
    shared = broadcast(pooled.astype(jnp.bfloat16), "phase", last_phase)
    own_prompts = lax.dynamic_index_in_dim(shared, phase_here, 0, keepdims=False).reshape(
        halves_here, PH, feature_cols
    )
    owner_ids = owner[0, :, :, 0]
    return_cap = max(2, PH // min(dp_count, 4))
    send_slots = owner_ids * return_cap + bucket_ranks(owner_ids, dp_count)
    parcel = (
        jnp.zeros((halves_here, dp_count * return_cap, feature_cols), jnp.bfloat16)
        .at[half_index, send_slots]
        .set(own_prompts)
    )
    returned = lax.all_to_all(
        parcel.reshape(halves_here, dp_count, return_cap, feature_cols),
        "dp",
        split_axis=1,
        concat_axis=1,
        tiled=True,
    )
    return returned.reshape(1, halves_here, dp_count * return_cap, feature_cols)


LAG = 2
CHIPS = 4
GROUP_Q = QH // KVH
Q_COLS = GROUP_Q * HD
KV_AT = Q_COLS + 2 * HD
MSG_COLS = KV_AT + 128
RANKS = 8
TABLE_ROW = 6
F32 = jnp.float32
BF16 = jnp.bfloat16


def vmem_spec():
    return pl.BlockSpec(memory_space=pltpu.VMEM)


def smem_spec():
    return pl.BlockSpec(memory_space=pltpu.SMEM)


def call(kernel, outs, args, specs, scratch=(), limit=6, token=None):
    count = len(args)

    def body(*refs):
        at = count + 1 + len(outs)
        refs[at][...] = jnp.zeros(refs[at].shape, F32)
        kernel(*refs[:count], *refs[count + 1 : at], *refs[at + 1 :])

    outs = list(outs)
    if token is not None:
        outs_all = outs + [jax.ShapeDtypeStruct((8, 128), F32)]
        args, specs = ((*args, token), [*specs, pl.BlockSpec(memory_space=pl.ANY)])
    else:
        outs_all = outs
    return pl.pallas_call(
        kernel if token is None else body,
        out_shape=outs_all,
        in_specs=specs,
        out_specs=[vmem_spec()] * len(outs_all),
        scratch_shapes=list(scratch),
        compiler_params=pltpu.CompilerParams(vmem_limit_bytes=limit * 1024 * 1024),
    )(*args)


def dot(a, b):
    return jnp.dot(a, b, preferred_element_type=F32)


def lane(start, size):
    return pl.ds(pl.multiple_of(start, size), size)


def iota(rows, cols, axis):
    return lax.broadcasted_iota(jnp.int32, (rows, cols), axis)


def as_column(row):
    count = row.shape[1]
    diagonal = iota(count, count, 0) == iota(count, count, 1)
    return jnp.sum(jnp.where(diagonal, row, 0), axis=1, keepdims=True)


def marks(hits):
    return hits.astype(F32).astype(BF16)


def pack_kernel(pos_ref, rows_ref, dest_ref, table_ref, *out_refs):
    chip = pos_ref[0]
    dest = dest_ref[pl.ds(chip, 1), :]
    count = dest.shape[1]
    half = count // 2
    group_row = dest // half
    group_col = as_column(group_row)
    source, here = (iota(count, count, 0), iota(count, count, 1))
    before = (group_col == group_row) & (source // half == here // half) & (source < here)
    rank = jnp.sum(jnp.where(before, 1, 0), axis=0, keepdims=True)
    target = group_row * (2 * RANKS) + (iota(1, count, 1) // half) * RANKS + rank
    width = out_refs[0].shape[1]
    message_row = iota(4 * RANKS, width, 0)
    for k in range(CHIPS):
        turn = chip ^ k
        core, block = (turn & 1, turn >> 1)
        pick = marks(iota(4 * RANKS, count, 0) + core * (4 * RANKS) == target)
        rows = dot(pick, rows_ref[:, lane(block * width, width)])
        rows = jnp.where(message_row == TABLE_ROW, table_ref[...], rows)
        out_refs[k][...] = rows.astype(BF16)


def unpack_kernel(pos_ref, m0, m1, m2, m3, dest_ref, out_ref, table_ref):
    chip, core = (pos_ref[0], pos_ref[2])
    count = dest_ref.shape[1]
    half = count // 2
    turn = 2 * (chip & 1) + core
    total = jnp.zeros(out_ref.shape, F32)
    table = jnp.zeros(table_ref.shape, F32)
    above, across = (iota(count, count, 0), iota(count, count, 1))
    for k, ref in enumerate((m0, m1, m2, m3)):
        loader = turn ^ k
        dest_row = dest_ref[pl.ds(loader, 1), :]
        group_row = dest_row // half
        group_col = as_column(group_row)
        earlier = (group_col == group_row) & (above // half == across // half) & (across < above)
        rank = jnp.sum(jnp.where(earlier, 1, 0), axis=1, keepdims=True)
        at = (group_col - 2 * core) * (2 * RANKS) + (iota(count, 1, 0) // half) * RANKS + rank
        from_message = marks(iota(count, 4 * RANKS, 1) == at)
        slot = (group_row - 2 * core) * count + (iota(1, count, 1) // half) * half + dest_row % half
        to_slot = marks(iota(2 * count, count, 0) == slot)
        rows = ref[...]
        total += dot(dot(to_slot, from_message).astype(BF16), rows)
        mine = (loader >> 1) == core
        table += jnp.where(mine, rows[TABLE_ROW : TABLE_ROW + 1].astype(F32), 0.0)
    out_ref[...] = total.astype(BF16)
    table_ref[...] = table


def pick_rows(pos_ref, wait_ref, recv_ref):
    if recv_ref is None:
        return wait_ref[...]
    if wait_ref is None:
        return recv_ref[...]
    return jnp.where(pos_ref[1] == 0, wait_ref[...], recv_ref[...])


def place_result(pos_ref, head, keep_ref, send_ref, cols, result):
    chip, core = (pos_ref[0], pos_ref[2])
    gap = head ^ chip
    first = 1 + core
    at = jnp.where((gap == 0) | (gap == first), 0, 1)
    away = (gap == first) | (gap == 3)

    @pl.when(away)
    def _():
        send_ref[at, :, cols] = result

    @pl.when(jnp.logical_not(away))
    def _():
        keep_ref[at, :, cols] = result


def project_kernel(has_wait, has_recv, pos_ref, *refs):
    refs = list(refs)
    wait_ref = refs.pop(0) if has_wait else None
    recv_ref = refs.pop(0) if has_recv else None
    gain_ref, *sources, keep_ref, send_ref = refs
    chip, core = (pos_ref[0], pos_ref[2])
    rows = pick_rows(pos_ref, wait_ref, recv_ref).astype(F32)
    depth = rows.shape[1]
    gated = (rows * gain_ref[:, lane(chip * depth, depth)]).astype(BF16)
    squares = jnp.sum(rows * rows, axis=1, keepdims=True)
    high = squares.astype(BF16).astype(F32)
    tail = jnp.where(iota(rows.shape[0], 128, 1) < 64, high, squares - high).astype(BF16)

    def spread(part, i, start, step, result):
        result = result.astype(BF16)
        if i == 0:
            inside = start % Q_COLS
            cols = slice(inside, inside + step)
            place_result(pos_ref, 2 * part + start // Q_COLS, keep_ref, send_ref, cols, result)
        else:
            inside = Q_COLS + (i - 1) * HD
            for j in range(2):
                piece = result[:, j * HD : (j + 1) * HD]
                place_result(pos_ref, 2 * part + j, keep_ref, send_ref, slice(inside, inside + HD), piece)

    for at, source in enumerate(sources):
        part = core if at < 3 else 1 - core
        step = min(source.shape[2], 512)
        for start in range(0, source.shape[2], step):
            spread(part, at % 3, start, step, dot(gated, source[0, :, start : start + step]))
    for j in range(2):
        keep_ref[j, :, KV_AT:] = tail
        send_ref[j, :, KV_AT:] = tail


def join_kernel(keep_ref, got_ref, out_ref):
    out_ref[...] = (keep_ref[1].astype(F32) + got_ref[1].astype(F32)).astype(BF16)


def means(table_ref, chunk, count, rows):
    number = iota(16, count, 0)
    segment = table_ref[:, chunk * 128 : chunk * 128 + count].astype(jnp.int32)
    hits = segment == (number % 8) + SEGS * (number // 8)
    hits = hits & (number % 8 < SEGS)
    counts = jnp.sum(jnp.where(hits, 1.0, 0.0), axis=1, keepdims=True)
    return dot(marks(hits), rows) / jnp.maximum(counts, 1.0)


def attend_kernel(features, slot, chunks, pool_chunk, pos_ref, keep_in, first_in, second_in, table_ref, *refs):
    own_ref, other_ref, keep_ref, send_ref = refs
    core = pos_ref[2]
    sums = keep_in[0].astype(F32) + first_in[0].astype(F32) + second_in[...].astype(F32)
    count = sums.shape[0]
    tail = sums[:, KV_AT:]
    squares = tail[:, 0:1] + tail[:, 64:65]
    scaled = (sums[:, :KV_AT] * lax.rsqrt(squares / features + NORM_EPS)).astype(BF16)
    query = jnp.concatenate([scaled[:, h * HD : (h + 1) * HD] for h in range(GROUP_Q)], axis=0)
    key = scaled[:, Q_COLS : Q_COLS + HD]
    value = scaled[:, Q_COLS + HD :]
    scores = lax.dot_general(query, key, (((1,), (1,)), ((), ())), preferred_element_type=F32)
    scores = (scores * HD ** (-0.5)).reshape(GROUP_Q, count, count)
    chunk = jnp.clip(slot - LAG * pos_ref[1], 0, chunks - 1)
    segment = table_ref[:, lane(chunk * 128, 128)][:, :count].astype(jnp.int32)
    allowed = (as_column(segment) == segment) & (iota(count, count, 1) <= iota(count, count, 0))
    scores = jnp.where(allowed[None], scores, -jnp.inf)
    top = jnp.max(scores, axis=2, keepdims=True)
    weights = jnp.exp(scores - top)
    probs = (weights / jnp.sum(weights, axis=2, keepdims=True)).astype(BF16)
    mixed = dot(probs.reshape(GROUP_Q * count, count), value).astype(BF16)
    mixed = jnp.concatenate([mixed[h * count : (h + 1) * count] for h in range(GROUP_Q)], axis=1)
    if pool_chunk is not None:
        mixed = means(table_ref, pool_chunk, count, mixed).astype(BF16)
    step = own_ref.shape[2] // 8
    for part, source in ((core, own_ref), (1 - core, other_ref)):
        for at in range(8):
            result = dot(mixed, source[0, :, at * step : (at + 1) * step]).astype(BF16)
            cols = slice((at % 4) * step, (at % 4 + 1) * step)
            place_result(pos_ref, 2 * part + at // 4, keep_ref, send_ref, cols, result)


def update_kernel(has_wait, has_recv, send, pool_chunk, pooled_sums, pos_ref, *refs):
    refs = list(refs)
    wait_ref = refs.pop(0) if has_wait else None
    recv_ref = refs.pop(0) if has_recv else None
    keep_in, first_in, second_in, table_ref, *out_refs = refs
    rows = pick_rows(pos_ref, wait_ref, recv_ref)
    if pooled_sums:
        total = means(table_ref, pool_chunk, rows.shape[0], rows)
    else:
        total = rows.astype(F32)
    total += keep_in[0].astype(F32) + first_in[0].astype(F32) + second_in[...].astype(F32)
    hidden = total.astype(BF16)
    if send:
        out_refs.pop(0)[...] = hidden
    if pooled_sums:
        out_refs.pop(0)[...] = hidden
    elif pool_chunk is not None:
        out_refs.pop(0)[...] = means(table_ref, pool_chunk, rows.shape[0], hidden).astype(BF16)


def parcel_kernel(owner_at, pos_ref, p0, p1, p2, p3, table_ref, *out_refs):
    chip, phase, core = (pos_ref[0], pos_ref[1], pos_ref[2])
    rows = jnp.where(phase == 0, p0[...], p1[...])
    rows = jnp.where(phase < 2, rows, jnp.where(phase == 2, p2[...], p3[...]))
    count = rows.shape[0]
    own_row = table_ref[:, owner_at : owner_at + count].astype(jnp.int32) - 1
    own_col = as_column(own_row)
    above, across = (iota(count, count, 0), iota(count, count, 1))
    same = (above // 8 == across // 8) & ((above % 8 >= PH) == (across % 8 >= PH))
    earlier = (own_col == own_row) & same & (above < across)
    rank = jnp.sum(jnp.where(earlier, 1, 0), axis=0, keepdims=True)
    place = iota(1, count, 1)
    half = jnp.where(place % 8 >= PH, 1, 0)
    slot = half * 8 + (2 * core + place // 8) * 2 + rank
    turn = 2 * (chip & 1) + core
    for k in range(CHIPS):
        pick = marks((iota(16, count, 0) == slot) & (own_row == (turn ^ k)))
        out_refs[k][...] = dot(pick, rows).astype(BF16)


def deliver_kernel(pos_ref, m0, m1, m2, m3, out_ref):
    chip = pos_ref[0]
    width = m0.shape[1]
    out_ref[...] = jnp.zeros_like(out_ref)
    for k, ref in enumerate((m0, m1, m2, m3)):
        cols = lane(((chip ^ k) >> 1) * width, width)
        out_ref[:, cols] = out_ref[:, cols] + ref[...]


def chip_shards(prompt_rows, row_dest, segment_ids, owner, gain, w_query, w_key, w_value, w_out):
    chip, phase, core = (lax.axis_index("dp"), lax.axis_index("phase"), lax.axis_index("mp"))
    phases = lax.axis_size("phase")
    pos = jnp.stack([chip, phase, core]).astype(jnp.int32)
    halves, half_rows, cols_here = prompt_rows.shape[1:]
    batch = halves * half_rows
    features = 2 * cols_here
    block = features // CHIPS
    count = 2 * batch
    square = [(e, k) for e in range(CHIPS) for k in range(2)]

    def crosswise(value, k):
        pairs = [(2 * e + m, 2 * (2 * m + ((e ^ k) >> 1)) + ((e ^ k) & 1)) for e, m in square]
        return lax.ppermute(value, ("dp", "mp"), pairs)

    def homewards(value, k):
        pairs = [(2 * e + c, 2 * ((2 * (e & 1) + c) ^ k) + (e >> 1)) for e, c in square]
        return lax.ppermute(value, ("dp", "mp"), pairs)

    def partner(value, first):
        pairs = [(2 * e + c, 2 * (e ^ (1 + c if first else 2 - c)) + c) for e, c in square]
        return lax.ppermute(value, ("dp", "mp"), pairs)

    def swap(value):
        return lax.ppermute(value, "mp", [(0, 1), (1, 0)])

    with jax.named_scope("packing"):
        parity = chip % 2
        owner_at = phases * 128
        table = jnp.zeros((phases, 128), F32)
        numbers = (segment_ids[0] + SEGS * parity).astype(F32)
        table = lax.dynamic_update_slice(table, numbers, (0, batch * parity)).reshape(1, -1)
        owners = (owner.reshape(1, -1) + 1).astype(F32)
        last = lax.dynamic_update_slice(jnp.zeros((1, block - owner_at), F32), owners, (0, 8 * parity))
        table = jnp.concatenate([table, last], axis=1)
        dest = row_dest.reshape(CHIPS, batch)
        packed = call(
            pack_kernel,
            [jax.ShapeDtypeStruct((4 * RANKS, block), BF16)] * CHIPS,
            (pos, prompt_rows.reshape(batch, cols_here), dest, table),
            [smem_spec()] + [vmem_spec()] * 3,
        )
        arrived = [crosswise(value, k) for k, value in enumerate(packed)]
        start, table = call(
            unpack_kernel,
            [jax.ShapeDtypeStruct((count, block), BF16), jax.ShapeDtypeStruct((1, block), F32)],
            (pos, *arrived, dest),
            [smem_spec()] + [vmem_spec()] * 5,
        )
        waiting = [start]

    with jax.named_scope("weights"):

        def held(values):
            return [pltpu.with_memory_space_constraint(value, pltpu.VMEM) for value in values]

        own_in = (w_query, w_key, w_value)
        own_late, *_ = lax.optimization_barrier((own_in, *packed))
        other_in = [swap(value) for value in own_late]
        last, _ = lax.optimization_barrier((w_out, start))
        w_in = held([*own_in, *other_in])
        w_back = held([w_out, swap(last)])

    hops, pooled, kept, first, second = ({}, {}, {}, {}, {})
    slots = phases + LAG * (phases - 1)
    token = jnp.zeros((8, 128), F32)

    def plan(slot):
        chunk = slot - LAG * (phases - 1)
        send = slot < phases + LAG * (phases - 2)
        pool_chunk = chunk if chunk >= 0 else None
        return (send, pool_chunk, pool_chunk is not None and not send)

    def entering(slot):
        inputs = waiting[slot : slot + 1] + [hops[at] for at in (slot - LAG,) if at >= 0]
        return (slot < phases, slot >= LAG, inputs, [smem_spec()] + [vmem_spec()] * len(inputs))

    def project(slot, token):
        has_wait, has_recv, inputs, specs = entering(slot)
        kept[slot], sent, token = call(
            functools.partial(project_kernel, has_wait, has_recv),
            [jax.ShapeDtypeStruct((2, count, MSG_COLS), BF16)] * 2,
            (pos, *inputs, gain, *w_in),
            specs + [vmem_spec()] * 7,
            limit=10,
            token=token,
        )
        first[slot] = partner(sent, True)
        return token

    def join(slot, token):
        joined, token = call(
            join_kernel,
            [jax.ShapeDtypeStruct(kept[slot].shape[1:], BF16)],
            (kept[slot], first[slot]),
            [vmem_spec()] * 2,
            token=token,
        )
        second[slot] = partner(joined, False)
        return token

    def attend(slot, token):
        _, pool_chunk, early_pool = plan(slot)
        rows = 16 if early_pool else count
        kept[slot], sent, token = call(
            functools.partial(attend_kernel, features, slot, phases, pool_chunk if early_pool else None),
            [jax.ShapeDtypeStruct((2, rows, block), BF16)] * 2,
            (pos, kept[slot], first[slot], second[slot], table, *w_back),
            [smem_spec()] + [vmem_spec()] * 6,
            limit=10,
            token=token,
        )
        first[slot] = partner(sent, True)
        return token

    def update(slot, token):
        has_wait, has_recv, inputs, specs = entering(slot)
        send, pool_chunk, early_pool = plan(slot)
        outs = [jax.ShapeDtypeStruct((count, block), BF16)] * send
        outs = outs + [jax.ShapeDtypeStruct((16, block), BF16)] * (pool_chunk is not None)
        *out, token = call(
            functools.partial(update_kernel, has_wait, has_recv, send, pool_chunk, early_pool),
            outs,
            (pos, *inputs, kept[slot], first[slot], second[slot], table),
            specs + [vmem_spec()] * 4,
            token=token,
        )
        if send:
            live = [p for p in range(phases - 1) if 0 <= slot - LAG * p < phases]
            hops[slot] = lax.ppermute(out.pop(0), "phase", [(p, p + 1) for p in live])
        if pool_chunk is not None:
            pooled[pool_chunk] = out.pop(0)
        return token

    for step in range(slots + 1):
        before, now = (step > 0, step < slots)
        if step < phases - 1:
            down = [(p, p - 1) for p in range(1, phases - step)]
            waiting.append(lax.ppermute(waiting[step], "phase", down))
        if now:
            with jax.named_scope("project"):
                token = project(step, token)
        if before:
            with jax.named_scope("join_output"):
                token = join(step - 1, token)
        if now:
            with jax.named_scope("join_projection"):
                token = join(step, token)
        if before:
            with jax.named_scope("update"):
                token = update(step - 1, token)
        if now:
            with jax.named_scope("attend"):
                token = attend(step, token)

    with jax.named_scope("deliver"):
        shares = [lax.ppermute(pooled[m], "phase", [(phases - 1, m)]) for m in range(phases - 1)]
        parcels = call(
            functools.partial(parcel_kernel, owner_at),
            [jax.ShapeDtypeStruct((16, block), BF16)] * CHIPS,
            (pos, *shares, pooled[phases - 1], table),
            [smem_spec()] + [vmem_spec()] * 5,
        )
        final = [homewards(value, k) for k, value in enumerate(parcels)]
        (result,) = call(
            deliver_kernel,
            [jax.ShapeDtypeStruct((16, cols_here), BF16)],
            (pos, *final),
            [smem_spec()] + [vmem_spec()] * 4,
        )
    return result.reshape(1, 2, 8, cols_here)


def solution(mesh):
    in_specs = (
        P("dp", "phase", None, "mp"),
        P(None, "phase", None),
        P("dp", None, None),
        P("dp", "phase", None, None),
        P("phase", None),
        P("phase", "dp", "mp"),
        P("phase", "dp", "mp"),
        P("phase", "dp", "mp"),
        P("phase", "dp", "mp"),
    )
    out_specs = P("dp", "phase", None, "mp")
    square = mesh.shape["dp"] == CHIPS and mesh.shape["mp"] == 2 and mesh.shape["phase"] == 4
    shards = chip_shards if square else general_shards
    return jax.shard_map(shards, mesh=mesh, in_specs=in_specs, out_specs=out_specs, check_vma=False)
```

```python
import functools

import jax
import jax.numpy as jnp
from jax import lax
from jax.experimental import pallas as pl
from jax.experimental.pallas import tpu as pltpu
from jax.sharding import PartitionSpec as P

D = 8192
HD = 128
QH = 32
KVH = 4
SEGS = 6
PH = 3


NORM_EPS = 1e-05


def from_behind(value, axis, steps):
    count = lax.axis_size(axis)
    initial, last = (max(0, -steps), min(count, count - steps))
    return lax.ppermute(value, axis, [(source, source + steps) for source in range(initial, last)])


def broadcast(value, axis, root):
    mine = lax.axis_index(axis) == root
    return lax.psum(jnp.where(mine, value, jnp.zeros_like(value)), axis)


def bucket_ranks(labels, buckets):
    hits_table = (labels[..., None] == jnp.arange(buckets, dtype=jnp.int32)).astype(jnp.int32)
    earlier = jnp.cumsum(hits_table, axis=-2) - hits_table
    return jnp.sum(earlier * hits_table, axis=-1)


def attend_heads(query, key_sel, value_sel, segments):
    head_dim = query.shape[2]
    scores = jnp.einsum("qhd,khd->hqk", query, key_sel, preferred_element_type=jnp.float32)
    scores = scores * head_dim ** (-0.5)
    places = jnp.arange(query.shape[0], dtype=jnp.int32)
    allowed = (segments[:, None] == segments[None, :]) & (places[None, :] <= places[:, None])
    scores = jnp.where(allowed[None, :, :], scores, -jnp.inf)
    row_top = jnp.max(scores, axis=2, keepdims=True)
    weights = jnp.exp(scores - row_top)
    probabilities = (weights / jnp.sum(weights, axis=2, keepdims=True)).astype(jnp.bfloat16)
    mixed = jnp.einsum("hqk,khd->qhd", probabilities, value_sel, preferred_element_type=jnp.float32)
    return mixed.astype(jnp.bfloat16).reshape(query.shape[0], -1)


def general_shards(prompt_rows, row_dest, segment_ids, owner, gain, w_query, w_key, w_value, w_out):
    dp_count = lax.axis_size("dp")
    phase_count = lax.axis_size("phase")
    group_here = lax.axis_index("dp")
    phase_here = lax.axis_index("phase")
    part_here = lax.axis_index("mp")
    halves_here = prompt_rows.shape[1]
    half_rows = prompt_rows.shape[2]
    feature_cols = prompt_rows.shape[3]
    batch_rows = halves_here * half_rows
    capacity = half_rows // min(dp_count, 4)
    half_index = jnp.arange(halves_here, dtype=jnp.int32)[:, None]
    dest_group = row_dest // half_rows
    dest_ranks = bucket_ranks(dest_group, dp_count)
    own_groups = lax.dynamic_index_in_dim(dest_group, group_here, 0, keepdims=False)
    own_ranks = lax.dynamic_index_in_dim(dest_ranks, group_here, 0, keepdims=False)
    send_at = own_groups * capacity + own_ranks
    outgoing = (
        jnp.zeros((halves_here, dp_count * capacity, feature_cols), jnp.bfloat16)
        .at[half_index, send_at]
        .set(prompt_rows[0])
    )
    incoming = lax.all_to_all(
        outgoing.reshape(halves_here, dp_count, capacity, feature_cols),
        "dp",
        split_axis=1,
        concat_axis=1,
        tiled=True,
    )
    source_ids = jnp.arange(dp_count, dtype=jnp.int32)[:, None, None]
    where_from = jnp.transpose(source_ids * capacity + dest_ranks, (1, 0, 2)).reshape(
        halves_here, -1
    )
    target = jnp.where(dest_group == group_here, row_dest % half_rows, half_rows)
    target = jnp.transpose(target, (1, 0, 2)).reshape(halves_here, -1)
    arrived = incoming.reshape(halves_here, dp_count * capacity, feature_cols)[
        half_index, where_from
    ]
    own_halves = (
        jnp.zeros((halves_here, half_rows, feature_cols), jnp.bfloat16)
        .at[half_index, target]
        .set(arrived, mode="drop")
    )
    own_batch = own_halves.reshape(batch_rows, feature_cols)
    waiting = lax.all_gather(own_batch, "phase", axis=0, tiled=True).reshape(
        phase_count, batch_rows, feature_cols
    )
    query_rows, key_rows, value_rows, back_rows = (
        lax.all_gather(w_query[0], "dp", axis=0, tiled=True),
        lax.all_gather(w_key[0], "dp", axis=0, tiled=True),
        lax.all_gather(w_value[0], "dp", axis=0, tiled=True),
        lax.all_gather(w_out[0], "dp", axis=0, tiled=True),
    )
    query_cols = query_rows.shape[1]
    pair_cols = key_rows.shape[1]
    w_proj = jnp.concatenate([query_rows, key_rows, value_rows], axis=1)
    proj_cols = w_proj.shape[1]
    heads_here = query_cols // HD
    group_size = QH // KVH
    key_heads = (part_here * heads_here + jnp.arange(heads_here, dtype=jnp.int32)) // group_size
    gain_row = gain[0]
    segment_table = segment_ids[0]
    last_phase = phase_count - 1
    prompt_numbers = jnp.arange(SEGS, dtype=jnp.int32)

    def advance(tick_index, loop_state):
        current, pooled = loop_state
        batch_index = tick_index - phase_here
        active = (batch_index >= 0) & (batch_index < phase_count)
        batch_slot = jnp.clip(batch_index, 0, phase_count - 1)
        fresh_rows = lax.dynamic_index_in_dim(
            waiting, jnp.clip(tick_index, 0, phase_count - 1), 0, keepdims=False
        )
        tok_rows = jnp.where(phase_here == 0, fresh_rows, current)
        tok_segments = lax.dynamic_index_in_dim(segment_table, batch_slot, 0, keepdims=False)
        tok_float = tok_rows.astype(jnp.float32)
        whole_rows = lax.all_gather(tok_rows, "mp", axis=1, tiled=True)
        whole_float = whole_rows.astype(jnp.float32)
        squares = jnp.sum(whole_float * whole_float, axis=1)
        projected = lax.cond(
            active,
            lambda: jnp.dot(
                (whole_float * gain_row[None, :]).astype(jnp.bfloat16),
                w_proj,
                preferred_element_type=jnp.float32,
            ),
            lambda: jnp.zeros((batch_rows, proj_cols), jnp.float32),
        )
        qkv_rows = (projected * lax.rsqrt(squares / D + NORM_EPS)[:, None]).astype(jnp.bfloat16)
        query = qkv_rows[:, :query_cols].reshape(batch_rows, heads_here, HD)
        key_own = qkv_rows[:, query_cols : query_cols + pair_cols]
        value_own = qkv_rows[:, query_cols + pair_cols :]
        key_all, value_all = (
            lax.all_gather(key_own, "mp", axis=1, tiled=True),
            lax.all_gather(value_own, "mp", axis=1, tiled=True),
        )
        key_sel = jnp.take(key_all.reshape(batch_rows, KVH, HD), key_heads, axis=1)
        value_sel = jnp.take(value_all.reshape(batch_rows, KVH, HD), key_heads, axis=1)
        mixed_own = attend_heads(query, key_sel, value_sel, tok_segments)
        mixed = lax.all_gather(mixed_own, "mp", axis=1, tiled=True)
        updated = lax.cond(
            active,
            lambda: (
                tok_float + jnp.dot(mixed, back_rows, preferred_element_type=jnp.float32)
            ).astype(jnp.bfloat16),
            lambda: tok_rows,
        )
        segment_hits = tok_segments[None, :] == prompt_numbers[:, None]
        segment_sums = jnp.dot(
            segment_hits.astype(jnp.bfloat16), updated, preferred_element_type=jnp.float32
        )
        counts = jnp.sum(segment_hits.astype(jnp.float32), axis=1)
        segment_means = segment_sums / counts[:, None]
        store_here = active & (phase_here == last_phase)
        stored = lax.dynamic_index_in_dim(pooled, batch_slot, 0, keepdims=False)
        pooled = lax.dynamic_update_index_in_dim(
            pooled, jnp.where(store_here, segment_means, stored), batch_slot, 0
        )
        passed = from_behind(updated, "phase", 1)
        return (passed, pooled)

    start_state = (
        jnp.zeros((batch_rows, feature_cols), jnp.bfloat16),
        jnp.zeros((phase_count, SEGS, feature_cols), jnp.float32),
    )
    current, pooled = lax.fori_loop(0, phase_count + phase_count - 1, advance, start_state)
    shared = broadcast(pooled.astype(jnp.bfloat16), "phase", last_phase)
    own_prompts = lax.dynamic_index_in_dim(shared, phase_here, 0, keepdims=False).reshape(
        halves_here, PH, feature_cols
    )
    owner_ids = owner[0, :, :, 0]
    return_cap = max(2, PH // min(dp_count, 4))
    send_slots = owner_ids * return_cap + bucket_ranks(owner_ids, dp_count)
    parcel = (
        jnp.zeros((halves_here, dp_count * return_cap, feature_cols), jnp.bfloat16)
        .at[half_index, send_slots]
        .set(own_prompts)
    )
    returned = lax.all_to_all(
        parcel.reshape(halves_here, dp_count, return_cap, feature_cols),
        "dp",
        split_axis=1,
        concat_axis=1,
        tiled=True,
    )
    return returned.reshape(1, halves_here, dp_count * return_cap, feature_cols)


LAG = 2
CHIPS = 4
GROUP_Q = QH // KVH
Q_COLS = GROUP_Q * HD
KV_AT = Q_COLS + 2 * HD
MSG_COLS = KV_AT + 128
RANKS = 8
TABLE_ROW = 6
F32 = jnp.float32
BF16 = jnp.bfloat16


def vmem_spec():
    return pl.BlockSpec(memory_space=pltpu.VMEM)


def smem_spec():
    return pl.BlockSpec(memory_space=pltpu.SMEM)


def hbm_spec():
    return pl.BlockSpec(memory_space=pl.ANY)


def call(kernel, outs, args, specs, scratch=(), limit=6, token=None):
    count = len(args)

    def body(*refs):
        at = count + 1 + len(outs)
        refs[at][...] = jnp.zeros(refs[at].shape, F32)
        kernel(*refs[:count], *refs[count + 1 : at], *refs[at + 1 :])

    outs = list(outs)
    if token is not None:
        outs_all = outs + [jax.ShapeDtypeStruct((8, 128), F32)]
        args, specs = ((*args, token), [*specs, pl.BlockSpec(memory_space=pl.ANY)])
    else:
        outs_all = outs
    return pl.pallas_call(
        kernel if token is None else body,
        out_shape=outs_all,
        in_specs=specs,
        out_specs=[vmem_spec()] * len(outs_all),
        scratch_shapes=list(scratch),
        compiler_params=pltpu.CompilerParams(vmem_limit_bytes=limit * 1024 * 1024),
    )(*args)


def dot(a, b):
    return jnp.dot(a, b, preferred_element_type=F32)


def lane(start, size):
    return pl.ds(pl.multiple_of(start, size), size)


def iota(rows, cols, axis):
    return lax.broadcasted_iota(jnp.int32, (rows, cols), axis)


def as_column(row):
    count = row.shape[1]
    diagonal = iota(count, count, 0) == iota(count, count, 1)
    return jnp.sum(jnp.where(diagonal, row, 0), axis=1, keepdims=True)


def marks(hits):
    return hits.astype(F32).astype(BF16)


def pack_kernel(pos_ref, rows_ref, dest_ref, table_ref, *out_refs):
    chip = pos_ref[0]
    dest = dest_ref[pl.ds(chip, 1), :]
    count = dest.shape[1]
    half = count // 2
    group_row = dest // half
    group_col = as_column(group_row)
    source, here = (iota(count, count, 0), iota(count, count, 1))
    before = (group_col == group_row) & (source // half == here // half) & (source < here)
    rank = jnp.sum(jnp.where(before, 1, 0), axis=0, keepdims=True)
    target = group_row * (2 * RANKS) + (iota(1, count, 1) // half) * RANKS + rank
    width = out_refs[0].shape[1]
    message_row = iota(4 * RANKS, width, 0)
    for k in range(CHIPS):
        turn = chip ^ k
        core, block = (turn & 1, turn >> 1)
        pick = marks(iota(4 * RANKS, count, 0) + core * (4 * RANKS) == target)
        rows = dot(pick, rows_ref[:, lane(block * width, width)])
        rows = jnp.where(message_row == TABLE_ROW, table_ref[...], rows)
        out_refs[k][...] = rows.astype(BF16)


def unpack_kernel(pos_ref, m0, m1, m2, m3, dest_ref, out_ref, table_ref):
    chip, core = (pos_ref[0], pos_ref[2])
    count = dest_ref.shape[1]
    half = count // 2
    turn = 2 * (chip & 1) + core
    total = jnp.zeros(out_ref.shape, F32)
    table = jnp.zeros(table_ref.shape, F32)
    above, across = (iota(count, count, 0), iota(count, count, 1))
    for k, ref in enumerate((m0, m1, m2, m3)):
        loader = turn ^ k
        dest_row = dest_ref[pl.ds(loader, 1), :]
        group_row = dest_row // half
        group_col = as_column(group_row)
        earlier = (group_col == group_row) & (above // half == across // half) & (across < above)
        rank = jnp.sum(jnp.where(earlier, 1, 0), axis=1, keepdims=True)
        at = (group_col - 2 * core) * (2 * RANKS) + (iota(count, 1, 0) // half) * RANKS + rank
        from_message = marks(iota(count, 4 * RANKS, 1) == at)
        slot = (group_row - 2 * core) * count + (iota(1, count, 1) // half) * half + dest_row % half
        to_slot = marks(iota(2 * count, count, 0) == slot)
        rows = ref[...]
        total += dot(dot(to_slot, from_message).astype(BF16), rows)
        mine = (loader >> 1) == core
        table += jnp.where(mine, rows[TABLE_ROW : TABLE_ROW + 1].astype(F32), 0.0)
    out_ref[...] = total.astype(BF16)
    table_ref[...] = table


def stage_kernel(*refs):
    *refs, sems = refs
    count = len(refs) // 2
    copies = [pltpu.make_async_copy(refs[i], refs[count + i], sems.at[i]) for i in range(count)]
    for copy in copies:
        copy.start()
    for copy in copies:
        copy.wait()


def pick_rows(slot, pos_ref, wait_ref, recv_ref):
    if wait_ref is None:
        return recv_ref[...]
    count = wait_ref.shape[0] // 2
    at = (slot % 2) * count
    waiting = wait_ref[at : at + count]
    if recv_ref is None:
        return waiting
    return jnp.where(pos_ref[1] == 0, waiting, recv_ref[...])


def place_of(pos_ref, head):
    gap = head ^ pos_ref[0]
    first = 1 + pos_ref[2]
    return jnp.where(gap == first, 2, jnp.where(gap == 3, 3, jnp.where(gap == 0, 0, 1)))


def hand_out(results_ref, keep_ref, send_ref):
    for j in range(2):
        keep_ref[j] = results_ref[j]
        send_ref[j] = results_ref[2 + j]


def project_kernel(slot, has_wait, has_recv, pos_ref, *refs):
    refs = list(refs)
    wait_ref = refs.pop(0) if has_wait else None
    recv_ref = refs.pop(0) if has_recv else None
    gain_ref, *sources, keep_ref, send_ref, results_ref = refs
    chip, core = (pos_ref[0], pos_ref[2])
    rows = pick_rows(slot, pos_ref, wait_ref, recv_ref).astype(F32)
    depth = rows.shape[1]
    gated = (rows * gain_ref[:, lane(chip * depth, depth)]).astype(BF16)
    squares = jnp.sum(rows * rows, axis=1, keepdims=True)
    high = squares.astype(BF16).astype(F32)
    tail = jnp.where(iota(rows.shape[0], 128, 1) < 64, high, squares - high).astype(BF16)

    for at, source in enumerate(sources):
        part, i = (core if at < 3 else 1 - core, at % 3)
        places = [place_of(pos_ref, 2 * part + j) for j in range(2)]
        step = min(source.shape[2], 512)
        for start in range(0, source.shape[2], step):
            result = dot(gated, source[0, :, start : start + step]).astype(BF16)
            if i == 0:
                inside = start % Q_COLS
                results_ref[places[start // Q_COLS], :, inside : inside + step] = result
            else:
                inside = Q_COLS + (i - 1) * HD
                for j in range(2):
                    results_ref[places[j], :, inside : inside + HD] = result[:, j * HD : (j + 1) * HD]
    for j in range(4):
        results_ref[j, :, KV_AT:] = tail
    hand_out(results_ref, keep_ref, send_ref)


def join_kernel(keep_ref, got_ref, out_ref):
    out_ref[...] = (keep_ref[1].astype(F32) + got_ref[1].astype(F32)).astype(BF16)


def means(table_ref, chunk, count, rows):
    segment = table_ref[:, chunk * 128 : chunk * 128 + count].astype(jnp.int32)
    hits = (segment == iota(16, count, 0)) & (iota(16, count, 0) < SEGS)
    counts = jnp.sum(jnp.where(hits, 1.0, 0.0), axis=1, keepdims=True)
    return dot(marks(hits), rows) / jnp.maximum(counts, 1.0)


def attend_kernel(features, slot, chunks, pool_chunk, pos_ref, keep_in, first_in, second_in, table_ref, *refs):
    own_ref, other_ref, keep_ref, send_ref, results_ref = refs
    core = pos_ref[2]
    sums = keep_in[0].astype(F32) + first_in[0].astype(F32) + second_in[...].astype(F32)
    count = sums.shape[0]
    tail = sums[:, KV_AT:]
    squares = tail[:, 0:1] + tail[:, 64:65]
    scaled = (sums[:, :KV_AT] * lax.rsqrt(squares / features + NORM_EPS)).astype(BF16)
    query = jnp.concatenate([scaled[:, h * HD : (h + 1) * HD] for h in range(GROUP_Q)], axis=0)
    key = scaled[:, Q_COLS : Q_COLS + HD]
    value = scaled[:, Q_COLS + HD :]
    scores = lax.dot_general(query, key, (((1,), (1,)), ((), ())), preferred_element_type=F32)
    scores = (scores * HD ** (-0.5)).reshape(GROUP_Q, count, count)
    chunk = jnp.clip(slot - LAG * pos_ref[1], 0, chunks - 1)
    segment = table_ref[:, lane(chunk * 128, 128)][:, :count].astype(jnp.int32)
    allowed = (as_column(segment) == segment) & (iota(count, count, 1) <= iota(count, count, 0))
    scores = jnp.where(allowed[None], scores, -jnp.inf)
    top = jnp.max(scores, axis=2, keepdims=True)
    weights = jnp.exp(scores - top)
    probs = (weights / jnp.sum(weights, axis=2, keepdims=True)).astype(BF16)
    mixed = dot(probs.reshape(GROUP_Q * count, count), value).astype(BF16)
    mixed = jnp.concatenate([mixed[h * count : (h + 1) * count] for h in range(GROUP_Q)], axis=1)
    if pool_chunk is not None:
        mixed = means(table_ref, pool_chunk, count, mixed).astype(BF16)
    step = own_ref.shape[2] // 8
    for part, source in ((core, own_ref), (1 - core, other_ref)):
        places = [place_of(pos_ref, 2 * part + j) for j in range(2)]
        for at in range(8):
            result = dot(mixed, source[0, :, at * step : (at + 1) * step]).astype(BF16)
            results_ref[places[at // 4], :, (at % 4) * step : (at % 4 + 1) * step] = result
    hand_out(results_ref, keep_ref, send_ref)


def update_kernel(slot, has_wait, has_recv, send, pool_chunk, pooled_sums, pos_ref, *refs):
    refs = list(refs)
    wait_ref = refs.pop(0) if has_wait else None
    recv_ref = refs.pop(0) if has_recv else None
    keep_in, first_in, second_in, table_ref, *refs = refs
    before_ref = refs.pop(0) if pool_chunk is not None and pool_chunk % 2 else None
    rows = pick_rows(slot, pos_ref, wait_ref, recv_ref)
    if pooled_sums:
        total = means(table_ref, pool_chunk, rows.shape[0], rows)
    else:
        total = rows.astype(F32)
    total += keep_in[0].astype(F32) + first_in[0].astype(F32) + second_in[...].astype(F32)
    hidden = total.astype(BF16)
    if send:
        refs.pop(0)[...] = hidden
    if pool_chunk is not None:
        pooled = hidden if pooled_sums else means(table_ref, pool_chunk, rows.shape[0], hidden).astype(BF16)
        if before_ref is None:
            refs.pop(0)[...] = pooled
        else:
            out_ref = refs.pop(0)
            out_ref[0] = before_ref[...]
            out_ref[1] = pooled


def parcel_kernel(owner_at, pos_ref, p0, p1, p2, p3, table_ref, *out_refs):
    chip, phase, core = (pos_ref[0], pos_ref[1], pos_ref[2])
    rows = jnp.where(phase == 0, p0[...], p1[...])
    rows = jnp.where(phase < 2, rows, jnp.where(phase == 2, p2[...], p3[...]))
    rows = jnp.concatenate([rows[0], rows[1]], axis=0)
    count = rows.shape[0]
    own_row = table_ref[:, owner_at : owner_at + count].astype(jnp.int32) - 1
    own_col = as_column(own_row)
    above, across = (iota(count, count, 0), iota(count, count, 1))
    same = (above // 16 == across // 16) & ((above % 16 >= PH) == (across % 16 >= PH))
    earlier = (own_col == own_row) & same & (above < across)
    rank = jnp.sum(jnp.where(earlier, 1, 0), axis=0, keepdims=True)
    place = iota(1, count, 1)
    half = jnp.where(place % 16 >= PH, 1, 0)
    slot = half * 8 + (2 * core + place // 16) * 2 + rank
    turn = 2 * (chip & 1) + core
    for k in range(CHIPS):
        pick = marks((iota(16, count, 0) == slot) & (own_row == (turn ^ k)))
        out_refs[k][...] = dot(pick, rows).astype(BF16)


def deliver_kernel(pos_ref, m0, m1, m2, m3, out_ref):
    chip = pos_ref[0]
    width = m0.shape[1]
    out_ref[...] = jnp.zeros_like(out_ref)
    for k, ref in enumerate((m0, m1, m2, m3)):
        cols = lane(((chip ^ k) >> 1) * width, width)
        out_ref[:, cols] = out_ref[:, cols] + ref[...]


def chip_shards(prompt_rows, row_dest, segment_ids, owner, gain, w_query, w_key, w_value, w_out):
    chip, phase, core = (lax.axis_index("dp"), lax.axis_index("phase"), lax.axis_index("mp"))
    phases = lax.axis_size("phase")
    pos = jnp.stack([chip, phase, core]).astype(jnp.int32)
    halves, half_rows, cols_here = prompt_rows.shape[1:]
    batch = halves * half_rows
    features = 2 * cols_here
    block = features // CHIPS
    count = batch
    square = [(e, k) for e in range(CHIPS) for k in range(2)]

    def crosswise(value, k):
        pairs = [(2 * e + m, 2 * (2 * m + ((e ^ k) >> 1)) + ((e ^ k) & 1)) for e, m in square]
        return lax.ppermute(value, ("dp", "mp"), pairs)

    def homewards(value, k):
        pairs = [(2 * e + c, 2 * ((2 * (e & 1) + c) ^ k) + (e >> 1)) for e, c in square]
        return lax.ppermute(value, ("dp", "mp"), pairs)

    def partner(value, first):
        pairs = [(2 * e + c, 2 * (e ^ (1 + c if first else 2 - c)) + c) for e, c in square]
        return lax.ppermute(value, ("dp", "mp"), pairs)

    def swap(value):
        return lax.ppermute(value, "mp", [(0, 1), (1, 0)])

    with jax.named_scope("packing"):
        parity = chip % 2
        chunks = 2 * phases
        owner_at = chunks * 128
        table = jnp.zeros((phases, 2, 128), F32)
        numbers = segment_ids[0][:, None, :].astype(F32)
        table = lax.dynamic_update_slice(table, numbers, (0, parity, 0)).reshape(1, -1)
        owners = (owner.reshape(1, -1) + 1).astype(F32)
        last = lax.dynamic_update_slice(jnp.zeros((1, block - owner_at), F32), owners, (0, 16 * parity))
        table = jnp.concatenate([table, last], axis=1)
        dest = row_dest.reshape(CHIPS, batch)
        *packed, token = call(
            pack_kernel,
            [jax.ShapeDtypeStruct((4 * RANKS, block), BF16)] * CHIPS,
            (pos, prompt_rows.reshape(batch, cols_here), dest, table),
            [smem_spec()] + [vmem_spec()] * 3,
            token=jnp.zeros((8, 128), F32),
        )
        own = (w_query, w_key, w_value, w_out)
        own = [pltpu.with_memory_space_constraint(w, pltpu.HBM) for w in own]
        *own, token = call(
            stage_kernel,
            [pltpu.VMEM(w.shape, BF16) for w in own],
            own,
            [hbm_spec()] * 4,
            (pltpu.SemaphoreType.DMA((4,)),),
            token=token,
        )
        arrived = [crosswise(value, k) for k, value in enumerate(packed)]
        start, table, token = call(
            unpack_kernel,
            [jax.ShapeDtypeStruct((2 * batch, block), BF16), jax.ShapeDtypeStruct((1, block), F32)],
            (pos, *arrived, dest),
            [smem_spec()] + [vmem_spec()] * 5,
            token=token,
        )
        waiting = [start]

    with jax.named_scope("weights"):

        def held(values):
            return [pltpu.with_memory_space_constraint(value, pltpu.VMEM) for value in values]

        other = [swap(w) for w in (w_query, w_key, w_value)]
        w_in = held([*own[:3], *other])
        last, *_ = lax.optimization_barrier((w_out, start, *other))
        w_back = held([own[3], swap(last)])

    hops, pooled, kept, first, second = ({}, {}, {}, {}, {})
    slots = chunks + LAG * (phases - 1)

    def plan(slot):
        chunk = slot - LAG * (phases - 1)
        send = slot < chunks + LAG * (phases - 2)
        pool_chunk = chunk if chunk >= 0 else None
        return (send, pool_chunk, pool_chunk is not None and not send)

    def entering(slot):
        inputs = waiting[slot // 2 : slot // 2 + 1] + [hops[at] for at in (slot - LAG,) if at >= 0]
        return (slot < chunks, slot >= LAG, inputs, [smem_spec()] + [vmem_spec()] * len(inputs))

    def project(slot, token):
        has_wait, has_recv, inputs, specs = entering(slot)
        kept[slot], sent, token = call(
            functools.partial(project_kernel, slot, has_wait, has_recv),
            [jax.ShapeDtypeStruct((2, count, MSG_COLS), BF16)] * 2,
            (pos, *inputs, gain, *w_in),
            specs + [vmem_spec()] * 7,
            (pltpu.VMEM((CHIPS, count, MSG_COLS), BF16),),
            10,
            token,
        )
        first[slot] = partner(sent, True)
        return token

    def join(slot, token):
        joined, token = call(
            join_kernel,
            [jax.ShapeDtypeStruct(kept[slot].shape[1:], BF16)],
            (kept[slot], first[slot]),
            [vmem_spec()] * 2,
            token=token,
        )
        second[slot] = partner(joined, False)
        return token

    def attend(slot, token):
        _, pool_chunk, early_pool = plan(slot)
        rows = 16 if early_pool else count
        kept[slot], sent, token = call(
            functools.partial(attend_kernel, features, slot, chunks, pool_chunk if early_pool else None),
            [jax.ShapeDtypeStruct((2, rows, block), BF16)] * 2,
            (pos, kept[slot], first[slot], second[slot], table, *w_back),
            [smem_spec()] + [vmem_spec()] * 6,
            (pltpu.VMEM((CHIPS, rows, block), BF16),),
            10,
            token,
        )
        first[slot] = partner(sent, True)
        return token

    def update(slot, token):
        has_wait, has_recv, inputs, specs = entering(slot)
        send, pool_chunk, early_pool = plan(slot)
        outs = [jax.ShapeDtypeStruct((count, block), BF16)] * send
        before = []
        if pool_chunk is not None:
            odd = pool_chunk % 2 == 1
            outs.append(jax.ShapeDtypeStruct((2, 16, block) if odd else (16, block), BF16))
            before = [pooled[pool_chunk - 1]] if odd else []
        *out, token = call(
            functools.partial(update_kernel, slot, has_wait, has_recv, send, pool_chunk, early_pool),
            outs,
            (pos, *inputs, kept[slot], first[slot], second[slot], table, *before),
            specs + [vmem_spec()] * (4 + len(before)),
            token=token,
        )
        if send:
            live = [p for p in range(phases - 1) if 0 <= slot - LAG * p < chunks]
            hops[slot] = lax.ppermute(out.pop(0), "phase", [(p, p + 1) for p in live])
        if pool_chunk is not None:
            pooled[pool_chunk] = out.pop(0)
        return token

    for step in range(slots + 1):
        before, now = (step > 0, step < slots)
        if step % 2 == 0 and step < chunks - 2:
            down = [(p, p - 1) for p in range(1, phases - step // 2)]
            waiting.append(lax.ppermute(waiting[-1], "phase", down))
        if now:
            with jax.named_scope("project"):
                token = project(step, token)
        if before:
            with jax.named_scope("join_output"):
                token = join(step - 1, token)
        if now:
            with jax.named_scope("join_projection"):
                token = join(step, token)
        if before:
            with jax.named_scope("update"):
                token = update(step - 1, token)
        if now:
            with jax.named_scope("attend"):
                token = attend(step, token)

    with jax.named_scope("deliver"):
        shares = [lax.ppermute(pooled[2 * m + 1], "phase", [(phases - 1, m)]) for m in range(phases - 1)]
        parcels = call(
            functools.partial(parcel_kernel, owner_at),
            [jax.ShapeDtypeStruct((16, block), BF16)] * CHIPS,
            (pos, *shares, pooled[chunks - 1], table),
            [smem_spec()] + [vmem_spec()] * 5,
        )
        final = [homewards(value, k) for k, value in enumerate(parcels)]
        (result,) = call(
            deliver_kernel,
            [jax.ShapeDtypeStruct((16, cols_here), BF16)],
            (pos, *final),
            [smem_spec()] + [vmem_spec()] * 4,
        )
    return result.reshape(1, 2, 8, cols_here)


def solution(mesh):
    in_specs = (
        P("dp", "phase", None, "mp"),
        P(None, "phase", None),
        P("dp", None, None),
        P("dp", "phase", None, None),
        P("phase", None),
        P("phase", "dp", "mp"),
        P("phase", "dp", "mp"),
        P("phase", "dp", "mp"),
        P("phase", "dp", "mp"),
    )
    out_specs = P("dp", "phase", None, "mp")
    square = mesh.shape["dp"] == CHIPS and mesh.shape["mp"] == 2 and mesh.shape["phase"] == 4
    shards = chip_shards if square else general_shards
    return jax.shard_map(shards, mesh=mesh, in_specs=in_specs, out_specs=out_specs, check_vma=False)
```

```python
import functools

import jax
import jax.numpy as jnp
from jax import lax
from jax.experimental import pallas as pl
from jax.experimental.pallas import tpu as pltpu
from jax.sharding import PartitionSpec as P

D = 8192
HD = 128
QH = 32
KVH = 4
SEGS = 6
PH = 3


NORM_EPS = 1e-05


def from_behind(value, axis, steps):
    count = lax.axis_size(axis)
    initial, last = (max(0, -steps), min(count, count - steps))
    return lax.ppermute(value, axis, [(source, source + steps) for source in range(initial, last)])


def broadcast(value, axis, root):
    mine = lax.axis_index(axis) == root
    return lax.psum(jnp.where(mine, value, jnp.zeros_like(value)), axis)


def bucket_ranks(labels, buckets):
    hits_table = (labels[..., None] == jnp.arange(buckets, dtype=jnp.int32)).astype(jnp.int32)
    earlier = jnp.cumsum(hits_table, axis=-2) - hits_table
    return jnp.sum(earlier * hits_table, axis=-1)


def attend_heads(query, key_sel, value_sel, segments):
    head_dim = query.shape[2]
    scores = jnp.einsum("qhd,khd->hqk", query, key_sel, preferred_element_type=jnp.float32)
    scores = scores * head_dim ** (-0.5)
    places = jnp.arange(query.shape[0], dtype=jnp.int32)
    allowed = (segments[:, None] == segments[None, :]) & (places[None, :] <= places[:, None])
    scores = jnp.where(allowed[None, :, :], scores, -jnp.inf)
    row_top = jnp.max(scores, axis=2, keepdims=True)
    weights = jnp.exp(scores - row_top)
    probabilities = (weights / jnp.sum(weights, axis=2, keepdims=True)).astype(jnp.bfloat16)
    mixed = jnp.einsum("hqk,khd->qhd", probabilities, value_sel, preferred_element_type=jnp.float32)
    return mixed.astype(jnp.bfloat16).reshape(query.shape[0], -1)


def general_shards(prompt_rows, row_dest, segment_ids, owner, gain, w_query, w_key, w_value, w_out):
    dp_count = lax.axis_size("dp")
    phase_count = lax.axis_size("phase")
    group_here = lax.axis_index("dp")
    phase_here = lax.axis_index("phase")
    part_here = lax.axis_index("mp")
    halves_here = prompt_rows.shape[1]
    half_rows = prompt_rows.shape[2]
    feature_cols = prompt_rows.shape[3]
    batch_rows = halves_here * half_rows
    capacity = half_rows // min(dp_count, 4)
    half_index = jnp.arange(halves_here, dtype=jnp.int32)[:, None]
    dest_group = row_dest // half_rows
    dest_ranks = bucket_ranks(dest_group, dp_count)
    own_groups = lax.dynamic_index_in_dim(dest_group, group_here, 0, keepdims=False)
    own_ranks = lax.dynamic_index_in_dim(dest_ranks, group_here, 0, keepdims=False)
    send_at = own_groups * capacity + own_ranks
    outgoing = (
        jnp.zeros((halves_here, dp_count * capacity, feature_cols), jnp.bfloat16)
        .at[half_index, send_at]
        .set(prompt_rows[0])
    )
    incoming = lax.all_to_all(
        outgoing.reshape(halves_here, dp_count, capacity, feature_cols),
        "dp",
        split_axis=1,
        concat_axis=1,
        tiled=True,
    )
    source_ids = jnp.arange(dp_count, dtype=jnp.int32)[:, None, None]
    where_from = jnp.transpose(source_ids * capacity + dest_ranks, (1, 0, 2)).reshape(
        halves_here, -1
    )
    target = jnp.where(dest_group == group_here, row_dest % half_rows, half_rows)
    target = jnp.transpose(target, (1, 0, 2)).reshape(halves_here, -1)
    arrived = incoming.reshape(halves_here, dp_count * capacity, feature_cols)[
        half_index, where_from
    ]
    own_halves = (
        jnp.zeros((halves_here, half_rows, feature_cols), jnp.bfloat16)
        .at[half_index, target]
        .set(arrived, mode="drop")
    )
    own_batch = own_halves.reshape(batch_rows, feature_cols)
    waiting = lax.all_gather(own_batch, "phase", axis=0, tiled=True).reshape(
        phase_count, batch_rows, feature_cols
    )
    query_rows, key_rows, value_rows, back_rows = (
        lax.all_gather(w_query[0], "dp", axis=0, tiled=True),
        lax.all_gather(w_key[0], "dp", axis=0, tiled=True),
        lax.all_gather(w_value[0], "dp", axis=0, tiled=True),
        lax.all_gather(w_out[0], "dp", axis=0, tiled=True),
    )
    query_cols = query_rows.shape[1]
    pair_cols = key_rows.shape[1]
    w_proj = jnp.concatenate([query_rows, key_rows, value_rows], axis=1)
    proj_cols = w_proj.shape[1]
    heads_here = query_cols // HD
    group_size = QH // KVH
    key_heads = (part_here * heads_here + jnp.arange(heads_here, dtype=jnp.int32)) // group_size
    gain_row = gain[0]
    segment_table = segment_ids[0]
    last_phase = phase_count - 1
    prompt_numbers = jnp.arange(SEGS, dtype=jnp.int32)

    def advance(tick_index, loop_state):
        current, pooled = loop_state
        batch_index = tick_index - phase_here
        active = (batch_index >= 0) & (batch_index < phase_count)
        batch_slot = jnp.clip(batch_index, 0, phase_count - 1)
        fresh_rows = lax.dynamic_index_in_dim(
            waiting, jnp.clip(tick_index, 0, phase_count - 1), 0, keepdims=False
        )
        tok_rows = jnp.where(phase_here == 0, fresh_rows, current)
        tok_segments = lax.dynamic_index_in_dim(segment_table, batch_slot, 0, keepdims=False)
        tok_float = tok_rows.astype(jnp.float32)
        whole_rows = lax.all_gather(tok_rows, "mp", axis=1, tiled=True)
        whole_float = whole_rows.astype(jnp.float32)
        squares = jnp.sum(whole_float * whole_float, axis=1)
        projected = lax.cond(
            active,
            lambda: jnp.dot(
                (whole_float * gain_row[None, :]).astype(jnp.bfloat16),
                w_proj,
                preferred_element_type=jnp.float32,
            ),
            lambda: jnp.zeros((batch_rows, proj_cols), jnp.float32),
        )
        qkv_rows = (projected * lax.rsqrt(squares / D + NORM_EPS)[:, None]).astype(jnp.bfloat16)
        query = qkv_rows[:, :query_cols].reshape(batch_rows, heads_here, HD)
        key_own = qkv_rows[:, query_cols : query_cols + pair_cols]
        value_own = qkv_rows[:, query_cols + pair_cols :]
        key_all, value_all = (
            lax.all_gather(key_own, "mp", axis=1, tiled=True),
            lax.all_gather(value_own, "mp", axis=1, tiled=True),
        )
        key_sel = jnp.take(key_all.reshape(batch_rows, KVH, HD), key_heads, axis=1)
        value_sel = jnp.take(value_all.reshape(batch_rows, KVH, HD), key_heads, axis=1)
        mixed_own = attend_heads(query, key_sel, value_sel, tok_segments)
        mixed = lax.all_gather(mixed_own, "mp", axis=1, tiled=True)
        updated = lax.cond(
            active,
            lambda: (
                tok_float + jnp.dot(mixed, back_rows, preferred_element_type=jnp.float32)
            ).astype(jnp.bfloat16),
            lambda: tok_rows,
        )
        segment_hits = tok_segments[None, :] == prompt_numbers[:, None]
        segment_sums = jnp.dot(
            segment_hits.astype(jnp.bfloat16), updated, preferred_element_type=jnp.float32
        )
        counts = jnp.sum(segment_hits.astype(jnp.float32), axis=1)
        segment_means = segment_sums / counts[:, None]
        store_here = active & (phase_here == last_phase)
        stored = lax.dynamic_index_in_dim(pooled, batch_slot, 0, keepdims=False)
        pooled = lax.dynamic_update_index_in_dim(
            pooled, jnp.where(store_here, segment_means, stored), batch_slot, 0
        )
        passed = from_behind(updated, "phase", 1)
        return (passed, pooled)

    start_state = (
        jnp.zeros((batch_rows, feature_cols), jnp.bfloat16),
        jnp.zeros((phase_count, SEGS, feature_cols), jnp.float32),
    )
    current, pooled = lax.fori_loop(0, phase_count + phase_count - 1, advance, start_state)
    shared = broadcast(pooled.astype(jnp.bfloat16), "phase", last_phase)
    own_prompts = lax.dynamic_index_in_dim(shared, phase_here, 0, keepdims=False).reshape(
        halves_here, PH, feature_cols
    )
    owner_ids = owner[0, :, :, 0]
    return_cap = max(2, PH // min(dp_count, 4))
    send_slots = owner_ids * return_cap + bucket_ranks(owner_ids, dp_count)
    parcel = (
        jnp.zeros((halves_here, dp_count * return_cap, feature_cols), jnp.bfloat16)
        .at[half_index, send_slots]
        .set(own_prompts)
    )
    returned = lax.all_to_all(
        parcel.reshape(halves_here, dp_count, return_cap, feature_cols),
        "dp",
        split_axis=1,
        concat_axis=1,
        tiled=True,
    )
    return returned.reshape(1, halves_here, dp_count * return_cap, feature_cols)


LAG = 2
CHIPS = 4
GROUP_Q = QH // KVH
Q_COLS = GROUP_Q * HD
KV_AT = Q_COLS + 2 * HD
MSG_COLS = KV_AT + 128
RANKS = 8
TABLE_ROW = 6
F32 = jnp.float32
BF16 = jnp.bfloat16


def vmem_spec():
    return pl.BlockSpec(memory_space=pltpu.VMEM)


def smem_spec():
    return pl.BlockSpec(memory_space=pltpu.SMEM)


def hbm_spec():
    return pl.BlockSpec(memory_space=pl.ANY)


def call(kernel, outs, args, specs, scratch=(), limit=6, token=None):
    count = len(args)

    def body(*refs):
        at = count + 1 + len(outs)
        refs[at][...] = jnp.zeros(refs[at].shape, F32)
        kernel(*refs[:count], *refs[count + 1 : at], *refs[at + 1 :])

    outs = list(outs)
    if token is not None:
        outs_all = outs + [jax.ShapeDtypeStruct((8, 128), F32)]
        args, specs = ((*args, token), [*specs, pl.BlockSpec(memory_space=pl.ANY)])
    else:
        outs_all = outs
    return pl.pallas_call(
        kernel if token is None else body,
        out_shape=outs_all,
        in_specs=specs,
        out_specs=[vmem_spec()] * len(outs_all),
        scratch_shapes=list(scratch),
        compiler_params=pltpu.CompilerParams(vmem_limit_bytes=limit * 1024 * 1024),
    )(*args)


def dot(a, b):
    return jnp.dot(a, b, preferred_element_type=F32)


def lane(start, size):
    return pl.ds(pl.multiple_of(start, size), size)


def iota(rows, cols, axis):
    return lax.broadcasted_iota(jnp.int32, (rows, cols), axis)


def as_column(row):
    count = row.shape[1]
    diagonal = iota(count, count, 0) == iota(count, count, 1)
    return jnp.sum(jnp.where(diagonal, row, 0), axis=1, keepdims=True)


def marks(hits):
    return hits.astype(F32).astype(BF16)


def pack_kernel(pos_ref, rows_ref, dest_ref, table_ref, *out_refs):
    chip = pos_ref[0]
    dest = dest_ref[pl.ds(chip, 1), :]
    count = dest.shape[1]
    half = count // 2
    group_row = dest // half
    group_col = as_column(group_row)
    source, here = (iota(count, count, 0), iota(count, count, 1))
    before = (group_col == group_row) & (source // half == here // half) & (source < here)
    rank = jnp.sum(jnp.where(before, 1, 0), axis=0, keepdims=True)
    target = group_row * (2 * RANKS) + (iota(1, count, 1) // half) * RANKS + rank
    width = out_refs[0].shape[1]
    message_row = iota(4 * RANKS, width, 0)
    for k in range(CHIPS):
        turn = chip ^ k
        core, block = (turn & 1, turn >> 1)
        pick = marks(iota(4 * RANKS, count, 0) + core * (4 * RANKS) == target)
        rows = dot(pick, rows_ref[:, lane(block * width, width)])
        rows = jnp.where(message_row == TABLE_ROW, table_ref[...], rows)
        out_refs[k][...] = rows.astype(BF16)


def unpack_kernel(pos_ref, m0, m1, m2, m3, dest_ref, out_ref, table_ref):
    chip, core = (pos_ref[0], pos_ref[2])
    count = dest_ref.shape[1]
    half = count // 2
    turn = 2 * (chip & 1) + core
    total = jnp.zeros(out_ref.shape, F32)
    table = jnp.zeros(table_ref.shape, F32)
    above, across = (iota(count, count, 0), iota(count, count, 1))
    for k, ref in enumerate((m0, m1, m2, m3)):
        loader = turn ^ k
        dest_row = dest_ref[pl.ds(loader, 1), :]
        group_row = dest_row // half
        group_col = as_column(group_row)
        earlier = (group_col == group_row) & (above // half == across // half) & (across < above)
        rank = jnp.sum(jnp.where(earlier, 1, 0), axis=1, keepdims=True)
        at = (group_col - 2 * core) * (2 * RANKS) + (iota(count, 1, 0) // half) * RANKS + rank
        from_message = marks(iota(count, 4 * RANKS, 1) == at)
        slot = (group_row - 2 * core) * count + (iota(1, count, 1) // half) * half + dest_row % half
        to_slot = marks(iota(2 * count, count, 0) == slot)
        rows = ref[...]
        total += dot(dot(to_slot, from_message).astype(BF16), rows)
        mine = (loader >> 1) == core
        table += jnp.where(mine, rows[TABLE_ROW : TABLE_ROW + 1].astype(F32), 0.0)
    out_ref[...] = total.astype(BF16)
    table_ref[...] = table


def added(messages):
    total = messages[0][...].astype(F32)
    for ref in messages[1:]:
        total += ref[...].astype(F32)
    return total


def stage_kernel(*refs):
    *refs, sems = refs
    count = len(refs) // 2
    copies = [pltpu.make_async_copy(refs[i], refs[count + i], sems.at[i]) for i in range(count)]
    for copy in copies:
        copy.start()
    for copy in copies:
        copy.wait()


def pick_rows(slot, pos_ref, wait_ref, recv_ref):
    if wait_ref is None:
        return recv_ref[...]
    count = wait_ref.shape[0] // 2
    at = (slot % 2) * count
    waiting = wait_ref[at : at + count]
    if recv_ref is None:
        return waiting
    return jnp.where(pos_ref[1] == 0, waiting, recv_ref[...])


def project_kernel(slot, has_wait, has_recv, pos_ref, *refs):
    refs = list(refs)
    wait_ref = refs.pop(0) if has_wait else None
    recv_ref = refs.pop(0) if has_recv else None
    gain_ref, *refs = refs
    sources, out_refs, results_ref = (refs[:6], refs[6:10], refs[10])
    chip, core = (pos_ref[0], pos_ref[2])
    rows = pick_rows(slot, pos_ref, wait_ref, recv_ref).astype(F32)
    depth = rows.shape[1]
    gated = (rows * gain_ref[:, lane(chip * depth, depth)]).astype(BF16)
    squares = jnp.sum(rows * rows, axis=1, keepdims=True)
    high = squares.astype(BF16).astype(F32)
    tail = jnp.where(iota(rows.shape[0], 128, 1) < 64, high, squares - high).astype(BF16)

    for at, source in enumerate(sources):
        part, i = (core if at < 3 else 1 - core, at % 3)
        places = [(2 * part + j) ^ pos_ref[0] for j in range(2)]
        step = min(source.shape[2], 512)
        for start in range(0, source.shape[2], step):
            result = dot(gated, source[0, :, start : start + step]).astype(BF16)
            if i == 0:
                inside = start % Q_COLS
                results_ref[places[start // Q_COLS], :, inside : inside + step] = result
            else:
                inside = Q_COLS + (i - 1) * HD
                for j in range(2):
                    results_ref[places[j], :, inside : inside + HD] = result[:, j * HD : (j + 1) * HD]
    for k, out_ref in enumerate(out_refs):
        out_ref[:, :KV_AT] = results_ref[k]
        out_ref[:, KV_AT:] = tail


def means(table_ref, chunk, count, rows):
    segment = table_ref[:, chunk * 128 : chunk * 128 + count].astype(jnp.int32)
    hits = (segment == iota(16, count, 0)) & (iota(16, count, 0) < SEGS)
    counts = jnp.sum(jnp.where(hits, 1.0, 0.0), axis=1, keepdims=True)
    return dot(marks(hits), rows) / jnp.maximum(counts, 1.0)


def attend_kernel(features, slot, chunks, pool_chunk, pos_ref, *refs):
    messages, (table_ref, own_ref, other_ref) = (refs[:CHIPS], refs[CHIPS : CHIPS + 3])
    out_refs, results_ref = (refs[CHIPS + 3 : -1], refs[-1])
    core = pos_ref[2]
    sums = added(messages)
    count = sums.shape[0]
    tail = sums[:, KV_AT:]
    squares = tail[:, 0:1] + tail[:, 64:65]
    scaled = (sums[:, :KV_AT] * lax.rsqrt(squares / features + NORM_EPS)).astype(BF16)
    query = jnp.concatenate([scaled[:, h * HD : (h + 1) * HD] for h in range(GROUP_Q)], axis=0)
    key = scaled[:, Q_COLS : Q_COLS + HD]
    value = scaled[:, Q_COLS + HD :]
    scores = lax.dot_general(query, key, (((1,), (1,)), ((), ())), preferred_element_type=F32)
    scores = (scores * HD ** (-0.5)).reshape(GROUP_Q, count, count)
    chunk = jnp.clip(slot - LAG * pos_ref[1], 0, chunks - 1)
    segment = table_ref[:, lane(chunk * 128, 128)][:, :count].astype(jnp.int32)
    allowed = (as_column(segment) == segment) & (iota(count, count, 1) <= iota(count, count, 0))
    scores = jnp.where(allowed[None], scores, -jnp.inf)
    top = jnp.max(scores, axis=2, keepdims=True)
    weights = jnp.exp(scores - top)
    probs = (weights / jnp.sum(weights, axis=2, keepdims=True)).astype(BF16)
    mixed = dot(probs.reshape(GROUP_Q * count, count), value).astype(BF16)
    mixed = jnp.concatenate([mixed[h * count : (h + 1) * count] for h in range(GROUP_Q)], axis=1)
    if pool_chunk is not None:
        mixed = means(table_ref, pool_chunk, count, mixed).astype(BF16)
    step = own_ref.shape[2] // 8
    for part, source in ((core, own_ref), (1 - core, other_ref)):
        places = [(2 * part + j) ^ pos_ref[0] for j in range(2)]
        for at in range(8):
            result = dot(mixed, source[0, :, at * step : (at + 1) * step]).astype(BF16)
            results_ref[places[at // 4], :, (at % 4) * step : (at % 4 + 1) * step] = result
    for k, out_ref in enumerate(out_refs):
        out_ref[...] = results_ref[k]


def update_kernel(slot, has_wait, has_recv, send, pool_chunk, pooled_sums, pos_ref, *refs):
    refs = list(refs)
    wait_ref = refs.pop(0) if has_wait else None
    recv_ref = refs.pop(0) if has_recv else None
    messages, refs = (refs[:CHIPS], refs[CHIPS:])
    table_ref = refs.pop(0)
    before_ref = refs.pop(0) if pool_chunk is not None and pool_chunk % 2 else None
    rows = pick_rows(slot, pos_ref, wait_ref, recv_ref)
    if pooled_sums:
        total = means(table_ref, pool_chunk, rows.shape[0], rows)
    else:
        total = rows.astype(F32)
    total += added(messages)
    hidden = total.astype(BF16)
    if send:
        refs.pop(0)[...] = hidden
    if pool_chunk is not None:
        pooled = hidden if pooled_sums else means(table_ref, pool_chunk, rows.shape[0], hidden).astype(BF16)
        if before_ref is None:
            refs.pop(0)[...] = pooled
        else:
            out_ref = refs.pop(0)
            out_ref[0] = before_ref[...]
            out_ref[1] = pooled


def parcel_kernel(owner_at, pos_ref, p0, p1, p2, p3, table_ref, *out_refs):
    chip, phase, core = (pos_ref[0], pos_ref[1], pos_ref[2])
    rows = jnp.where(phase == 0, p0[...], p1[...])
    rows = jnp.where(phase < 2, rows, jnp.where(phase == 2, p2[...], p3[...]))
    rows = jnp.concatenate([rows[0], rows[1]], axis=0)
    count = rows.shape[0]
    own_row = table_ref[:, owner_at : owner_at + count].astype(jnp.int32) - 1
    own_col = as_column(own_row)
    above, across = (iota(count, count, 0), iota(count, count, 1))
    same = (above // 16 == across // 16) & ((above % 16 >= PH) == (across % 16 >= PH))
    earlier = (own_col == own_row) & same & (above < across)
    rank = jnp.sum(jnp.where(earlier, 1, 0), axis=0, keepdims=True)
    place = iota(1, count, 1)
    half = jnp.where(place % 16 >= PH, 1, 0)
    slot = half * 8 + (2 * core + place // 16) * 2 + rank
    turn = 2 * (chip & 1) + core
    for k in range(CHIPS):
        pick = marks((iota(16, count, 0) == slot) & (own_row == (turn ^ k)))
        out_refs[k][...] = dot(pick, rows).astype(BF16)


def deliver_kernel(pos_ref, m0, m1, m2, m3, out_ref):
    chip = pos_ref[0]
    width = m0.shape[1]
    out_ref[...] = jnp.zeros_like(out_ref)
    for k, ref in enumerate((m0, m1, m2, m3)):
        cols = lane(((chip ^ k) >> 1) * width, width)
        out_ref[:, cols] = out_ref[:, cols] + ref[...]


def chip_shards(prompt_rows, row_dest, segment_ids, owner, gain, w_query, w_key, w_value, w_out):
    chip, phase, core = (lax.axis_index("dp"), lax.axis_index("phase"), lax.axis_index("mp"))
    phases = lax.axis_size("phase")
    pos = jnp.stack([chip, phase, core]).astype(jnp.int32)
    halves, half_rows, cols_here = prompt_rows.shape[1:]
    batch = halves * half_rows
    features = 2 * cols_here
    block = features // CHIPS
    count = batch
    square = [(e, k) for e in range(CHIPS) for k in range(2)]

    def crosswise(value, k):
        pairs = [(2 * e + m, 2 * (2 * m + ((e ^ k) >> 1)) + ((e ^ k) & 1)) for e, m in square]
        return lax.ppermute(value, ("dp", "mp"), pairs)

    def homewards(value, k):
        pairs = [(2 * e + c, 2 * ((2 * (e & 1) + c) ^ k) + (e >> 1)) for e, c in square]
        return lax.ppermute(value, ("dp", "mp"), pairs)

    def exchange(values):
        got = [values[0]]
        for k in range(1, CHIPS):
            got.append(lax.ppermute(values[k], "dp", [(e, e ^ k) for e in range(CHIPS)]))
        return got

    def swap(value):
        return lax.ppermute(value, "mp", [(0, 1), (1, 0)])

    with jax.named_scope("packing"):
        parity = chip % 2
        chunks = 2 * phases
        owner_at = chunks * 128
        table = jnp.zeros((phases, 2, 128), F32)
        numbers = segment_ids[0][:, None, :].astype(F32)
        table = lax.dynamic_update_slice(table, numbers, (0, parity, 0)).reshape(1, -1)
        owners = (owner.reshape(1, -1) + 1).astype(F32)
        last = lax.dynamic_update_slice(jnp.zeros((1, block - owner_at), F32), owners, (0, 16 * parity))
        table = jnp.concatenate([table, last], axis=1)
        dest = row_dest.reshape(CHIPS, batch)
        own = (w_query, w_key, w_value, w_out)
        sources, *_ = lax.optimization_barrier((own, pos, table, dest))
        *own, token = call(
            stage_kernel,
            [pltpu.VMEM(w.shape, BF16) for w in own],
            [pltpu.with_memory_space_constraint(w, pltpu.HBM) for w in own],
            [hbm_spec()] * 4,
            (pltpu.SemaphoreType.DMA((4,)),),
            token=jnp.zeros((8, 128), F32),
        )
        *packed, token = call(
            pack_kernel,
            [jax.ShapeDtypeStruct((4 * RANKS, block), BF16)] * CHIPS,
            (pos, prompt_rows.reshape(batch, cols_here), dest, table),
            [smem_spec()] + [vmem_spec()] * 3,
            token=token,
        )
        arrived = [crosswise(value, k) for k, value in enumerate(packed)]
        start, table, token = call(
            unpack_kernel,
            [jax.ShapeDtypeStruct((2 * batch, block), BF16), jax.ShapeDtypeStruct((1, block), F32)],
            (pos, *arrived, dest),
            [smem_spec()] + [vmem_spec()] * 5,
            token=token,
        )
        waiting = [start]

    with jax.named_scope("weights"):

        def held(values):
            return [pltpu.with_memory_space_constraint(value, pltpu.VMEM) for value in values]

        other = [swap(w) for w in sources[:3]]
        w_in = held([*own[:3], *other])
        last, *_ = lax.optimization_barrier((sources[3], start, *other))
        w_back = held([own[3], swap(last)])

    hops, pooled, got = ({}, {}, {})
    slots = chunks + LAG * (phases - 1)

    def plan(slot):
        chunk = slot - LAG * (phases - 1)
        send = slot < chunks + LAG * (phases - 2)
        pool_chunk = chunk if chunk >= 0 else None
        return (send, pool_chunk, pool_chunk is not None and not send)

    def entering(slot):
        inputs = waiting[slot // 2 : slot // 2 + 1] + [hops[at] for at in (slot - LAG,) if at >= 0]
        return (slot < chunks, slot >= LAG, inputs, [smem_spec()] + [vmem_spec()] * len(inputs))

    def project(slot, token):
        has_wait, has_recv, inputs, specs = entering(slot)
        *sent, token = call(
            functools.partial(project_kernel, slot, has_wait, has_recv),
            [jax.ShapeDtypeStruct((count, MSG_COLS), BF16)] * CHIPS,
            (pos, *inputs, gain, *w_in),
            specs + [vmem_spec()] * 7,
            (pltpu.VMEM((CHIPS, count, KV_AT), BF16),),
            10,
            token,
        )
        got[slot] = exchange(sent)
        return token

    def attend(slot, token):
        _, pool_chunk, early_pool = plan(slot)
        rows = 16 if early_pool else count
        *sent, token = call(
            functools.partial(attend_kernel, features, slot, chunks, pool_chunk if early_pool else None),
            [jax.ShapeDtypeStruct((rows, block), BF16)] * CHIPS,
            (pos, *got[slot], table, *w_back),
            [smem_spec()] + [vmem_spec()] * (CHIPS + 3),
            (pltpu.VMEM((CHIPS, rows, block), BF16),),
            10,
            token,
        )
        got[slot] = exchange(sent)
        return token

    def update(slot, token):
        has_wait, has_recv, inputs, specs = entering(slot)
        send, pool_chunk, early_pool = plan(slot)
        outs = [jax.ShapeDtypeStruct((count, block), BF16)] * send
        before = []
        if pool_chunk is not None:
            odd = pool_chunk % 2 == 1
            outs.append(jax.ShapeDtypeStruct((2, 16, block) if odd else (16, block), BF16))
            before = [pooled[pool_chunk - 1]] if odd else []
        *out, token = call(
            functools.partial(update_kernel, slot, has_wait, has_recv, send, pool_chunk, early_pool),
            outs,
            (pos, *inputs, *got[slot], table, *before),
            specs + [vmem_spec()] * (CHIPS + 1 + len(before)),
            token=token,
        )
        if send:
            live = [p for p in range(phases - 1) if 0 <= slot - LAG * p < chunks]
            hops[slot] = lax.ppermute(out.pop(0), "phase", [(p, p + 1) for p in live])
        if pool_chunk is not None:
            pooled[pool_chunk] = out.pop(0)
        return token

    for step in range(slots + 1):
        before, now = (step > 0, step < slots)
        if step % 2 == 0 and step < chunks - 2:
            down = [(p, p - 1) for p in range(1, phases - step // 2)]
            waiting.append(lax.ppermute(waiting[-1], "phase", down))
        if now:
            with jax.named_scope("project"):
                token = project(step, token)
        if before:
            with jax.named_scope("update"):
                token = update(step - 1, token)
        if now:
            with jax.named_scope("attend"):
                token = attend(step, token)

    with jax.named_scope("deliver"):
        shares = [lax.ppermute(pooled[2 * m + 1], "phase", [(phases - 1, m)]) for m in range(phases - 1)]
        parcels = call(
            functools.partial(parcel_kernel, owner_at),
            [jax.ShapeDtypeStruct((16, block), BF16)] * CHIPS,
            (pos, *shares, pooled[chunks - 1], table),
            [smem_spec()] + [vmem_spec()] * 5,
        )
        final = [homewards(value, k) for k, value in enumerate(parcels)]
        (result,) = call(
            deliver_kernel,
            [jax.ShapeDtypeStruct((16, cols_here), BF16)],
            (pos, *final),
            [smem_spec()] + [vmem_spec()] * 4,
        )
    return result.reshape(1, 2, 8, cols_here)


def solution(mesh):
    in_specs = (
        P("dp", "phase", None, "mp"),
        P(None, "phase", None),
        P("dp", None, None),
        P("dp", "phase", None, None),
        P("phase", None),
        P("phase", "dp", "mp"),
        P("phase", "dp", "mp"),
        P("phase", "dp", "mp"),
        P("phase", "dp", "mp"),
    )
    out_specs = P("dp", "phase", None, "mp")
    square = mesh.shape["dp"] == CHIPS and mesh.shape["mp"] == 2 and mesh.shape["phase"] == 4
    shards = chip_shards if square else general_shards
    return jax.shard_map(shards, mesh=mesh, in_specs=in_specs, out_specs=out_specs, check_vma=False)
```

```python
import functools

import jax
import jax.numpy as jnp
from jax import lax
from jax.experimental import pallas as pl
from jax.experimental.pallas import tpu as pltpu
from jax.sharding import PartitionSpec as P

D = 8192
HD = 128
QH = 32
KVH = 4
SEGS = 6
PH = 3


NORM_EPS = 1e-05


def from_behind(value, axis, steps):
    count = lax.axis_size(axis)
    initial, last = (max(0, -steps), min(count, count - steps))
    return lax.ppermute(value, axis, [(source, source + steps) for source in range(initial, last)])


def broadcast(value, axis, root):
    mine = lax.axis_index(axis) == root
    return lax.psum(jnp.where(mine, value, jnp.zeros_like(value)), axis)


def bucket_ranks(labels, buckets):
    hits_table = (labels[..., None] == jnp.arange(buckets, dtype=jnp.int32)).astype(jnp.int32)
    earlier = jnp.cumsum(hits_table, axis=-2) - hits_table
    return jnp.sum(earlier * hits_table, axis=-1)


def attend_heads(query, key_sel, value_sel, segments):
    head_dim = query.shape[2]
    scores = jnp.einsum("qhd,khd->hqk", query, key_sel, preferred_element_type=jnp.float32)
    scores = scores * head_dim ** (-0.5)
    places = jnp.arange(query.shape[0], dtype=jnp.int32)
    allowed = (segments[:, None] == segments[None, :]) & (places[None, :] <= places[:, None])
    scores = jnp.where(allowed[None, :, :], scores, -jnp.inf)
    row_top = jnp.max(scores, axis=2, keepdims=True)
    weights = jnp.exp(scores - row_top)
    probabilities = (weights / jnp.sum(weights, axis=2, keepdims=True)).astype(jnp.bfloat16)
    mixed = jnp.einsum("hqk,khd->qhd", probabilities, value_sel, preferred_element_type=jnp.float32)
    return mixed.astype(jnp.bfloat16).reshape(query.shape[0], -1)


def general_shards(prompt_rows, row_dest, segment_ids, owner, gain, w_query, w_key, w_value, w_out):
    dp_count = lax.axis_size("dp")
    phase_count = lax.axis_size("phase")
    group_here = lax.axis_index("dp")
    phase_here = lax.axis_index("phase")
    part_here = lax.axis_index("mp")
    halves_here = prompt_rows.shape[1]
    half_rows = prompt_rows.shape[2]
    feature_cols = prompt_rows.shape[3]
    batch_rows = halves_here * half_rows
    capacity = half_rows // min(dp_count, 4)
    half_index = jnp.arange(halves_here, dtype=jnp.int32)[:, None]
    dest_group = row_dest // half_rows
    dest_ranks = bucket_ranks(dest_group, dp_count)
    own_groups = lax.dynamic_index_in_dim(dest_group, group_here, 0, keepdims=False)
    own_ranks = lax.dynamic_index_in_dim(dest_ranks, group_here, 0, keepdims=False)
    send_at = own_groups * capacity + own_ranks
    outgoing = (
        jnp.zeros((halves_here, dp_count * capacity, feature_cols), jnp.bfloat16)
        .at[half_index, send_at]
        .set(prompt_rows[0])
    )
    incoming = lax.all_to_all(
        outgoing.reshape(halves_here, dp_count, capacity, feature_cols),
        "dp",
        split_axis=1,
        concat_axis=1,
        tiled=True,
    )
    source_ids = jnp.arange(dp_count, dtype=jnp.int32)[:, None, None]
    where_from = jnp.transpose(source_ids * capacity + dest_ranks, (1, 0, 2)).reshape(
        halves_here, -1
    )
    target = jnp.where(dest_group == group_here, row_dest % half_rows, half_rows)
    target = jnp.transpose(target, (1, 0, 2)).reshape(halves_here, -1)
    arrived = incoming.reshape(halves_here, dp_count * capacity, feature_cols)[
        half_index, where_from
    ]
    own_halves = (
        jnp.zeros((halves_here, half_rows, feature_cols), jnp.bfloat16)
        .at[half_index, target]
        .set(arrived, mode="drop")
    )
    own_batch = own_halves.reshape(batch_rows, feature_cols)
    waiting = lax.all_gather(own_batch, "phase", axis=0, tiled=True).reshape(
        phase_count, batch_rows, feature_cols
    )
    query_rows, key_rows, value_rows, back_rows = (
        lax.all_gather(w_query[0], "dp", axis=0, tiled=True),
        lax.all_gather(w_key[0], "dp", axis=0, tiled=True),
        lax.all_gather(w_value[0], "dp", axis=0, tiled=True),
        lax.all_gather(w_out[0], "dp", axis=0, tiled=True),
    )
    query_cols = query_rows.shape[1]
    pair_cols = key_rows.shape[1]
    w_proj = jnp.concatenate([query_rows, key_rows, value_rows], axis=1)
    proj_cols = w_proj.shape[1]
    heads_here = query_cols // HD
    group_size = QH // KVH
    key_heads = (part_here * heads_here + jnp.arange(heads_here, dtype=jnp.int32)) // group_size
    gain_row = gain[0]
    segment_table = segment_ids[0]
    last_phase = phase_count - 1
    prompt_numbers = jnp.arange(SEGS, dtype=jnp.int32)

    def advance(tick_index, loop_state):
        current, pooled = loop_state
        batch_index = tick_index - phase_here
        active = (batch_index >= 0) & (batch_index < phase_count)
        batch_slot = jnp.clip(batch_index, 0, phase_count - 1)
        fresh_rows = lax.dynamic_index_in_dim(
            waiting, jnp.clip(tick_index, 0, phase_count - 1), 0, keepdims=False
        )
        tok_rows = jnp.where(phase_here == 0, fresh_rows, current)
        tok_segments = lax.dynamic_index_in_dim(segment_table, batch_slot, 0, keepdims=False)
        tok_float = tok_rows.astype(jnp.float32)
        whole_rows = lax.all_gather(tok_rows, "mp", axis=1, tiled=True)
        whole_float = whole_rows.astype(jnp.float32)
        squares = jnp.sum(whole_float * whole_float, axis=1)
        projected = lax.cond(
            active,
            lambda: jnp.dot(
                (whole_float * gain_row[None, :]).astype(jnp.bfloat16),
                w_proj,
                preferred_element_type=jnp.float32,
            ),
            lambda: jnp.zeros((batch_rows, proj_cols), jnp.float32),
        )
        qkv_rows = (projected * lax.rsqrt(squares / D + NORM_EPS)[:, None]).astype(jnp.bfloat16)
        query = qkv_rows[:, :query_cols].reshape(batch_rows, heads_here, HD)
        key_own = qkv_rows[:, query_cols : query_cols + pair_cols]
        value_own = qkv_rows[:, query_cols + pair_cols :]
        key_all, value_all = (
            lax.all_gather(key_own, "mp", axis=1, tiled=True),
            lax.all_gather(value_own, "mp", axis=1, tiled=True),
        )
        key_sel = jnp.take(key_all.reshape(batch_rows, KVH, HD), key_heads, axis=1)
        value_sel = jnp.take(value_all.reshape(batch_rows, KVH, HD), key_heads, axis=1)
        mixed_own = attend_heads(query, key_sel, value_sel, tok_segments)
        mixed = lax.all_gather(mixed_own, "mp", axis=1, tiled=True)
        updated = lax.cond(
            active,
            lambda: (
                tok_float + jnp.dot(mixed, back_rows, preferred_element_type=jnp.float32)
            ).astype(jnp.bfloat16),
            lambda: tok_rows,
        )
        segment_hits = tok_segments[None, :] == prompt_numbers[:, None]
        segment_sums = jnp.dot(
            segment_hits.astype(jnp.bfloat16), updated, preferred_element_type=jnp.float32
        )
        counts = jnp.sum(segment_hits.astype(jnp.float32), axis=1)
        segment_means = segment_sums / counts[:, None]
        store_here = active & (phase_here == last_phase)
        stored = lax.dynamic_index_in_dim(pooled, batch_slot, 0, keepdims=False)
        pooled = lax.dynamic_update_index_in_dim(
            pooled, jnp.where(store_here, segment_means, stored), batch_slot, 0
        )
        passed = from_behind(updated, "phase", 1)
        return (passed, pooled)

    start_state = (
        jnp.zeros((batch_rows, feature_cols), jnp.bfloat16),
        jnp.zeros((phase_count, SEGS, feature_cols), jnp.float32),
    )
    current, pooled = lax.fori_loop(0, phase_count + phase_count - 1, advance, start_state)
    shared = broadcast(pooled.astype(jnp.bfloat16), "phase", last_phase)
    own_prompts = lax.dynamic_index_in_dim(shared, phase_here, 0, keepdims=False).reshape(
        halves_here, PH, feature_cols
    )
    owner_ids = owner[0, :, :, 0]
    return_cap = max(2, PH // min(dp_count, 4))
    send_slots = owner_ids * return_cap + bucket_ranks(owner_ids, dp_count)
    parcel = (
        jnp.zeros((halves_here, dp_count * return_cap, feature_cols), jnp.bfloat16)
        .at[half_index, send_slots]
        .set(own_prompts)
    )
    returned = lax.all_to_all(
        parcel.reshape(halves_here, dp_count, return_cap, feature_cols),
        "dp",
        split_axis=1,
        concat_axis=1,
        tiled=True,
    )
    return returned.reshape(1, halves_here, dp_count * return_cap, feature_cols)


LAG = 2
CHIPS = 4
GROUP_Q = QH // KVH
Q_COLS = GROUP_Q * HD
KV_AT = Q_COLS + 2 * HD
MSG_COLS = KV_AT + 128
RANKS = 8
TABLE_ROW = 6
F32 = jnp.float32
BF16 = jnp.bfloat16


def vmem_spec():
    return pl.BlockSpec(memory_space=pltpu.VMEM)


def smem_spec():
    return pl.BlockSpec(memory_space=pltpu.SMEM)


def hbm_spec():
    return pl.BlockSpec(memory_space=pl.ANY)


def call(kernel, outs, args, specs, scratch=(), limit=6, token=None, after=(), span=None):
    count = len(args)
    others = len(after)

    def body(*refs):
        first = count + 1 + others
        at = first + len(outs)
        refs[at][...] = jnp.zeros(refs[at].shape, F32)

        def run():
            kernel(*refs[:count], *refs[first:at], *refs[at + 1 :])

        if span is None:
            run()
        else:
            slot, chunks = span
            chunk = slot - LAG * refs[0][1]
            pl.when((chunk >= 0) & (chunk < chunks))(run)

    outs = list(outs)
    if token is not None:
        outs_all = outs + [jax.ShapeDtypeStruct((8, 128), F32)]
        args, specs = ((*args, token, *after), [*specs] + [hbm_spec()] * (1 + others))
    else:
        outs_all = outs
    return pl.pallas_call(
        kernel if token is None else body,
        out_shape=outs_all,
        in_specs=specs,
        out_specs=[vmem_spec()] * len(outs_all),
        scratch_shapes=list(scratch),
        compiler_params=pltpu.CompilerParams(vmem_limit_bytes=limit * 1024 * 1024),
    )(*args)


def dot(a, b):
    return jnp.dot(a, b, preferred_element_type=F32)


def lane(start, size):
    return pl.ds(pl.multiple_of(start, size), size)


def iota(rows, cols, axis):
    return lax.broadcasted_iota(jnp.int32, (rows, cols), axis)


def as_column(row):
    count = row.shape[1]
    diagonal = iota(count, count, 0) == iota(count, count, 1)
    return jnp.sum(jnp.where(diagonal, row, 0), axis=1, keepdims=True)


def marks(hits):
    return hits.astype(F32).astype(BF16)


def pack_kernel(pos_ref, rows_ref, dest_ref, table_ref, *out_refs):
    chip = pos_ref[0]
    dest = dest_ref[pl.ds(chip, 1), :]
    count = dest.shape[1]
    half = count // 2
    group_row = dest // half
    group_col = as_column(group_row)
    source, here = (iota(count, count, 0), iota(count, count, 1))
    before = (group_col == group_row) & (source // half == here // half) & (source < here)
    rank = jnp.sum(jnp.where(before, 1, 0), axis=0, keepdims=True)
    target = group_row * (2 * RANKS) + (iota(1, count, 1) // half) * RANKS + rank
    width = out_refs[0].shape[1]
    message_row = iota(4 * RANKS, width, 0)
    for k in range(CHIPS):
        turn = chip ^ k
        core, block = (turn >> 1, turn & 1)
        pick = marks(iota(4 * RANKS, count, 0) + core * (4 * RANKS) == target)
        rows = dot(pick, rows_ref[:, lane(block * width, width)])
        rows = jnp.where(message_row == TABLE_ROW, table_ref[...], rows)
        out_refs[k][...] = rows.astype(BF16)


def unpack_kernel(pos_ref, m0, m1, m2, m3, dest_ref, out_ref, table_ref):
    chip, core = (pos_ref[0], pos_ref[2])
    count = dest_ref.shape[1]
    half = count // 2
    turn = 2 * core + (chip & 1)
    total = jnp.zeros(out_ref.shape, F32)
    table = jnp.zeros(table_ref.shape, F32)
    above, across = (iota(count, count, 0), iota(count, count, 1))
    for k, ref in enumerate((m0, m1, m2, m3)):
        loader = turn ^ k
        dest_row = dest_ref[pl.ds(loader, 1), :]
        group_row = dest_row // half
        group_col = as_column(group_row)
        earlier = (group_col == group_row) & (above // half == across // half) & (across < above)
        rank = jnp.sum(jnp.where(earlier, 1, 0), axis=1, keepdims=True)
        at = (group_col - 2 * core) * (2 * RANKS) + (iota(count, 1, 0) // half) * RANKS + rank
        from_message = marks(iota(count, 4 * RANKS, 1) == at)
        slot = (group_row - 2 * core) * count + (iota(1, count, 1) // half) * half + dest_row % half
        to_slot = marks(iota(2 * count, count, 0) == slot)
        rows = ref[...]
        total += dot(dot(to_slot, from_message).astype(BF16), rows)
        mine = (loader >> 1) == core
        table += jnp.where(mine, rows[TABLE_ROW : TABLE_ROW + 1].astype(F32), 0.0)
    out_ref[...] = total.astype(BF16)
    table_ref[...] = table


def added(messages):
    total = messages[0][...].astype(F32)
    for ref in messages[1:]:
        total += ref[...].astype(F32)
    return total


def stage_kernel(*refs):
    *refs, sems = refs
    count = len(refs) // 2
    copies = [pltpu.make_async_copy(refs[i], refs[count + i], sems.at[i]) for i in range(count)]
    for copy in copies:
        copy.start()
    for copy in copies:
        copy.wait()


def pick_rows(slot, pos_ref, wait_ref, recv_ref):
    if wait_ref is None:
        return recv_ref[...]
    count = wait_ref.shape[0] // 2
    at = (slot % 2) * count
    waiting = wait_ref[at : at + count]
    if recv_ref is None:
        return waiting
    return jnp.where(pos_ref[1] == 0, waiting, recv_ref[...])


def project_kernel(slot, has_wait, has_recv, pos_ref, *refs):
    refs = list(refs)
    wait_ref = refs.pop(0) if has_wait else None
    recv_ref = refs.pop(0) if has_recv else None
    gain_ref, *refs = refs
    sources, out_refs, results_ref = (refs[:6], refs[6:10], refs[10])
    chip, core = (pos_ref[0], pos_ref[2])
    rows = pick_rows(slot, pos_ref, wait_ref, recv_ref).astype(F32)
    depth = rows.shape[1]
    gated = (rows * gain_ref[:, lane(chip * depth, depth)]).astype(BF16)
    squares = jnp.sum(rows * rows, axis=1, keepdims=True)
    high = squares.astype(BF16).astype(F32)
    tail = jnp.where(iota(rows.shape[0], 128, 1) < 64, high, squares - high).astype(BF16)

    for at, source in enumerate(sources):
        part, i = (core if at < 3 else 1 - core, at % 3)
        places = [(2 * part + j) ^ pos_ref[0] for j in range(2)]
        step = min(source.shape[2], 512)
        for start in range(0, source.shape[2], step):
            result = dot(gated, source[0, :, start : start + step]).astype(BF16)
            if i == 0:
                inside = start % Q_COLS
                results_ref[places[start // Q_COLS], :, inside : inside + step] = result
            else:
                inside = Q_COLS + (i - 1) * HD
                for j in range(2):
                    results_ref[places[j], :, inside : inside + HD] = result[:, j * HD : (j + 1) * HD]
    for k, out_ref in enumerate(out_refs):
        out_ref[:, :KV_AT] = results_ref[k]
        out_ref[:, KV_AT:] = tail


def means(table_ref, chunk, count, rows):
    segment = table_ref[:, chunk * 128 : chunk * 128 + count].astype(jnp.int32)
    hits = (segment == iota(16, count, 0)) & (iota(16, count, 0) < SEGS)
    counts = jnp.sum(jnp.where(hits, 1.0, 0.0), axis=1, keepdims=True)
    return dot(marks(hits), rows) / jnp.maximum(counts, 1.0)


def attend_kernel(features, slot, chunks, pool_chunk, pos_ref, *refs):
    messages, (table_ref, own_ref, other_ref) = (refs[:CHIPS], refs[CHIPS : CHIPS + 3])
    out_refs, results_ref = (refs[CHIPS + 3 : -1], refs[-1])
    core = pos_ref[2]
    sums = added(messages)
    count = sums.shape[0]
    tail = sums[:, KV_AT:]
    squares = tail[:, 0:1] + tail[:, 64:65]
    scaled = (sums[:, :KV_AT] * lax.rsqrt(squares / features + NORM_EPS)).astype(BF16)
    query = jnp.concatenate([scaled[:, h * HD : (h + 1) * HD] for h in range(GROUP_Q)], axis=0)
    key = scaled[:, Q_COLS : Q_COLS + HD]
    value = scaled[:, Q_COLS + HD :]
    scores = lax.dot_general(query, key, (((1,), (1,)), ((), ())), preferred_element_type=F32)
    scores = (scores * HD ** (-0.5)).reshape(GROUP_Q, count, count)
    chunk = jnp.clip(slot - LAG * pos_ref[1], 0, chunks - 1)
    segment = table_ref[:, lane(chunk * 128, 128)][:, :count].astype(jnp.int32)
    allowed = (as_column(segment) == segment) & (iota(count, count, 1) <= iota(count, count, 0))
    scores = jnp.where(allowed[None], scores, -jnp.inf)
    top = jnp.max(scores, axis=2, keepdims=True)
    weights = jnp.exp(scores - top)
    probs = (weights / jnp.sum(weights, axis=2, keepdims=True)).astype(BF16)
    mixed = dot(probs.reshape(GROUP_Q * count, count), value).astype(BF16)
    mixed = jnp.concatenate([mixed[h * count : (h + 1) * count] for h in range(GROUP_Q)], axis=1)
    if pool_chunk is not None:
        mixed = means(table_ref, pool_chunk, count, mixed).astype(BF16)
    step = own_ref.shape[2] // 8
    for part, source in ((core, own_ref), (1 - core, other_ref)):
        places = [(2 * part + j) ^ pos_ref[0] for j in range(2)]
        for at in range(8):
            result = dot(mixed, source[0, :, at * step : (at + 1) * step]).astype(BF16)
            results_ref[places[at // 4], :, (at % 4) * step : (at % 4 + 1) * step] = result
    for k, out_ref in enumerate(out_refs):
        out_ref[...] = results_ref[k]


def update_kernel(slot, has_wait, has_recv, send, pool_chunk, pooled_sums, pos_ref, *refs):
    refs = list(refs)
    wait_ref = refs.pop(0) if has_wait else None
    recv_ref = refs.pop(0) if has_recv else None
    messages, refs = (refs[:CHIPS], refs[CHIPS:])
    table_ref = refs.pop(0)
    before_ref = refs.pop(0) if pool_chunk is not None and pool_chunk % 2 else None
    rows = pick_rows(slot, pos_ref, wait_ref, recv_ref)
    if pooled_sums:
        total = means(table_ref, pool_chunk, rows.shape[0], rows)
    else:
        total = rows.astype(F32)
    total += added(messages)
    hidden = total.astype(BF16)
    if send:
        refs.pop(0)[...] = hidden
    if pool_chunk is not None:
        pooled = hidden if pooled_sums else means(table_ref, pool_chunk, rows.shape[0], hidden).astype(BF16)
        if before_ref is None:
            refs.pop(0)[...] = pooled
        else:
            out_ref = refs.pop(0)
            out_ref[0] = before_ref[...]
            out_ref[1] = pooled


def parcels(owner_at, pos_ref, rows, table_ref, out_refs):
    chip, core = (pos_ref[0], pos_ref[2])
    count = rows.shape[0]
    own_row = table_ref[:, owner_at : owner_at + count].astype(jnp.int32) - 1
    own_col = as_column(own_row)
    above, across = (iota(count, count, 0), iota(count, count, 1))
    same = (above // 16 == across // 16) & ((above % 16 >= PH) == (across % 16 >= PH))
    earlier = (own_col == own_row) & same & (above < across)
    rank = jnp.sum(jnp.where(earlier, 1, 0), axis=0, keepdims=True)
    place = iota(1, count, 1)
    half = jnp.where(place % 16 >= PH, 1, 0)
    slot = half * 8 + (2 * core + place // 16) * 2 + rank
    turn = 2 * core + (chip & 1)
    for k, out_ref in enumerate(out_refs):
        pick = marks((iota(16, count, 0) == slot) & (own_row == (turn ^ k)))
        out_ref[...] = dot(pick, rows).astype(BF16)


def carry_kernel(last, pos_ref, pooled_ref, share_ref, out_ref):
    out_ref[...] = jnp.where(pos_ref[1] == last, pooled_ref[...], share_ref[...])


def finish_kernel(last, chunk, owner_at, pos_ref, recv_ref, m0, m1, m2, m3, table_ref, before_ref, *refs):
    share_ref, *out_refs, pooled_ref = refs
    count = before_ref.shape[0]
    final = pos_ref[1] == last

    @pl.when(final)
    def _():
        rows = recv_ref[...]
        total = means(table_ref, chunk, rows.shape[0], rows) + added((m0, m1, m2, m3))
        pooled_ref[:count] = before_ref[...]
        pooled_ref[count:] = total.astype(BF16)

    @pl.when(jnp.logical_not(final))
    def _():
        pooled_ref[:count] = share_ref[0]
        pooled_ref[count:] = share_ref[1]

    parcels(owner_at, pos_ref, pooled_ref[...], table_ref, out_refs)


def deliver_kernel(pos_ref, m0, m1, m2, m3, out_ref):
    chip = pos_ref[0]
    width = m0.shape[1]
    out_ref[...] = jnp.zeros_like(out_ref)
    for k, ref in enumerate((m0, m1, m2, m3)):
        cols = lane(((chip ^ k) & 1) * width, width)
        out_ref[:, cols] = out_ref[:, cols] + ref[...]


def chip_shards(prompt_rows, row_dest, segment_ids, owner, gain, w_query, w_key, w_value, w_out):
    chip, phase, core = (lax.axis_index("dp"), lax.axis_index("phase"), lax.axis_index("mp"))
    phases = lax.axis_size("phase")
    pos = jnp.stack([chip, phase, core]).astype(jnp.int32)
    halves, half_rows, cols_here = prompt_rows.shape[1:]
    batch = halves * half_rows
    features = 2 * cols_here
    block = features // CHIPS
    count = batch
    square = [(e, k) for e in range(CHIPS) for k in range(2)]

    def crosswise(value, k):
        pairs = [(2 * e + m, 2 * (2 * m + ((e ^ k) & 1)) + ((e ^ k) >> 1)) for e, m in square]
        return lax.ppermute(value, ("dp", "mp"), pairs)

    def homewards(value, k):
        pairs = [(2 * e + c, 2 * ((2 * c + (e & 1)) ^ k) + (e >> 1)) for e, c in square]
        return lax.ppermute(value, ("dp", "mp"), pairs)

    def exchange(values, slot):
        live = range(min(phases, slot // LAG + 1))
        got = [values[0]]
        for k in range(1, CHIPS):
            pairs = [(e * phases + p, (e ^ k) * phases + p) for e in range(CHIPS) for p in live]
            got.append(lax.ppermute(values[k], ("dp", "phase"), pairs))
        return got

    def lower(value):
        return lax.ppermute(value, "phase", [(p, p - 1) for p in range(1, phases)])

    def swap(value):
        return lax.ppermute(value, "mp", [(0, 1), (1, 0)])

    with jax.named_scope("packing"):
        parity = chip % 2
        chunks = 2 * phases
        owner_at = chunks * 128
        table = jnp.zeros((phases, 2, 128), F32)
        numbers = segment_ids[0][:, None, :].astype(F32)
        table = lax.dynamic_update_slice(table, numbers, (0, parity, 0)).reshape(1, -1)
        owners = (owner.reshape(1, -1) + 1).astype(F32)
        last = lax.dynamic_update_slice(jnp.zeros((1, block - owner_at), F32), owners, (0, 16 * parity))
        table = jnp.concatenate([table, last], axis=1)
        dest = row_dest.reshape(CHIPS, batch)
        own = (w_query, w_key, w_value, w_out)
        sources, *_ = lax.optimization_barrier((own, pos, table, dest))
        *own, token = call(
            stage_kernel,
            [pltpu.VMEM(w.shape, BF16) for w in own],
            [pltpu.with_memory_space_constraint(w, pltpu.HBM) for w in own],
            [hbm_spec()] * 4,
            (pltpu.SemaphoreType.DMA((4,)),),
            token=jnp.zeros((8, 128), F32),
        )
        *packed, token = call(
            pack_kernel,
            [jax.ShapeDtypeStruct((4 * RANKS, block), BF16)] * CHIPS,
            (pos, prompt_rows.reshape(batch, cols_here), dest, table),
            [smem_spec()] + [vmem_spec()] * 3,
            token=token,
        )
        arrived = [crosswise(value, k) for k, value in enumerate(packed)]
        start, table, token = call(
            unpack_kernel,
            [jax.ShapeDtypeStruct((2 * batch, block), BF16), jax.ShapeDtypeStruct((1, block), F32)],
            (pos, *arrived, dest),
            [smem_spec()] + [vmem_spec()] * 5,
            token=token,
        )
        waiting = [start]

    with jax.named_scope("weights"):

        def held(values):
            return [pltpu.with_memory_space_constraint(value, pltpu.VMEM) for value in values]

        other = [swap(w) for w in sources[:3]]
        w_in = held([*own[:3], *other])
        last, *_ = lax.optimization_barrier((sources[3], start, *other))
        w_back = held([own[3], swap(last)])

    hops, pooled, got, shares = ({}, {}, {}, {})
    slots = chunks + LAG * (phases - 1)

    def plan(slot):
        chunk = slot - LAG * (phases - 1)
        send = slot < chunks + LAG * (phases - 2)
        pool_chunk = chunk if chunk >= 0 else None
        return (send, pool_chunk, pool_chunk is not None and not send)

    def entering(slot):
        inputs = waiting[slot // 2 : slot // 2 + 1] + [hops[at] for at in (slot - LAG,) if at >= 0]
        return (slot < chunks, slot >= LAG, inputs, [smem_spec()] + [vmem_spec()] * len(inputs))

    def project(slot, token):
        has_wait, has_recv, inputs, specs = entering(slot)
        *sent, token = call(
            functools.partial(project_kernel, slot, has_wait, has_recv),
            [jax.ShapeDtypeStruct((count, MSG_COLS), BF16)] * CHIPS,
            (pos, *inputs, gain, *w_in),
            specs + [vmem_spec()] * 7,
            (pltpu.VMEM((CHIPS, count, KV_AT), BF16),),
            10,
            token,
            span=(slot, chunks),
        )
        got[slot] = exchange(sent, slot)
        return token

    def attend(slot, token):
        _, pool_chunk, early_pool = plan(slot)
        rows = 16 if early_pool else count
        *sent, token = call(
            functools.partial(attend_kernel, features, slot, chunks, pool_chunk if early_pool else None),
            [jax.ShapeDtypeStruct((rows, block), BF16)] * CHIPS,
            (pos, *got[slot], table, *w_back),
            [smem_spec()] + [vmem_spec()] * (CHIPS + 3),
            (pltpu.VMEM((CHIPS, rows, block), BF16),),
            10,
            token,
            [shares[m] for m in shares if slot == 2 * m + 3 + LAG * (phases - 1)],
            (slot, chunks),
        )
        got[slot] = exchange(sent, slot)
        return token

    def finish(slot, token):
        chunk = chunks - 1
        *sent, token = call(
            functools.partial(finish_kernel, phases - 1, chunk, owner_at),
            [jax.ShapeDtypeStruct((16, block), BF16)] * CHIPS,
            (pos, hops[slot - LAG], *got[slot], table, pooled[chunk - 1], shares[max(shares)]),
            [smem_spec()] + [vmem_spec()] * (CHIPS + 4),
            (pltpu.VMEM((32, block), BF16),),
            token=token,
        )
        return sent

    def update(slot, token):
        has_wait, has_recv, inputs, specs = entering(slot)
        send, pool_chunk, early_pool = plan(slot)
        outs = [jax.ShapeDtypeStruct((count, block), BF16)] * send
        before = []
        if pool_chunk is not None:
            odd = pool_chunk % 2 == 1
            outs.append(jax.ShapeDtypeStruct((2, 16, block) if odd else (16, block), BF16))
            before = [pooled[pool_chunk - 1]] if odd else []
        *out, token = call(
            functools.partial(update_kernel, slot, has_wait, has_recv, send, pool_chunk, early_pool),
            outs,
            (pos, *inputs, *got[slot], table, *before),
            specs + [vmem_spec()] * (CHIPS + 1 + len(before)),
            token=token,
            span=(slot, chunks),
        )
        if send:
            hops[slot] = lax.ppermute(out.pop(0), "phase", [(p, p + 1) for p in range(phases - 1)])
        if pool_chunk is not None:
            pooled[pool_chunk] = out.pop(0)
            if pool_chunk % 2:
                share = pooled[pool_chunk]
                if shares:
                    share, token = call(
                        functools.partial(carry_kernel, phases - 1),
                        [jax.ShapeDtypeStruct((2, 16, block), BF16)],
                        (pos, share, shares[max(shares)]),
                        [smem_spec()] + [vmem_spec()] * 2,
                        token=token,
                    )
                shares[pool_chunk // 2] = lower(share)
        return token

    for step in range(slots):
        if step % 2 == 0 and step < chunks - 2:
            waiting.append(lower(waiting[-1]))
        with jax.named_scope("project"):
            token = project(step, token)
        if step > 0:
            with jax.named_scope("update"):
                token = update(step - 1, token)
        with jax.named_scope("attend"):
            token = attend(step, token)

    with jax.named_scope("deliver"):
        final = [homewards(value, k) for k, value in enumerate(finish(slots - 1, token))]
        (result,) = call(
            deliver_kernel,
            [jax.ShapeDtypeStruct((16, cols_here), BF16)],
            (pos, *final),
            [smem_spec()] + [vmem_spec()] * 4,
        )
    return result.reshape(1, 2, 8, cols_here)


def solution(mesh):
    in_specs = (
        P("dp", "phase", None, "mp"),
        P(None, "phase", None),
        P("dp", None, None),
        P("dp", "phase", None, None),
        P("phase", None),
        P("phase", "dp", "mp"),
        P("phase", "dp", "mp"),
        P("phase", "dp", "mp"),
        P("phase", "dp", "mp"),
    )
    out_specs = P("dp", "phase", None, "mp")
    square = mesh.shape["dp"] == CHIPS and mesh.shape["mp"] == 2 and mesh.shape["phase"] == 4
    shards = chip_shards if square else general_shards
    return jax.shard_map(shards, mesh=mesh, in_specs=in_specs, out_specs=out_specs, check_vma=False)
```

```python
import functools

import jax
import jax.numpy as jnp
from jax import lax
from jax.experimental import pallas as pl
from jax.experimental.pallas import tpu as pltpu
from jax.sharding import PartitionSpec as P

D = 8192
HD = 128
QH = 32
KVH = 4
SEGS = 6
PH = 3


NORM_EPS = 1e-05


def from_behind(value, axis, steps):
    count = lax.axis_size(axis)
    initial, last = (max(0, -steps), min(count, count - steps))
    return lax.ppermute(value, axis, [(source, source + steps) for source in range(initial, last)])


def broadcast(value, axis, root):
    mine = lax.axis_index(axis) == root
    return lax.psum(jnp.where(mine, value, jnp.zeros_like(value)), axis)


def bucket_ranks(labels, buckets):
    hits_table = (labels[..., None] == jnp.arange(buckets, dtype=jnp.int32)).astype(jnp.int32)
    earlier = jnp.cumsum(hits_table, axis=-2) - hits_table
    return jnp.sum(earlier * hits_table, axis=-1)


def attend_heads(query, key_sel, value_sel, segments):
    head_dim = query.shape[2]
    scores = jnp.einsum("qhd,khd->hqk", query, key_sel, preferred_element_type=jnp.float32)
    scores = scores * head_dim ** (-0.5)
    places = jnp.arange(query.shape[0], dtype=jnp.int32)
    allowed = (segments[:, None] == segments[None, :]) & (places[None, :] <= places[:, None])
    scores = jnp.where(allowed[None, :, :], scores, -jnp.inf)
    row_top = jnp.max(scores, axis=2, keepdims=True)
    weights = jnp.exp(scores - row_top)
    probabilities = (weights / jnp.sum(weights, axis=2, keepdims=True)).astype(jnp.bfloat16)
    mixed = jnp.einsum("hqk,khd->qhd", probabilities, value_sel, preferred_element_type=jnp.float32)
    return mixed.astype(jnp.bfloat16).reshape(query.shape[0], -1)


def general_shards(prompt_rows, row_dest, segment_ids, owner, gain, w_query, w_key, w_value, w_out):
    dp_count = lax.axis_size("dp")
    phase_count = lax.axis_size("phase")
    group_here = lax.axis_index("dp")
    phase_here = lax.axis_index("phase")
    part_here = lax.axis_index("mp")
    halves_here = prompt_rows.shape[1]
    half_rows = prompt_rows.shape[2]
    feature_cols = prompt_rows.shape[3]
    batch_rows = halves_here * half_rows
    capacity = half_rows // min(dp_count, 4)
    half_index = jnp.arange(halves_here, dtype=jnp.int32)[:, None]
    dest_group = row_dest // half_rows
    dest_ranks = bucket_ranks(dest_group, dp_count)
    own_groups = lax.dynamic_index_in_dim(dest_group, group_here, 0, keepdims=False)
    own_ranks = lax.dynamic_index_in_dim(dest_ranks, group_here, 0, keepdims=False)
    send_at = own_groups * capacity + own_ranks
    outgoing = (
        jnp.zeros((halves_here, dp_count * capacity, feature_cols), jnp.bfloat16)
        .at[half_index, send_at]
        .set(prompt_rows[0])
    )
    incoming = lax.all_to_all(
        outgoing.reshape(halves_here, dp_count, capacity, feature_cols),
        "dp",
        split_axis=1,
        concat_axis=1,
        tiled=True,
    )
    source_ids = jnp.arange(dp_count, dtype=jnp.int32)[:, None, None]
    where_from = jnp.transpose(source_ids * capacity + dest_ranks, (1, 0, 2)).reshape(
        halves_here, -1
    )
    target = jnp.where(dest_group == group_here, row_dest % half_rows, half_rows)
    target = jnp.transpose(target, (1, 0, 2)).reshape(halves_here, -1)
    arrived = incoming.reshape(halves_here, dp_count * capacity, feature_cols)[
        half_index, where_from
    ]
    own_halves = (
        jnp.zeros((halves_here, half_rows, feature_cols), jnp.bfloat16)
        .at[half_index, target]
        .set(arrived, mode="drop")
    )
    own_batch = own_halves.reshape(batch_rows, feature_cols)
    waiting = lax.all_gather(own_batch, "phase", axis=0, tiled=True).reshape(
        phase_count, batch_rows, feature_cols
    )
    query_rows, key_rows, value_rows, back_rows = (
        lax.all_gather(w_query[0], "dp", axis=0, tiled=True),
        lax.all_gather(w_key[0], "dp", axis=0, tiled=True),
        lax.all_gather(w_value[0], "dp", axis=0, tiled=True),
        lax.all_gather(w_out[0], "dp", axis=0, tiled=True),
    )
    query_cols = query_rows.shape[1]
    pair_cols = key_rows.shape[1]
    w_proj = jnp.concatenate([query_rows, key_rows, value_rows], axis=1)
    proj_cols = w_proj.shape[1]
    heads_here = query_cols // HD
    group_size = QH // KVH
    key_heads = (part_here * heads_here + jnp.arange(heads_here, dtype=jnp.int32)) // group_size
    gain_row = gain[0]
    segment_table = segment_ids[0]
    last_phase = phase_count - 1
    prompt_numbers = jnp.arange(SEGS, dtype=jnp.int32)

    def advance(tick_index, loop_state):
        current, pooled = loop_state
        batch_index = tick_index - phase_here
        active = (batch_index >= 0) & (batch_index < phase_count)
        batch_slot = jnp.clip(batch_index, 0, phase_count - 1)
        fresh_rows = lax.dynamic_index_in_dim(
            waiting, jnp.clip(tick_index, 0, phase_count - 1), 0, keepdims=False
        )
        tok_rows = jnp.where(phase_here == 0, fresh_rows, current)
        tok_segments = lax.dynamic_index_in_dim(segment_table, batch_slot, 0, keepdims=False)
        tok_float = tok_rows.astype(jnp.float32)
        whole_rows = lax.all_gather(tok_rows, "mp", axis=1, tiled=True)
        whole_float = whole_rows.astype(jnp.float32)
        squares = jnp.sum(whole_float * whole_float, axis=1)
        projected = lax.cond(
            active,
            lambda: jnp.dot(
                (whole_float * gain_row[None, :]).astype(jnp.bfloat16),
                w_proj,
                preferred_element_type=jnp.float32,
            ),
            lambda: jnp.zeros((batch_rows, proj_cols), jnp.float32),
        )
        qkv_rows = (projected * lax.rsqrt(squares / D + NORM_EPS)[:, None]).astype(jnp.bfloat16)
        query = qkv_rows[:, :query_cols].reshape(batch_rows, heads_here, HD)
        key_own = qkv_rows[:, query_cols : query_cols + pair_cols]
        value_own = qkv_rows[:, query_cols + pair_cols :]
        key_all, value_all = (
            lax.all_gather(key_own, "mp", axis=1, tiled=True),
            lax.all_gather(value_own, "mp", axis=1, tiled=True),
        )
        key_sel = jnp.take(key_all.reshape(batch_rows, KVH, HD), key_heads, axis=1)
        value_sel = jnp.take(value_all.reshape(batch_rows, KVH, HD), key_heads, axis=1)
        mixed_own = attend_heads(query, key_sel, value_sel, tok_segments)
        mixed = lax.all_gather(mixed_own, "mp", axis=1, tiled=True)
        updated = lax.cond(
            active,
            lambda: (
                tok_float + jnp.dot(mixed, back_rows, preferred_element_type=jnp.float32)
            ).astype(jnp.bfloat16),
            lambda: tok_rows,
        )
        segment_hits = tok_segments[None, :] == prompt_numbers[:, None]
        segment_sums = jnp.dot(
            segment_hits.astype(jnp.bfloat16), updated, preferred_element_type=jnp.float32
        )
        counts = jnp.sum(segment_hits.astype(jnp.float32), axis=1)
        segment_means = segment_sums / counts[:, None]
        store_here = active & (phase_here == last_phase)
        stored = lax.dynamic_index_in_dim(pooled, batch_slot, 0, keepdims=False)
        pooled = lax.dynamic_update_index_in_dim(
            pooled, jnp.where(store_here, segment_means, stored), batch_slot, 0
        )
        passed = from_behind(updated, "phase", 1)
        return (passed, pooled)

    start_state = (
        jnp.zeros((batch_rows, feature_cols), jnp.bfloat16),
        jnp.zeros((phase_count, SEGS, feature_cols), jnp.float32),
    )
    current, pooled = lax.fori_loop(0, phase_count + phase_count - 1, advance, start_state)
    shared = broadcast(pooled.astype(jnp.bfloat16), "phase", last_phase)
    own_prompts = lax.dynamic_index_in_dim(shared, phase_here, 0, keepdims=False).reshape(
        halves_here, PH, feature_cols
    )
    owner_ids = owner[0, :, :, 0]
    return_cap = max(2, PH // min(dp_count, 4))
    send_slots = owner_ids * return_cap + bucket_ranks(owner_ids, dp_count)
    parcel = (
        jnp.zeros((halves_here, dp_count * return_cap, feature_cols), jnp.bfloat16)
        .at[half_index, send_slots]
        .set(own_prompts)
    )
    returned = lax.all_to_all(
        parcel.reshape(halves_here, dp_count, return_cap, feature_cols),
        "dp",
        split_axis=1,
        concat_axis=1,
        tiled=True,
    )
    return returned.reshape(1, halves_here, dp_count * return_cap, feature_cols)


LAG = 2
CHIPS = 4
GROUP_Q = QH // KVH
Q_COLS = GROUP_Q * HD
KV_AT = Q_COLS + 2 * HD
MSG_COLS = KV_AT + 128
RANKS = 8
TABLE_ROW = 6
F32 = jnp.float32
BF16 = jnp.bfloat16


def vmem_spec():
    return pl.BlockSpec(memory_space=pltpu.VMEM)


def smem_spec():
    return pl.BlockSpec(memory_space=pltpu.SMEM)


def hbm_spec():
    return pl.BlockSpec(memory_space=pl.ANY)


def call(kernel, outs, args, specs, scratch=(), limit=6, token=None, after=(), span=None):
    count = len(args)
    others = len(after)

    def body(*refs):
        first = count + 1 + others
        at = first + len(outs)
        refs[at][...] = jnp.zeros(refs[at].shape, F32)

        def run():
            kernel(*refs[:count], *refs[first:at], *refs[at + 1 :])

        if span is None:
            run()
        else:
            slot, chunks = span
            chunk = slot - LAG * refs[0][1]
            pl.when((chunk >= 0) & (chunk < chunks))(run)

    outs = list(outs)
    if token is not None:
        outs_all = outs + [jax.ShapeDtypeStruct((8, 128), F32)]
        args, specs = ((*args, token, *after), [*specs] + [hbm_spec()] * (1 + others))
    else:
        outs_all = outs
    return pl.pallas_call(
        kernel if token is None else body,
        out_shape=outs_all,
        in_specs=specs,
        out_specs=[vmem_spec()] * len(outs_all),
        scratch_shapes=list(scratch),
        compiler_params=pltpu.CompilerParams(vmem_limit_bytes=limit * 1024 * 1024),
    )(*args)


def dot(a, b):
    return jnp.dot(a, b, preferred_element_type=F32)


def lane(start, size):
    return pl.ds(pl.multiple_of(start, size), size)


def iota(rows, cols, axis):
    return lax.broadcasted_iota(jnp.int32, (rows, cols), axis)


def as_column(row):
    count = row.shape[1]
    diagonal = iota(count, count, 0) == iota(count, count, 1)
    return jnp.sum(jnp.where(diagonal, row, 0), axis=1, keepdims=True)


def marks(hits):
    return hits.astype(F32).astype(BF16)


def pack_kernel(pos_ref, rows_ref, dest_ref, table_ref, *out_refs):
    chip = pos_ref[0]
    dest = dest_ref[pl.ds(chip, 1), :]
    count = dest.shape[1]
    half = count // 2
    group_row = dest // half
    group_col = as_column(group_row)
    source, here = (iota(count, count, 0), iota(count, count, 1))
    before = (group_col == group_row) & (source // half == here // half) & (source < here)
    rank = jnp.sum(jnp.where(before, 1, 0), axis=0, keepdims=True)
    target = group_row * (2 * RANKS) + (iota(1, count, 1) // half) * RANKS + rank
    width = out_refs[0].shape[1]
    message_row = iota(4 * RANKS, width, 0)
    for k in range(CHIPS):
        turn = chip ^ k
        core, block = (turn >> 1, turn & 1)
        pick = marks(iota(4 * RANKS, count, 0) + core * (4 * RANKS) == target)
        rows = dot(pick, rows_ref[:, lane(block * width, width)])
        rows = jnp.where(message_row == TABLE_ROW, table_ref[...], rows)
        out_refs[k][...] = rows.astype(BF16)


def unpack_kernel(pos_ref, m0, m1, m2, m3, dest_ref, out_ref, table_ref):
    chip, core = (pos_ref[0], pos_ref[2])
    count = dest_ref.shape[1]
    half = count // 2
    turn = 2 * core + (chip & 1)
    total = jnp.zeros(out_ref.shape, F32)
    table = jnp.zeros(table_ref.shape, F32)
    above, across = (iota(count, count, 0), iota(count, count, 1))
    for k, ref in enumerate((m0, m1, m2, m3)):
        loader = turn ^ k
        dest_row = dest_ref[pl.ds(loader, 1), :]
        group_row = dest_row // half
        group_col = as_column(group_row)
        earlier = (group_col == group_row) & (above // half == across // half) & (across < above)
        rank = jnp.sum(jnp.where(earlier, 1, 0), axis=1, keepdims=True)
        at = (group_col - 2 * core) * (2 * RANKS) + (iota(count, 1, 0) // half) * RANKS + rank
        from_message = marks(iota(count, 4 * RANKS, 1) == at)
        slot = (group_row - 2 * core) * count + (iota(1, count, 1) // half) * half + dest_row % half
        to_slot = marks(iota(2 * count, count, 0) == slot)
        rows = ref[...]
        total += dot(dot(to_slot, from_message).astype(BF16), rows)
        mine = (loader >> 1) == core
        table += jnp.where(mine, rows[TABLE_ROW : TABLE_ROW + 1].astype(F32), 0.0)
    out_ref[...] = total.astype(BF16)
    table_ref[...] = table


def added(messages):
    total = messages[0][...].astype(F32)
    for ref in messages[1:]:
        total += ref[...].astype(F32)
    return total


def stage_kernel(*refs):
    *refs, sems = refs
    count = len(refs) // 2
    copies = [pltpu.make_async_copy(refs[i], refs[count + i], sems.at[i]) for i in range(count)]
    for copy in copies:
        copy.start()
    for copy in copies:
        copy.wait()


def pick_rows(slot, pos_ref, wait_ref, recv_ref):
    if wait_ref is None:
        return recv_ref[...]
    count = wait_ref.shape[0] // 2
    at = (slot % 2) * count
    waiting = wait_ref[at : at + count]
    if recv_ref is None:
        return waiting
    return jnp.where(pos_ref[1] == 0, waiting, recv_ref[...])


def project_kernel(slot, has_wait, has_recv, pos_ref, *refs):
    refs = list(refs)
    wait_ref = refs.pop(0) if has_wait else None
    recv_ref = refs.pop(0) if has_recv else None
    gain_ref, *refs = refs
    sources, out_refs, results_ref = (refs[:6], refs[6:10], refs[10])
    chip, core = (pos_ref[0], pos_ref[2])
    rows = pick_rows(slot, pos_ref, wait_ref, recv_ref).astype(F32)
    depth = rows.shape[1]
    gated = (rows * gain_ref[:, lane(chip * depth, depth)]).astype(BF16)
    squares = jnp.sum(rows * rows, axis=1, keepdims=True)
    high = squares.astype(BF16).astype(F32)
    tail = jnp.where(iota(rows.shape[0], 128, 1) < 64, high, squares - high).astype(BF16)

    for at, source in enumerate(sources):
        part, i = (core if at < 3 else 1 - core, at % 3)
        places = [(2 * part + j) ^ pos_ref[0] for j in range(2)]
        step = min(source.shape[2], 512)
        for start in range(0, source.shape[2], step):
            result = dot(gated, source[0, :, start : start + step]).astype(BF16)
            if i == 0:
                inside = start % Q_COLS
                results_ref[places[start // Q_COLS], :, inside : inside + step] = result
            else:
                inside = Q_COLS + (i - 1) * HD
                for j in range(2):
                    results_ref[places[j], :, inside : inside + HD] = result[:, j * HD : (j + 1) * HD]
    for k, out_ref in enumerate(out_refs):
        out_ref[:, :KV_AT] = results_ref[k]
        out_ref[:, KV_AT:] = tail


def means(table_ref, chunk, count, rows):
    segment = table_ref[:, chunk * 128 : chunk * 128 + count].astype(jnp.int32)
    hits = (segment == iota(16, count, 0)) & (iota(16, count, 0) < SEGS)
    counts = jnp.sum(jnp.where(hits, 1.0, 0.0), axis=1, keepdims=True)
    return dot(marks(hits), rows) / jnp.maximum(counts, 1.0)


def attend_kernel(features, slot, chunks, pool_chunk, pos_ref, *refs):
    messages, (table_ref, own_ref, other_ref) = (refs[:CHIPS], refs[CHIPS : CHIPS + 3])
    out_refs, results_ref = (refs[CHIPS + 3 : -1], refs[-1])
    core = pos_ref[2]
    sums = added(messages)
    count = sums.shape[0]
    tail = sums[:, KV_AT:]
    squares = tail[:, 0:1] + tail[:, 64:65]
    scaled = (sums[:, :KV_AT] * lax.rsqrt(squares / features + NORM_EPS)).astype(BF16)
    query = jnp.concatenate([scaled[:, h * HD : (h + 1) * HD] for h in range(GROUP_Q)], axis=0)
    key = scaled[:, Q_COLS : Q_COLS + HD]
    value = scaled[:, Q_COLS + HD :]
    scores = lax.dot_general(query, key, (((1,), (1,)), ((), ())), preferred_element_type=F32)
    scores = (scores * HD ** (-0.5)).reshape(GROUP_Q, count, count)
    chunk = jnp.clip(slot - LAG * pos_ref[1], 0, chunks - 1)
    segment = table_ref[:, lane(chunk * 128, 128)][:, :count].astype(jnp.int32)
    allowed = (as_column(segment) == segment) & (iota(count, count, 1) <= iota(count, count, 0))
    scores = jnp.where(allowed[None], scores, -jnp.inf)
    top = jnp.max(scores, axis=2, keepdims=True)
    weights = jnp.exp(scores - top)
    probs = (weights / jnp.sum(weights, axis=2, keepdims=True)).astype(BF16)
    mixed = dot(probs.reshape(GROUP_Q * count, count), value).astype(BF16)
    mixed = jnp.concatenate([mixed[h * count : (h + 1) * count] for h in range(GROUP_Q)], axis=1)
    if pool_chunk is not None:
        mixed = means(table_ref, pool_chunk, count, mixed).astype(BF16)
    step = own_ref.shape[2] // 8
    for part, source in ((core, own_ref), (1 - core, other_ref)):
        places = [(2 * part + j) ^ pos_ref[0] for j in range(2)]
        for at in range(8):
            result = dot(mixed, source[0, :, at * step : (at + 1) * step]).astype(BF16)
            results_ref[places[at // 4], :, (at % 4) * step : (at % 4 + 1) * step] = result
    for k, out_ref in enumerate(out_refs):
        out_ref[...] = results_ref[k]


def update_kernel(slot, has_wait, has_recv, send, pool_chunk, pooled_sums, pos_ref, *refs):
    refs = list(refs)
    wait_ref = refs.pop(0) if has_wait else None
    recv_ref = refs.pop(0) if has_recv else None
    messages, refs = (refs[:CHIPS], refs[CHIPS:])
    table_ref = refs.pop(0)
    before_ref = refs.pop(0) if pool_chunk is not None and pool_chunk % 2 else None
    rows = pick_rows(slot, pos_ref, wait_ref, recv_ref)
    if pooled_sums:
        total = means(table_ref, pool_chunk, rows.shape[0], rows)
    else:
        total = rows.astype(F32)
    total += added(messages)
    hidden = total.astype(BF16)
    if send:
        refs.pop(0)[...] = hidden
    if pool_chunk is not None:
        pooled = hidden if pooled_sums else means(table_ref, pool_chunk, rows.shape[0], hidden).astype(BF16)
        if before_ref is None:
            refs.pop(0)[...] = pooled
        else:
            out_ref = refs.pop(0)
            out_ref[0] = before_ref[...]
            out_ref[1] = pooled


def parcels(owner_at, pos_ref, rows, table_ref, out_refs):
    chip, core = (pos_ref[0], pos_ref[2])
    count = rows.shape[0]
    own_row = table_ref[:, owner_at : owner_at + count].astype(jnp.int32) - 1
    own_col = as_column(own_row)
    above, across = (iota(count, count, 0), iota(count, count, 1))
    same = (above // 16 == across // 16) & ((above % 16 >= PH) == (across % 16 >= PH))
    earlier = (own_col == own_row) & same & (above < across)
    rank = jnp.sum(jnp.where(earlier, 1, 0), axis=0, keepdims=True)
    place = iota(1, count, 1)
    half = jnp.where(place % 16 >= PH, 1, 0)
    slot = half * 8 + (2 * core + place // 16) * 2 + rank
    turn = 2 * core + (chip & 1)
    for k, out_ref in enumerate(out_refs):
        pick = marks((iota(16, count, 0) == slot) & (own_row == (turn ^ k)))
        out_ref[...] = dot(pick, rows).astype(BF16)


def carry_kernel(last, pos_ref, pooled_ref, share_ref, out_ref):
    out_ref[...] = jnp.where(pos_ref[1] == last, pooled_ref[...], share_ref[...])


def finish_kernel(last, chunk, owner_at, pos_ref, recv_ref, m0, m1, m2, m3, table_ref, before_ref, *refs):
    share_ref, *out_refs, pooled_ref = refs
    count = before_ref.shape[0]
    final = pos_ref[1] == last

    @pl.when(final)
    def _():
        rows = recv_ref[...]
        total = means(table_ref, chunk, rows.shape[0], rows) + added((m0, m1, m2, m3))
        pooled_ref[:count] = before_ref[...]
        pooled_ref[count:] = total.astype(BF16)

    @pl.when(jnp.logical_not(final))
    def _():
        pooled_ref[:count] = share_ref[0]
        pooled_ref[count:] = share_ref[1]

    parcels(owner_at, pos_ref, pooled_ref[...], table_ref, out_refs)


def deliver_kernel(pos_ref, m0, m1, m2, m3, out_ref):
    chip = pos_ref[0]
    width = m0.shape[1]
    out_ref[...] = jnp.zeros_like(out_ref)
    for k, ref in enumerate((m0, m1, m2, m3)):
        cols = lane(((chip ^ k) & 1) * width, width)
        out_ref[:, cols] = out_ref[:, cols] + ref[...]


def chip_shards(prompt_rows, row_dest, segment_ids, owner, gain, w_query, w_key, w_value, w_out):
    chip, phase, core = (lax.axis_index("dp"), lax.axis_index("phase"), lax.axis_index("mp"))
    phases = lax.axis_size("phase")
    pos = jnp.stack([chip, phase, core]).astype(jnp.int32)
    halves, half_rows, cols_here = prompt_rows.shape[1:]
    batch = halves * half_rows
    features = 2 * cols_here
    block = features // CHIPS
    count = batch
    square = [(e, k) for e in range(CHIPS) for k in range(2)]

    def crosswise(value, k):
        pairs = [(2 * e + m, 2 * (2 * m + ((e ^ k) & 1)) + ((e ^ k) >> 1)) for e, m in square]
        return lax.ppermute(value, ("dp", "mp"), pairs)

    def homewards(value, k):
        pairs = [(2 * e + c, 2 * ((2 * c + (e & 1)) ^ k) + (e >> 1)) for e, c in square]
        return lax.ppermute(value, ("dp", "mp"), pairs)

    def exchange(values):
        got = [values[0]]
        for k in range(1, CHIPS):
            got.append(lax.ppermute(values[k], "dp", [(e, e ^ k) for e in range(CHIPS)]))
        return got

    def lower(value):
        return lax.ppermute(value, "phase", [(p, p - 1) for p in range(1, phases)])

    def swap(value):
        return lax.ppermute(value, "mp", [(0, 1), (1, 0)])

    with jax.named_scope("packing"):
        parity = chip % 2
        chunks = 2 * phases
        owner_at = chunks * 128
        table = jnp.zeros((phases, 2, 128), F32)
        numbers = segment_ids[0][:, None, :].astype(F32)
        table = lax.dynamic_update_slice(table, numbers, (0, parity, 0)).reshape(1, -1)
        owners = (owner.reshape(1, -1) + 1).astype(F32)
        last = lax.dynamic_update_slice(jnp.zeros((1, block - owner_at), F32), owners, (0, 16 * parity))
        table = jnp.concatenate([table, last], axis=1)
        dest = row_dest.reshape(CHIPS, batch)
        own = (w_query, w_key, w_value, w_out)
        sources, *_ = lax.optimization_barrier((own, pos, table, dest))
        *own, token = call(
            stage_kernel,
            [pltpu.VMEM(w.shape, BF16) for w in own],
            [pltpu.with_memory_space_constraint(w, pltpu.HBM) for w in own],
            [hbm_spec()] * 4,
            (pltpu.SemaphoreType.DMA((4,)),),
            token=jnp.zeros((8, 128), F32),
        )
        *packed, token = call(
            pack_kernel,
            [jax.ShapeDtypeStruct((4 * RANKS, block), BF16)] * CHIPS,
            (pos, prompt_rows.reshape(batch, cols_here), dest, table),
            [smem_spec()] + [vmem_spec()] * 3,
            token=token,
        )
        arrived = [crosswise(value, k) for k, value in enumerate(packed)]
        start, table, token = call(
            unpack_kernel,
            [jax.ShapeDtypeStruct((2 * batch, block), BF16), jax.ShapeDtypeStruct((1, block), F32)],
            (pos, *arrived, dest),
            [smem_spec()] + [vmem_spec()] * 5,
            token=token,
        )
        waiting = [start]

    with jax.named_scope("weights"):

        def held(values):
            return [pltpu.with_memory_space_constraint(value, pltpu.VMEM) for value in values]

        other = [swap(w) for w in sources[:3]]
        w_in = held([*own[:3], *other])
        last, *_ = lax.optimization_barrier((sources[3], start, *other))
        w_back = held([own[3], swap(last)])

    hops, pooled, got, shares = ({}, {}, {}, {})
    slots = chunks + LAG * (phases - 1)

    def plan(slot):
        chunk = slot - LAG * (phases - 1)
        send = slot < chunks + LAG * (phases - 2)
        pool_chunk = chunk if chunk >= 0 else None
        return (send, pool_chunk, pool_chunk is not None and not send)

    def entering(slot):
        inputs = waiting[slot // 2 : slot // 2 + 1] + [hops[at] for at in (slot - LAG,) if at >= 0]
        return (slot < chunks, slot >= LAG, inputs, [smem_spec()] + [vmem_spec()] * len(inputs))

    def project(slot, token):
        has_wait, has_recv, inputs, specs = entering(slot)
        *sent, token = call(
            functools.partial(project_kernel, slot, has_wait, has_recv),
            [jax.ShapeDtypeStruct((count, MSG_COLS), BF16)] * CHIPS,
            (pos, *inputs, gain, *w_in),
            specs + [vmem_spec()] * 7,
            (pltpu.VMEM((CHIPS, count, KV_AT), BF16),),
            10,
            token,
            span=(slot, chunks),
        )
        got[slot] = exchange(sent)
        return token

    def attend(slot, token):
        _, pool_chunk, early_pool = plan(slot)
        rows = 16 if early_pool else count
        *sent, token = call(
            functools.partial(attend_kernel, features, slot, chunks, pool_chunk if early_pool else None),
            [jax.ShapeDtypeStruct((rows, block), BF16)] * CHIPS,
            (pos, *got[slot], table, *w_back),
            [smem_spec()] + [vmem_spec()] * (CHIPS + 3),
            (pltpu.VMEM((CHIPS, rows, block), BF16),),
            10,
            token,
            [shares[m] for m in shares if slot == 2 * m + 3 + LAG * (phases - 1)],
            (slot, chunks),
        )
        got[slot] = exchange(sent)
        return token

    def finish(slot, token):
        chunk = chunks - 1
        *sent, token = call(
            functools.partial(finish_kernel, phases - 1, chunk, owner_at),
            [jax.ShapeDtypeStruct((16, block), BF16)] * CHIPS,
            (pos, hops[slot - LAG], *got[slot], table, pooled[chunk - 1], shares[max(shares)]),
            [smem_spec()] + [vmem_spec()] * (CHIPS + 4),
            (pltpu.VMEM((32, block), BF16),),
            token=token,
        )
        return sent

    def update(slot, token):
        has_wait, has_recv, inputs, specs = entering(slot)
        send, pool_chunk, early_pool = plan(slot)
        outs = [jax.ShapeDtypeStruct((count, block), BF16)] * send
        before = []
        if pool_chunk is not None:
            odd = pool_chunk % 2 == 1
            outs.append(jax.ShapeDtypeStruct((2, 16, block) if odd else (16, block), BF16))
            before = [pooled[pool_chunk - 1]] if odd else []
        *out, token = call(
            functools.partial(update_kernel, slot, has_wait, has_recv, send, pool_chunk, early_pool),
            outs,
            (pos, *inputs, *got[slot], table, *before),
            specs + [vmem_spec()] * (CHIPS + 1 + len(before)),
            token=token,
            span=(slot, chunks),
        )
        if send:
            hops[slot] = lax.ppermute(out.pop(0), "phase", [(p, (p + 1) % phases) for p in range(phases)])
        if pool_chunk is not None:
            pooled[pool_chunk] = out.pop(0)
            if pool_chunk % 2:
                share = pooled[pool_chunk]
                if shares:
                    share, token = call(
                        functools.partial(carry_kernel, phases - 1),
                        [jax.ShapeDtypeStruct((2, 16, block), BF16)],
                        (pos, share, shares[max(shares)]),
                        [smem_spec()] + [vmem_spec()] * 2,
                        token=token,
                    )
                shares[pool_chunk // 2] = lower(share)
        return token

    for step in range(slots):
        if step % 2 == 0 and step < chunks - 2:
            waiting.append(lower(waiting[-1]))
        with jax.named_scope("project"):
            token = project(step, token)
        if step > 0:
            with jax.named_scope("update"):
                token = update(step - 1, token)
        with jax.named_scope("attend"):
            token = attend(step, token)

    with jax.named_scope("deliver"):
        final = [homewards(value, k) for k, value in enumerate(finish(slots - 1, token))]
        (result,) = call(
            deliver_kernel,
            [jax.ShapeDtypeStruct((16, cols_here), BF16)],
            (pos, *final),
            [smem_spec()] + [vmem_spec()] * 4,
        )
    return result.reshape(1, 2, 8, cols_here)


def solution(mesh):
    in_specs = (
        P("dp", "phase", None, "mp"),
        P(None, "phase", None),
        P("dp", None, None),
        P("dp", "phase", None, None),
        P("phase", None),
        P("phase", "dp", "mp"),
        P("phase", "dp", "mp"),
        P("phase", "dp", "mp"),
        P("phase", "dp", "mp"),
    )
    out_specs = P("dp", "phase", None, "mp")
    square = mesh.shape["dp"] == CHIPS and mesh.shape["mp"] == 2 and mesh.shape["phase"] == 4
    shards = chip_shards if square else general_shards
    return jax.shard_map(shards, mesh=mesh, in_specs=in_specs, out_specs=out_specs, check_vma=False)
```

```python
import functools

import jax
import jax.numpy as jnp
from jax import lax
from jax.experimental import pallas as pl
from jax.experimental.pallas import tpu as pltpu
from jax.sharding import PartitionSpec as P

D = 8192
HD = 128
QH = 32
KVH = 4
SEGS = 6
PH = 3


NORM_EPS = 1e-05


def from_behind(value, axis, steps):
    count = lax.axis_size(axis)
    initial, last = (max(0, -steps), min(count, count - steps))
    return lax.ppermute(value, axis, [(source, source + steps) for source in range(initial, last)])


def broadcast(value, axis, root):
    mine = lax.axis_index(axis) == root
    return lax.psum(jnp.where(mine, value, jnp.zeros_like(value)), axis)


def bucket_ranks(labels, buckets):
    hits_table = (labels[..., None] == jnp.arange(buckets, dtype=jnp.int32)).astype(jnp.int32)
    earlier = jnp.cumsum(hits_table, axis=-2) - hits_table
    return jnp.sum(earlier * hits_table, axis=-1)


def attend_heads(query, key_sel, value_sel, segments):
    head_dim = query.shape[2]
    scores = jnp.einsum("qhd,khd->hqk", query, key_sel, preferred_element_type=jnp.float32)
    scores = scores * head_dim ** (-0.5)
    places = jnp.arange(query.shape[0], dtype=jnp.int32)
    allowed = (segments[:, None] == segments[None, :]) & (places[None, :] <= places[:, None])
    scores = jnp.where(allowed[None, :, :], scores, -jnp.inf)
    row_top = jnp.max(scores, axis=2, keepdims=True)
    weights = jnp.exp(scores - row_top)
    probabilities = (weights / jnp.sum(weights, axis=2, keepdims=True)).astype(jnp.bfloat16)
    mixed = jnp.einsum("hqk,khd->qhd", probabilities, value_sel, preferred_element_type=jnp.float32)
    return mixed.astype(jnp.bfloat16).reshape(query.shape[0], -1)


def general_shards(prompt_rows, row_dest, segment_ids, owner, gain, w_query, w_key, w_value, w_out):
    dp_count = lax.axis_size("dp")
    phase_count = lax.axis_size("phase")
    group_here = lax.axis_index("dp")
    phase_here = lax.axis_index("phase")
    part_here = lax.axis_index("mp")
    halves_here = prompt_rows.shape[1]
    half_rows = prompt_rows.shape[2]
    feature_cols = prompt_rows.shape[3]
    batch_rows = halves_here * half_rows
    capacity = half_rows // min(dp_count, 4)
    half_index = jnp.arange(halves_here, dtype=jnp.int32)[:, None]
    dest_group = row_dest // half_rows
    dest_ranks = bucket_ranks(dest_group, dp_count)
    own_groups = lax.dynamic_index_in_dim(dest_group, group_here, 0, keepdims=False)
    own_ranks = lax.dynamic_index_in_dim(dest_ranks, group_here, 0, keepdims=False)
    send_at = own_groups * capacity + own_ranks
    outgoing = (
        jnp.zeros((halves_here, dp_count * capacity, feature_cols), jnp.bfloat16)
        .at[half_index, send_at]
        .set(prompt_rows[0])
    )
    incoming = lax.all_to_all(
        outgoing.reshape(halves_here, dp_count, capacity, feature_cols),
        "dp",
        split_axis=1,
        concat_axis=1,
        tiled=True,
    )
    source_ids = jnp.arange(dp_count, dtype=jnp.int32)[:, None, None]
    where_from = jnp.transpose(source_ids * capacity + dest_ranks, (1, 0, 2)).reshape(
        halves_here, -1
    )
    target = jnp.where(dest_group == group_here, row_dest % half_rows, half_rows)
    target = jnp.transpose(target, (1, 0, 2)).reshape(halves_here, -1)
    arrived = incoming.reshape(halves_here, dp_count * capacity, feature_cols)[
        half_index, where_from
    ]
    own_halves = (
        jnp.zeros((halves_here, half_rows, feature_cols), jnp.bfloat16)
        .at[half_index, target]
        .set(arrived, mode="drop")
    )
    own_batch = own_halves.reshape(batch_rows, feature_cols)
    waiting = lax.all_gather(own_batch, "phase", axis=0, tiled=True).reshape(
        phase_count, batch_rows, feature_cols
    )
    query_rows, key_rows, value_rows, back_rows = (
        lax.all_gather(w_query[0], "dp", axis=0, tiled=True),
        lax.all_gather(w_key[0], "dp", axis=0, tiled=True),
        lax.all_gather(w_value[0], "dp", axis=0, tiled=True),
        lax.all_gather(w_out[0], "dp", axis=0, tiled=True),
    )
    query_cols = query_rows.shape[1]
    pair_cols = key_rows.shape[1]
    w_proj = jnp.concatenate([query_rows, key_rows, value_rows], axis=1)
    proj_cols = w_proj.shape[1]
    heads_here = query_cols // HD
    group_size = QH // KVH
    key_heads = (part_here * heads_here + jnp.arange(heads_here, dtype=jnp.int32)) // group_size
    gain_row = gain[0]
    segment_table = segment_ids[0]
    last_phase = phase_count - 1
    prompt_numbers = jnp.arange(SEGS, dtype=jnp.int32)

    def advance(tick_index, loop_state):
        current, pooled = loop_state
        batch_index = tick_index - phase_here
        active = (batch_index >= 0) & (batch_index < phase_count)
        batch_slot = jnp.clip(batch_index, 0, phase_count - 1)
        fresh_rows = lax.dynamic_index_in_dim(
            waiting, jnp.clip(tick_index, 0, phase_count - 1), 0, keepdims=False
        )
        tok_rows = jnp.where(phase_here == 0, fresh_rows, current)
        tok_segments = lax.dynamic_index_in_dim(segment_table, batch_slot, 0, keepdims=False)
        tok_float = tok_rows.astype(jnp.float32)
        whole_rows = lax.all_gather(tok_rows, "mp", axis=1, tiled=True)
        whole_float = whole_rows.astype(jnp.float32)
        squares = jnp.sum(whole_float * whole_float, axis=1)
        projected = lax.cond(
            active,
            lambda: jnp.dot(
                (whole_float * gain_row[None, :]).astype(jnp.bfloat16),
                w_proj,
                preferred_element_type=jnp.float32,
            ),
            lambda: jnp.zeros((batch_rows, proj_cols), jnp.float32),
        )
        qkv_rows = (projected * lax.rsqrt(squares / D + NORM_EPS)[:, None]).astype(jnp.bfloat16)
        query = qkv_rows[:, :query_cols].reshape(batch_rows, heads_here, HD)
        key_own = qkv_rows[:, query_cols : query_cols + pair_cols]
        value_own = qkv_rows[:, query_cols + pair_cols :]
        key_all, value_all = (
            lax.all_gather(key_own, "mp", axis=1, tiled=True),
            lax.all_gather(value_own, "mp", axis=1, tiled=True),
        )
        key_sel = jnp.take(key_all.reshape(batch_rows, KVH, HD), key_heads, axis=1)
        value_sel = jnp.take(value_all.reshape(batch_rows, KVH, HD), key_heads, axis=1)
        mixed_own = attend_heads(query, key_sel, value_sel, tok_segments)
        mixed = lax.all_gather(mixed_own, "mp", axis=1, tiled=True)
        updated = lax.cond(
            active,
            lambda: (
                tok_float + jnp.dot(mixed, back_rows, preferred_element_type=jnp.float32)
            ).astype(jnp.bfloat16),
            lambda: tok_rows,
        )
        segment_hits = tok_segments[None, :] == prompt_numbers[:, None]
        segment_sums = jnp.dot(
            segment_hits.astype(jnp.bfloat16), updated, preferred_element_type=jnp.float32
        )
        counts = jnp.sum(segment_hits.astype(jnp.float32), axis=1)
        segment_means = segment_sums / counts[:, None]
        store_here = active & (phase_here == last_phase)
        stored = lax.dynamic_index_in_dim(pooled, batch_slot, 0, keepdims=False)
        pooled = lax.dynamic_update_index_in_dim(
            pooled, jnp.where(store_here, segment_means, stored), batch_slot, 0
        )
        passed = from_behind(updated, "phase", 1)
        return (passed, pooled)

    start_state = (
        jnp.zeros((batch_rows, feature_cols), jnp.bfloat16),
        jnp.zeros((phase_count, SEGS, feature_cols), jnp.float32),
    )
    current, pooled = lax.fori_loop(0, phase_count + phase_count - 1, advance, start_state)
    shared = broadcast(pooled.astype(jnp.bfloat16), "phase", last_phase)
    own_prompts = lax.dynamic_index_in_dim(shared, phase_here, 0, keepdims=False).reshape(
        halves_here, PH, feature_cols
    )
    owner_ids = owner[0, :, :, 0]
    return_cap = max(2, PH // min(dp_count, 4))
    send_slots = owner_ids * return_cap + bucket_ranks(owner_ids, dp_count)
    parcel = (
        jnp.zeros((halves_here, dp_count * return_cap, feature_cols), jnp.bfloat16)
        .at[half_index, send_slots]
        .set(own_prompts)
    )
    returned = lax.all_to_all(
        parcel.reshape(halves_here, dp_count, return_cap, feature_cols),
        "dp",
        split_axis=1,
        concat_axis=1,
        tiled=True,
    )
    return returned.reshape(1, halves_here, dp_count * return_cap, feature_cols)


LAG = 2
CHIPS = 4
GROUP_Q = QH // KVH
Q_COLS = GROUP_Q * HD
KV_AT = Q_COLS + 2 * HD
MSG_COLS = KV_AT + 128
RANKS = 8
TABLE_ROW = 6
F32 = jnp.float32
BF16 = jnp.bfloat16


def vmem_spec():
    return pl.BlockSpec(memory_space=pltpu.VMEM)


def smem_spec():
    return pl.BlockSpec(memory_space=pltpu.SMEM)


def hbm_spec():
    return pl.BlockSpec(memory_space=pl.ANY)


def call(kernel, outs, args, specs, scratch=(), limit=6, token=None, after=(), span=None):
    count = len(args)
    others = len(after)

    def body(*refs):
        first = count + 1 + others
        at = first + len(outs)
        refs[at][...] = jnp.zeros(refs[at].shape, F32)

        def run():
            kernel(*refs[:count], *refs[first:at], *refs[at + 1 :])

        if span is None:
            run()
        else:
            slot, chunks = span
            chunk = slot - LAG * refs[0][1]
            pl.when((chunk >= 0) & (chunk < chunks))(run)

    outs = list(outs)
    if token is not None:
        outs_all = outs + [jax.ShapeDtypeStruct((8, 128), F32)]
        args, specs = ((*args, token, *after), [*specs] + [hbm_spec()] * (1 + others))
    else:
        outs_all = outs
    return pl.pallas_call(
        kernel if token is None else body,
        out_shape=outs_all,
        in_specs=specs,
        out_specs=[vmem_spec()] * len(outs_all),
        scratch_shapes=list(scratch),
        compiler_params=pltpu.CompilerParams(vmem_limit_bytes=limit * 1024 * 1024),
    )(*args)


def dot(a, b):
    return jnp.dot(a, b, preferred_element_type=F32)


def lane(start, size):
    return pl.ds(pl.multiple_of(start, size), size)


def iota(rows, cols, axis):
    return lax.broadcasted_iota(jnp.int32, (rows, cols), axis)


def as_column(row):
    count = row.shape[1]
    diagonal = iota(count, count, 0) == iota(count, count, 1)
    return jnp.sum(jnp.where(diagonal, row, 0), axis=1, keepdims=True)


def marks(hits):
    return hits.astype(F32).astype(BF16)


def pack_kernel(pos_ref, rows_ref, dest_ref, table_ref, *out_refs):
    chip = pos_ref[0]
    dest = dest_ref[pl.ds(chip, 1), :]
    count = dest.shape[1]
    half = count // 2
    group_row = dest // half
    group_col = as_column(group_row)
    source, here = (iota(count, count, 0), iota(count, count, 1))
    before = (group_col == group_row) & (source // half == here // half) & (source < here)
    rank = jnp.sum(jnp.where(before, 1, 0), axis=0, keepdims=True)
    target = group_row * (2 * RANKS) + (iota(1, count, 1) // half) * RANKS + rank
    width = out_refs[0].shape[1]
    message_row = iota(4 * RANKS, width, 0)
    for k in range(CHIPS):
        turn = chip ^ k
        core, block = (turn >> 1, turn & 1)
        pick = marks(iota(4 * RANKS, count, 0) + core * (4 * RANKS) == target)
        rows = dot(pick, rows_ref[:, lane(block * width, width)])
        rows = jnp.where(message_row == TABLE_ROW, table_ref[...], rows)
        out_refs[k][...] = rows.astype(BF16)


def unpack_kernel(pos_ref, m0, m1, m2, m3, dest_ref, out_ref, table_ref):
    chip, core = (pos_ref[0], pos_ref[2])
    count = dest_ref.shape[1]
    half = count // 2
    turn = 2 * core + (chip & 1)
    total = jnp.zeros(out_ref.shape, F32)
    table = jnp.zeros(table_ref.shape, F32)
    above, across = (iota(count, count, 0), iota(count, count, 1))
    for k, ref in enumerate((m0, m1, m2, m3)):
        loader = turn ^ k
        dest_row = dest_ref[pl.ds(loader, 1), :]
        group_row = dest_row // half
        group_col = as_column(group_row)
        earlier = (group_col == group_row) & (above // half == across // half) & (across < above)
        rank = jnp.sum(jnp.where(earlier, 1, 0), axis=1, keepdims=True)
        at = (group_col - 2 * core) * (2 * RANKS) + (iota(count, 1, 0) // half) * RANKS + rank
        from_message = marks(iota(count, 4 * RANKS, 1) == at)
        slot = (group_row - 2 * core) * count + (iota(1, count, 1) // half) * half + dest_row % half
        to_slot = marks(iota(2 * count, count, 0) == slot)
        rows = ref[...]
        total += dot(dot(to_slot, from_message).astype(BF16), rows)
        mine = (loader >> 1) == core
        table += jnp.where(mine, rows[TABLE_ROW : TABLE_ROW + 1].astype(F32), 0.0)
    out_ref[...] = total.astype(BF16)
    table_ref[...] = table


def added(messages):
    total = messages[0][...].astype(F32)
    for ref in messages[1:]:
        total += ref[...].astype(F32)
    return total


def stage_kernel(*refs):
    *refs, sems = refs
    count = len(refs) // 2
    copies = [pltpu.make_async_copy(refs[i], refs[count + i], sems.at[i]) for i in range(count)]
    for copy in copies:
        copy.start()
    for copy in copies:
        copy.wait()


def pick_rows(slot, pos_ref, wait_ref, recv_ref):
    if wait_ref is None:
        return recv_ref[...]
    count = wait_ref.shape[0] // 2
    at = (slot % 2) * count
    waiting = wait_ref[at : at + count]
    if recv_ref is None:
        return waiting
    return jnp.where(pos_ref[1] == 0, waiting, recv_ref[...])


def project_kernel(slot, has_wait, has_recv, near, pos_ref, *refs):
    refs = list(refs)
    wait_ref = refs.pop(0) if has_wait else None
    recv_ref = refs.pop(0) if has_recv else None
    gain_ref, *refs = refs
    own, other, out_refs, results_ref = (refs[:3], refs[3:6], refs[6:8], refs[8])
    chip, core = (pos_ref[0], pos_ref[2])
    rows = pick_rows(slot, pos_ref, wait_ref, recv_ref).astype(F32)
    depth = rows.shape[1]
    gated = (rows * gain_ref[:, lane(chip * depth, depth)]).astype(BF16)
    squares = jnp.sum(rows * rows, axis=1, keepdims=True)
    high = squares.astype(BF16).astype(F32)
    tail = jnp.where(iota(rows.shape[0], 128, 1) < 64, high, squares - high).astype(BF16)


    def multiply(sources):
        places = [j ^ (chip & 1) for j in range(2)]
        for i, source in enumerate(sources):
            step = min(source.shape[2], 512)
            for start in range(0, source.shape[2], step):
                result = dot(gated, source[0, :, start : start + step]).astype(BF16)
                if i == 0:
                    inside = start % Q_COLS
                    results_ref[places[start // Q_COLS], :, inside : inside + step] = result
                else:
                    inside = Q_COLS + (i - 1) * HD
                    for j in range(2):
                        results_ref[places[j], :, inside : inside + HD] = result[:, j * HD : (j + 1) * HD]

    part = chip >> 1 if near else 1 - (chip >> 1)
    pl.when(part == core)(lambda: multiply(own))
    pl.when(part != core)(lambda: multiply(other))
    for k, out_ref in enumerate(out_refs):
        out_ref[:, :KV_AT] = results_ref[k]
        out_ref[:, KV_AT:] = tail


def means(table_ref, chunk, count, rows):
    segment = table_ref[:, chunk * 128 : chunk * 128 + count].astype(jnp.int32)
    hits = (segment == iota(16, count, 0)) & (iota(16, count, 0) < SEGS)
    counts = jnp.sum(jnp.where(hits, 1.0, 0.0), axis=1, keepdims=True)
    return dot(marks(hits), rows) / jnp.maximum(counts, 1.0)


def attend_kernel(features, slot, chunks, pool_chunk, pos_ref, *refs):
    messages, (table_ref, own_ref, other_ref) = (refs[:CHIPS], refs[CHIPS : CHIPS + 3])
    out_refs, results_ref = (refs[CHIPS + 3 : -1], refs[-1])
    core = pos_ref[2]
    sums = added(messages)
    count = sums.shape[0]
    tail = sums[:, KV_AT:]
    squares = tail[:, 0:1] + tail[:, 64:65]
    scaled = (sums[:, :KV_AT] * lax.rsqrt(squares / features + NORM_EPS)).astype(BF16)
    query = jnp.concatenate([scaled[:, h * HD : (h + 1) * HD] for h in range(GROUP_Q)], axis=0)
    key = scaled[:, Q_COLS : Q_COLS + HD]
    value = scaled[:, Q_COLS + HD :]
    scores = lax.dot_general(query, key, (((1,), (1,)), ((), ())), preferred_element_type=F32)
    scores = (scores * HD ** (-0.5)).reshape(GROUP_Q, count, count)
    chunk = jnp.clip(slot - LAG * pos_ref[1], 0, chunks - 1)
    segment = table_ref[:, lane(chunk * 128, 128)][:, :count].astype(jnp.int32)
    allowed = (as_column(segment) == segment) & (iota(count, count, 1) <= iota(count, count, 0))
    scores = jnp.where(allowed[None], scores, -jnp.inf)
    top = jnp.max(scores, axis=2, keepdims=True)
    weights = jnp.exp(scores - top)
    probs = (weights / jnp.sum(weights, axis=2, keepdims=True)).astype(BF16)
    mixed = dot(probs.reshape(GROUP_Q * count, count), value).astype(BF16)
    mixed = jnp.concatenate([mixed[h * count : (h + 1) * count] for h in range(GROUP_Q)], axis=1)
    if pool_chunk is not None:
        mixed = means(table_ref, pool_chunk, count, mixed).astype(BF16)
    step = own_ref.shape[2] // 8
    for part, source in ((core, own_ref), (1 - core, other_ref)):
        places = [(2 * part + j) ^ pos_ref[0] for j in range(2)]
        for at in range(8):
            result = dot(mixed, source[0, :, at * step : (at + 1) * step]).astype(BF16)
            results_ref[places[at // 4], :, (at % 4) * step : (at % 4 + 1) * step] = result
    for k, out_ref in enumerate(out_refs):
        out_ref[...] = results_ref[k]


def update_kernel(slot, has_wait, has_recv, send, pool_chunk, pooled_sums, pos_ref, *refs):
    refs = list(refs)
    wait_ref = refs.pop(0) if has_wait else None
    recv_ref = refs.pop(0) if has_recv else None
    messages, refs = (refs[:CHIPS], refs[CHIPS:])
    table_ref = refs.pop(0)
    before_ref = refs.pop(0) if pool_chunk is not None and pool_chunk % 2 else None
    rows = pick_rows(slot, pos_ref, wait_ref, recv_ref)
    if pooled_sums:
        total = means(table_ref, pool_chunk, rows.shape[0], rows)
    else:
        total = rows.astype(F32)
    total += added(messages)
    hidden = total.astype(BF16)
    if send:
        refs.pop(0)[...] = hidden
    if pool_chunk is not None:
        pooled = hidden if pooled_sums else means(table_ref, pool_chunk, rows.shape[0], hidden).astype(BF16)
        if before_ref is None:
            refs.pop(0)[...] = pooled
        else:
            out_ref = refs.pop(0)
            out_ref[0] = before_ref[...]
            out_ref[1] = pooled


def parcels(owner_at, pos_ref, rows, table_ref, out_refs):
    chip, core = (pos_ref[0], pos_ref[2])
    count = rows.shape[0]
    own_row = table_ref[:, owner_at : owner_at + count].astype(jnp.int32) - 1
    own_col = as_column(own_row)
    above, across = (iota(count, count, 0), iota(count, count, 1))
    same = (above // 16 == across // 16) & ((above % 16 >= PH) == (across % 16 >= PH))
    earlier = (own_col == own_row) & same & (above < across)
    rank = jnp.sum(jnp.where(earlier, 1, 0), axis=0, keepdims=True)
    place = iota(1, count, 1)
    half = jnp.where(place % 16 >= PH, 1, 0)
    slot = half * 8 + (2 * core + place // 16) * 2 + rank
    turn = 2 * core + (chip & 1)
    for k, out_ref in enumerate(out_refs):
        pick = marks((iota(16, count, 0) == slot) & (own_row == (turn ^ k)))
        out_ref[...] = dot(pick, rows).astype(BF16)


def carry_kernel(last, pos_ref, pooled_ref, share_ref, out_ref):
    out_ref[...] = jnp.where(pos_ref[1] == last, pooled_ref[...], share_ref[...])


def finish_kernel(last, chunk, owner_at, pos_ref, recv_ref, m0, m1, m2, m3, table_ref, before_ref, *refs):
    share_ref, *out_refs, pooled_ref = refs
    count = before_ref.shape[0]
    final = pos_ref[1] == last

    @pl.when(final)
    def _():
        rows = recv_ref[...]
        total = means(table_ref, chunk, rows.shape[0], rows) + added((m0, m1, m2, m3))
        pooled_ref[:count] = before_ref[...]
        pooled_ref[count:] = total.astype(BF16)

    @pl.when(jnp.logical_not(final))
    def _():
        pooled_ref[:count] = share_ref[0]
        pooled_ref[count:] = share_ref[1]

    parcels(owner_at, pos_ref, pooled_ref[...], table_ref, out_refs)


def deliver_kernel(pos_ref, m0, m1, m2, m3, out_ref):
    chip = pos_ref[0]
    width = m0.shape[1]
    out_ref[...] = jnp.zeros_like(out_ref)
    for k, ref in enumerate((m0, m1, m2, m3)):
        cols = lane(((chip ^ k) & 1) * width, width)
        out_ref[:, cols] = out_ref[:, cols] + ref[...]


def chip_shards(prompt_rows, row_dest, segment_ids, owner, gain, w_query, w_key, w_value, w_out):
    chip, phase, core = (lax.axis_index("dp"), lax.axis_index("phase"), lax.axis_index("mp"))
    phases = lax.axis_size("phase")
    pos = jnp.stack([chip, phase, core]).astype(jnp.int32)
    halves, half_rows, cols_here = prompt_rows.shape[1:]
    batch = halves * half_rows
    features = 2 * cols_here
    block = features // CHIPS
    count = batch
    square = [(e, k) for e in range(CHIPS) for k in range(2)]

    def crosswise(value, k):
        pairs = [(2 * e + m, 2 * (2 * m + ((e ^ k) & 1)) + ((e ^ k) >> 1)) for e, m in square]
        return lax.ppermute(value, ("dp", "mp"), pairs)

    def homewards(value, k):
        pairs = [(2 * e + c, 2 * ((2 * c + (e & 1)) ^ k) + (e >> 1)) for e, c in square]
        return lax.ppermute(value, ("dp", "mp"), pairs)

    def across(value, k):
        return lax.ppermute(value, "dp", [(e, e ^ k) for e in range(CHIPS)])

    def lower(value):
        return lax.ppermute(value, "phase", [(p, (p - 1) % phases) for p in range(phases)])

    def swap(value):
        return lax.ppermute(value, "mp", [(0, 1), (1, 0)])

    with jax.named_scope("packing"):
        parity = chip % 2
        chunks = 2 * phases
        owner_at = chunks * 128
        table = jnp.zeros((phases, 2, 128), F32)
        numbers = segment_ids[0][:, None, :].astype(F32)
        table = lax.dynamic_update_slice(table, numbers, (0, parity, 0)).reshape(1, -1)
        owners = (owner.reshape(1, -1) + 1).astype(F32)
        last = lax.dynamic_update_slice(jnp.zeros((1, block - owner_at), F32), owners, (0, 16 * parity))
        table = jnp.concatenate([table, last], axis=1)
        dest = row_dest.reshape(CHIPS, batch)
        own = (w_query, w_key, w_value, w_out)
        sources, *_ = lax.optimization_barrier((own, pos, table, dest))
        *own, token = call(
            stage_kernel,
            [pltpu.VMEM(w.shape, BF16) for w in own],
            [pltpu.with_memory_space_constraint(w, pltpu.HBM) for w in own],
            [hbm_spec()] * 4,
            (pltpu.SemaphoreType.DMA((4,)),),
            token=jnp.zeros((8, 128), F32),
        )
        *packed, token = call(
            pack_kernel,
            [jax.ShapeDtypeStruct((4 * RANKS, block), BF16)] * CHIPS,
            (pos, prompt_rows.reshape(batch, cols_here), dest, table),
            [smem_spec()] + [vmem_spec()] * 3,
            token=token,
        )
        arrived = [crosswise(value, k) for k, value in enumerate(packed)]
        start, table, token = call(
            unpack_kernel,
            [jax.ShapeDtypeStruct((2 * batch, block), BF16), jax.ShapeDtypeStruct((1, block), F32)],
            (pos, *arrived, dest),
            [smem_spec()] + [vmem_spec()] * 5,
            token=token,
        )
        waiting = [start]

    with jax.named_scope("weights"):

        def held(values):
            return [pltpu.with_memory_space_constraint(value, pltpu.VMEM) for value in values]

        other = [swap(w) for w in sources[:3]]
        w_in = held([*own[:3], *other])
        last, *_ = lax.optimization_barrier((sources[3], start, *other))
        w_back = held([own[3], swap(last)])

    hops, pooled, got, shares = ({}, {}, {}, {})
    slots = chunks + LAG * (phases - 1)

    def plan(slot):
        chunk = slot - LAG * (phases - 1)
        send = slot < chunks + LAG * (phases - 2)
        pool_chunk = chunk if chunk >= 0 else None
        return (send, pool_chunk, pool_chunk is not None and not send)

    def entering(slot):
        inputs = waiting[slot // 2 : slot // 2 + 1] + [hops[at] for at in (slot - LAG,) if at >= 0]
        return (slot < chunks, slot >= LAG, inputs, [smem_spec()] + [vmem_spec()] * len(inputs))

    def project(slot, token):
        has_wait, has_recv, inputs, specs = entering(slot)
        sent = {}
        for near in (False, True):
            *values, token = call(
                functools.partial(project_kernel, slot, has_wait, has_recv, near),
                [jax.ShapeDtypeStruct((count, MSG_COLS), BF16)] * 2,
                (pos, *inputs, gain, *w_in),
                specs + [vmem_spec()] * 7,
                (pltpu.VMEM((2, count, KV_AT), BF16),),
                10,
                token,
                span=(slot, chunks),
            )
            for j, value in enumerate(values):
                k = j if near else 2 + j
                sent[k] = across(value, k) if k else value
        got[slot] = [sent[k] for k in range(CHIPS)]
        return token

    def attend(slot, token):
        _, pool_chunk, early_pool = plan(slot)
        rows = 16 if early_pool else count
        *sent, token = call(
            functools.partial(attend_kernel, features, slot, chunks, pool_chunk if early_pool else None),
            [jax.ShapeDtypeStruct((rows, block), BF16)] * CHIPS,
            (pos, *got[slot], table, *w_back),
            [smem_spec()] + [vmem_spec()] * (CHIPS + 3),
            (pltpu.VMEM((CHIPS, rows, block), BF16),),
            10,
            token,
            [shares[m] for m in shares if slot == 2 * m + 3 + LAG * (phases - 1)],
            (slot, chunks),
        )
        got[slot] = [across(value, k) if k else value for k, value in enumerate(sent)]
        return token

    def finish(slot, token):
        chunk = chunks - 1
        *sent, token = call(
            functools.partial(finish_kernel, phases - 1, chunk, owner_at),
            [jax.ShapeDtypeStruct((16, block), BF16)] * CHIPS,
            (pos, hops[slot - LAG], *got[slot], table, pooled[chunk - 1], shares[max(shares)]),
            [smem_spec()] + [vmem_spec()] * (CHIPS + 4),
            (pltpu.VMEM((32, block), BF16),),
            token=token,
        )
        return sent

    def update(slot, token, after):
        has_wait, has_recv, inputs, specs = entering(slot)
        send, pool_chunk, early_pool = plan(slot)
        outs = [jax.ShapeDtypeStruct((count, block), BF16)] * send
        before = []
        if pool_chunk is not None:
            odd = pool_chunk % 2 == 1
            outs.append(jax.ShapeDtypeStruct((2, 16, block) if odd else (16, block), BF16))
            before = [pooled[pool_chunk - 1]] if odd else []
        *out, token = call(
            functools.partial(update_kernel, slot, has_wait, has_recv, send, pool_chunk, early_pool),
            outs,
            (pos, *inputs, *got[slot], table, *before),
            specs + [vmem_spec()] * (CHIPS + 1 + len(before)),
            token=token,
            after=after,
            span=(slot, chunks),
        )
        if send:
            hops[slot] = lax.ppermute(out.pop(0), "phase", [(p, (p + 1) % phases) for p in range(phases)])
        if pool_chunk is not None:
            pooled[pool_chunk] = out.pop(0)
            if pool_chunk % 2:
                share = pooled[pool_chunk]
                if shares:
                    share, token = call(
                        functools.partial(carry_kernel, phases - 1),
                        [jax.ShapeDtypeStruct((2, 16, block), BF16)],
                        (pos, share, shares[max(shares)]),
                        [smem_spec()] + [vmem_spec()] * 2,
                        token=token,
                    )
                shares[pool_chunk // 2] = lower(share)
        return token

    for step in range(slots):
        if step % 2 == 0 and step < chunks - 2:
            waiting.append(lower(waiting[-1]))
        with jax.named_scope("project"):
            token = project(step, token)
        if step > 0:
            with jax.named_scope("update"):
                token = update(step - 1, token, got[step][2:])
        with jax.named_scope("attend"):
            token = attend(step, token)

    with jax.named_scope("deliver"):
        final = [homewards(value, k) for k, value in enumerate(finish(slots - 1, token))]
        (result,) = call(
            deliver_kernel,
            [jax.ShapeDtypeStruct((16, cols_here), BF16)],
            (pos, *final),
            [smem_spec()] + [vmem_spec()] * 4,
        )
    return result.reshape(1, 2, 8, cols_here)


def solution(mesh):
    in_specs = (
        P("dp", "phase", None, "mp"),
        P(None, "phase", None),
        P("dp", None, None),
        P("dp", "phase", None, None),
        P("phase", None),
        P("phase", "dp", "mp"),
        P("phase", "dp", "mp"),
        P("phase", "dp", "mp"),
        P("phase", "dp", "mp"),
    )
    out_specs = P("dp", "phase", None, "mp")
    square = mesh.shape["dp"] == CHIPS and mesh.shape["mp"] == 2 and mesh.shape["phase"] == 4
    shards = chip_shards if square else general_shards
    return jax.shard_map(shards, mesh=mesh, in_specs=in_specs, out_specs=out_specs, check_vma=False)
```

```python
import functools

import jax
import jax.numpy as jnp
from jax import lax
from jax.experimental import pallas as pl
from jax.experimental.pallas import tpu as pltpu
from jax.sharding import PartitionSpec as P

D = 8192
HD = 128
QH = 32
KVH = 4
SEGS = 6
PH = 3


NORM_EPS = 1e-05


def from_behind(value, axis, steps):
    count = lax.axis_size(axis)
    initial, last = (max(0, -steps), min(count, count - steps))
    return lax.ppermute(value, axis, [(source, source + steps) for source in range(initial, last)])


def broadcast(value, axis, root):
    mine = lax.axis_index(axis) == root
    return lax.psum(jnp.where(mine, value, jnp.zeros_like(value)), axis)


def bucket_ranks(labels, buckets):
    hits_table = (labels[..., None] == jnp.arange(buckets, dtype=jnp.int32)).astype(jnp.int32)
    earlier = jnp.cumsum(hits_table, axis=-2) - hits_table
    return jnp.sum(earlier * hits_table, axis=-1)


def attend_heads(query, key_sel, value_sel, segments):
    head_dim = query.shape[2]
    scores = jnp.einsum("qhd,khd->hqk", query, key_sel, preferred_element_type=jnp.float32)
    scores = scores * head_dim ** (-0.5)
    places = jnp.arange(query.shape[0], dtype=jnp.int32)
    allowed = (segments[:, None] == segments[None, :]) & (places[None, :] <= places[:, None])
    scores = jnp.where(allowed[None, :, :], scores, -jnp.inf)
    row_top = jnp.max(scores, axis=2, keepdims=True)
    weights = jnp.exp(scores - row_top)
    probabilities = (weights / jnp.sum(weights, axis=2, keepdims=True)).astype(jnp.bfloat16)
    mixed = jnp.einsum("hqk,khd->qhd", probabilities, value_sel, preferred_element_type=jnp.float32)
    return mixed.astype(jnp.bfloat16).reshape(query.shape[0], -1)


def general_shards(prompt_rows, row_dest, segment_ids, owner, gain, w_query, w_key, w_value, w_out):
    dp_count = lax.axis_size("dp")
    phase_count = lax.axis_size("phase")
    group_here = lax.axis_index("dp")
    phase_here = lax.axis_index("phase")
    part_here = lax.axis_index("mp")
    halves_here = prompt_rows.shape[1]
    half_rows = prompt_rows.shape[2]
    feature_cols = prompt_rows.shape[3]
    batch_rows = halves_here * half_rows
    capacity = half_rows // min(dp_count, 4)
    half_index = jnp.arange(halves_here, dtype=jnp.int32)[:, None]
    dest_group = row_dest // half_rows
    dest_ranks = bucket_ranks(dest_group, dp_count)
    own_groups = lax.dynamic_index_in_dim(dest_group, group_here, 0, keepdims=False)
    own_ranks = lax.dynamic_index_in_dim(dest_ranks, group_here, 0, keepdims=False)
    send_at = own_groups * capacity + own_ranks
    outgoing = (
        jnp.zeros((halves_here, dp_count * capacity, feature_cols), jnp.bfloat16)
        .at[half_index, send_at]
        .set(prompt_rows[0])
    )
    incoming = lax.all_to_all(
        outgoing.reshape(halves_here, dp_count, capacity, feature_cols),
        "dp",
        split_axis=1,
        concat_axis=1,
        tiled=True,
    )
    source_ids = jnp.arange(dp_count, dtype=jnp.int32)[:, None, None]
    where_from = jnp.transpose(source_ids * capacity + dest_ranks, (1, 0, 2)).reshape(
        halves_here, -1
    )
    target = jnp.where(dest_group == group_here, row_dest % half_rows, half_rows)
    target = jnp.transpose(target, (1, 0, 2)).reshape(halves_here, -1)
    arrived = incoming.reshape(halves_here, dp_count * capacity, feature_cols)[
        half_index, where_from
    ]
    own_halves = (
        jnp.zeros((halves_here, half_rows, feature_cols), jnp.bfloat16)
        .at[half_index, target]
        .set(arrived, mode="drop")
    )
    own_batch = own_halves.reshape(batch_rows, feature_cols)
    waiting = lax.all_gather(own_batch, "phase", axis=0, tiled=True).reshape(
        phase_count, batch_rows, feature_cols
    )
    query_rows, key_rows, value_rows, back_rows = (
        lax.all_gather(w_query[0], "dp", axis=0, tiled=True),
        lax.all_gather(w_key[0], "dp", axis=0, tiled=True),
        lax.all_gather(w_value[0], "dp", axis=0, tiled=True),
        lax.all_gather(w_out[0], "dp", axis=0, tiled=True),
    )
    query_cols = query_rows.shape[1]
    pair_cols = key_rows.shape[1]
    w_proj = jnp.concatenate([query_rows, key_rows, value_rows], axis=1)
    proj_cols = w_proj.shape[1]
    heads_here = query_cols // HD
    group_size = QH // KVH
    key_heads = (part_here * heads_here + jnp.arange(heads_here, dtype=jnp.int32)) // group_size
    gain_row = gain[0]
    segment_table = segment_ids[0]
    last_phase = phase_count - 1
    prompt_numbers = jnp.arange(SEGS, dtype=jnp.int32)

    def advance(tick_index, loop_state):
        current, pooled = loop_state
        batch_index = tick_index - phase_here
        active = (batch_index >= 0) & (batch_index < phase_count)
        batch_slot = jnp.clip(batch_index, 0, phase_count - 1)
        fresh_rows = lax.dynamic_index_in_dim(
            waiting, jnp.clip(tick_index, 0, phase_count - 1), 0, keepdims=False
        )
        tok_rows = jnp.where(phase_here == 0, fresh_rows, current)
        tok_segments = lax.dynamic_index_in_dim(segment_table, batch_slot, 0, keepdims=False)
        tok_float = tok_rows.astype(jnp.float32)
        whole_rows = lax.all_gather(tok_rows, "mp", axis=1, tiled=True)
        whole_float = whole_rows.astype(jnp.float32)
        squares = jnp.sum(whole_float * whole_float, axis=1)
        projected = lax.cond(
            active,
            lambda: jnp.dot(
                (whole_float * gain_row[None, :]).astype(jnp.bfloat16),
                w_proj,
                preferred_element_type=jnp.float32,
            ),
            lambda: jnp.zeros((batch_rows, proj_cols), jnp.float32),
        )
        qkv_rows = (projected * lax.rsqrt(squares / D + NORM_EPS)[:, None]).astype(jnp.bfloat16)
        query = qkv_rows[:, :query_cols].reshape(batch_rows, heads_here, HD)
        key_own = qkv_rows[:, query_cols : query_cols + pair_cols]
        value_own = qkv_rows[:, query_cols + pair_cols :]
        key_all, value_all = (
            lax.all_gather(key_own, "mp", axis=1, tiled=True),
            lax.all_gather(value_own, "mp", axis=1, tiled=True),
        )
        key_sel = jnp.take(key_all.reshape(batch_rows, KVH, HD), key_heads, axis=1)
        value_sel = jnp.take(value_all.reshape(batch_rows, KVH, HD), key_heads, axis=1)
        mixed_own = attend_heads(query, key_sel, value_sel, tok_segments)
        mixed = lax.all_gather(mixed_own, "mp", axis=1, tiled=True)
        updated = lax.cond(
            active,
            lambda: (
                tok_float + jnp.dot(mixed, back_rows, preferred_element_type=jnp.float32)
            ).astype(jnp.bfloat16),
            lambda: tok_rows,
        )
        segment_hits = tok_segments[None, :] == prompt_numbers[:, None]
        segment_sums = jnp.dot(
            segment_hits.astype(jnp.bfloat16), updated, preferred_element_type=jnp.float32
        )
        counts = jnp.sum(segment_hits.astype(jnp.float32), axis=1)
        segment_means = segment_sums / counts[:, None]
        store_here = active & (phase_here == last_phase)
        stored = lax.dynamic_index_in_dim(pooled, batch_slot, 0, keepdims=False)
        pooled = lax.dynamic_update_index_in_dim(
            pooled, jnp.where(store_here, segment_means, stored), batch_slot, 0
        )
        passed = from_behind(updated, "phase", 1)
        return (passed, pooled)

    start_state = (
        jnp.zeros((batch_rows, feature_cols), jnp.bfloat16),
        jnp.zeros((phase_count, SEGS, feature_cols), jnp.float32),
    )
    current, pooled = lax.fori_loop(0, phase_count + phase_count - 1, advance, start_state)
    shared = broadcast(pooled.astype(jnp.bfloat16), "phase", last_phase)
    own_prompts = lax.dynamic_index_in_dim(shared, phase_here, 0, keepdims=False).reshape(
        halves_here, PH, feature_cols
    )
    owner_ids = owner[0, :, :, 0]
    return_cap = max(2, PH // min(dp_count, 4))
    send_slots = owner_ids * return_cap + bucket_ranks(owner_ids, dp_count)
    parcel = (
        jnp.zeros((halves_here, dp_count * return_cap, feature_cols), jnp.bfloat16)
        .at[half_index, send_slots]
        .set(own_prompts)
    )
    returned = lax.all_to_all(
        parcel.reshape(halves_here, dp_count, return_cap, feature_cols),
        "dp",
        split_axis=1,
        concat_axis=1,
        tiled=True,
    )
    return returned.reshape(1, halves_here, dp_count * return_cap, feature_cols)


LAG = 2
CHIPS = 4
GROUP_Q = QH // KVH
Q_COLS = GROUP_Q * HD
KV_AT = Q_COLS + 2 * HD
MSG_COLS = KV_AT + 128
RANKS = 8
TABLE_ROW = 6
F32 = jnp.float32
BF16 = jnp.bfloat16


def vmem_spec():
    return pl.BlockSpec(memory_space=pltpu.VMEM)


def smem_spec():
    return pl.BlockSpec(memory_space=pltpu.SMEM)


def hbm_spec():
    return pl.BlockSpec(memory_space=pl.ANY)


def call(kernel, outs, args, specs, scratch=(), limit=6, token=None, after=(), span=None):
    count = len(args)
    others = len(after)

    def body(*refs):
        first = count + 1 + others
        at = first + len(outs)
        refs[at][...] = jnp.zeros(refs[at].shape, F32)

        def run():
            kernel(*refs[:count], *refs[first:at], *refs[at + 1 :])

        if span is None:
            run()
        else:
            slot, chunks = span
            chunk = slot - LAG * refs[0][1]
            pl.when((chunk >= 0) & (chunk < chunks))(run)

    outs = list(outs)
    if token is not None:
        outs_all = outs + [jax.ShapeDtypeStruct((8, 128), F32)]
        args, specs = ((*args, token, *after), [*specs] + [hbm_spec()] * (1 + others))
    else:
        outs_all = outs
    return pl.pallas_call(
        kernel if token is None else body,
        out_shape=outs_all,
        in_specs=specs,
        out_specs=[vmem_spec()] * len(outs_all),
        scratch_shapes=list(scratch),
        compiler_params=pltpu.CompilerParams(vmem_limit_bytes=limit * 1024 * 1024),
    )(*args)


def dot(a, b):
    return jnp.dot(a, b, preferred_element_type=F32)


def lane(start, size):
    return pl.ds(pl.multiple_of(start, size), size)


def iota(rows, cols, axis):
    return lax.broadcasted_iota(jnp.int32, (rows, cols), axis)


def as_column(row):
    count = row.shape[1]
    diagonal = iota(count, count, 0) == iota(count, count, 1)
    return jnp.sum(jnp.where(diagonal, row, 0), axis=1, keepdims=True)


def marks(hits):
    return hits.astype(F32).astype(BF16)


def pack_kernel(pos_ref, rows_ref, dest_ref, table_ref, *out_refs):
    chip = pos_ref[0]
    dest = dest_ref[pl.ds(chip, 1), :]
    count = dest.shape[1]
    half = count // 2
    group_row = dest // half
    group_col = as_column(group_row)
    source, here = (iota(count, count, 0), iota(count, count, 1))
    before = (group_col == group_row) & (source // half == here // half) & (source < here)
    rank = jnp.sum(jnp.where(before, 1, 0), axis=0, keepdims=True)
    target = group_row * (2 * RANKS) + (iota(1, count, 1) // half) * RANKS + rank
    width = out_refs[0].shape[1]
    message_row = iota(4 * RANKS, width, 0)
    for k in range(CHIPS):
        turn = chip ^ k
        core, block = (turn >> 1, turn & 1)
        pick = marks(iota(4 * RANKS, count, 0) + core * (4 * RANKS) == target)
        rows = dot(pick, rows_ref[:, lane(block * width, width)])
        rows = jnp.where(message_row == TABLE_ROW, table_ref[...], rows)
        out_refs[k][...] = rows.astype(BF16)


def unpack_kernel(pos_ref, m0, m1, m2, m3, dest_ref, out_ref, table_ref):
    chip, core = (pos_ref[0], pos_ref[2])
    count = dest_ref.shape[1]
    half = count // 2
    turn = 2 * core + (chip & 1)
    total = jnp.zeros(out_ref.shape, F32)
    table = jnp.zeros(table_ref.shape, F32)
    above, across = (iota(count, count, 0), iota(count, count, 1))
    for k, ref in enumerate((m0, m1, m2, m3)):
        loader = turn ^ k
        dest_row = dest_ref[pl.ds(loader, 1), :]
        group_row = dest_row // half
        group_col = as_column(group_row)
        earlier = (group_col == group_row) & (above // half == across // half) & (across < above)
        rank = jnp.sum(jnp.where(earlier, 1, 0), axis=1, keepdims=True)
        at = (group_col - 2 * core) * (2 * RANKS) + (iota(count, 1, 0) // half) * RANKS + rank
        from_message = marks(iota(count, 4 * RANKS, 1) == at)
        slot = (group_row - 2 * core) * count + (iota(1, count, 1) // half) * half + dest_row % half
        to_slot = marks(iota(2 * count, count, 0) == slot)
        rows = ref[...]
        total += dot(dot(to_slot, from_message).astype(BF16), rows)
        mine = (loader >> 1) == core
        table += jnp.where(mine, rows[TABLE_ROW : TABLE_ROW + 1].astype(F32), 0.0)
    out_ref[...] = total.astype(BF16)
    table_ref[...] = table


def added(messages):
    total = messages[0][...].astype(F32)
    for ref in messages[1:]:
        total += ref[...].astype(F32)
    return total


def stage_kernel(*refs):
    *refs, sems = refs
    count = len(refs) // 2
    copies = [pltpu.make_async_copy(refs[i], refs[count + i], sems.at[i]) for i in range(count)]
    for copy in copies:
        copy.start()
    for copy in copies:
        copy.wait()


def pick_rows(slot, pos_ref, wait_ref, recv_ref):
    if wait_ref is None:
        return recv_ref[...]
    count = wait_ref.shape[0] // 2
    at = (slot % 2) * count
    waiting = wait_ref[at : at + count]
    if recv_ref is None:
        return waiting
    return jnp.where(pos_ref[1] == 0, waiting, recv_ref[...])


def project_kernel(slot, has_wait, has_recv, pos_ref, *refs):
    refs = list(refs)
    wait_ref = refs.pop(0) if has_wait else None
    recv_ref = refs.pop(0) if has_recv else None
    gain_ref, *refs = refs
    sources, out_refs, results_ref = (refs[:6], refs[6:10], refs[10])
    chip, core = (pos_ref[0], pos_ref[2])
    rows = pick_rows(slot, pos_ref, wait_ref, recv_ref).astype(F32)
    depth = rows.shape[1]
    gated = (rows * gain_ref[:, lane(chip * depth, depth)]).astype(BF16)
    squares = jnp.sum(rows * rows, axis=1, keepdims=True)
    high = squares.astype(BF16).astype(F32)
    tail = jnp.where(iota(rows.shape[0], 128, 1) < 64, high, squares - high).astype(BF16)

    for at, source in enumerate(sources):
        part, i = (core if at < 3 else 1 - core, at % 3)
        places = [(2 * part + j) ^ pos_ref[0] for j in range(2)]
        step = min(source.shape[2], 1024)
        for start in range(0, source.shape[2], step):
            result = dot(gated, source[0, :, start : start + step]).astype(BF16)
            if i == 0:
                inside = start % Q_COLS
                results_ref[places[start // Q_COLS], :, inside : inside + step] = result
            else:
                inside = Q_COLS + (i - 1) * HD
                for j in range(2):
                    results_ref[places[j], :, inside : inside + HD] = result[:, j * HD : (j + 1) * HD]
    for k, out_ref in enumerate(out_refs):
        out_ref[:, :KV_AT] = results_ref[k]
        out_ref[:, KV_AT:] = tail


def means(table_ref, chunk, count, rows):
    segment = table_ref[:, chunk * 128 : chunk * 128 + count].astype(jnp.int32)
    hits = (segment == iota(16, count, 0)) & (iota(16, count, 0) < SEGS)
    counts = jnp.sum(jnp.where(hits, 1.0, 0.0), axis=1, keepdims=True)
    return dot(marks(hits), rows) / jnp.maximum(counts, 1.0)


def attend_kernel(features, slot, chunks, pool_chunk, pos_ref, *refs):
    messages, (table_ref, own_ref, other_ref) = (refs[:CHIPS], refs[CHIPS : CHIPS + 3])
    out_refs, results_ref = (refs[CHIPS + 3 : -1], refs[-1])
    core = pos_ref[2]
    sums = added(messages)
    count = sums.shape[0]
    tail = sums[:, KV_AT:]
    squares = tail[:, 0:1] + tail[:, 64:65]
    scaled = (sums[:, :KV_AT] * lax.rsqrt(squares / features + NORM_EPS)).astype(BF16)
    query = jnp.concatenate([scaled[:, h * HD : (h + 1) * HD] for h in range(GROUP_Q)], axis=0)
    key = scaled[:, Q_COLS : Q_COLS + HD]
    value = scaled[:, Q_COLS + HD :]
    scores = lax.dot_general(query, key, (((1,), (1,)), ((), ())), preferred_element_type=F32)
    scores = (scores * HD ** (-0.5)).reshape(GROUP_Q, count, count)
    chunk = jnp.clip(slot - LAG * pos_ref[1], 0, chunks - 1)
    segment = table_ref[:, lane(chunk * 128, 128)][:, :count].astype(jnp.int32)
    allowed = (as_column(segment) == segment) & (iota(count, count, 1) <= iota(count, count, 0))
    scores = jnp.where(allowed[None], scores, -jnp.inf)
    top = jnp.max(scores, axis=2, keepdims=True)
    weights = jnp.exp(scores - top)
    probs = (weights / jnp.sum(weights, axis=2, keepdims=True)).astype(BF16)
    mixed = dot(probs.reshape(GROUP_Q * count, count), value).astype(BF16)
    mixed = jnp.concatenate([mixed[h * count : (h + 1) * count] for h in range(GROUP_Q)], axis=1)
    if pool_chunk is not None:
        mixed = means(table_ref, pool_chunk, count, mixed).astype(BF16)
    step = own_ref.shape[2] // 4
    for part, source in ((core, own_ref), (1 - core, other_ref)):
        places = [(2 * part + j) ^ pos_ref[0] for j in range(2)]
        for at in range(4):
            result = dot(mixed, source[0, :, at * step : (at + 1) * step]).astype(BF16)
            results_ref[places[at // 2], :, (at % 2) * step : (at % 2 + 1) * step] = result
    for k, out_ref in enumerate(out_refs):
        out_ref[...] = results_ref[k]


def update_kernel(slot, has_wait, has_recv, send, pool_chunk, pooled_sums, pos_ref, *refs):
    refs = list(refs)
    wait_ref = refs.pop(0) if has_wait else None
    recv_ref = refs.pop(0) if has_recv else None
    messages, refs = (refs[:CHIPS], refs[CHIPS:])
    table_ref = refs.pop(0)
    before_ref = refs.pop(0) if pool_chunk is not None and pool_chunk % 2 else None
    rows = pick_rows(slot, pos_ref, wait_ref, recv_ref)
    if pooled_sums:
        total = means(table_ref, pool_chunk, rows.shape[0], rows)
    else:
        total = rows.astype(F32)
    total += added(messages)
    hidden = total.astype(BF16)
    if send:
        refs.pop(0)[...] = hidden
    if pool_chunk is not None:
        pooled = hidden if pooled_sums else means(table_ref, pool_chunk, rows.shape[0], hidden).astype(BF16)
        if before_ref is None:
            refs.pop(0)[...] = pooled
        else:
            out_ref = refs.pop(0)
            out_ref[0] = before_ref[...]
            out_ref[1] = pooled


def parcels(owner_at, pos_ref, rows, table_ref, out_refs):
    chip, core = (pos_ref[0], pos_ref[2])
    count = rows.shape[0]
    own_row = table_ref[:, owner_at : owner_at + count].astype(jnp.int32) - 1
    own_col = as_column(own_row)
    above, across = (iota(count, count, 0), iota(count, count, 1))
    same = (above // 16 == across // 16) & ((above % 16 >= PH) == (across % 16 >= PH))
    earlier = (own_col == own_row) & same & (above < across)
    rank = jnp.sum(jnp.where(earlier, 1, 0), axis=0, keepdims=True)
    place = iota(1, count, 1)
    half = jnp.where(place % 16 >= PH, 1, 0)
    slot = half * 8 + (2 * core + place // 16) * 2 + rank
    turn = 2 * core + (chip & 1)
    for k, out_ref in enumerate(out_refs):
        pick = marks((iota(16, count, 0) == slot) & (own_row == (turn ^ k)))
        out_ref[...] = dot(pick, rows).astype(BF16)


def finish_kernel(last, chunk, owner_at, pos_ref, recv_ref, m0, m1, m2, m3, table_ref, before_ref, *refs):
    *refs, pooled_ref = refs
    shares, out_refs = (refs[:-CHIPS], refs[-CHIPS:])
    count = before_ref.shape[0]
    phase = pos_ref[1]

    @pl.when(phase == last)
    def _():
        rows = recv_ref[...]
        total = means(table_ref, chunk, rows.shape[0], rows) + added((m0, m1, m2, m3))
        pooled_ref[:count] = before_ref[...]
        pooled_ref[count:] = total.astype(BF16)

    for m, ref in enumerate(shares):

        @pl.when(phase == m)
        def _(ref=ref):
            pooled_ref[:count] = ref[0]
            pooled_ref[count:] = ref[1]

    parcels(owner_at, pos_ref, pooled_ref[...], table_ref, out_refs)


def deliver_kernel(pos_ref, m0, m1, m2, m3, out_ref):
    chip = pos_ref[0]
    width = m0.shape[1]
    out_ref[...] = jnp.zeros_like(out_ref)
    for k, ref in enumerate((m0, m1, m2, m3)):
        cols = lane(((chip ^ k) & 1) * width, width)
        out_ref[:, cols] = out_ref[:, cols] + ref[...]


def chip_shards(prompt_rows, row_dest, segment_ids, owner, gain, w_query, w_key, w_value, w_out):
    chip, phase, core = (lax.axis_index("dp"), lax.axis_index("phase"), lax.axis_index("mp"))
    phases = lax.axis_size("phase")
    pos = jnp.stack([chip, phase, core]).astype(jnp.int32)
    halves, half_rows, cols_here = prompt_rows.shape[1:]
    batch = halves * half_rows
    features = 2 * cols_here
    block = features // CHIPS
    count = batch
    square = [(e, k) for e in range(CHIPS) for k in range(2)]

    def crosswise(value, k):
        pairs = [(2 * e + m, 2 * (2 * m + ((e ^ k) & 1)) + ((e ^ k) >> 1)) for e, m in square]
        return lax.ppermute(value, ("dp", "mp"), pairs)

    def homewards(value, k):
        pairs = [(2 * e + c, 2 * ((2 * c + (e & 1)) ^ k) + (e >> 1)) for e, c in square]
        return lax.ppermute(value, ("dp", "mp"), pairs)

    def exchange(values):
        got = [values[0]]
        for k in range(1, CHIPS):
            got.append(lax.ppermute(values[k], "dp", [(e, e ^ k) for e in range(CHIPS)]))
        return got

    def lower(value):
        return lax.ppermute(value, "phase", [(p, p - 1) for p in range(1, phases)])

    def swap(value):
        return lax.ppermute(value, "mp", [(0, 1), (1, 0)])

    with jax.named_scope("packing"):
        parity = chip % 2
        chunks = 2 * phases
        owner_at = chunks * 128
        table = jnp.zeros((phases, 2, 128), F32)
        numbers = segment_ids[0][:, None, :].astype(F32)
        table = lax.dynamic_update_slice(table, numbers, (0, parity, 0)).reshape(1, -1)
        owners = (owner.reshape(1, -1) + 1).astype(F32)
        last = lax.dynamic_update_slice(jnp.zeros((1, block - owner_at), F32), owners, (0, 16 * parity))
        table = jnp.concatenate([table, last], axis=1)
        dest = row_dest.reshape(CHIPS, batch)
        own = (w_query, w_key, w_value, w_out)
        sources, *_ = lax.optimization_barrier((own, pos, table, dest))
        *own, token = call(
            stage_kernel,
            [pltpu.VMEM(w.shape, BF16) for w in own],
            [pltpu.with_memory_space_constraint(w, pltpu.HBM) for w in own],
            [hbm_spec()] * 4,
            (pltpu.SemaphoreType.DMA((4,)),),
            token=jnp.zeros((8, 128), F32),
        )
        *packed, token = call(
            pack_kernel,
            [jax.ShapeDtypeStruct((4 * RANKS, block), BF16)] * CHIPS,
            (pos, prompt_rows.reshape(batch, cols_here), dest, table),
            [smem_spec()] + [vmem_spec()] * 3,
            token=token,
        )
        arrived = [crosswise(value, k) for k, value in enumerate(packed)]
        start, table, token = call(
            unpack_kernel,
            [jax.ShapeDtypeStruct((2 * batch, block), BF16), jax.ShapeDtypeStruct((1, block), F32)],
            (pos, *arrived, dest),
            [smem_spec()] + [vmem_spec()] * 5,
            token=token,
        )
        waiting = [start]

    with jax.named_scope("weights"):

        def held(values):
            return [pltpu.with_memory_space_constraint(value, pltpu.VMEM) for value in values]

        other = [swap(w) for w in sources[:3]]
        w_in = held([*own[:3], *other])
        last, *_ = lax.optimization_barrier((sources[3], start, *other))
        w_back = held([own[3], swap(last)])

    hops, pooled, got, shares = ({}, {}, {}, {})
    slots = chunks + LAG * (phases - 1)

    def plan(slot):
        chunk = slot - LAG * (phases - 1)
        send = slot < chunks + LAG * (phases - 2)
        pool_chunk = chunk if chunk >= 0 else None
        return (send, pool_chunk, pool_chunk is not None and not send)

    def entering(slot):
        inputs = waiting[slot // 2 : slot // 2 + 1] + [hops[at] for at in (slot - LAG,) if at >= 0]
        return (slot < chunks, slot >= LAG, inputs, [smem_spec()] + [vmem_spec()] * len(inputs))

    def project(slot, token):
        has_wait, has_recv, inputs, specs = entering(slot)
        *sent, token = call(
            functools.partial(project_kernel, slot, has_wait, has_recv),
            [jax.ShapeDtypeStruct((count, MSG_COLS), BF16)] * CHIPS,
            (pos, *inputs, gain, *w_in),
            specs + [vmem_spec()] * 7,
            (pltpu.VMEM((CHIPS, count, KV_AT), BF16),),
            10,
            token,
            span=(slot, chunks),
        )
        got[slot] = exchange(sent)
        return token

    def attend(slot, token):
        _, pool_chunk, early_pool = plan(slot)
        rows = 16 if early_pool else count
        if slot == slots - 1:
            for m in range(phases - 1):
                shares[m] = lax.ppermute(pooled[2 * m + 1], "phase", [(phases - 1, m)])
        *sent, token = call(
            functools.partial(attend_kernel, features, slot, chunks, pool_chunk if early_pool else None),
            [jax.ShapeDtypeStruct((rows, block), BF16)] * CHIPS,
            (pos, *got[slot], table, *w_back),
            [smem_spec()] + [vmem_spec()] * (CHIPS + 3),
            (pltpu.VMEM((CHIPS, rows, block), BF16),),
            10,
            token,
            list(shares.values()),
            (slot, chunks),
        )
        got[slot] = exchange(sent)
        return token

    def finish(slot, token):
        chunk = chunks - 1
        *sent, token = call(
            functools.partial(finish_kernel, phases - 1, chunk, owner_at),
            [jax.ShapeDtypeStruct((16, block), BF16)] * CHIPS,
            (pos, hops[slot - LAG], *got[slot], table, pooled[chunk - 1], *shares.values()),
            [smem_spec()] + [vmem_spec()] * (CHIPS + 3 + len(shares)),
            (pltpu.VMEM((32, block), BF16),),
            token=token,
        )
        return sent

    def update(slot, token):
        has_wait, has_recv, inputs, specs = entering(slot)
        send, pool_chunk, early_pool = plan(slot)
        outs = [jax.ShapeDtypeStruct((count, block), BF16)] * send
        before = []
        if pool_chunk is not None:
            odd = pool_chunk % 2 == 1
            outs.append(jax.ShapeDtypeStruct((2, 16, block) if odd else (16, block), BF16))
            before = [pooled[pool_chunk - 1]] if odd else []
        *out, token = call(
            functools.partial(update_kernel, slot, has_wait, has_recv, send, pool_chunk, early_pool),
            outs,
            (pos, *inputs, *got[slot], table, *before),
            specs + [vmem_spec()] * (CHIPS + 1 + len(before)),
            token=token,
            span=(slot, chunks),
        )
        if send:
            hops[slot] = lax.ppermute(out.pop(0), "phase", [(p, (p + 1) % phases) for p in range(phases)])
        if pool_chunk is not None:
            pooled[pool_chunk] = out.pop(0)
        return token

    for step in range(slots):
        if step % 2 == 0 and step < chunks - 2:
            waiting.append(lower(waiting[-1]))
        with jax.named_scope("project"):
            token = project(step, token)
        if step > 0:
            with jax.named_scope("update"):
                token = update(step - 1, token)
        with jax.named_scope("attend"):
            token = attend(step, token)

    with jax.named_scope("deliver"):
        final = [homewards(value, k) for k, value in enumerate(finish(slots - 1, token))]
        (result,) = call(
            deliver_kernel,
            [jax.ShapeDtypeStruct((16, cols_here), BF16)],
            (pos, *final),
            [smem_spec()] + [vmem_spec()] * 4,
        )
    return result.reshape(1, 2, 8, cols_here)


def solution(mesh):
    in_specs = (
        P("dp", "phase", None, "mp"),
        P(None, "phase", None),
        P("dp", None, None),
        P("dp", "phase", None, None),
        P("phase", None),
        P("phase", "dp", "mp"),
        P("phase", "dp", "mp"),
        P("phase", "dp", "mp"),
        P("phase", "dp", "mp"),
    )
    out_specs = P("dp", "phase", None, "mp")
    square = mesh.shape["dp"] == CHIPS and mesh.shape["mp"] == 2 and mesh.shape["phase"] == 4
    shards = chip_shards if square else general_shards
    return jax.shard_map(shards, mesh=mesh, in_specs=in_specs, out_specs=out_specs, check_vma=False)
```

```python
import functools

import jax
import jax.numpy as jnp
from jax import lax
from jax.experimental import pallas as pl
from jax.experimental.pallas import tpu as pltpu
from jax.sharding import PartitionSpec as P

D = 8192
HD = 128
QH = 32
KVH = 4
SEGS = 6
PH = 3


NORM_EPS = 1e-05


def from_behind(value, axis, steps):
    count = lax.axis_size(axis)
    initial, last = (max(0, -steps), min(count, count - steps))
    return lax.ppermute(value, axis, [(source, source + steps) for source in range(initial, last)])


def broadcast(value, axis, root):
    mine = lax.axis_index(axis) == root
    return lax.psum(jnp.where(mine, value, jnp.zeros_like(value)), axis)


def bucket_ranks(labels, buckets):
    hits_table = (labels[..., None] == jnp.arange(buckets, dtype=jnp.int32)).astype(jnp.int32)
    earlier = jnp.cumsum(hits_table, axis=-2) - hits_table
    return jnp.sum(earlier * hits_table, axis=-1)


def attend_heads(query, key_sel, value_sel, segments):
    head_dim = query.shape[2]
    scores = jnp.einsum("qhd,khd->hqk", query, key_sel, preferred_element_type=jnp.float32)
    scores = scores * head_dim ** (-0.5)
    places = jnp.arange(query.shape[0], dtype=jnp.int32)
    allowed = (segments[:, None] == segments[None, :]) & (places[None, :] <= places[:, None])
    scores = jnp.where(allowed[None, :, :], scores, -jnp.inf)
    row_top = jnp.max(scores, axis=2, keepdims=True)
    weights = jnp.exp(scores - row_top)
    probabilities = (weights / jnp.sum(weights, axis=2, keepdims=True)).astype(jnp.bfloat16)
    mixed = jnp.einsum("hqk,khd->qhd", probabilities, value_sel, preferred_element_type=jnp.float32)
    return mixed.astype(jnp.bfloat16).reshape(query.shape[0], -1)


def general_shards(prompt_rows, row_dest, segment_ids, owner, gain, w_query, w_key, w_value, w_out):
    dp_count = lax.axis_size("dp")
    phase_count = lax.axis_size("phase")
    group_here = lax.axis_index("dp")
    phase_here = lax.axis_index("phase")
    part_here = lax.axis_index("mp")
    halves_here = prompt_rows.shape[1]
    half_rows = prompt_rows.shape[2]
    feature_cols = prompt_rows.shape[3]
    batch_rows = halves_here * half_rows
    capacity = half_rows // min(dp_count, 4)
    half_index = jnp.arange(halves_here, dtype=jnp.int32)[:, None]
    dest_group = row_dest // half_rows
    dest_ranks = bucket_ranks(dest_group, dp_count)
    own_groups = lax.dynamic_index_in_dim(dest_group, group_here, 0, keepdims=False)
    own_ranks = lax.dynamic_index_in_dim(dest_ranks, group_here, 0, keepdims=False)
    send_at = own_groups * capacity + own_ranks
    outgoing = (
        jnp.zeros((halves_here, dp_count * capacity, feature_cols), jnp.bfloat16)
        .at[half_index, send_at]
        .set(prompt_rows[0])
    )
    incoming = lax.all_to_all(
        outgoing.reshape(halves_here, dp_count, capacity, feature_cols),
        "dp",
        split_axis=1,
        concat_axis=1,
        tiled=True,
    )
    source_ids = jnp.arange(dp_count, dtype=jnp.int32)[:, None, None]
    where_from = jnp.transpose(source_ids * capacity + dest_ranks, (1, 0, 2)).reshape(
        halves_here, -1
    )
    target = jnp.where(dest_group == group_here, row_dest % half_rows, half_rows)
    target = jnp.transpose(target, (1, 0, 2)).reshape(halves_here, -1)
    arrived = incoming.reshape(halves_here, dp_count * capacity, feature_cols)[
        half_index, where_from
    ]
    own_halves = (
        jnp.zeros((halves_here, half_rows, feature_cols), jnp.bfloat16)
        .at[half_index, target]
        .set(arrived, mode="drop")
    )
    own_batch = own_halves.reshape(batch_rows, feature_cols)
    waiting = lax.all_gather(own_batch, "phase", axis=0, tiled=True).reshape(
        phase_count, batch_rows, feature_cols
    )
    query_rows, key_rows, value_rows, back_rows = (
        lax.all_gather(w_query[0], "dp", axis=0, tiled=True),
        lax.all_gather(w_key[0], "dp", axis=0, tiled=True),
        lax.all_gather(w_value[0], "dp", axis=0, tiled=True),
        lax.all_gather(w_out[0], "dp", axis=0, tiled=True),
    )
    query_cols = query_rows.shape[1]
    pair_cols = key_rows.shape[1]
    w_proj = jnp.concatenate([query_rows, key_rows, value_rows], axis=1)
    proj_cols = w_proj.shape[1]
    heads_here = query_cols // HD
    group_size = QH // KVH
    key_heads = (part_here * heads_here + jnp.arange(heads_here, dtype=jnp.int32)) // group_size
    gain_row = gain[0]
    segment_table = segment_ids[0]
    last_phase = phase_count - 1
    prompt_numbers = jnp.arange(SEGS, dtype=jnp.int32)

    def advance(tick_index, loop_state):
        current, pooled = loop_state
        batch_index = tick_index - phase_here
        active = (batch_index >= 0) & (batch_index < phase_count)
        batch_slot = jnp.clip(batch_index, 0, phase_count - 1)
        fresh_rows = lax.dynamic_index_in_dim(
            waiting, jnp.clip(tick_index, 0, phase_count - 1), 0, keepdims=False
        )
        tok_rows = jnp.where(phase_here == 0, fresh_rows, current)
        tok_segments = lax.dynamic_index_in_dim(segment_table, batch_slot, 0, keepdims=False)
        tok_float = tok_rows.astype(jnp.float32)
        whole_rows = lax.all_gather(tok_rows, "mp", axis=1, tiled=True)
        whole_float = whole_rows.astype(jnp.float32)
        squares = jnp.sum(whole_float * whole_float, axis=1)
        projected = lax.cond(
            active,
            lambda: jnp.dot(
                (whole_float * gain_row[None, :]).astype(jnp.bfloat16),
                w_proj,
                preferred_element_type=jnp.float32,
            ),
            lambda: jnp.zeros((batch_rows, proj_cols), jnp.float32),
        )
        qkv_rows = (projected * lax.rsqrt(squares / D + NORM_EPS)[:, None]).astype(jnp.bfloat16)
        query = qkv_rows[:, :query_cols].reshape(batch_rows, heads_here, HD)
        key_own = qkv_rows[:, query_cols : query_cols + pair_cols]
        value_own = qkv_rows[:, query_cols + pair_cols :]
        key_all, value_all = (
            lax.all_gather(key_own, "mp", axis=1, tiled=True),
            lax.all_gather(value_own, "mp", axis=1, tiled=True),
        )
        key_sel = jnp.take(key_all.reshape(batch_rows, KVH, HD), key_heads, axis=1)
        value_sel = jnp.take(value_all.reshape(batch_rows, KVH, HD), key_heads, axis=1)
        mixed_own = attend_heads(query, key_sel, value_sel, tok_segments)
        mixed = lax.all_gather(mixed_own, "mp", axis=1, tiled=True)
        updated = lax.cond(
            active,
            lambda: (
                tok_float + jnp.dot(mixed, back_rows, preferred_element_type=jnp.float32)
            ).astype(jnp.bfloat16),
            lambda: tok_rows,
        )
        segment_hits = tok_segments[None, :] == prompt_numbers[:, None]
        segment_sums = jnp.dot(
            segment_hits.astype(jnp.bfloat16), updated, preferred_element_type=jnp.float32
        )
        counts = jnp.sum(segment_hits.astype(jnp.float32), axis=1)
        segment_means = segment_sums / counts[:, None]
        store_here = active & (phase_here == last_phase)
        stored = lax.dynamic_index_in_dim(pooled, batch_slot, 0, keepdims=False)
        pooled = lax.dynamic_update_index_in_dim(
            pooled, jnp.where(store_here, segment_means, stored), batch_slot, 0
        )
        passed = from_behind(updated, "phase", 1)
        return (passed, pooled)

    start_state = (
        jnp.zeros((batch_rows, feature_cols), jnp.bfloat16),
        jnp.zeros((phase_count, SEGS, feature_cols), jnp.float32),
    )
    current, pooled = lax.fori_loop(0, phase_count + phase_count - 1, advance, start_state)
    shared = broadcast(pooled.astype(jnp.bfloat16), "phase", last_phase)
    own_prompts = lax.dynamic_index_in_dim(shared, phase_here, 0, keepdims=False).reshape(
        halves_here, PH, feature_cols
    )
    owner_ids = owner[0, :, :, 0]
    return_cap = max(2, PH // min(dp_count, 4))
    send_slots = owner_ids * return_cap + bucket_ranks(owner_ids, dp_count)
    parcel = (
        jnp.zeros((halves_here, dp_count * return_cap, feature_cols), jnp.bfloat16)
        .at[half_index, send_slots]
        .set(own_prompts)
    )
    returned = lax.all_to_all(
        parcel.reshape(halves_here, dp_count, return_cap, feature_cols),
        "dp",
        split_axis=1,
        concat_axis=1,
        tiled=True,
    )
    return returned.reshape(1, halves_here, dp_count * return_cap, feature_cols)


LAG = 2
CHIPS = 4
GROUP_Q = QH // KVH
Q_COLS = GROUP_Q * HD
KV_AT = Q_COLS + 2 * HD
MSG_COLS = KV_AT + 128
RANKS = 8
TABLE_ROW = 6
F32 = jnp.float32
BF16 = jnp.bfloat16


def vmem_spec():
    return pl.BlockSpec(memory_space=pltpu.VMEM)


def smem_spec():
    return pl.BlockSpec(memory_space=pltpu.SMEM)


def hbm_spec():
    return pl.BlockSpec(memory_space=pl.ANY)


def call(kernel, outs, args, specs, scratch=(), limit=6, token=None, after=(), span=None):
    count = len(args)
    others = len(after)

    def body(*refs):
        first = count + 1 + others
        at = first + len(outs)
        refs[at][...] = jnp.zeros(refs[at].shape, F32)

        def run():
            kernel(*refs[:count], *refs[first:at], *refs[at + 1 :])

        if span is None:
            run()
        else:
            slot, chunks = span
            chunk = slot - LAG * refs[0][1]
            pl.when((chunk >= 0) & (chunk < chunks))(run)

    outs = list(outs)
    if token is not None:
        outs_all = outs + [jax.ShapeDtypeStruct((8, 128), F32)]
        args, specs = ((*args, token, *after), [*specs] + [hbm_spec()] * (1 + others))
    else:
        outs_all = outs
    return pl.pallas_call(
        kernel if token is None else body,
        out_shape=outs_all,
        in_specs=specs,
        out_specs=[vmem_spec()] * len(outs_all),
        scratch_shapes=list(scratch),
        compiler_params=pltpu.CompilerParams(vmem_limit_bytes=limit * 1024 * 1024),
    )(*args)


def dot(a, b):
    return jnp.dot(a, b, preferred_element_type=F32)


def lane(start, size):
    return pl.ds(pl.multiple_of(start, size), size)


def iota(rows, cols, axis):
    return lax.broadcasted_iota(jnp.int32, (rows, cols), axis)


def as_column(row):
    count = row.shape[1]
    diagonal = iota(count, count, 0) == iota(count, count, 1)
    return jnp.sum(jnp.where(diagonal, row, 0), axis=1, keepdims=True)


def marks(hits):
    return hits.astype(F32).astype(BF16)


def pack_kernel(pos_ref, rows_ref, dest_ref, table_ref, *out_refs):
    chip = pos_ref[0]
    dest = dest_ref[pl.ds(chip, 1), :]
    count = dest.shape[1]
    half = count // 2
    group_row = dest // half
    group_col = as_column(group_row)
    source, here = (iota(count, count, 0), iota(count, count, 1))
    before = (group_col == group_row) & (source // half == here // half) & (source < here)
    rank = jnp.sum(jnp.where(before, 1, 0), axis=0, keepdims=True)
    target = group_row * (2 * RANKS) + (iota(1, count, 1) // half) * RANKS + rank
    width = out_refs[0].shape[1]
    message_row = iota(4 * RANKS, width, 0)
    for k in range(CHIPS):
        turn = chip ^ k
        core, block = (turn >> 1, turn & 1)
        pick = marks(iota(4 * RANKS, count, 0) + core * (4 * RANKS) == target)
        rows = dot(pick, rows_ref[:, lane(block * width, width)])
        rows = jnp.where(message_row == TABLE_ROW, table_ref[...], rows)
        out_refs[k][...] = rows.astype(BF16)


def unpack_kernel(pos_ref, m0, m1, m2, m3, dest_ref, out_ref, table_ref):
    chip, core = (pos_ref[0], pos_ref[2])
    count = dest_ref.shape[1]
    half = count // 2
    turn = 2 * core + (chip & 1)
    total = jnp.zeros(out_ref.shape, F32)
    table = jnp.zeros(table_ref.shape, F32)
    above, across = (iota(count, count, 0), iota(count, count, 1))
    for k, ref in enumerate((m0, m1, m2, m3)):
        loader = turn ^ k
        dest_row = dest_ref[pl.ds(loader, 1), :]
        group_row = dest_row // half
        group_col = as_column(group_row)
        earlier = (group_col == group_row) & (above // half == across // half) & (across < above)
        rank = jnp.sum(jnp.where(earlier, 1, 0), axis=1, keepdims=True)
        at = (group_col - 2 * core) * (2 * RANKS) + (iota(count, 1, 0) // half) * RANKS + rank
        from_message = marks(iota(count, 4 * RANKS, 1) == at)
        slot = (group_row - 2 * core) * count + (iota(1, count, 1) // half) * half + dest_row % half
        to_slot = marks(iota(2 * count, count, 0) == slot)
        rows = ref[...]
        total += dot(dot(to_slot, from_message).astype(BF16), rows)
        mine = (loader >> 1) == core
        table += jnp.where(mine, rows[TABLE_ROW : TABLE_ROW + 1].astype(F32), 0.0)
    out_ref[...] = total.astype(BF16)
    table_ref[...] = table


def added(messages):
    total = messages[0][...].astype(F32)
    for ref in messages[1:]:
        total += ref[...].astype(F32)
    return total


def stage_kernel(*refs):
    *refs, sems = refs
    count = len(refs) // 2
    copies = [pltpu.make_async_copy(refs[i], refs[count + i], sems.at[i]) for i in range(count)]
    for copy in copies:
        copy.start()
    for copy in copies:
        copy.wait()


def pick_rows(slot, pos_ref, wait_ref, recv_ref):
    if wait_ref is None:
        return recv_ref[...]
    count = wait_ref.shape[0] // 2
    at = (slot % 2) * count
    waiting = wait_ref[at : at + count]
    if recv_ref is None:
        return waiting
    return jnp.where(pos_ref[1] == 0, waiting, recv_ref[...])


def project_kernel(slot, has_wait, has_recv, pos_ref, *refs):
    refs = list(refs)
    wait_ref = refs.pop(0) if has_wait else None
    recv_ref = refs.pop(0) if has_recv else None
    gain_ref, *refs = refs
    sources, out_refs, results_ref = (refs[:6], refs[6:10], refs[10])
    chip, core = (pos_ref[0], pos_ref[2])
    rows = pick_rows(slot, pos_ref, wait_ref, recv_ref).astype(F32)
    depth = rows.shape[1]
    gated = (rows * gain_ref[:, lane(chip * depth, depth)]).astype(BF16)
    squares = jnp.sum(rows * rows, axis=1, keepdims=True)
    high = squares.astype(BF16).astype(F32)
    tail = jnp.where(iota(rows.shape[0], 128, 1) < 64, high, squares - high).astype(BF16)

    for at, source in enumerate(sources):
        part, i = (core if at < 3 else 1 - core, at % 3)
        places = [(2 * part + j) ^ pos_ref[0] for j in range(2)]
        step = min(source.shape[2], 1024)
        for start in range(0, source.shape[2], step):
            result = dot(gated, source[0, :, start : start + step]).astype(BF16)
            if i == 0:
                inside = start % Q_COLS
                results_ref[places[start // Q_COLS], :, inside : inside + step] = result
            else:
                inside = Q_COLS + (i - 1) * HD
                for j in range(2):
                    results_ref[places[j], :, inside : inside + HD] = result[:, j * HD : (j + 1) * HD]
    for k, out_ref in enumerate(out_refs):
        out_ref[:, :KV_AT] = results_ref[k]
        out_ref[:, KV_AT:] = tail


def means(table_ref, chunk, count, rows):
    segment = table_ref[:, chunk * 128 : chunk * 128 + count].astype(jnp.int32)
    hits = (segment == iota(16, count, 0)) & (iota(16, count, 0) < SEGS)
    counts = jnp.sum(jnp.where(hits, 1.0, 0.0), axis=1, keepdims=True)
    return dot(marks(hits), rows) / jnp.maximum(counts, 1.0)


def attend_kernel(features, slot, chunks, pool_chunk, pos_ref, *refs):
    messages, (table_ref, own_ref, other_ref) = (refs[:CHIPS], refs[CHIPS : CHIPS + 3])
    out_refs, results_ref = (refs[CHIPS + 3 : -1], refs[-1])
    core = pos_ref[2]
    sums = added(messages)
    count = sums.shape[0]
    tail = sums[:, KV_AT:]
    squares = tail[:, 0:1] + tail[:, 64:65]
    scaled = (sums[:, :KV_AT] * lax.rsqrt(squares / features + NORM_EPS)).astype(BF16)
    query = jnp.concatenate([scaled[:, h * HD : (h + 1) * HD] for h in range(GROUP_Q)], axis=0)
    key = scaled[:, Q_COLS : Q_COLS + HD]
    value = scaled[:, Q_COLS + HD :]
    scores = lax.dot_general(query, key, (((1,), (1,)), ((), ())), preferred_element_type=F32)
    scores = (scores * HD ** (-0.5)).reshape(GROUP_Q, count, count)
    chunk = jnp.clip(slot - LAG * pos_ref[1], 0, chunks - 1)
    segment = table_ref[:, lane(chunk * 128, 128)][:, :count].astype(jnp.int32)
    allowed = (as_column(segment) == segment) & (iota(count, count, 1) <= iota(count, count, 0))
    scores = jnp.where(allowed[None], scores, -jnp.inf)
    top = jnp.max(scores, axis=2, keepdims=True)
    weights = jnp.exp(scores - top)
    probs = (weights / jnp.sum(weights, axis=2, keepdims=True)).astype(BF16)
    mixed = dot(probs.reshape(GROUP_Q * count, count), value).astype(BF16)
    mixed = jnp.concatenate([mixed[h * count : (h + 1) * count] for h in range(GROUP_Q)], axis=1)
    if pool_chunk is not None:
        mixed = means(table_ref, pool_chunk, count, mixed).astype(BF16)
    step = own_ref.shape[2] // 4
    for part, source in ((core, own_ref), (1 - core, other_ref)):
        places = [(2 * part + j) ^ pos_ref[0] for j in range(2)]
        for at in range(4):
            result = dot(mixed, source[0, :, at * step : (at + 1) * step]).astype(BF16)
            results_ref[places[at // 2], :, (at % 2) * step : (at % 2 + 1) * step] = result
    for k, out_ref in enumerate(out_refs):
        out_ref[...] = results_ref[k]


def update_kernel(slot, has_wait, has_recv, send, pool_chunk, pooled_sums, pos_ref, *refs):
    refs = list(refs)
    wait_ref = refs.pop(0) if has_wait else None
    recv_ref = refs.pop(0) if has_recv else None
    messages, refs = (refs[:CHIPS], refs[CHIPS:])
    table_ref = refs.pop(0)
    before_ref = refs.pop(0) if pool_chunk is not None and pool_chunk % 2 else None
    rows = pick_rows(slot, pos_ref, wait_ref, recv_ref)
    if pooled_sums:
        total = means(table_ref, pool_chunk, rows.shape[0], rows)
    else:
        total = rows.astype(F32)
    total += added(messages)
    hidden = total.astype(BF16)
    if send:
        refs.pop(0)[...] = hidden
    if pool_chunk is not None:
        pooled = hidden if pooled_sums else means(table_ref, pool_chunk, rows.shape[0], hidden).astype(BF16)
        if before_ref is None:
            refs.pop(0)[...] = pooled
        else:
            out_ref = refs.pop(0)
            out_ref[0] = before_ref[...]
            out_ref[1] = pooled


def parcels(owner_at, pos_ref, rows, table_ref, out_refs):
    chip, core = (pos_ref[0], pos_ref[2])
    count = rows.shape[0]
    own_row = table_ref[:, owner_at : owner_at + count].astype(jnp.int32) - 1
    own_col = as_column(own_row)
    above, across = (iota(count, count, 0), iota(count, count, 1))
    same = (above // 16 == across // 16) & ((above % 16 >= PH) == (across % 16 >= PH))
    earlier = (own_col == own_row) & same & (above < across)
    rank = jnp.sum(jnp.where(earlier, 1, 0), axis=0, keepdims=True)
    place = iota(1, count, 1)
    half = jnp.where(place % 16 >= PH, 1, 0)
    slot = half * 8 + (2 * core + place // 16) * 2 + rank
    turn = 2 * core + (chip & 1)
    for k, out_ref in enumerate(out_refs):
        pick = marks((iota(16, count, 0) == slot) & (own_row == (turn ^ k)))
        out_ref[...] = dot(pick, rows).astype(BF16)


def finish_kernel(last, chunk, owner_at, pos_ref, recv_ref, m0, m1, m2, m3, table_ref, before_ref, *refs):
    *refs, pooled_ref = refs
    shares, out_refs = (refs[:-CHIPS], refs[-CHIPS:])
    count = before_ref.shape[0]
    phase = pos_ref[1]

    @pl.when(phase == last)
    def _():
        rows = recv_ref[...]
        total = means(table_ref, chunk, rows.shape[0], rows) + added((m0, m1, m2, m3))
        pooled_ref[:count] = before_ref[...]
        pooled_ref[count:] = total.astype(BF16)

    for m, ref in enumerate(shares):

        @pl.when(phase == m)
        def _(ref=ref):
            pooled_ref[:count] = ref[0]
            pooled_ref[count:] = ref[1]

    parcels(owner_at, pos_ref, pooled_ref[...], table_ref, out_refs)


def deliver_kernel(pos_ref, m0, m1, m2, m3, out_ref):
    chip = pos_ref[0]
    width = m0.shape[1]
    out_ref[...] = jnp.zeros_like(out_ref)
    for k, ref in enumerate((m0, m1, m2, m3)):
        cols = lane(((chip ^ k) & 1) * width, width)
        out_ref[:, cols] = out_ref[:, cols] + ref[...]


def chip_shards(prompt_rows, row_dest, segment_ids, owner, gain, w_query, w_key, w_value, w_out):
    chip, phase, core = (lax.axis_index("dp"), lax.axis_index("phase"), lax.axis_index("mp"))
    phases = lax.axis_size("phase")
    pos = jnp.stack([chip, phase, core]).astype(jnp.int32)
    halves, half_rows, cols_here = prompt_rows.shape[1:]
    batch = halves * half_rows
    features = 2 * cols_here
    block = features // CHIPS
    count = batch
    square = [(e, k) for e in range(CHIPS) for k in range(2)]

    def crosswise(value, k):
        pairs = [(2 * e + m, 2 * (2 * m + ((e ^ k) & 1)) + ((e ^ k) >> 1)) for e, m in square]
        return lax.ppermute(value, ("dp", "mp"), pairs)

    def homewards(value, k):
        pairs = [(2 * e + c, 2 * ((2 * c + (e & 1)) ^ k) + (e >> 1)) for e, c in square]
        return lax.ppermute(value, ("dp", "mp"), pairs)

    def exchange(values):
        got = [values[0]]
        for k in (3, 1, 2):
            got.append(lax.ppermute(values[k], "dp", [(e, e ^ k) for e in range(CHIPS)]))
        return got

    def lower(value):
        return lax.ppermute(value, "phase", [(p, p - 1) for p in range(1, phases)])

    def swap(value):
        return lax.ppermute(value, "mp", [(0, 1), (1, 0)])

    with jax.named_scope("packing"):
        parity = chip % 2
        chunks = 2 * phases
        owner_at = chunks * 128
        table = jnp.zeros((phases, 2, 128), F32)
        numbers = segment_ids[0][:, None, :].astype(F32)
        table = lax.dynamic_update_slice(table, numbers, (0, parity, 0)).reshape(1, -1)
        owners = (owner.reshape(1, -1) + 1).astype(F32)
        last = lax.dynamic_update_slice(jnp.zeros((1, block - owner_at), F32), owners, (0, 16 * parity))
        table = jnp.concatenate([table, last], axis=1)
        dest = row_dest.reshape(CHIPS, batch)
        own = (w_query, w_key, w_value, w_out)
        sources, *_ = lax.optimization_barrier((own, pos, table, dest))
        *own, token = call(
            stage_kernel,
            [pltpu.VMEM(w.shape, BF16) for w in own],
            [pltpu.with_memory_space_constraint(w, pltpu.HBM) for w in own],
            [hbm_spec()] * 4,
            (pltpu.SemaphoreType.DMA((4,)),),
            token=jnp.zeros((8, 128), F32),
        )
        *packed, token = call(
            pack_kernel,
            [jax.ShapeDtypeStruct((4 * RANKS, block), BF16)] * CHIPS,
            (pos, prompt_rows.reshape(batch, cols_here), dest, table),
            [smem_spec()] + [vmem_spec()] * 3,
            token=token,
        )
        arrived = [crosswise(value, k) for k, value in enumerate(packed)]
        start, table, token = call(
            unpack_kernel,
            [jax.ShapeDtypeStruct((2 * batch, block), BF16), jax.ShapeDtypeStruct((1, block), F32)],
            (pos, *arrived, dest),
            [smem_spec()] + [vmem_spec()] * 5,
            token=token,
        )
        waiting = [start]

    with jax.named_scope("weights"):

        def held(values):
            return [pltpu.with_memory_space_constraint(value, pltpu.VMEM) for value in values]

        other = [swap(w) for w in sources[:3]]
        w_in = held([*own[:3], *other])
        last, *_ = lax.optimization_barrier((sources[3], start, *other))
        w_back = held([own[3], swap(last)])

    hops, pooled, got, shares = ({}, {}, {}, {})
    slots = chunks + LAG * (phases - 1)

    def plan(slot):
        chunk = slot - LAG * (phases - 1)
        send = slot < chunks + LAG * (phases - 2)
        pool_chunk = chunk if chunk >= 0 else None
        return (send, pool_chunk, pool_chunk is not None and not send)

    def entering(slot):
        inputs = waiting[slot // 2 : slot // 2 + 1] + [hops[at] for at in (slot - LAG,) if at >= 0]
        return (slot < chunks, slot >= LAG, inputs, [smem_spec()] + [vmem_spec()] * len(inputs))

    def project(slot, token):
        has_wait, has_recv, inputs, specs = entering(slot)
        *sent, token = call(
            functools.partial(project_kernel, slot, has_wait, has_recv),
            [jax.ShapeDtypeStruct((count, MSG_COLS), BF16)] * CHIPS,
            (pos, *inputs, gain, *w_in),
            specs + [vmem_spec()] * 7,
            (pltpu.VMEM((CHIPS, count, KV_AT), BF16),),
            10,
            token,
            span=(slot, chunks),
        )
        got[slot] = exchange(sent)
        return token

    def attend(slot, token):
        _, pool_chunk, early_pool = plan(slot)
        rows = 16 if early_pool else count
        if slot == slots - 1:
            for m in range(phases - 1):
                shares[m] = lax.ppermute(pooled[2 * m + 1], "phase", [(phases - 1, m)])
        *sent, token = call(
            functools.partial(attend_kernel, features, slot, chunks, pool_chunk if early_pool else None),
            [jax.ShapeDtypeStruct((rows, block), BF16)] * CHIPS,
            (pos, *got[slot], table, *w_back),
            [smem_spec()] + [vmem_spec()] * (CHIPS + 3),
            (pltpu.VMEM((CHIPS, rows, block), BF16),),
            10,
            token,
            list(shares.values()),
            (slot, chunks),
        )
        got[slot] = exchange(sent)
        return token

    def finish(slot, token):
        chunk = chunks - 1
        *sent, token = call(
            functools.partial(finish_kernel, phases - 1, chunk, owner_at),
            [jax.ShapeDtypeStruct((16, block), BF16)] * CHIPS,
            (pos, hops[slot - LAG], *got[slot], table, pooled[chunk - 1], *shares.values()),
            [smem_spec()] + [vmem_spec()] * (CHIPS + 3 + len(shares)),
            (pltpu.VMEM((32, block), BF16),),
            token=token,
        )
        return sent

    def update(slot, token):
        has_wait, has_recv, inputs, specs = entering(slot)
        send, pool_chunk, early_pool = plan(slot)
        outs = [jax.ShapeDtypeStruct((count, block), BF16)] * send
        before = []
        if pool_chunk is not None:
            odd = pool_chunk % 2 == 1
            outs.append(jax.ShapeDtypeStruct((2, 16, block) if odd else (16, block), BF16))
            before = [pooled[pool_chunk - 1]] if odd else []
        *out, token = call(
            functools.partial(update_kernel, slot, has_wait, has_recv, send, pool_chunk, early_pool),
            outs,
            (pos, *inputs, *got[slot], table, *before),
            specs + [vmem_spec()] * (CHIPS + 1 + len(before)),
            token=token,
            span=(slot, chunks),
        )
        if send:
            hops[slot] = lax.ppermute(out.pop(0), "phase", [(p, (p + 1) % phases) for p in range(phases)])
        if pool_chunk is not None:
            pooled[pool_chunk] = out.pop(0)
        return token

    for step in range(slots):
        if step % 2 == 0 and step < chunks - 2:
            waiting.append(lower(waiting[-1]))
        with jax.named_scope("project"):
            token = project(step, token)
        if step > 0:
            with jax.named_scope("update"):
                token = update(step - 1, token)
        with jax.named_scope("attend"):
            token = attend(step, token)

    with jax.named_scope("deliver"):
        final = [homewards(value, k) for k, value in enumerate(finish(slots - 1, token))]
        (result,) = call(
            deliver_kernel,
            [jax.ShapeDtypeStruct((16, cols_here), BF16)],
            (pos, *final),
            [smem_spec()] + [vmem_spec()] * 4,
        )
    return result.reshape(1, 2, 8, cols_here)


def solution(mesh):
    in_specs = (
        P("dp", "phase", None, "mp"),
        P(None, "phase", None),
        P("dp", None, None),
        P("dp", "phase", None, None),
        P("phase", None),
        P("phase", "dp", "mp"),
        P("phase", "dp", "mp"),
        P("phase", "dp", "mp"),
        P("phase", "dp", "mp"),
    )
    out_specs = P("dp", "phase", None, "mp")
    square = mesh.shape["dp"] == CHIPS and mesh.shape["mp"] == 2 and mesh.shape["phase"] == 4
    shards = chip_shards if square else general_shards
    return jax.shard_map(shards, mesh=mesh, in_specs=in_specs, out_specs=out_specs, check_vma=False)
```

```python
import functools

import jax
import jax.numpy as jnp
from jax import lax
from jax.experimental import pallas as pl
from jax.experimental.pallas import tpu as pltpu
from jax.sharding import PartitionSpec as P

D = 8192
HD = 128
QH = 32
KVH = 4
SEGS = 6
PH = 3


NORM_EPS = 1e-05


def from_behind(value, axis, steps):
    count = lax.axis_size(axis)
    initial, last = (max(0, -steps), min(count, count - steps))
    return lax.ppermute(value, axis, [(source, source + steps) for source in range(initial, last)])


def broadcast(value, axis, root):
    mine = lax.axis_index(axis) == root
    return lax.psum(jnp.where(mine, value, jnp.zeros_like(value)), axis)


def bucket_ranks(labels, buckets):
    hits_table = (labels[..., None] == jnp.arange(buckets, dtype=jnp.int32)).astype(jnp.int32)
    earlier = jnp.cumsum(hits_table, axis=-2) - hits_table
    return jnp.sum(earlier * hits_table, axis=-1)


def attend_heads(query, key_sel, value_sel, segments):
    head_dim = query.shape[2]
    scores = jnp.einsum("qhd,khd->hqk", query, key_sel, preferred_element_type=jnp.float32)
    scores = scores * head_dim ** (-0.5)
    places = jnp.arange(query.shape[0], dtype=jnp.int32)
    allowed = (segments[:, None] == segments[None, :]) & (places[None, :] <= places[:, None])
    scores = jnp.where(allowed[None, :, :], scores, -jnp.inf)
    row_top = jnp.max(scores, axis=2, keepdims=True)
    weights = jnp.exp(scores - row_top)
    probabilities = (weights / jnp.sum(weights, axis=2, keepdims=True)).astype(jnp.bfloat16)
    mixed = jnp.einsum("hqk,khd->qhd", probabilities, value_sel, preferred_element_type=jnp.float32)
    return mixed.astype(jnp.bfloat16).reshape(query.shape[0], -1)


def general_shards(prompt_rows, row_dest, segment_ids, owner, gain, w_query, w_key, w_value, w_out):
    dp_count = lax.axis_size("dp")
    phase_count = lax.axis_size("phase")
    group_here = lax.axis_index("dp")
    phase_here = lax.axis_index("phase")
    part_here = lax.axis_index("mp")
    halves_here = prompt_rows.shape[1]
    half_rows = prompt_rows.shape[2]
    feature_cols = prompt_rows.shape[3]
    batch_rows = halves_here * half_rows
    capacity = half_rows // min(dp_count, 4)
    half_index = jnp.arange(halves_here, dtype=jnp.int32)[:, None]
    dest_group = row_dest // half_rows
    dest_ranks = bucket_ranks(dest_group, dp_count)
    own_groups = lax.dynamic_index_in_dim(dest_group, group_here, 0, keepdims=False)
    own_ranks = lax.dynamic_index_in_dim(dest_ranks, group_here, 0, keepdims=False)
    send_at = own_groups * capacity + own_ranks
    outgoing = (
        jnp.zeros((halves_here, dp_count * capacity, feature_cols), jnp.bfloat16)
        .at[half_index, send_at]
        .set(prompt_rows[0])
    )
    incoming = lax.all_to_all(
        outgoing.reshape(halves_here, dp_count, capacity, feature_cols),
        "dp",
        split_axis=1,
        concat_axis=1,
        tiled=True,
    )
    source_ids = jnp.arange(dp_count, dtype=jnp.int32)[:, None, None]
    where_from = jnp.transpose(source_ids * capacity + dest_ranks, (1, 0, 2)).reshape(
        halves_here, -1
    )
    target = jnp.where(dest_group == group_here, row_dest % half_rows, half_rows)
    target = jnp.transpose(target, (1, 0, 2)).reshape(halves_here, -1)
    arrived = incoming.reshape(halves_here, dp_count * capacity, feature_cols)[
        half_index, where_from
    ]
    own_halves = (
        jnp.zeros((halves_here, half_rows, feature_cols), jnp.bfloat16)
        .at[half_index, target]
        .set(arrived, mode="drop")
    )
    own_batch = own_halves.reshape(batch_rows, feature_cols)
    waiting = lax.all_gather(own_batch, "phase", axis=0, tiled=True).reshape(
        phase_count, batch_rows, feature_cols
    )
    query_rows, key_rows, value_rows, back_rows = (
        lax.all_gather(w_query[0], "dp", axis=0, tiled=True),
        lax.all_gather(w_key[0], "dp", axis=0, tiled=True),
        lax.all_gather(w_value[0], "dp", axis=0, tiled=True),
        lax.all_gather(w_out[0], "dp", axis=0, tiled=True),
    )
    query_cols = query_rows.shape[1]
    pair_cols = key_rows.shape[1]
    w_proj = jnp.concatenate([query_rows, key_rows, value_rows], axis=1)
    proj_cols = w_proj.shape[1]
    heads_here = query_cols // HD
    group_size = QH // KVH
    key_heads = (part_here * heads_here + jnp.arange(heads_here, dtype=jnp.int32)) // group_size
    gain_row = gain[0]
    segment_table = segment_ids[0]
    last_phase = phase_count - 1
    prompt_numbers = jnp.arange(SEGS, dtype=jnp.int32)

    def advance(tick_index, loop_state):
        current, pooled = loop_state
        batch_index = tick_index - phase_here
        active = (batch_index >= 0) & (batch_index < phase_count)
        batch_slot = jnp.clip(batch_index, 0, phase_count - 1)
        fresh_rows = lax.dynamic_index_in_dim(
            waiting, jnp.clip(tick_index, 0, phase_count - 1), 0, keepdims=False
        )
        tok_rows = jnp.where(phase_here == 0, fresh_rows, current)
        tok_segments = lax.dynamic_index_in_dim(segment_table, batch_slot, 0, keepdims=False)
        tok_float = tok_rows.astype(jnp.float32)
        whole_rows = lax.all_gather(tok_rows, "mp", axis=1, tiled=True)
        whole_float = whole_rows.astype(jnp.float32)
        squares = jnp.sum(whole_float * whole_float, axis=1)
        projected = lax.cond(
            active,
            lambda: jnp.dot(
                (whole_float * gain_row[None, :]).astype(jnp.bfloat16),
                w_proj,
                preferred_element_type=jnp.float32,
            ),
            lambda: jnp.zeros((batch_rows, proj_cols), jnp.float32),
        )
        qkv_rows = (projected * lax.rsqrt(squares / D + NORM_EPS)[:, None]).astype(jnp.bfloat16)
        query = qkv_rows[:, :query_cols].reshape(batch_rows, heads_here, HD)
        key_own = qkv_rows[:, query_cols : query_cols + pair_cols]
        value_own = qkv_rows[:, query_cols + pair_cols :]
        key_all, value_all = (
            lax.all_gather(key_own, "mp", axis=1, tiled=True),
            lax.all_gather(value_own, "mp", axis=1, tiled=True),
        )
        key_sel = jnp.take(key_all.reshape(batch_rows, KVH, HD), key_heads, axis=1)
        value_sel = jnp.take(value_all.reshape(batch_rows, KVH, HD), key_heads, axis=1)
        mixed_own = attend_heads(query, key_sel, value_sel, tok_segments)
        mixed = lax.all_gather(mixed_own, "mp", axis=1, tiled=True)
        updated = lax.cond(
            active,
            lambda: (
                tok_float + jnp.dot(mixed, back_rows, preferred_element_type=jnp.float32)
            ).astype(jnp.bfloat16),
            lambda: tok_rows,
        )
        segment_hits = tok_segments[None, :] == prompt_numbers[:, None]
        segment_sums = jnp.dot(
            segment_hits.astype(jnp.bfloat16), updated, preferred_element_type=jnp.float32
        )
        counts = jnp.sum(segment_hits.astype(jnp.float32), axis=1)
        segment_means = segment_sums / counts[:, None]
        store_here = active & (phase_here == last_phase)
        stored = lax.dynamic_index_in_dim(pooled, batch_slot, 0, keepdims=False)
        pooled = lax.dynamic_update_index_in_dim(
            pooled, jnp.where(store_here, segment_means, stored), batch_slot, 0
        )
        passed = from_behind(updated, "phase", 1)
        return (passed, pooled)

    start_state = (
        jnp.zeros((batch_rows, feature_cols), jnp.bfloat16),
        jnp.zeros((phase_count, SEGS, feature_cols), jnp.float32),
    )
    current, pooled = lax.fori_loop(0, phase_count + phase_count - 1, advance, start_state)
    shared = broadcast(pooled.astype(jnp.bfloat16), "phase", last_phase)
    own_prompts = lax.dynamic_index_in_dim(shared, phase_here, 0, keepdims=False).reshape(
        halves_here, PH, feature_cols
    )
    owner_ids = owner[0, :, :, 0]
    return_cap = max(2, PH // min(dp_count, 4))
    send_slots = owner_ids * return_cap + bucket_ranks(owner_ids, dp_count)
    parcel = (
        jnp.zeros((halves_here, dp_count * return_cap, feature_cols), jnp.bfloat16)
        .at[half_index, send_slots]
        .set(own_prompts)
    )
    returned = lax.all_to_all(
        parcel.reshape(halves_here, dp_count, return_cap, feature_cols),
        "dp",
        split_axis=1,
        concat_axis=1,
        tiled=True,
    )
    return returned.reshape(1, halves_here, dp_count * return_cap, feature_cols)


LAG = 2
CHIPS = 4
GROUP_Q = QH // KVH
Q_COLS = GROUP_Q * HD
KV_AT = Q_COLS + 2 * HD
MSG_COLS = KV_AT + 128
RANKS = 8
ORDER = (3, 1, 2, 0)
TABLE_ROW = 6
F32 = jnp.float32
BF16 = jnp.bfloat16


def vmem_spec():
    return pl.BlockSpec(memory_space=pltpu.VMEM)


def smem_spec():
    return pl.BlockSpec(memory_space=pltpu.SMEM)


def hbm_spec():
    return pl.BlockSpec(memory_space=pl.ANY)


def call(kernel, outs, args, specs, scratch=(), limit=6, token=None, after=(), span=None):
    count = len(args)
    others = len(after)

    def body(*refs):
        first = count + 1 + others
        at = first + len(outs)
        refs[at][...] = jnp.zeros(refs[at].shape, F32)

        def run():
            kernel(*refs[:count], *refs[first:at], *refs[at + 1 :])

        if span is None:
            run()
        else:
            slot, chunks = span
            chunk = slot - LAG * refs[0][1]
            pl.when((chunk >= 0) & (chunk < chunks))(run)

    outs = list(outs)
    if token is not None:
        outs_all = outs + [jax.ShapeDtypeStruct((8, 128), F32)]
        args, specs = ((*args, token, *after), [*specs] + [hbm_spec()] * (1 + others))
    else:
        outs_all = outs
    return pl.pallas_call(
        kernel if token is None else body,
        out_shape=outs_all,
        in_specs=specs,
        out_specs=[vmem_spec()] * len(outs_all),
        scratch_shapes=list(scratch),
        compiler_params=pltpu.CompilerParams(vmem_limit_bytes=limit * 1024 * 1024),
    )(*args)


def dot(a, b):
    return jnp.dot(a, b, preferred_element_type=F32)


def lane(start, size):
    return pl.ds(pl.multiple_of(start, size), size)


def iota(rows, cols, axis):
    return lax.broadcasted_iota(jnp.int32, (rows, cols), axis)


def as_column(row):
    count = row.shape[1]
    diagonal = iota(count, count, 0) == iota(count, count, 1)
    return jnp.sum(jnp.where(diagonal, row, 0), axis=1, keepdims=True)


def marks(hits):
    return hits.astype(F32).astype(BF16)


def pack_kernel(pos_ref, rows_ref, dest_ref, table_ref, *out_refs):
    chip = pos_ref[0]
    dest = dest_ref[pl.ds(chip, 1), :]
    count = dest.shape[1]
    half = count // 2
    group_row = dest // half
    group_col = as_column(group_row)
    source, here = (iota(count, count, 0), iota(count, count, 1))
    before = (group_col == group_row) & (source // half == here // half) & (source < here)
    rank = jnp.sum(jnp.where(before, 1, 0), axis=0, keepdims=True)
    target = group_row * (2 * RANKS) + (iota(1, count, 1) // half) * RANKS + rank
    width = out_refs[0].shape[1]
    message_row = iota(4 * RANKS, width, 0)
    for k in range(CHIPS):
        turn = chip ^ k
        core, block = (turn >> 1, turn & 1)
        pick = marks(iota(4 * RANKS, count, 0) + core * (4 * RANKS) == target)
        rows = dot(pick, rows_ref[:, lane(block * width, width)])
        rows = jnp.where(message_row == TABLE_ROW, table_ref[...], rows)
        out_refs[k][...] = rows.astype(BF16)


def unpack_kernel(pos_ref, m0, m1, m2, m3, dest_ref, out_ref, table_ref):
    chip, core = (pos_ref[0], pos_ref[2])
    count = dest_ref.shape[1]
    half = count // 2
    turn = 2 * core + (chip & 1)
    total = jnp.zeros(out_ref.shape, F32)
    table = jnp.zeros(table_ref.shape, F32)
    above, across = (iota(count, count, 0), iota(count, count, 1))
    for k, ref in zip(ORDER, (m0, m1, m2, m3)):
        loader = turn ^ k
        dest_row = dest_ref[pl.ds(loader, 1), :]
        group_row = dest_row // half
        group_col = as_column(group_row)
        earlier = (group_col == group_row) & (above // half == across // half) & (across < above)
        rank = jnp.sum(jnp.where(earlier, 1, 0), axis=1, keepdims=True)
        at = (group_col - 2 * core) * (2 * RANKS) + (iota(count, 1, 0) // half) * RANKS + rank
        from_message = marks(iota(count, 4 * RANKS, 1) == at)
        slot = (group_row - 2 * core) * count + (iota(1, count, 1) // half) * half + dest_row % half
        to_slot = marks(iota(2 * count, count, 0) == slot)
        rows = ref[...]
        total += dot(dot(to_slot, from_message).astype(BF16), rows)
        mine = (loader >> 1) == core
        table += jnp.where(mine, rows[TABLE_ROW : TABLE_ROW + 1].astype(F32), 0.0)
    out_ref[...] = total.astype(BF16)
    table_ref[...] = table


def added(messages):
    total = messages[0][...].astype(F32)
    for ref in messages[1:]:
        total += ref[...].astype(F32)
    return total


def stage_kernel(*refs):
    *refs, sems = refs
    count = len(refs) // 2
    copies = [pltpu.make_async_copy(refs[i], refs[count + i], sems.at[i]) for i in range(count)]
    for copy in copies:
        copy.start()
    for copy in copies:
        copy.wait()


def pick_rows(slot, pos_ref, wait_ref, recv_ref):
    if wait_ref is None:
        return recv_ref[...]
    count = wait_ref.shape[0] // 2
    at = (slot % 2) * count
    waiting = wait_ref[at : at + count]
    if recv_ref is None:
        return waiting
    return jnp.where(pos_ref[1] == 0, waiting, recv_ref[...])


def project_kernel(slot, has_wait, has_recv, pos_ref, *refs):
    refs = list(refs)
    wait_ref = refs.pop(0) if has_wait else None
    recv_ref = refs.pop(0) if has_recv else None
    gain_ref, *refs = refs
    sources, out_refs, results_ref = (refs[:6], refs[6:10], refs[10])
    chip, core = (pos_ref[0], pos_ref[2])
    rows = pick_rows(slot, pos_ref, wait_ref, recv_ref).astype(F32)
    depth = rows.shape[1]
    gated = (rows * gain_ref[:, lane(chip * depth, depth)]).astype(BF16)
    squares = jnp.sum(rows * rows, axis=1, keepdims=True)
    high = squares.astype(BF16).astype(F32)
    tail = jnp.where(iota(rows.shape[0], 128, 1) < 64, high, squares - high).astype(BF16)

    for at, source in enumerate(sources):
        part, i = (core if at < 3 else 1 - core, at % 3)
        places = [(2 * part + j) ^ pos_ref[0] for j in range(2)]
        step = min(source.shape[2], 1024)
        for start in range(0, source.shape[2], step):
            result = dot(gated, source[0, :, start : start + step]).astype(BF16)
            if i == 0:
                inside = start % Q_COLS
                results_ref[places[start // Q_COLS], :, inside : inside + step] = result
            else:
                inside = Q_COLS + (i - 1) * HD
                for j in range(2):
                    results_ref[places[j], :, inside : inside + HD] = result[:, j * HD : (j + 1) * HD]
    for k, out_ref in enumerate(out_refs):
        out_ref[:, :KV_AT] = results_ref[k]
        out_ref[:, KV_AT:] = tail


def means(table_ref, chunk, count, rows):
    segment = table_ref[:, chunk * 128 : chunk * 128 + count].astype(jnp.int32)
    hits = (segment == iota(16, count, 0)) & (iota(16, count, 0) < SEGS)
    counts = jnp.sum(jnp.where(hits, 1.0, 0.0), axis=1, keepdims=True)
    return dot(marks(hits), rows) / jnp.maximum(counts, 1.0)


def attend_kernel(features, slot, chunks, pool_chunk, pos_ref, *refs):
    messages, (table_ref, own_ref, other_ref) = (refs[:CHIPS], refs[CHIPS : CHIPS + 3])
    out_refs, results_ref = (refs[CHIPS + 3 : -1], refs[-1])
    core = pos_ref[2]
    sums = added(messages)
    count = sums.shape[0]
    tail = sums[:, KV_AT:]
    squares = tail[:, 0:1] + tail[:, 64:65]
    scaled = (sums[:, :KV_AT] * lax.rsqrt(squares / features + NORM_EPS)).astype(BF16)
    query = jnp.concatenate([scaled[:, h * HD : (h + 1) * HD] for h in range(GROUP_Q)], axis=0)
    key = scaled[:, Q_COLS : Q_COLS + HD]
    value = scaled[:, Q_COLS + HD :]
    scores = lax.dot_general(query, key, (((1,), (1,)), ((), ())), preferred_element_type=F32)
    scores = (scores * HD ** (-0.5)).reshape(GROUP_Q, count, count)
    chunk = jnp.clip(slot - LAG * pos_ref[1], 0, chunks - 1)
    segment = table_ref[:, lane(chunk * 128, 128)][:, :count].astype(jnp.int32)
    allowed = (as_column(segment) == segment) & (iota(count, count, 1) <= iota(count, count, 0))
    scores = jnp.where(allowed[None], scores, -jnp.inf)
    top = jnp.max(scores, axis=2, keepdims=True)
    weights = jnp.exp(scores - top)
    probs = (weights / jnp.sum(weights, axis=2, keepdims=True)).astype(BF16)
    mixed = dot(probs.reshape(GROUP_Q * count, count), value).astype(BF16)
    mixed = jnp.concatenate([mixed[h * count : (h + 1) * count] for h in range(GROUP_Q)], axis=1)
    if pool_chunk is not None:
        mixed = means(table_ref, pool_chunk, count, mixed).astype(BF16)
    step = own_ref.shape[2] // 4
    for part, source in ((core, own_ref), (1 - core, other_ref)):
        places = [(2 * part + j) ^ pos_ref[0] for j in range(2)]
        for at in range(4):
            result = dot(mixed, source[0, :, at * step : (at + 1) * step]).astype(BF16)
            results_ref[places[at // 2], :, (at % 2) * step : (at % 2 + 1) * step] = result
    for k, out_ref in enumerate(out_refs):
        out_ref[...] = results_ref[k]


def update_kernel(slot, has_wait, has_recv, send, pool_chunk, pooled_sums, pos_ref, *refs):
    refs = list(refs)
    wait_ref = refs.pop(0) if has_wait else None
    recv_ref = refs.pop(0) if has_recv else None
    messages, refs = (refs[:CHIPS], refs[CHIPS:])
    table_ref = refs.pop(0)
    before_ref = refs.pop(0) if pool_chunk is not None and pool_chunk % 2 else None
    rows = pick_rows(slot, pos_ref, wait_ref, recv_ref)
    if pooled_sums:
        total = means(table_ref, pool_chunk, rows.shape[0], rows)
    else:
        total = rows.astype(F32)
    total += added(messages)
    hidden = total.astype(BF16)
    if send:
        refs.pop(0)[...] = hidden
    if pool_chunk is not None:
        pooled = hidden if pooled_sums else means(table_ref, pool_chunk, rows.shape[0], hidden).astype(BF16)
        if before_ref is None:
            refs.pop(0)[...] = pooled
        else:
            out_ref = refs.pop(0)
            out_ref[0] = before_ref[...]
            out_ref[1] = pooled


def parcels(owner_at, pos_ref, rows, table_ref, out_refs):
    chip, core = (pos_ref[0], pos_ref[2])
    count = rows.shape[0]
    own_row = table_ref[:, owner_at : owner_at + count].astype(jnp.int32) - 1
    own_col = as_column(own_row)
    above, across = (iota(count, count, 0), iota(count, count, 1))
    same = (above // 16 == across // 16) & ((above % 16 >= PH) == (across % 16 >= PH))
    earlier = (own_col == own_row) & same & (above < across)
    rank = jnp.sum(jnp.where(earlier, 1, 0), axis=0, keepdims=True)
    place = iota(1, count, 1)
    half = jnp.where(place % 16 >= PH, 1, 0)
    slot = half * 8 + (2 * core + place // 16) * 2 + rank
    turn = 2 * core + (chip & 1)
    for k, out_ref in enumerate(out_refs):
        pick = marks((iota(16, count, 0) == slot) & (own_row == (turn ^ k)))
        out_ref[...] = dot(pick, rows).astype(BF16)


def finish_kernel(last, chunk, owner_at, pos_ref, recv_ref, m0, m1, m2, m3, table_ref, before_ref, *refs):
    *refs, pooled_ref = refs
    shares, out_refs = (refs[:-CHIPS], refs[-CHIPS:])
    count = before_ref.shape[0]
    phase = pos_ref[1]

    @pl.when(phase == last)
    def _():
        rows = recv_ref[...]
        total = means(table_ref, chunk, rows.shape[0], rows) + added((m0, m1, m2, m3))
        pooled_ref[:count] = before_ref[...]
        pooled_ref[count:] = total.astype(BF16)

    for m, ref in enumerate(shares):

        @pl.when(phase == m)
        def _(ref=ref):
            pooled_ref[:count] = ref[0]
            pooled_ref[count:] = ref[1]

    parcels(owner_at, pos_ref, pooled_ref[...], table_ref, out_refs)


def deliver_kernel(pos_ref, m0, m1, m2, m3, out_ref):
    chip = pos_ref[0]
    width = m0.shape[1]
    out_ref[...] = jnp.zeros_like(out_ref)
    for k, ref in zip(ORDER, (m0, m1, m2, m3)):
        cols = lane(((chip ^ k) & 1) * width, width)
        out_ref[:, cols] = out_ref[:, cols] + ref[...]


def chip_shards(prompt_rows, row_dest, segment_ids, owner, gain, w_query, w_key, w_value, w_out):
    chip, phase, core = (lax.axis_index("dp"), lax.axis_index("phase"), lax.axis_index("mp"))
    phases = lax.axis_size("phase")
    pos = jnp.stack([chip, phase, core]).astype(jnp.int32)
    halves, half_rows, cols_here = prompt_rows.shape[1:]
    batch = halves * half_rows
    features = 2 * cols_here
    block = features // CHIPS
    count = batch
    square = [(e, k) for e in range(CHIPS) for k in range(2)]

    def crosswise(value, k):
        pairs = [(2 * e + m, 2 * (2 * m + ((e ^ k) & 1)) + ((e ^ k) >> 1)) for e, m in square]
        return lax.ppermute(value, ("dp", "mp"), pairs)

    def homewards(value, k):
        pairs = [(2 * e + c, 2 * ((2 * c + (e & 1)) ^ k) + (e >> 1)) for e, c in square]
        return lax.ppermute(value, ("dp", "mp"), pairs)

    def exchange(values):
        got = [values[0]]
        for k in (3, 1, 2):
            got.append(lax.ppermute(values[k], "dp", [(e, e ^ k) for e in range(CHIPS)]))
        return got

    def lower(value):
        return lax.ppermute(value, "phase", [(p, p - 1) for p in range(1, phases)])

    def swap(value):
        return lax.ppermute(value, "mp", [(0, 1), (1, 0)])

    with jax.named_scope("packing"):
        parity = chip % 2
        chunks = 2 * phases
        owner_at = chunks * 128
        table = jnp.zeros((phases, 2, 128), F32)
        numbers = segment_ids[0][:, None, :].astype(F32)
        table = lax.dynamic_update_slice(table, numbers, (0, parity, 0)).reshape(1, -1)
        owners = (owner.reshape(1, -1) + 1).astype(F32)
        last = lax.dynamic_update_slice(jnp.zeros((1, block - owner_at), F32), owners, (0, 16 * parity))
        table = jnp.concatenate([table, last], axis=1)
        dest = row_dest.reshape(CHIPS, batch)
        own = (w_query, w_key, w_value, w_out)
        sources, *_ = lax.optimization_barrier((own, pos, table, dest))
        *own, token = call(
            stage_kernel,
            [pltpu.VMEM(w.shape, BF16) for w in own],
            [pltpu.with_memory_space_constraint(w, pltpu.HBM) for w in own],
            [hbm_spec()] * 4,
            (pltpu.SemaphoreType.DMA((4,)),),
            token=jnp.zeros((8, 128), F32),
        )
        *packed, token = call(
            pack_kernel,
            [jax.ShapeDtypeStruct((4 * RANKS, block), BF16)] * CHIPS,
            (pos, prompt_rows.reshape(batch, cols_here), dest, table),
            [smem_spec()] + [vmem_spec()] * 3,
            token=token,
        )
        arrived = [crosswise(packed[k], k) for k in ORDER]
        start, table, token = call(
            unpack_kernel,
            [jax.ShapeDtypeStruct((2 * batch, block), BF16), jax.ShapeDtypeStruct((1, block), F32)],
            (pos, *arrived, dest),
            [smem_spec()] + [vmem_spec()] * 5,
            token=token,
        )
        waiting = [start]

    with jax.named_scope("weights"):

        def held(values):
            return [pltpu.with_memory_space_constraint(value, pltpu.VMEM) for value in values]

        other = [swap(w) for w in sources[:3]]
        w_in = held([*own[:3], *other])
        last, *_ = lax.optimization_barrier((sources[3], start, *other))
        w_back = held([own[3], swap(last)])

    hops, pooled, got, shares = ({}, {}, {}, {})
    slots = chunks + LAG * (phases - 1)

    def plan(slot):
        chunk = slot - LAG * (phases - 1)
        send = slot < chunks + LAG * (phases - 2)
        pool_chunk = chunk if chunk >= 0 else None
        return (send, pool_chunk, pool_chunk is not None and not send)

    def entering(slot):
        inputs = waiting[slot // 2 : slot // 2 + 1] + [hops[at] for at in (slot - LAG,) if at >= 0]
        return (slot < chunks, slot >= LAG, inputs, [smem_spec()] + [vmem_spec()] * len(inputs))

    def project(slot, token):
        has_wait, has_recv, inputs, specs = entering(slot)
        *sent, token = call(
            functools.partial(project_kernel, slot, has_wait, has_recv),
            [jax.ShapeDtypeStruct((count, MSG_COLS), BF16)] * CHIPS,
            (pos, *inputs, gain, *w_in),
            specs + [vmem_spec()] * 7,
            (pltpu.VMEM((CHIPS, count, KV_AT), BF16),),
            10,
            token,
            (),
            (slot, chunks),
        )
        got[slot] = exchange(sent)
        return token

    def attend(slot, token):
        _, pool_chunk, early_pool = plan(slot)
        rows = 16 if early_pool else count
        if slot == slots - 1:
            for m in range(phases - 1):
                shares[m] = lax.ppermute(pooled[2 * m + 1], "phase", [(phases - 1, m)])
        *sent, token = call(
            functools.partial(attend_kernel, features, slot, chunks, pool_chunk if early_pool else None),
            [jax.ShapeDtypeStruct((rows, block), BF16)] * CHIPS,
            (pos, *got[slot], table, *w_back),
            [smem_spec()] + [vmem_spec()] * (CHIPS + 3),
            (pltpu.VMEM((CHIPS, rows, block), BF16),),
            10,
            token,
            list(shares.values()) + (waiting[phases - 1 :] if slot == 2 else []),
            (slot, chunks),
        )
        got[slot] = exchange(sent)
        return token

    def finish(slot, token):
        chunk = chunks - 1
        *sent, token = call(
            functools.partial(finish_kernel, phases - 1, chunk, owner_at),
            [jax.ShapeDtypeStruct((16, block), BF16)] * CHIPS,
            (pos, hops[slot - LAG], *got[slot], table, pooled[chunk - 1], *shares.values()),
            [smem_spec()] + [vmem_spec()] * (CHIPS + 3 + len(shares)),
            (pltpu.VMEM((32, block), BF16),),
            token=token,
        )
        return sent

    def update(slot, token):
        has_wait, has_recv, inputs, specs = entering(slot)
        send, pool_chunk, early_pool = plan(slot)
        outs = [jax.ShapeDtypeStruct((count, block), BF16)] * send
        before = []
        if pool_chunk is not None:
            odd = pool_chunk % 2 == 1
            outs.append(jax.ShapeDtypeStruct((2, 16, block) if odd else (16, block), BF16))
            before = [pooled[pool_chunk - 1]] if odd else []
        *out, token = call(
            functools.partial(update_kernel, slot, has_wait, has_recv, send, pool_chunk, early_pool),
            outs,
            (pos, *inputs, *got[slot], table, *before),
            specs + [vmem_spec()] * (CHIPS + 1 + len(before)),
            token=token,
            span=(slot, chunks),
        )
        if send:
            hops[slot] = lax.ppermute(out.pop(0), "phase", [(p, p + 1) for p in range(phases - 1)])
        if pool_chunk is not None:
            pooled[pool_chunk] = out.pop(0)
        return token

    def move_down(token):
        above, _ = lax.optimization_barrier((waiting[-1], token))
        waiting.append(lower(above))

    waiting.append(lower(start))
    for step in range(slots):
        with jax.named_scope("project"):
            token = project(step, token)
        if step > 0:
            with jax.named_scope("update"):
                token = update(step - 1, token)
        if step == 1:
            move_down(token)
        with jax.named_scope("attend"):
            token = attend(step, token)
        if step == 0:
            move_down(token)

    with jax.named_scope("deliver"):
        values = finish(slots - 1, token)
        final = [homewards(values[k], k) for k in ORDER]
        (result,) = call(
            deliver_kernel,
            [jax.ShapeDtypeStruct((16, cols_here), BF16)],
            (pos, *final),
            [smem_spec()] + [vmem_spec()] * 4,
        )
    return result.reshape(1, 2, 8, cols_here)


def solution(mesh):
    in_specs = (
        P("dp", "phase", None, "mp"),
        P(None, "phase", None),
        P("dp", None, None),
        P("dp", "phase", None, None),
        P("phase", None),
        P("phase", "dp", "mp"),
        P("phase", "dp", "mp"),
        P("phase", "dp", "mp"),
        P("phase", "dp", "mp"),
    )
    out_specs = P("dp", "phase", None, "mp")
    square = mesh.shape["dp"] == CHIPS and mesh.shape["mp"] == 2 and mesh.shape["phase"] == 4
    shards = chip_shards if square else general_shards
    return jax.shard_map(shards, mesh=mesh, in_specs=in_specs, out_specs=out_specs, check_vma=False)
```

```python
import functools

import jax
import jax.numpy as jnp
from jax import lax
from jax.experimental import pallas as pl
from jax.experimental.pallas import tpu as pltpu
from jax.sharding import PartitionSpec as P

D = 8192
HD = 128
QH = 32
KVH = 4
SEGS = 6
PH = 3


NORM_EPS = 1e-05


def from_behind(value, axis, steps):
    count = lax.axis_size(axis)
    initial, last = (max(0, -steps), min(count, count - steps))
    return lax.ppermute(value, axis, [(source, source + steps) for source in range(initial, last)])


def broadcast(value, axis, root):
    mine = lax.axis_index(axis) == root
    return lax.psum(jnp.where(mine, value, jnp.zeros_like(value)), axis)


def bucket_ranks(labels, buckets):
    hits_table = (labels[..., None] == jnp.arange(buckets, dtype=jnp.int32)).astype(jnp.int32)
    earlier = jnp.cumsum(hits_table, axis=-2) - hits_table
    return jnp.sum(earlier * hits_table, axis=-1)


def attend_heads(query, key_sel, value_sel, segments):
    head_dim = query.shape[2]
    scores = jnp.einsum("qhd,khd->hqk", query, key_sel, preferred_element_type=jnp.float32)
    scores = scores * head_dim ** (-0.5)
    places = jnp.arange(query.shape[0], dtype=jnp.int32)
    allowed = (segments[:, None] == segments[None, :]) & (places[None, :] <= places[:, None])
    scores = jnp.where(allowed[None, :, :], scores, -jnp.inf)
    row_top = jnp.max(scores, axis=2, keepdims=True)
    weights = jnp.exp(scores - row_top)
    probabilities = (weights / jnp.sum(weights, axis=2, keepdims=True)).astype(jnp.bfloat16)
    mixed = jnp.einsum("hqk,khd->qhd", probabilities, value_sel, preferred_element_type=jnp.float32)
    return mixed.astype(jnp.bfloat16).reshape(query.shape[0], -1)


def general_shards(prompt_rows, row_dest, segment_ids, owner, gain, w_query, w_key, w_value, w_out):
    dp_count = lax.axis_size("dp")
    phase_count = lax.axis_size("phase")
    group_here = lax.axis_index("dp")
    phase_here = lax.axis_index("phase")
    part_here = lax.axis_index("mp")
    halves_here = prompt_rows.shape[1]
    half_rows = prompt_rows.shape[2]
    feature_cols = prompt_rows.shape[3]
    batch_rows = halves_here * half_rows
    capacity = half_rows // min(dp_count, 4)
    half_index = jnp.arange(halves_here, dtype=jnp.int32)[:, None]
    dest_group = row_dest // half_rows
    dest_ranks = bucket_ranks(dest_group, dp_count)
    own_groups = lax.dynamic_index_in_dim(dest_group, group_here, 0, keepdims=False)
    own_ranks = lax.dynamic_index_in_dim(dest_ranks, group_here, 0, keepdims=False)
    send_at = own_groups * capacity + own_ranks
    outgoing = (
        jnp.zeros((halves_here, dp_count * capacity, feature_cols), jnp.bfloat16)
        .at[half_index, send_at]
        .set(prompt_rows[0])
    )
    incoming = lax.all_to_all(
        outgoing.reshape(halves_here, dp_count, capacity, feature_cols),
        "dp",
        split_axis=1,
        concat_axis=1,
        tiled=True,
    )
    source_ids = jnp.arange(dp_count, dtype=jnp.int32)[:, None, None]
    where_from = jnp.transpose(source_ids * capacity + dest_ranks, (1, 0, 2)).reshape(
        halves_here, -1
    )
    target = jnp.where(dest_group == group_here, row_dest % half_rows, half_rows)
    target = jnp.transpose(target, (1, 0, 2)).reshape(halves_here, -1)
    arrived = incoming.reshape(halves_here, dp_count * capacity, feature_cols)[
        half_index, where_from
    ]
    own_halves = (
        jnp.zeros((halves_here, half_rows, feature_cols), jnp.bfloat16)
        .at[half_index, target]
        .set(arrived, mode="drop")
    )
    own_batch = own_halves.reshape(batch_rows, feature_cols)
    waiting = lax.all_gather(own_batch, "phase", axis=0, tiled=True).reshape(
        phase_count, batch_rows, feature_cols
    )
    query_rows, key_rows, value_rows, back_rows = (
        lax.all_gather(w_query[0], "dp", axis=0, tiled=True),
        lax.all_gather(w_key[0], "dp", axis=0, tiled=True),
        lax.all_gather(w_value[0], "dp", axis=0, tiled=True),
        lax.all_gather(w_out[0], "dp", axis=0, tiled=True),
    )
    query_cols = query_rows.shape[1]
    pair_cols = key_rows.shape[1]
    w_proj = jnp.concatenate([query_rows, key_rows, value_rows], axis=1)
    proj_cols = w_proj.shape[1]
    heads_here = query_cols // HD
    group_size = QH // KVH
    key_heads = (part_here * heads_here + jnp.arange(heads_here, dtype=jnp.int32)) // group_size
    gain_row = gain[0]
    segment_table = segment_ids[0]
    last_phase = phase_count - 1
    prompt_numbers = jnp.arange(SEGS, dtype=jnp.int32)

    def advance(tick_index, loop_state):
        current, pooled = loop_state
        batch_index = tick_index - phase_here
        active = (batch_index >= 0) & (batch_index < phase_count)
        batch_slot = jnp.clip(batch_index, 0, phase_count - 1)
        fresh_rows = lax.dynamic_index_in_dim(
            waiting, jnp.clip(tick_index, 0, phase_count - 1), 0, keepdims=False
        )
        tok_rows = jnp.where(phase_here == 0, fresh_rows, current)
        tok_segments = lax.dynamic_index_in_dim(segment_table, batch_slot, 0, keepdims=False)
        tok_float = tok_rows.astype(jnp.float32)
        whole_rows = lax.all_gather(tok_rows, "mp", axis=1, tiled=True)
        whole_float = whole_rows.astype(jnp.float32)
        squares = jnp.sum(whole_float * whole_float, axis=1)
        projected = lax.cond(
            active,
            lambda: jnp.dot(
                (whole_float * gain_row[None, :]).astype(jnp.bfloat16),
                w_proj,
                preferred_element_type=jnp.float32,
            ),
            lambda: jnp.zeros((batch_rows, proj_cols), jnp.float32),
        )
        qkv_rows = (projected * lax.rsqrt(squares / D + NORM_EPS)[:, None]).astype(jnp.bfloat16)
        query = qkv_rows[:, :query_cols].reshape(batch_rows, heads_here, HD)
        key_own = qkv_rows[:, query_cols : query_cols + pair_cols]
        value_own = qkv_rows[:, query_cols + pair_cols :]
        key_all, value_all = (
            lax.all_gather(key_own, "mp", axis=1, tiled=True),
            lax.all_gather(value_own, "mp", axis=1, tiled=True),
        )
        key_sel = jnp.take(key_all.reshape(batch_rows, KVH, HD), key_heads, axis=1)
        value_sel = jnp.take(value_all.reshape(batch_rows, KVH, HD), key_heads, axis=1)
        mixed_own = attend_heads(query, key_sel, value_sel, tok_segments)
        mixed = lax.all_gather(mixed_own, "mp", axis=1, tiled=True)
        updated = lax.cond(
            active,
            lambda: (
                tok_float + jnp.dot(mixed, back_rows, preferred_element_type=jnp.float32)
            ).astype(jnp.bfloat16),
            lambda: tok_rows,
        )
        segment_hits = tok_segments[None, :] == prompt_numbers[:, None]
        segment_sums = jnp.dot(
            segment_hits.astype(jnp.bfloat16), updated, preferred_element_type=jnp.float32
        )
        counts = jnp.sum(segment_hits.astype(jnp.float32), axis=1)
        segment_means = segment_sums / counts[:, None]
        store_here = active & (phase_here == last_phase)
        stored = lax.dynamic_index_in_dim(pooled, batch_slot, 0, keepdims=False)
        pooled = lax.dynamic_update_index_in_dim(
            pooled, jnp.where(store_here, segment_means, stored), batch_slot, 0
        )
        passed = from_behind(updated, "phase", 1)
        return (passed, pooled)

    start_state = (
        jnp.zeros((batch_rows, feature_cols), jnp.bfloat16),
        jnp.zeros((phase_count, SEGS, feature_cols), jnp.float32),
    )
    current, pooled = lax.fori_loop(0, phase_count + phase_count - 1, advance, start_state)
    shared = broadcast(pooled.astype(jnp.bfloat16), "phase", last_phase)
    own_prompts = lax.dynamic_index_in_dim(shared, phase_here, 0, keepdims=False).reshape(
        halves_here, PH, feature_cols
    )
    owner_ids = owner[0, :, :, 0]
    return_cap = max(2, PH // min(dp_count, 4))
    send_slots = owner_ids * return_cap + bucket_ranks(owner_ids, dp_count)
    parcel = (
        jnp.zeros((halves_here, dp_count * return_cap, feature_cols), jnp.bfloat16)
        .at[half_index, send_slots]
        .set(own_prompts)
    )
    returned = lax.all_to_all(
        parcel.reshape(halves_here, dp_count, return_cap, feature_cols),
        "dp",
        split_axis=1,
        concat_axis=1,
        tiled=True,
    )
    return returned.reshape(1, halves_here, dp_count * return_cap, feature_cols)


LAG = 2
CHIPS = 4
GROUP_Q = QH // KVH
Q_COLS = GROUP_Q * HD
KV_AT = Q_COLS + 2 * HD
MSG_COLS = KV_AT + 128
RANKS = 8
ORDER = (3, 1, 2, 0)
TABLE_ROW = 6
F32 = jnp.float32
BF16 = jnp.bfloat16


def vmem_spec():
    return pl.BlockSpec(memory_space=pltpu.VMEM)


def smem_spec():
    return pl.BlockSpec(memory_space=pltpu.SMEM)


def hbm_spec():
    return pl.BlockSpec(memory_space=pl.ANY)


def call(kernel, outs, args, specs, scratch=(), limit=6, token=None, after=(), span=None):
    count = len(args)
    others = len(after)

    def body(*refs):
        first = count + 1 + others
        at = first + len(outs)
        refs[at][...] = jnp.zeros(refs[at].shape, F32)

        def run():
            kernel(*refs[:count], *refs[first:at], *refs[at + 1 :])

        if span is None:
            run()
        else:
            slot, chunks = span
            chunk = slot - LAG * refs[0][1]
            pl.when((chunk >= 0) & (chunk < chunks))(run)

    outs = list(outs)
    if token is not None:
        outs_all = outs + [jax.ShapeDtypeStruct((8, 128), F32)]
        args, specs = ((*args, token, *after), [*specs] + [hbm_spec()] * (1 + others))
    else:
        outs_all = outs
    return pl.pallas_call(
        kernel if token is None else body,
        out_shape=outs_all,
        in_specs=specs,
        out_specs=[vmem_spec()] * len(outs_all),
        scratch_shapes=list(scratch),
        compiler_params=pltpu.CompilerParams(vmem_limit_bytes=limit * 1024 * 1024),
    )(*args)


def dot(a, b):
    return jnp.dot(a, b, preferred_element_type=F32)


def lane(start, size):
    return pl.ds(pl.multiple_of(start, size), size)


def iota(rows, cols, axis):
    return lax.broadcasted_iota(jnp.int32, (rows, cols), axis)


def as_column(row):
    count = row.shape[1]
    diagonal = iota(count, count, 0) == iota(count, count, 1)
    return jnp.sum(jnp.where(diagonal, row, 0), axis=1, keepdims=True)


def marks(hits):
    return hits.astype(F32).astype(BF16)


def pack_kernel(pos_ref, rows_ref, dest_ref, table_ref, *out_refs):
    chip = pos_ref[0]
    dest = dest_ref[pl.ds(chip, 1), :]
    count = dest.shape[1]
    half = count // 2
    group_row = dest // half
    group_col = as_column(group_row)
    source, here = (iota(count, count, 0), iota(count, count, 1))
    before = (group_col == group_row) & (source // half == here // half) & (source < here)
    rank = jnp.sum(jnp.where(before, 1, 0), axis=0, keepdims=True)
    target = group_row * (2 * RANKS) + (iota(1, count, 1) // half) * RANKS + rank
    width = out_refs[0].shape[1]
    message_row = iota(4 * RANKS, width, 0)
    for k in range(CHIPS):
        turn = chip ^ k
        core, block = (turn >> 1, turn & 1)
        pick = marks(iota(4 * RANKS, count, 0) + core * (4 * RANKS) == target)
        rows = dot(pick, rows_ref[:, lane(block * width, width)])
        rows = jnp.where(message_row == TABLE_ROW, table_ref[...], rows)
        out_refs[k][...] = rows.astype(BF16)


def unpack_kernel(pos_ref, m0, m1, m2, m3, dest_ref, out_ref, table_ref):
    chip, core = (pos_ref[0], pos_ref[2])
    count = dest_ref.shape[1]
    half = count // 2
    turn = 2 * core + (chip & 1)
    total = jnp.zeros(out_ref.shape, F32)
    table = jnp.zeros(table_ref.shape, F32)
    above, across = (iota(count, count, 0), iota(count, count, 1))
    for k, ref in enumerate((m0, m1, m2, m3)):
        loader = turn ^ k
        dest_row = dest_ref[pl.ds(loader, 1), :]
        group_row = dest_row // half
        group_col = as_column(group_row)
        earlier = (group_col == group_row) & (above // half == across // half) & (across < above)
        rank = jnp.sum(jnp.where(earlier, 1, 0), axis=1, keepdims=True)
        at = (group_col - 2 * core) * (2 * RANKS) + (iota(count, 1, 0) // half) * RANKS + rank
        from_message = marks(iota(count, 4 * RANKS, 1) == at)
        slot = (group_row - 2 * core) * count + (iota(1, count, 1) // half) * half + dest_row % half
        to_slot = marks(iota(2 * count, count, 0) == slot)
        rows = ref[...]
        total += dot(dot(to_slot, from_message).astype(BF16), rows)
        mine = (loader >> 1) == core
        table += jnp.where(mine, rows[TABLE_ROW : TABLE_ROW + 1].astype(F32), 0.0)
    out_ref[...] = total.astype(BF16)
    table_ref[...] = table


def added(messages):
    total = messages[0][...].astype(F32)
    for ref in messages[1:]:
        total += ref[...].astype(F32)
    return total


def stage_kernel(*refs):
    *refs, sems = refs
    count = len(refs) // 2
    copies = [pltpu.make_async_copy(refs[i], refs[count + i], sems.at[i]) for i in range(count)]
    for copy in copies:
        copy.start()
    for copy in copies:
        copy.wait()


def pick_rows(slot, pos_ref, wait_ref, recv_ref):
    if wait_ref is None:
        return recv_ref[...]
    count = wait_ref.shape[0] // 2
    at = (slot % 2) * count
    waiting = wait_ref[at : at + count]
    if recv_ref is None:
        return waiting
    return jnp.where(pos_ref[1] == 0, waiting, recv_ref[...])


def project_kernel(slot, has_wait, has_recv, pos_ref, *refs):
    refs = list(refs)
    wait_ref = refs.pop(0) if has_wait else None
    recv_ref = refs.pop(0) if has_recv else None
    gain_ref, *refs = refs
    sources, out_refs, results_ref = (refs[:6], refs[6:10], refs[10])
    chip, core = (pos_ref[0], pos_ref[2])
    rows = pick_rows(slot, pos_ref, wait_ref, recv_ref).astype(F32)
    depth = rows.shape[1]
    gated = (rows * gain_ref[:, lane(chip * depth, depth)]).astype(BF16)
    squares = jnp.sum(rows * rows, axis=1, keepdims=True)
    high = squares.astype(BF16).astype(F32)
    tail = jnp.where(iota(rows.shape[0], 128, 1) < 64, high, squares - high).astype(BF16)

    for at, source in enumerate(sources):
        part, i = (core if at < 3 else 1 - core, at % 3)
        places = [(2 * part + j) ^ pos_ref[0] for j in range(2)]
        step = min(source.shape[2], 1024)
        for start in range(0, source.shape[2], step):
            result = dot(gated, source[0, :, start : start + step]).astype(BF16)
            if i == 0:
                inside = start % Q_COLS
                results_ref[places[start // Q_COLS], :, inside : inside + step] = result
            else:
                inside = Q_COLS + (i - 1) * HD
                for j in range(2):
                    results_ref[places[j], :, inside : inside + HD] = result[:, j * HD : (j + 1) * HD]
    for k, out_ref in enumerate(out_refs):
        out_ref[:, :KV_AT] = results_ref[k]
        out_ref[:, KV_AT:] = tail


def means(table_ref, chunk, count, rows):
    segment = table_ref[:, chunk * 128 : chunk * 128 + count].astype(jnp.int32)
    hits = (segment == iota(16, count, 0)) & (iota(16, count, 0) < SEGS)
    counts = jnp.sum(jnp.where(hits, 1.0, 0.0), axis=1, keepdims=True)
    return dot(marks(hits), rows) / jnp.maximum(counts, 1.0)


def attend_kernel(features, slot, chunks, pool_chunk, pos_ref, *refs):
    messages, (table_ref, own_ref, other_ref) = (refs[:CHIPS], refs[CHIPS : CHIPS + 3])
    out_refs, results_ref = (refs[CHIPS + 3 : -1], refs[-1])
    core = pos_ref[2]
    sums = added(messages)
    count = sums.shape[0]
    tail = sums[:, KV_AT:]
    squares = tail[:, 0:1] + tail[:, 64:65]
    scaled = (sums[:, :KV_AT] * lax.rsqrt(squares / features + NORM_EPS)).astype(BF16)
    query = jnp.concatenate([scaled[:, h * HD : (h + 1) * HD] for h in range(GROUP_Q)], axis=0)
    key = scaled[:, Q_COLS : Q_COLS + HD]
    value = scaled[:, Q_COLS + HD :]
    scores = lax.dot_general(query, key, (((1,), (1,)), ((), ())), preferred_element_type=F32)
    scores = (scores * HD ** (-0.5)).reshape(GROUP_Q, count, count)
    chunk = jnp.clip(slot - LAG * pos_ref[1], 0, chunks - 1)
    segment = table_ref[:, lane(chunk * 128, 128)][:, :count].astype(jnp.int32)
    allowed = (as_column(segment) == segment) & (iota(count, count, 1) <= iota(count, count, 0))
    scores = jnp.where(allowed[None], scores, -jnp.inf)
    top = jnp.max(scores, axis=2, keepdims=True)
    weights = jnp.exp(scores - top)
    probs = (weights / jnp.sum(weights, axis=2, keepdims=True)).astype(BF16)
    mixed = dot(probs.reshape(GROUP_Q * count, count), value).astype(BF16)
    mixed = jnp.concatenate([mixed[h * count : (h + 1) * count] for h in range(GROUP_Q)], axis=1)
    if pool_chunk is not None:
        mixed = means(table_ref, pool_chunk, count, mixed).astype(BF16)
    step = own_ref.shape[2] // 4
    for part, source in ((core, own_ref), (1 - core, other_ref)):
        places = [(2 * part + j) ^ pos_ref[0] for j in range(2)]
        for at in range(4):
            result = dot(mixed, source[0, :, at * step : (at + 1) * step]).astype(BF16)
            results_ref[places[at // 2], :, (at % 2) * step : (at % 2 + 1) * step] = result
    for k, out_ref in enumerate(out_refs):
        out_ref[...] = results_ref[k]


def update_kernel(slot, has_wait, has_recv, send, pool_chunk, pooled_sums, pos_ref, *refs):
    refs = list(refs)
    wait_ref = refs.pop(0) if has_wait else None
    recv_ref = refs.pop(0) if has_recv else None
    messages, refs = (refs[:CHIPS], refs[CHIPS:])
    table_ref = refs.pop(0)
    before_ref = refs.pop(0) if pool_chunk is not None and pool_chunk % 2 else None
    rows = pick_rows(slot, pos_ref, wait_ref, recv_ref)
    if pooled_sums:
        total = means(table_ref, pool_chunk, rows.shape[0], rows)
    else:
        total = rows.astype(F32)
    total += added(messages)
    hidden = total.astype(BF16)
    if send:
        refs.pop(0)[...] = hidden
    if pool_chunk is not None:
        pooled = hidden if pooled_sums else means(table_ref, pool_chunk, rows.shape[0], hidden).astype(BF16)
        if before_ref is None:
            refs.pop(0)[...] = pooled
        else:
            out_ref = refs.pop(0)
            out_ref[0] = before_ref[...]
            out_ref[1] = pooled


def parcels(owner_at, pos_ref, rows, table_ref, out_refs):
    chip, core = (pos_ref[0], pos_ref[2])
    count = rows.shape[0]
    own_row = table_ref[:, owner_at : owner_at + count].astype(jnp.int32) - 1
    own_col = as_column(own_row)
    above, across = (iota(count, count, 0), iota(count, count, 1))
    same = (above // 16 == across // 16) & ((above % 16 >= PH) == (across % 16 >= PH))
    earlier = (own_col == own_row) & same & (above < across)
    rank = jnp.sum(jnp.where(earlier, 1, 0), axis=0, keepdims=True)
    place = iota(1, count, 1)
    half = jnp.where(place % 16 >= PH, 1, 0)
    slot = half * 8 + (2 * core + place // 16) * 2 + rank
    turn = 2 * core + (chip & 1)
    for k, out_ref in enumerate(out_refs):
        pick = marks((iota(16, count, 0) == slot) & (own_row == (turn ^ k)))
        out_ref[...] = dot(pick, rows).astype(BF16)


def finish_kernel(last, chunk, owner_at, pos_ref, recv_ref, m0, m1, m2, m3, table_ref, before_ref, *refs):
    *refs, pooled_ref = refs
    shares, out_refs = (refs[:-CHIPS], refs[-CHIPS:])
    count = before_ref.shape[0]
    phase = pos_ref[1]

    @pl.when(phase == last)
    def _():
        rows = recv_ref[...]
        total = means(table_ref, chunk, rows.shape[0], rows) + added((m0, m1, m2, m3))
        pooled_ref[:count] = before_ref[...]
        pooled_ref[count:] = total.astype(BF16)

    for m, ref in enumerate(shares):

        @pl.when(phase == m)
        def _(ref=ref):
            pooled_ref[:count] = ref[0]
            pooled_ref[count:] = ref[1]

    parcels(owner_at, pos_ref, pooled_ref[...], table_ref, out_refs)


def deliver_kernel(pos_ref, m0, m1, m2, m3, out_ref):
    chip = pos_ref[0]
    width = m0.shape[1]
    out_ref[...] = jnp.zeros_like(out_ref)
    for k, ref in zip(ORDER, (m0, m1, m2, m3)):
        cols = lane(((chip ^ k) & 1) * width, width)
        out_ref[:, cols] = out_ref[:, cols] + ref[...]


def chip_shards(prompt_rows, row_dest, segment_ids, owner, gain, w_query, w_key, w_value, w_out):
    chip, phase, core = (lax.axis_index("dp"), lax.axis_index("phase"), lax.axis_index("mp"))
    phases = lax.axis_size("phase")
    pos = jnp.stack([chip, phase, core]).astype(jnp.int32)
    halves, half_rows, cols_here = prompt_rows.shape[1:]
    batch = halves * half_rows
    features = 2 * cols_here
    block = features // CHIPS
    count = batch
    square = [(e, k) for e in range(CHIPS) for k in range(2)]

    def crosswise(value, k):
        pairs = [(2 * e + m, 2 * (2 * m + ((e ^ k) & 1)) + ((e ^ k) >> 1)) for e, m in square]
        return lax.ppermute(value, ("dp", "mp"), pairs)

    def homewards(value, k):
        pairs = [(2 * e + c, 2 * ((2 * c + (e & 1)) ^ k) + (e >> 1)) for e, c in square]
        return lax.ppermute(value, ("dp", "mp"), pairs)

    def exchange(values):
        got = [values[0]]
        for k in (3, 1, 2):
            got.append(lax.ppermute(values[k], "dp", [(e, e ^ k) for e in range(CHIPS)]))
        return got

    def lower(value):
        return lax.ppermute(value, "phase", [(p, p - 1) for p in range(1, phases)])

    def swap(value):
        return lax.ppermute(value, "mp", [(0, 1), (1, 0)])

    with jax.named_scope("packing"):
        parity = chip % 2
        chunks = 2 * phases
        owner_at = chunks * 128
        table = jnp.zeros((phases, 2, 128), F32)
        numbers = segment_ids[0][:, None, :].astype(F32)
        table = lax.dynamic_update_slice(table, numbers, (0, parity, 0)).reshape(1, -1)
        owners = (owner.reshape(1, -1) + 1).astype(F32)
        last = lax.dynamic_update_slice(jnp.zeros((1, block - owner_at), F32), owners, (0, 16 * parity))
        table = jnp.concatenate([table, last], axis=1)
        dest = row_dest.reshape(CHIPS, batch)
        own = (w_query, w_key, w_value, w_out)
        sources, *_ = lax.optimization_barrier((own, pos, table, dest))
        *own, token = call(
            stage_kernel,
            [pltpu.VMEM(w.shape, BF16) for w in own],
            [pltpu.with_memory_space_constraint(w, pltpu.HBM) for w in own],
            [hbm_spec()] * 4,
            (pltpu.SemaphoreType.DMA((4,)),),
            token=jnp.zeros((8, 128), F32),
        )
        *packed, token = call(
            pack_kernel,
            [jax.ShapeDtypeStruct((4 * RANKS, block), BF16)] * CHIPS,
            (pos, prompt_rows.reshape(batch, cols_here), dest, table),
            [smem_spec()] + [vmem_spec()] * 3,
            token=token,
        )
        arrived = [crosswise(value, k) for k, value in enumerate(packed)]
        start, table, token = call(
            unpack_kernel,
            [jax.ShapeDtypeStruct((2 * batch, block), BF16), jax.ShapeDtypeStruct((1, block), F32)],
            (pos, *arrived, dest),
            [smem_spec()] + [vmem_spec()] * 5,
            token=token,
        )
        waiting = [start]

    with jax.named_scope("weights"):

        def held(values):
            return [pltpu.with_memory_space_constraint(value, pltpu.VMEM) for value in values]

        other = [swap(w) for w in sources[:3]]
        w_in = held([*own[:3], *other])
        last, *_ = lax.optimization_barrier((sources[3], start, *other))
        w_back = held([own[3], swap(last)])

    hops, pooled, got, shares = ({}, {}, {}, {})
    slots = chunks + LAG * (phases - 1)

    def plan(slot):
        chunk = slot - LAG * (phases - 1)
        send = slot < chunks + LAG * (phases - 2)
        pool_chunk = chunk if chunk >= 0 else None
        return (send, pool_chunk, pool_chunk is not None and not send)

    def entering(slot):
        inputs = waiting[slot // 2 : slot // 2 + 1] + [hops[at] for at in (slot - LAG,) if at >= 0]
        return (slot < chunks, slot >= LAG, inputs, [smem_spec()] + [vmem_spec()] * len(inputs))

    def project(slot, token):
        has_wait, has_recv, inputs, specs = entering(slot)
        *sent, token = call(
            functools.partial(project_kernel, slot, has_wait, has_recv),
            [jax.ShapeDtypeStruct((count, MSG_COLS), BF16)] * CHIPS,
            (pos, *inputs, gain, *w_in),
            specs + [vmem_spec()] * 7,
            (pltpu.VMEM((CHIPS, count, KV_AT), BF16),),
            10,
            token,
            (),
            (slot, chunks),
        )
        got[slot] = exchange(sent)
        return token

    def attend(slot, token):
        _, pool_chunk, early_pool = plan(slot)
        rows = 16 if early_pool else count
        if slot == slots - 1:
            for m in range(phases - 1):
                shares[m] = lax.ppermute(pooled[2 * m + 1], "phase", [(phases - 1, m)])
        *sent, token = call(
            functools.partial(attend_kernel, features, slot, chunks, pool_chunk if early_pool else None),
            [jax.ShapeDtypeStruct((rows, block), BF16)] * CHIPS,
            (pos, *got[slot], table, *w_back),
            [smem_spec()] + [vmem_spec()] * (CHIPS + 3),
            (pltpu.VMEM((CHIPS, rows, block), BF16),),
            10,
            token,
            list(shares.values()) + (waiting[phases - 1 :] if slot == 2 else []),
            (slot, chunks),
        )
        got[slot] = exchange(sent)
        return token

    def finish(slot, token):
        chunk = chunks - 1
        *sent, token = call(
            functools.partial(finish_kernel, phases - 1, chunk, owner_at),
            [jax.ShapeDtypeStruct((16, block), BF16)] * CHIPS,
            (pos, hops[slot - LAG], *got[slot], table, pooled[chunk - 1], *shares.values()),
            [smem_spec()] + [vmem_spec()] * (CHIPS + 3 + len(shares)),
            (pltpu.VMEM((32, block), BF16),),
            token=token,
        )
        return sent

    def update(slot, token):
        has_wait, has_recv, inputs, specs = entering(slot)
        send, pool_chunk, early_pool = plan(slot)
        outs = [jax.ShapeDtypeStruct((count, block), BF16)] * send
        before = []
        if pool_chunk is not None:
            odd = pool_chunk % 2 == 1
            outs.append(jax.ShapeDtypeStruct((2, 16, block) if odd else (16, block), BF16))
            before = [pooled[pool_chunk - 1]] if odd else []
        *out, token = call(
            functools.partial(update_kernel, slot, has_wait, has_recv, send, pool_chunk, early_pool),
            outs,
            (pos, *inputs, *got[slot], table, *before),
            specs + [vmem_spec()] * (CHIPS + 1 + len(before)),
            token=token,
            span=(slot, chunks),
        )
        if send:
            hops[slot] = lax.ppermute(out.pop(0), "phase", [(p, (p + 1) % phases) for p in range(phases)])
        if pool_chunk is not None:
            pooled[pool_chunk] = out.pop(0)
        return token

    def move_down(token):
        above, _ = lax.optimization_barrier((waiting[-1], token))
        waiting.append(lower(above))

    for step in range(slots):
        with jax.named_scope("project"):
            token = project(step, token)
        if step == 0:
            move_down(token)
        if step > 0:
            with jax.named_scope("update"):
                token = update(step - 1, token)
        if step == 1:
            move_down(token)
        with jax.named_scope("attend"):
            token = attend(step, token)
        if step == 0:
            move_down(token)

    with jax.named_scope("deliver"):
        values = finish(slots - 1, token)
        final = [homewards(values[k], k) for k in ORDER]
        (result,) = call(
            deliver_kernel,
            [jax.ShapeDtypeStruct((16, cols_here), BF16)],
            (pos, *final),
            [smem_spec()] + [vmem_spec()] * 4,
        )
    return result.reshape(1, 2, 8, cols_here)


def solution(mesh):
    in_specs = (
        P("dp", "phase", None, "mp"),
        P(None, "phase", None),
        P("dp", None, None),
        P("dp", "phase", None, None),
        P("phase", None),
        P("phase", "dp", "mp"),
        P("phase", "dp", "mp"),
        P("phase", "dp", "mp"),
        P("phase", "dp", "mp"),
    )
    out_specs = P("dp", "phase", None, "mp")
    square = mesh.shape["dp"] == CHIPS and mesh.shape["mp"] == 2 and mesh.shape["phase"] == 4
    shards = chip_shards if square else general_shards
    return jax.shard_map(shards, mesh=mesh, in_specs=in_specs, out_specs=out_specs, check_vma=False)
```

```python
import functools

import jax
import jax.numpy as jnp
from jax import lax
from jax.experimental import pallas as pl
from jax.experimental.pallas import tpu as pltpu
from jax.sharding import PartitionSpec as P

D = 8192
HD = 128
QH = 32
KVH = 4
SEGS = 6
PH = 3


NORM_EPS = 1e-05


def from_behind(value, axis, steps):
    count = lax.axis_size(axis)
    initial, last = (max(0, -steps), min(count, count - steps))
    return lax.ppermute(value, axis, [(source, source + steps) for source in range(initial, last)])


def broadcast(value, axis, root):
    mine = lax.axis_index(axis) == root
    return lax.psum(jnp.where(mine, value, jnp.zeros_like(value)), axis)


def bucket_ranks(labels, buckets):
    hits_table = (labels[..., None] == jnp.arange(buckets, dtype=jnp.int32)).astype(jnp.int32)
    earlier = jnp.cumsum(hits_table, axis=-2) - hits_table
    return jnp.sum(earlier * hits_table, axis=-1)


def attend_heads(query, key_sel, value_sel, segments):
    head_dim = query.shape[2]
    scores = jnp.einsum("qhd,khd->hqk", query, key_sel, preferred_element_type=jnp.float32)
    scores = scores * head_dim ** (-0.5)
    places = jnp.arange(query.shape[0], dtype=jnp.int32)
    allowed = (segments[:, None] == segments[None, :]) & (places[None, :] <= places[:, None])
    scores = jnp.where(allowed[None, :, :], scores, -jnp.inf)
    row_top = jnp.max(scores, axis=2, keepdims=True)
    weights = jnp.exp(scores - row_top)
    probabilities = (weights / jnp.sum(weights, axis=2, keepdims=True)).astype(jnp.bfloat16)
    mixed = jnp.einsum("hqk,khd->qhd", probabilities, value_sel, preferred_element_type=jnp.float32)
    return mixed.astype(jnp.bfloat16).reshape(query.shape[0], -1)


def general_shards(prompt_rows, row_dest, segment_ids, owner, gain, w_query, w_key, w_value, w_out):
    dp_count = lax.axis_size("dp")
    phase_count = lax.axis_size("phase")
    group_here = lax.axis_index("dp")
    phase_here = lax.axis_index("phase")
    part_here = lax.axis_index("mp")
    halves_here = prompt_rows.shape[1]
    half_rows = prompt_rows.shape[2]
    feature_cols = prompt_rows.shape[3]
    batch_rows = halves_here * half_rows
    capacity = half_rows // min(dp_count, 4)
    half_index = jnp.arange(halves_here, dtype=jnp.int32)[:, None]
    dest_group = row_dest // half_rows
    dest_ranks = bucket_ranks(dest_group, dp_count)
    own_groups = lax.dynamic_index_in_dim(dest_group, group_here, 0, keepdims=False)
    own_ranks = lax.dynamic_index_in_dim(dest_ranks, group_here, 0, keepdims=False)
    send_at = own_groups * capacity + own_ranks
    outgoing = (
        jnp.zeros((halves_here, dp_count * capacity, feature_cols), jnp.bfloat16)
        .at[half_index, send_at]
        .set(prompt_rows[0])
    )
    incoming = lax.all_to_all(
        outgoing.reshape(halves_here, dp_count, capacity, feature_cols),
        "dp",
        split_axis=1,
        concat_axis=1,
        tiled=True,
    )
    source_ids = jnp.arange(dp_count, dtype=jnp.int32)[:, None, None]
    where_from = jnp.transpose(source_ids * capacity + dest_ranks, (1, 0, 2)).reshape(
        halves_here, -1
    )
    target = jnp.where(dest_group == group_here, row_dest % half_rows, half_rows)
    target = jnp.transpose(target, (1, 0, 2)).reshape(halves_here, -1)
    arrived = incoming.reshape(halves_here, dp_count * capacity, feature_cols)[
        half_index, where_from
    ]
    own_halves = (
        jnp.zeros((halves_here, half_rows, feature_cols), jnp.bfloat16)
        .at[half_index, target]
        .set(arrived, mode="drop")
    )
    own_batch = own_halves.reshape(batch_rows, feature_cols)
    waiting = lax.all_gather(own_batch, "phase", axis=0, tiled=True).reshape(
        phase_count, batch_rows, feature_cols
    )
    query_rows, key_rows, value_rows, back_rows = (
        lax.all_gather(w_query[0], "dp", axis=0, tiled=True),
        lax.all_gather(w_key[0], "dp", axis=0, tiled=True),
        lax.all_gather(w_value[0], "dp", axis=0, tiled=True),
        lax.all_gather(w_out[0], "dp", axis=0, tiled=True),
    )
    query_cols = query_rows.shape[1]
    pair_cols = key_rows.shape[1]
    w_proj = jnp.concatenate([query_rows, key_rows, value_rows], axis=1)
    proj_cols = w_proj.shape[1]
    heads_here = query_cols // HD
    group_size = QH // KVH
    key_heads = (part_here * heads_here + jnp.arange(heads_here, dtype=jnp.int32)) // group_size
    gain_row = gain[0]
    segment_table = segment_ids[0]
    last_phase = phase_count - 1
    prompt_numbers = jnp.arange(SEGS, dtype=jnp.int32)

    def advance(tick_index, loop_state):
        current, pooled = loop_state
        batch_index = tick_index - phase_here
        active = (batch_index >= 0) & (batch_index < phase_count)
        batch_slot = jnp.clip(batch_index, 0, phase_count - 1)
        fresh_rows = lax.dynamic_index_in_dim(
            waiting, jnp.clip(tick_index, 0, phase_count - 1), 0, keepdims=False
        )
        tok_rows = jnp.where(phase_here == 0, fresh_rows, current)
        tok_segments = lax.dynamic_index_in_dim(segment_table, batch_slot, 0, keepdims=False)
        tok_float = tok_rows.astype(jnp.float32)
        whole_rows = lax.all_gather(tok_rows, "mp", axis=1, tiled=True)
        whole_float = whole_rows.astype(jnp.float32)
        squares = jnp.sum(whole_float * whole_float, axis=1)
        projected = lax.cond(
            active,
            lambda: jnp.dot(
                (whole_float * gain_row[None, :]).astype(jnp.bfloat16),
                w_proj,
                preferred_element_type=jnp.float32,
            ),
            lambda: jnp.zeros((batch_rows, proj_cols), jnp.float32),
        )
        qkv_rows = (projected * lax.rsqrt(squares / D + NORM_EPS)[:, None]).astype(jnp.bfloat16)
        query = qkv_rows[:, :query_cols].reshape(batch_rows, heads_here, HD)
        key_own = qkv_rows[:, query_cols : query_cols + pair_cols]
        value_own = qkv_rows[:, query_cols + pair_cols :]
        key_all, value_all = (
            lax.all_gather(key_own, "mp", axis=1, tiled=True),
            lax.all_gather(value_own, "mp", axis=1, tiled=True),
        )
        key_sel = jnp.take(key_all.reshape(batch_rows, KVH, HD), key_heads, axis=1)
        value_sel = jnp.take(value_all.reshape(batch_rows, KVH, HD), key_heads, axis=1)
        mixed_own = attend_heads(query, key_sel, value_sel, tok_segments)
        mixed = lax.all_gather(mixed_own, "mp", axis=1, tiled=True)
        updated = lax.cond(
            active,
            lambda: (
                tok_float + jnp.dot(mixed, back_rows, preferred_element_type=jnp.float32)
            ).astype(jnp.bfloat16),
            lambda: tok_rows,
        )
        segment_hits = tok_segments[None, :] == prompt_numbers[:, None]
        segment_sums = jnp.dot(
            segment_hits.astype(jnp.bfloat16), updated, preferred_element_type=jnp.float32
        )
        counts = jnp.sum(segment_hits.astype(jnp.float32), axis=1)
        segment_means = segment_sums / counts[:, None]
        store_here = active & (phase_here == last_phase)
        stored = lax.dynamic_index_in_dim(pooled, batch_slot, 0, keepdims=False)
        pooled = lax.dynamic_update_index_in_dim(
            pooled, jnp.where(store_here, segment_means, stored), batch_slot, 0
        )
        passed = from_behind(updated, "phase", 1)
        return (passed, pooled)

    start_state = (
        jnp.zeros((batch_rows, feature_cols), jnp.bfloat16),
        jnp.zeros((phase_count, SEGS, feature_cols), jnp.float32),
    )
    current, pooled = lax.fori_loop(0, phase_count + phase_count - 1, advance, start_state)
    shared = broadcast(pooled.astype(jnp.bfloat16), "phase", last_phase)
    own_prompts = lax.dynamic_index_in_dim(shared, phase_here, 0, keepdims=False).reshape(
        halves_here, PH, feature_cols
    )
    owner_ids = owner[0, :, :, 0]
    return_cap = max(2, PH // min(dp_count, 4))
    send_slots = owner_ids * return_cap + bucket_ranks(owner_ids, dp_count)
    parcel = (
        jnp.zeros((halves_here, dp_count * return_cap, feature_cols), jnp.bfloat16)
        .at[half_index, send_slots]
        .set(own_prompts)
    )
    returned = lax.all_to_all(
        parcel.reshape(halves_here, dp_count, return_cap, feature_cols),
        "dp",
        split_axis=1,
        concat_axis=1,
        tiled=True,
    )
    return returned.reshape(1, halves_here, dp_count * return_cap, feature_cols)


LAG = 2
CHIPS = 4
GROUP_Q = QH // KVH
Q_COLS = GROUP_Q * HD
KV_AT = Q_COLS + 2 * HD
MSG_COLS = KV_AT + 128
RANKS = 8
ORDER = (3, 1, 2, 0)
TABLE_ROW = 6
F32 = jnp.float32
BF16 = jnp.bfloat16


def vmem_spec():
    return pl.BlockSpec(memory_space=pltpu.VMEM)


def smem_spec():
    return pl.BlockSpec(memory_space=pltpu.SMEM)


def hbm_spec():
    return pl.BlockSpec(memory_space=pl.ANY)


def call(kernel, outs, args, specs, scratch=(), limit=6, token=None, after=(), span=None):
    count = len(args)
    others = len(after)

    def body(*refs):
        first = count + 1 + others
        at = first + len(outs)
        refs[at][...] = jnp.zeros(refs[at].shape, F32)

        def run():
            kernel(*refs[:count], *refs[first:at], *refs[at + 1 :])

        if span is None:
            run()
        else:
            slot, chunks = span
            chunk = slot - LAG * refs[0][1]
            pl.when((chunk >= 0) & (chunk < chunks))(run)

    outs = list(outs)
    if token is not None:
        outs_all = outs + [jax.ShapeDtypeStruct((8, 128), F32)]
        args, specs = ((*args, token, *after), [*specs] + [hbm_spec()] * (1 + others))
    else:
        outs_all = outs
    return pl.pallas_call(
        kernel if token is None else body,
        out_shape=outs_all,
        in_specs=specs,
        out_specs=[vmem_spec()] * len(outs_all),
        scratch_shapes=list(scratch),
        compiler_params=pltpu.CompilerParams(vmem_limit_bytes=limit * 1024 * 1024),
    )(*args)


def dot(a, b):
    return jnp.dot(a, b, preferred_element_type=F32)


def lane(start, size):
    return pl.ds(pl.multiple_of(start, size), size)


def iota(rows, cols, axis):
    return lax.broadcasted_iota(jnp.int32, (rows, cols), axis)


def as_column(row):
    count = row.shape[1]
    diagonal = iota(count, count, 0) == iota(count, count, 1)
    return jnp.sum(jnp.where(diagonal, row, 0), axis=1, keepdims=True)


def marks(hits):
    return hits.astype(F32).astype(BF16)


def pack_kernel(pos_ref, rows_ref, dest_ref, table_ref, *out_refs):
    chip = pos_ref[0]
    dest = dest_ref[pl.ds(chip, 1), :]
    count = dest.shape[1]
    half = count // 2
    group_row = dest // half
    group_col = as_column(group_row)
    source, here = (iota(count, count, 0), iota(count, count, 1))
    before = (group_col == group_row) & (source // half == here // half) & (source < here)
    rank = jnp.sum(jnp.where(before, 1, 0), axis=0, keepdims=True)
    target = group_row * (2 * RANKS) + (iota(1, count, 1) // half) * RANKS + rank
    width = out_refs[0].shape[1]
    message_row = iota(4 * RANKS, width, 0)
    for k in range(CHIPS):
        turn = chip ^ k
        core, block = (turn >> 1, turn & 1)
        pick = marks(iota(4 * RANKS, count, 0) + core * (4 * RANKS) == target)
        rows = dot(pick, rows_ref[:, lane(block * width, width)])
        rows = jnp.where(message_row == TABLE_ROW, table_ref[...], rows)
        out_refs[k][...] = rows.astype(BF16)


def unpack_kernel(pos_ref, m0, m1, m2, m3, dest_ref, out_ref, table_ref):
    chip, core = (pos_ref[0], pos_ref[2])
    count = dest_ref.shape[1]
    half = count // 2
    turn = 2 * core + (chip & 1)
    total = jnp.zeros(out_ref.shape, F32)
    table = jnp.zeros(table_ref.shape, F32)
    above, across = (iota(count, count, 0), iota(count, count, 1))
    for k, ref in enumerate((m0, m1, m2, m3)):
        loader = turn ^ k
        dest_row = dest_ref[pl.ds(loader, 1), :]
        group_row = dest_row // half
        group_col = as_column(group_row)
        earlier = (group_col == group_row) & (above // half == across // half) & (across < above)
        rank = jnp.sum(jnp.where(earlier, 1, 0), axis=1, keepdims=True)
        at = (group_col - 2 * core) * (2 * RANKS) + (iota(count, 1, 0) // half) * RANKS + rank
        from_message = marks(iota(count, 4 * RANKS, 1) == at)
        slot = (group_row - 2 * core) * count + (iota(1, count, 1) // half) * half + dest_row % half
        to_slot = marks(iota(2 * count, count, 0) == slot)
        rows = ref[...]
        total += dot(dot(to_slot, from_message).astype(BF16), rows)
        mine = (loader >> 1) == core
        table += jnp.where(mine, rows[TABLE_ROW : TABLE_ROW + 1].astype(F32), 0.0)
    out_ref[...] = total.astype(BF16)
    table_ref[...] = table


def added(messages):
    total = messages[0][...].astype(F32)
    for ref in messages[1:]:
        total += ref[...].astype(F32)
    return total


def stage_kernel(*refs):
    *refs, sems = refs
    count = len(refs) // 2
    copies = [pltpu.make_async_copy(refs[i], refs[count + i], sems.at[i]) for i in range(count)]
    for copy in copies:
        copy.start()
    for copy in copies:
        copy.wait()


def pick_rows(slot, pos_ref, wait_ref, recv_ref):
    if wait_ref is None:
        return recv_ref[...]
    count = wait_ref.shape[0] // 2
    at = (slot % 2) * count
    waiting = wait_ref[at : at + count]
    if recv_ref is None:
        return waiting
    return jnp.where(pos_ref[1] == 0, waiting, recv_ref[...])


def project_kernel(slot, has_wait, has_recv, pos_ref, *refs):
    refs = list(refs)
    wait_ref = refs.pop(0) if has_wait else None
    recv_ref = refs.pop(0) if has_recv else None
    gain_ref, *refs = refs
    sources, out_refs, results_ref = (refs[:6], refs[6:10], refs[10])
    chip, core = (pos_ref[0], pos_ref[2])
    rows = pick_rows(slot, pos_ref, wait_ref, recv_ref).astype(F32)
    depth = rows.shape[1]
    gated = (rows * gain_ref[:, lane(chip * depth, depth)]).astype(BF16)
    squares = jnp.sum(rows * rows, axis=1, keepdims=True)
    high = squares.astype(BF16).astype(F32)
    tail = jnp.where(iota(rows.shape[0], 128, 1) < 64, high, squares - high).astype(BF16)

    for at, source in enumerate(sources):
        part, i = (core if at < 3 else 1 - core, at % 3)
        places = [(2 * part + j) ^ pos_ref[0] for j in range(2)]
        step = min(source.shape[2], 1024)
        for start in range(0, source.shape[2], step):
            result = dot(gated, source[0, :, start : start + step]).astype(BF16)
            if i == 0:
                inside = start % Q_COLS
                results_ref[places[start // Q_COLS], :, inside : inside + step] = result
            else:
                inside = Q_COLS + (i - 1) * HD
                for j in range(2):
                    results_ref[places[j], :, inside : inside + HD] = result[:, j * HD : (j + 1) * HD]
    for k, out_ref in enumerate(out_refs):
        out_ref[:, :KV_AT] = results_ref[k]
        out_ref[:, KV_AT:] = tail


def means(table_ref, chunk, count, rows):
    segment = table_ref[:, chunk * 128 : chunk * 128 + count].astype(jnp.int32)
    hits = (segment == iota(16, count, 0)) & (iota(16, count, 0) < SEGS)
    counts = jnp.sum(jnp.where(hits, 1.0, 0.0), axis=1, keepdims=True)
    return dot(marks(hits), rows) / jnp.maximum(counts, 1.0)


def attend_kernel(features, slot, chunks, pool_chunk, pos_ref, *refs):
    messages, (table_ref, own_ref, other_ref) = (refs[:CHIPS], refs[CHIPS : CHIPS + 3])
    out_refs, results_ref = (refs[CHIPS + 3 : -1], refs[-1])
    core = pos_ref[2]
    sums = added(messages)
    count = sums.shape[0]
    tail = sums[:, KV_AT:]
    squares = tail[:, 0:1] + tail[:, 64:65]
    scaled = (sums[:, :KV_AT] * lax.rsqrt(squares / features + NORM_EPS)).astype(BF16)
    query = jnp.concatenate([scaled[:, h * HD : (h + 1) * HD] for h in range(GROUP_Q)], axis=0)
    key = scaled[:, Q_COLS : Q_COLS + HD]
    value = scaled[:, Q_COLS + HD :]
    scores = lax.dot_general(query, key, (((1,), (1,)), ((), ())), preferred_element_type=F32)
    scores = (scores * HD ** (-0.5)).reshape(GROUP_Q, count, count)
    chunk = jnp.clip(slot - LAG * pos_ref[1], 0, chunks - 1)
    segment = table_ref[:, lane(chunk * 128, 128)][:, :count].astype(jnp.int32)
    allowed = (as_column(segment) == segment) & (iota(count, count, 1) <= iota(count, count, 0))
    scores = jnp.where(allowed[None], scores, -jnp.inf)
    top = jnp.max(scores, axis=2, keepdims=True)
    weights = jnp.exp(scores - top)
    probs = (weights / jnp.sum(weights, axis=2, keepdims=True)).astype(BF16)
    mixed = dot(probs.reshape(GROUP_Q * count, count), value).astype(BF16)
    mixed = jnp.concatenate([mixed[h * count : (h + 1) * count] for h in range(GROUP_Q)], axis=1)
    if pool_chunk is not None:
        mixed = means(table_ref, pool_chunk, count, mixed).astype(BF16)
    step = own_ref.shape[2] // 4
    for part, source in ((core, own_ref), (1 - core, other_ref)):
        places = [(2 * part + j) ^ pos_ref[0] for j in range(2)]
        for at in range(4):
            result = dot(mixed, source[0, :, at * step : (at + 1) * step]).astype(BF16)
            results_ref[places[at // 2], :, (at % 2) * step : (at % 2 + 1) * step] = result
    for k, out_ref in enumerate(out_refs):
        out_ref[...] = results_ref[k]


def update_kernel(slot, has_wait, has_recv, send, pool_chunk, pooled_sums, pos_ref, *refs):
    refs = list(refs)
    wait_ref = refs.pop(0) if has_wait else None
    recv_ref = refs.pop(0) if has_recv else None
    messages, refs = (refs[:CHIPS], refs[CHIPS:])
    table_ref = refs.pop(0)
    before_ref = refs.pop(0) if pool_chunk is not None and pool_chunk % 2 else None
    rows = pick_rows(slot, pos_ref, wait_ref, recv_ref)
    if pooled_sums:
        total = means(table_ref, pool_chunk, rows.shape[0], rows)
    else:
        total = rows.astype(F32)
    total += added(messages)
    hidden = total.astype(BF16)
    if send:
        refs.pop(0)[...] = hidden
    if pool_chunk is not None:
        pooled = hidden if pooled_sums else means(table_ref, pool_chunk, rows.shape[0], hidden).astype(BF16)
        if before_ref is None:
            refs.pop(0)[...] = pooled
        else:
            out_ref = refs.pop(0)
            out_ref[0] = before_ref[...]
            out_ref[1] = pooled


def parcels(owner_at, pos_ref, rows, table_ref, out_refs):
    chip, core = (pos_ref[0], pos_ref[2])
    count = rows.shape[0]
    own_row = table_ref[:, owner_at : owner_at + count].astype(jnp.int32) - 1
    own_col = as_column(own_row)
    above, across = (iota(count, count, 0), iota(count, count, 1))
    same = (above // 16 == across // 16) & ((above % 16 >= PH) == (across % 16 >= PH))
    earlier = (own_col == own_row) & same & (above < across)
    rank = jnp.sum(jnp.where(earlier, 1, 0), axis=0, keepdims=True)
    place = iota(1, count, 1)
    half = jnp.where(place % 16 >= PH, 1, 0)
    slot = half * 8 + (2 * core + place // 16) * 2 + rank
    turn = 2 * core + (chip & 1)
    for k, out_ref in enumerate(out_refs):
        pick = marks((iota(16, count, 0) == slot) & (own_row == (turn ^ k)))
        out_ref[...] = dot(pick, rows).astype(BF16)


def finish_kernel(last, chunk, owner_at, pos_ref, recv_ref, m0, m1, m2, m3, table_ref, before_ref, *refs):
    *refs, pooled_ref = refs
    shares, out_refs = (refs[:-CHIPS], refs[-CHIPS:])
    count = before_ref.shape[0]
    phase = pos_ref[1]

    @pl.when(phase == last)
    def _():
        rows = recv_ref[...]
        total = means(table_ref, chunk, rows.shape[0], rows) + added((m0, m1, m2, m3))
        pooled_ref[:count] = before_ref[...]
        pooled_ref[count:] = total.astype(BF16)

    for m, ref in enumerate(shares):

        @pl.when(phase == m)
        def _(ref=ref):
            pooled_ref[:count] = ref[0]
            pooled_ref[count:] = ref[1]

    parcels(owner_at, pos_ref, pooled_ref[...], table_ref, out_refs)


def deliver_kernel(pos_ref, m0, m1, m2, m3, out_ref):
    chip = pos_ref[0]
    width = m0.shape[1]
    out_ref[...] = jnp.zeros_like(out_ref)
    for k, ref in zip(ORDER, (m0, m1, m2, m3)):
        cols = lane(((chip ^ k) & 1) * width, width)
        out_ref[:, cols] = out_ref[:, cols] + ref[...]


def chip_shards(prompt_rows, row_dest, segment_ids, owner, gain, w_query, w_key, w_value, w_out):
    chip, phase, core = (lax.axis_index("dp"), lax.axis_index("phase"), lax.axis_index("mp"))
    phases = lax.axis_size("phase")
    pos = jnp.stack([chip, phase, core]).astype(jnp.int32)
    halves, half_rows, cols_here = prompt_rows.shape[1:]
    batch = halves * half_rows
    features = 2 * cols_here
    block = features // CHIPS
    count = batch
    square = [(e, k) for e in range(CHIPS) for k in range(2)]

    def crosswise(value, k):
        pairs = [(2 * e + m, 2 * (2 * m + ((e ^ k) & 1)) + ((e ^ k) >> 1)) for e, m in square]
        return lax.ppermute(value, ("dp", "mp"), pairs)

    def homewards(value, k):
        pairs = [(2 * e + c, 2 * ((2 * c + (e & 1)) ^ k) + (e >> 1)) for e, c in square]
        return lax.ppermute(value, ("dp", "mp"), pairs)

    def exchange(values):
        got = [values[0]]
        for k in (3, 1, 2):
            got.append(lax.ppermute(values[k], "dp", [(e, e ^ k) for e in range(CHIPS)]))
        return got

    def lower(value):
        return lax.ppermute(value, "phase", [(p, p - 1) for p in range(1, phases)])

    def swap(value):
        return lax.ppermute(value, "mp", [(0, 1), (1, 0)])

    with jax.named_scope("packing"):
        parity = chip % 2
        chunks = 2 * phases
        owner_at = chunks * 128
        table = jnp.zeros((phases, 2, 128), F32)
        numbers = segment_ids[0][:, None, :].astype(F32)
        table = lax.dynamic_update_slice(table, numbers, (0, parity, 0)).reshape(1, -1)
        owners = (owner.reshape(1, -1) + 1).astype(F32)
        last = lax.dynamic_update_slice(jnp.zeros((1, block - owner_at), F32), owners, (0, 16 * parity))
        table = jnp.concatenate([table, last], axis=1)
        dest = row_dest.reshape(CHIPS, batch)
        own = (w_query, w_key, w_value, w_out)
        sources, *_ = lax.optimization_barrier((own, pos, table, dest))
        *own, token = call(
            stage_kernel,
            [pltpu.VMEM(w.shape, BF16) for w in own],
            [pltpu.with_memory_space_constraint(w, pltpu.HBM) for w in own],
            [hbm_spec()] * 4,
            (pltpu.SemaphoreType.DMA((4,)),),
            token=jnp.zeros((8, 128), F32),
        )
        *packed, token = call(
            pack_kernel,
            [jax.ShapeDtypeStruct((4 * RANKS, block), BF16)] * CHIPS,
            (pos, prompt_rows.reshape(batch, cols_here), dest, table),
            [smem_spec()] + [vmem_spec()] * 3,
            token=token,
        )
        arrived = [crosswise(value, k) for k, value in enumerate(packed)]
        start, table, token = call(
            unpack_kernel,
            [jax.ShapeDtypeStruct((2 * batch, block), BF16), jax.ShapeDtypeStruct((1, block), F32)],
            (pos, *arrived, dest),
            [smem_spec()] + [vmem_spec()] * 5,
            token=token,
        )
        waiting = [start]

    with jax.named_scope("weights"):

        def held(values):
            return [pltpu.with_memory_space_constraint(value, pltpu.VMEM) for value in values]

        other = [swap(w) for w in sources[:3]]
        w_in = held([*own[:3], *other])
        last, *_ = lax.optimization_barrier((sources[3], start, *other))
        w_back = held([own[3], swap(last)])

    hops, pooled, got, shares = ({}, {}, {}, {})
    slots = chunks + LAG * (phases - 1)

    def plan(slot):
        chunk = slot - LAG * (phases - 1)
        send = slot < chunks + LAG * (phases - 2)
        pool_chunk = chunk if chunk >= 0 else None
        return (send, pool_chunk, pool_chunk is not None and not send)

    def entering(slot):
        inputs = waiting[slot // 2 : slot // 2 + 1] + [hops[at] for at in (slot - LAG,) if at >= 0]
        return (slot < chunks, slot >= LAG, inputs, [smem_spec()] + [vmem_spec()] * len(inputs))

    def project(slot, token):
        has_wait, has_recv, inputs, specs = entering(slot)
        *sent, token = call(
            functools.partial(project_kernel, slot, has_wait, has_recv),
            [jax.ShapeDtypeStruct((count, MSG_COLS), BF16)] * CHIPS,
            (pos, *inputs, gain, *w_in),
            specs + [vmem_spec()] * 7,
            (pltpu.VMEM((CHIPS, count, KV_AT), BF16),),
            10,
            token,
            span=(slot, chunks),
        )
        got[slot] = exchange(sent)
        return token

    def attend(slot, token):
        _, pool_chunk, early_pool = plan(slot)
        rows = 16 if early_pool else count
        if slot == slots - 1:
            for m in range(phases - 1):
                shares[m] = lax.ppermute(pooled[2 * m + 1], "phase", [(phases - 1, m)])
        *sent, token = call(
            functools.partial(attend_kernel, features, slot, chunks, pool_chunk if early_pool else None),
            [jax.ShapeDtypeStruct((rows, block), BF16)] * CHIPS,
            (pos, *got[slot], table, *w_back),
            [smem_spec()] + [vmem_spec()] * (CHIPS + 3),
            (pltpu.VMEM((CHIPS, rows, block), BF16),),
            10,
            token,
            list(shares.values()),
            (slot, chunks),
        )
        got[slot] = exchange(sent)
        return token

    def finish(slot, token):
        chunk = chunks - 1
        *sent, token = call(
            functools.partial(finish_kernel, phases - 1, chunk, owner_at),
            [jax.ShapeDtypeStruct((16, block), BF16)] * CHIPS,
            (pos, hops[slot - LAG], *got[slot], table, pooled[chunk - 1], *shares.values()),
            [smem_spec()] + [vmem_spec()] * (CHIPS + 3 + len(shares)),
            (pltpu.VMEM((32, block), BF16),),
            token=token,
        )
        return sent

    def update(slot, token):
        has_wait, has_recv, inputs, specs = entering(slot)
        send, pool_chunk, early_pool = plan(slot)
        outs = [jax.ShapeDtypeStruct((count, block), BF16)] * send
        before = []
        if pool_chunk is not None:
            odd = pool_chunk % 2 == 1
            outs.append(jax.ShapeDtypeStruct((2, 16, block) if odd else (16, block), BF16))
            before = [pooled[pool_chunk - 1]] if odd else []
        *out, token = call(
            functools.partial(update_kernel, slot, has_wait, has_recv, send, pool_chunk, early_pool),
            outs,
            (pos, *inputs, *got[slot], table, *before),
            specs + [vmem_spec()] * (CHIPS + 1 + len(before)),
            token=token,
            span=(slot, chunks),
        )
        if send:
            hops[slot] = lax.ppermute(out.pop(0), "phase", [(p, (p + 1) % phases) for p in range(phases)])
        if pool_chunk is not None:
            pooled[pool_chunk] = out.pop(0)
        return token

    for step in range(slots):
        if step % 2 == 0 and step < chunks - 2:
            waiting.append(lower(waiting[-1]))
        with jax.named_scope("project"):
            token = project(step, token)
        if step > 0:
            with jax.named_scope("update"):
                token = update(step - 1, token)
        with jax.named_scope("attend"):
            token = attend(step, token)

    with jax.named_scope("deliver"):
        values = finish(slots - 1, token)
        final = [homewards(values[k], k) for k in ORDER]
        (result,) = call(
            deliver_kernel,
            [jax.ShapeDtypeStruct((16, cols_here), BF16)],
            (pos, *final),
            [smem_spec()] + [vmem_spec()] * 4,
        )
    return result.reshape(1, 2, 8, cols_here)


def solution(mesh):
    in_specs = (
        P("dp", "phase", None, "mp"),
        P(None, "phase", None),
        P("dp", None, None),
        P("dp", "phase", None, None),
        P("phase", None),
        P("phase", "dp", "mp"),
        P("phase", "dp", "mp"),
        P("phase", "dp", "mp"),
        P("phase", "dp", "mp"),
    )
    out_specs = P("dp", "phase", None, "mp")
    square = mesh.shape["dp"] == CHIPS and mesh.shape["mp"] == 2 and mesh.shape["phase"] == 4
    shards = chip_shards if square else general_shards
    return jax.shard_map(shards, mesh=mesh, in_specs=in_specs, out_specs=out_specs, check_vma=False)
```
